256 devices in a mesh: ctx: 32 (over z_lo, y, core), wsh: 8 (over z_hi, x).
Axes of the slice: x: 4, y: 4, z: 8 (z_hi: 2, z_lo: 4; z = z_hi * 4 + z_lo), core: 2. Of those that a mesh axis runs over, the one named last changes fastest.
Arguments:
- tokens: bfloat16 [8, 16384, 768], P('wsh', 'ctx'), may hold values from -6 to 6
- teacher: bfloat16 [8, 16384, 768], P('wsh', 'ctx'), may hold values from -6 to 6
- clusters: int32 [8, 12, 16384], P('wsh', None, 'ctx'), may hold values from 0 to 127, as said below
- segments: int32 [8, 16384], P('wsh', 'ctx'), may hold values from 0 to 23, never falling along the last dimension, each value on 1 to 2000 neighbouring positions
- counted: int32 [8, 16384], P('wsh', 'ctx'), may hold values from 0 to 1, as said below
- w_qkv: bfloat16 [768, 2304], P('wsh'), may hold values from -0.21875 to 0.21875
- w_out: bfloat16 [768, 768], P('wsh'), may hold values from -0.4375 to 0.4375
- w_up: bfloat16 [768, 3072], P('wsh'), may hold values from -0.21875 to 0.21875
- w_down: bfloat16 [3072, 768], P('wsh'), may hold values from -0.109375 to 0.109375
- norms: bfloat16 [4, 768], P(None, 'wsh'), may hold values from -0.45 to 1.45
Outputs:
- activations: bfloat16 [8, 16384, 768], P('wsh', 'ctx')
- input_grad: float32 [8, 16384, 768], P('wsh', 'ctx')
- loss: float32 [], replicated
- grad_w_qkv: float32 [768, 2304], P('wsh', 'ctx')
- grad_w_out: float32 [768, 768], P('wsh', 'ctx')
- grad_w_up: float32 [768, 3072], P('wsh', 'ctx')
- grad_w_down: float32 [3072, 768], P('wsh', 'ctx')
- grad_norms: float32 [4, 768], P(None, ('ctx', 'wsh'))
The draws below stay inside these ranges and needn't reach their ends.
Inputs may be any that keep to these rules, and one draw needn't show every extreme that they name: `clusters`: for each sequence and head every cluster number is held by exactly 128 tokens, and each aligned block of 512 positions gives exactly 16 tokens to each aligned group of 4 consecutive cluster numbers. `segments`: document numbers never fall along a sequence; a document holds 1 to 2000 tokens. `counted`: 1 on a prefix of each sequence and 0 after it; the prefix covers at least half and at most seven eighths of the sequence.
All inputs are finite; a program needn't handle non-finite values.
Results may differ from the reference program's by a relative error of at most 0.02.
Values may be sent and summed in bfloat16 or wider, within the bound.
A program may use at most 128 MiB of HBM per device.

```python
import math
import jax
import jax.numpy as jnp
import numpy as np
from jax import lax

D = 768
H = 12
HD = 64
FF = 3072
CLUSTER = 128
TOK_DEV = 512
SEQ_LEN = 16384
SEQS = 8
TOKENS = 131072
DOC_MOST = 2000
DOC_COUNT = 24


def draw_clusters(key, part):
    peer_count = SEQ_LEN // TOK_DEV
    share_size = TOK_DEV // peer_count
    per_device = TOK_DEV // CLUSTER
    base_key = jax.random.fold_in(key, 11)
    first_key, second_key = jax.random.split(base_key)
    token_iota = jnp.arange(TOK_DEV, dtype=jnp.int32)
    first_score = jax.random.randint(first_key, (SEQS, H, peer_count, TOK_DEV), 0, 1 << 20, dtype=jnp.int32) * TOK_DEV + token_iota
    first_rank = jnp.argsort(jnp.argsort(first_score, axis=-1), axis=-1).astype(jnp.int32)
    target_dev = first_rank // share_size
    arrival = jnp.arange(peer_count, dtype=jnp.int32)[:, None] * share_size + first_rank % share_size
    second_score = jax.random.randint(second_key, (SEQS, H, peer_count, TOK_DEV), 0, 1 << 20, dtype=jnp.int32) * TOK_DEV + token_iota
    second_rank = jnp.argsort(jnp.argsort(second_score, axis=-1), axis=-1).astype(jnp.int32)
    flat_rank = second_rank.reshape(SEQS, H, peer_count * TOK_DEV)
    gather_index = (target_dev * TOK_DEV + arrival).reshape(SEQS, H, SEQ_LEN)
    picked = jnp.take_along_axis(flat_rank, gather_index, axis=-1)
    return (target_dev.reshape(SEQS, H, SEQ_LEN) * per_device + picked // CLUSTER).astype(jnp.int32)


def draw_counted(key, part):
    cut_point = jax.random.randint(jax.random.fold_in(key, 5), (SEQS, 1), SEQ_LEN // 2, SEQ_LEN - SEQ_LEN // 8 + 1, dtype=jnp.int32)
    return (jnp.arange(SEQ_LEN, dtype=jnp.int32)[None, :] < cut_point).astype(jnp.int32)


def draw_norms(key, part):
    spread_key = jax.random.fold_in(key, 7)
    spread = jax.random.uniform(spread_key, (4, D), jnp.float32, -0.35, 0.35)
    centre_rows = jnp.array([1.0, 0.0, 1.0, 0.0], jnp.float32)[:, None]
    return (centre_rows + spread).astype(jnp.bfloat16)


def shard_levels(key, dims, shards, low, largest):
    gain, own = 1.0, jax.random.fold_in(key, 6)
    for axis_at, shards_of in shards:
        heights = jnp.exp(jax.random.uniform(jax.random.fold_in(own, axis_at), (shards_of,), jnp.float32, low / len(shards), largest / len(shards)))
        gain = gain * jnp.repeat(heights, dims[axis_at] // shards_of).reshape([-1 if axis == axis_at else 1 for axis in range(len(dims))])
    return gain


def length_profile(number_of, total, limit, slope):
    weights = [(1 << 20) // math.isqrt(grade ** slope) + 1 for grade in range(2, number_of + 1)]
    surplus, holding = total - limit - (number_of - 1), [1] * (number_of - 1)
    while surplus > 0:
        movable = [i for i in range(number_of - 1) if holding[i] < limit]
        whole, budget = sum([weights[i] for i in movable]), surplus
        for i in movable:
            addition = min(limit - holding[i], max(1, budget * weights[i] // whole), surplus)
            holding[i] = holding[i] + addition
            surplus = surplus - addition
    return np.array([limit] + holding)


def uneven(stream_key, number_of, total, most, slope):
    if number_of == 2:
        one = jax.random.randint(stream_key, (), max(1, total - most), min(most, total - 1) + 1)
        return jnp.stack([one, total - one])
    lengths = jnp.asarray(length_profile(number_of, total, most, slope), jnp.int32)
    couples = (number_of - 1) // 2
    giver, sink = lengths[1:1 + 2 * couples:2], lengths[2:2 + 2 * couples:2]
    slack = jnp.minimum(giver - 1, most - sink)
    shifted = jax.random.randint(jax.random.fold_in(stream_key, 1), (couples,), 0, 1 << 20) % (slack + 1)
    lengths = lengths.at[1:1 + 2 * couples:2].set(giver - shifted).at[2:2 + 2 * couples:2].set(sink + shifted)
    return lengths[jax.random.permutation(jax.random.fold_in(stream_key, 2), number_of)]


def noise(rng, dims, width, limit, shards=(), kind=jnp.bfloat16):
    factor_of = shard_levels(rng, dims, shards, -0.22, 0.18) if shards else 1.0
    values = jax.random.normal(rng, dims, jnp.float32) * width * factor_of
    return jnp.minimum(jnp.maximum(values, -limit), limit).astype(kind)


def setup_inputs(seed: int = 0) -> dict:
    streams_of = jax.random.split(jax.random.key(seed), 11)
    return {
        "tokens": noise(streams_of[0], (SEQS, SEQ_LEN, D), 1.0, 6.0, ((0, 8), (1, 32))),
        "teacher": noise(streams_of[1], (SEQS, SEQ_LEN, D), 1.0, 6.0, ((0, 8), (1, 32))),
        "clusters": draw_clusters(jax.random.fold_in(streams_of[10], 71), 0),
        "segments": jax.vmap(lambda own: jnp.searchsorted(jnp.cumsum(uneven(own, DOC_COUNT, SEQ_LEN, DOC_MOST, 0)), jnp.arange(SEQ_LEN), side="right"))(jax.random.split(streams_of[3], SEQS)).reshape((SEQS, SEQ_LEN)).astype(jnp.int32),
        "counted": draw_counted(jax.random.fold_in(streams_of[10], 71), 0),
        "w_qkv": noise(streams_of[5], (D, 3 * D), D ** -0.5, 0.21875, ((0, 8),)),
        "w_out": noise(streams_of[6], (D, D), (D // 4) ** -0.5, 0.4375, ((0, 8),)),
        "w_up": noise(streams_of[7], (D, FF), D ** -0.5, 0.21875, ((0, 8),)),
        "w_down": noise(streams_of[8], (FF, D), FF ** -0.5, 0.109375, ((0, 8),)),
        "norms": draw_norms(jax.random.fold_in(streams_of[10], 71), 0),
    }


@jax.custom_vjp
def low(v):
    return lax.optimization_barrier(v.astype(jnp.bfloat16)).astype(jnp.float32)

@jax.custom_vjp
def low_back(v):
    return v

def low_keep(v):
    return (low(v), None)

def low_pass(kept, grad):
    return (grad,)

def back_keep(v):
    return (v, None)

def back_low(kept, grad):
    return (low(grad),)
low.defvjp(low_keep, low_pass)
low_back.defvjp(back_keep, back_low)

def matmul(left, right):
    return jnp.dot(left, right, precision=lax.Precision.HIGHEST)

def layer_norm(values, gain_row, shift_row):
    row_mean = lax.optimization_barrier(jnp.mean(values, axis=-1, keepdims=True))
    centered = values - row_mean
    return centered * lax.rsqrt(lax.optimization_barrier(jnp.mean(centered * centered, axis=-1, keepdims=True)) + 1e-05) * gain_row + shift_row

def gelu_exact(values):
    return jax.nn.gelu(values, approximate=False)

def head_attention(query_rows, key_rows, value_rows, cluster_row, segment_row):
    groups = SEQ_LEN // CLUSTER
    order_index = jnp.argsort(cluster_row)

    def sorted_rows(array):
        return array[order_index].reshape(groups, CLUSTER, HD)
    query_sorted = sorted_rows(query_rows)
    key_sorted = sorted_rows(key_rows)
    value_sorted = sorted_rows(value_rows)
    segment_sorted = segment_row[order_index].reshape(groups, CLUSTER)
    raw_scores = jnp.einsum('gqd,gkd->gqk', query_sorted, key_sorted, precision=lax.Precision.HIGHEST)
    scores = low_back(raw_scores * HD ** (-0.5))
    allowed = segment_sorted[:, :, None] == segment_sorted[:, None, :]
    masked = jnp.where(allowed, scores, -1e+30)
    row_top = lax.optimization_barrier(jnp.max(masked, axis=-1, keepdims=True))
    row_total = lax.optimization_barrier(jnp.sum(jnp.where(allowed, jnp.exp(masked - row_top), 0.0), axis=-1, keepdims=True))
    logsum = row_top + jnp.log(row_total)
    weights = jnp.where(allowed, jnp.exp(scores - logsum), 0.0)
    attended = jnp.einsum('gqk,gkd->gqd', low(weights), value_sorted, precision=lax.Precision.HIGHEST)
    inverse = jnp.argsort(order_index)
    return attended.reshape(SEQ_LEN, HD)[inverse]

def sequence_forward(params, x_seq, cluster_seq, segment_seq):
    w_qkv, w_out, w_up, w_down, norms = params
    qkv = low(low_back(matmul(x_seq, w_qkv)))
    per_head = qkv.reshape(SEQ_LEN, 3, H, HD).transpose(1, 2, 0, 3)

    def one_head(pieces):
        return head_attention(pieces[0], pieces[1], pieces[2], pieces[3], segment_seq)
    heads_out = lax.map(jax.checkpoint(one_head), (per_head[0], per_head[1], per_head[2], cluster_seq))
    attended = low(low_back(heads_out.transpose(1, 0, 2).reshape(SEQ_LEN, D)))
    first_sum = x_seq + low_back(matmul(attended, w_out))
    normed_one = layer_norm(first_sum, norms[0], norms[1])
    upper_rows = low_back(matmul(low(normed_one), w_up))
    active = low(gelu_exact(upper_rows))
    second = normed_one + low_back(matmul(active, w_down))
    return layer_norm(second, norms[2], norms[3])

def reference(tokens, teacher, clusters, segments, counted, w_qkv, w_out, w_up, w_down, norms):
    params = (w_qkv.astype(jnp.float32), w_out.astype(jnp.float32), w_up.astype(jnp.float32), w_down.astype(jnp.float32), norms.astype(jnp.float32))
    x_all = tokens.astype(jnp.float32)
    target = teacher.astype(jnp.float32)
    mask_rows = counted.astype(jnp.float32)
    total_count = jnp.sum(mask_rows)

    def objective(params_in, x_in):

        def one_sequence(pieces):
            return sequence_forward(params_in, pieces[0], pieces[1], pieces[2])
        result = lax.map(jax.checkpoint(one_sequence), (x_in, clusters, segments))
        errors = result - target
        loss_value = jnp.sum(mask_rows * lax.optimization_barrier(jnp.mean(errors * errors, axis=-1))) / total_count
        return (loss_value * (TOKENS * D / 2), (loss_value, result))
    scaled, pullback, extras = jax.vjp(objective, params, x_all, has_aux=True)
    grad_params, grad_input = pullback(jnp.ones((), jnp.float32))
    loss_value, result = extras
    return (result.astype(jnp.bfloat16), grad_input, loss_value, grad_params[0], grad_params[1], grad_params[2], grad_params[3], grad_params[4])
```

```python
import functools
import jax
import jax.numpy as jnp
from jax import lax
from jax.experimental import pallas as pl
from jax.experimental.pallas import tpu as pltpu
from jax.sharding import PartitionSpec as P

CLUSTER = 128
MESH = pl.DeviceIdType.MESH
BF16 = jnp.bfloat16
F32 = jnp.float32


class Place:
    def __init__(self):
        self.ctx = lax.axis_index("ctx")
        self.wsh = lax.axis_index("wsh")
        self.zlo = self.ctx // 8
        self.y = (self.ctx // 2) % 4
        self.core = self.ctx % 2
        self.zhi = self.wsh // 4
        self.x = self.wsh % 4

    def at(self, zlo=None, y=None, core=None, zhi=None, x=None):
        zlo = self.zlo if zlo is None else zlo
        y = self.y if y is None else y
        core = self.core if core is None else core
        zhi = self.zhi if zhi is None else zhi
        x = self.x if x is None else x
        return (zlo * 8 + y * 2 + core, zhi * 4 + x)

    def sibling(self):
        return self.at(core=1 - self.core)

    def x_peer(self, step):
        return self.at(x=(self.x + step) % 4)

    def y_peer(self, step):
        return self.at(y=(self.y + step) % 4)

    def z_far(self):
        return self.at(zhi=1 - self.zhi)

    def doubling(self):
        return (
            self.sibling(),
            self.at(y=self.y + 1 - 2 * (self.y % 2)),
            self.at(y=(self.y + 2) % 4),
            self.at(x=self.x + 1 - 2 * (self.x % 2)),
            self.at(x=(self.x + 2) % 4),
            self.at(zlo=self.zlo + 1 - 2 * (self.zlo % 2)),
            self.at(zlo=(self.zlo + 2) % 4),
            self.z_far(),
        )


def greet(devices):
    barrier = pltpu.get_barrier_semaphore()
    for device in devices:
        pl.semaphore_signal(barrier, inc=1, device_id=device, device_id_type=MESH)
    pl.semaphore_wait(barrier, len(devices))


def remote(source, target, send_sem, recv_sem, device):
    return pltpu.make_async_remote_copy(
        src_ref=source,
        dst_ref=target,
        send_sem=send_sem,
        recv_sem=recv_sem,
        device_id=device,
        device_id_type=MESH,
    )


def half_of(width, which):
    half = width // 2
    return pl.ds(pl.multiple_of(which * half, 128), half)


class Doubling:
    def __init__(self, place, tile, slots, send_sems, recv_sems):
        self.partners = place.doubling()
        self.tile, self.slots = tile, slots
        self.send_sems, self.recv_sems = send_sems, recv_sems
        self.step = 0
        self.copies = []

    def start(self):
        k = self.step
        copy = remote(
            self.tile.at[k], self.slots.at[k], self.send_sems.at[k], self.recv_sems.at[k], self.partners[k]
        )
        copy.start()
        self.copies.append(copy)

    def advance(self):
        k = self.step
        self.copies[k].wait_recv()
        self.tile[k + 1] = self.tile[k] + self.slots[k]
        self.step = k + 1
        if self.step < 8:
            self.start()

    def drain(self):
        for copy in self.copies:
            copy.wait_send()


def gather_kernel(
    wq, wo, wu, wd, wn, count, fq, fo, fu, fd, fn, total,
    tile, slots, send_sem, recv_sem, local_sem, tile_send, tile_recv,
):
    place = Place()
    own, far = place.wsh, (1 - place.zhi) * 4 + place.x
    greet(
        [place.x_peer(d) for d in (1, 2, 3)]
        + [place.z_far(), place.sibling()]
        + [place.doubling()[k] for k in (1, 2, 5, 6)]
    )
    arrays = ((wq, fq), (wo, fo), (wu, fu), (wd, fd), (wn, fn))
    tile[0] = count[...]
    doubling = Doubling(place, tile, slots, tile_send, tile_recv)
    doubling.start()
    sends = []

    def half(ref, which):
        width = ref.shape[-1]
        if width < 256:
            return ref
        return ref.at[:, half_of(width, which)]

    locals_ = []
    first = []
    for i, (shard, full) in enumerate(arrays):
        copy = pltpu.make_async_copy(shard, full.at[own], local_sem.at[i])
        copy.start()
        locals_.append(copy)
        copies = []
        for k, device in enumerate([place.x_peer(d) for d in (1, 2, 3)] + [place.z_far()]):
            copies.append(
                remote(
                    half(shard, place.core), half(full.at[own], place.core),
                    send_sem.at[i, k], recv_sem.at[i, k], device,
                )
            )
            copies[-1].start()
        first.append(copies)
    forwards = []

    def forward(i, k, index):
        shard, full = arrays[i]
        if shard.shape[-1] < 256:
            return
        part = half(full.at[index], place.core)
        copy = remote(part, part, send_sem.at[i, 7 + k], recv_sem.at[i, 7 + k], place.sibling())
        copy.start()
        forwards.append(copy)

    second = []
    for i, (shard, full) in enumerate(arrays):
        first[i][3].wait_recv()
        copies = []
        for k, d in enumerate((1, 2, 3)):
            part = half(full.at[far], place.core)
            copies.append(
                remote(part, part, send_sem.at[i, 4 + k], recv_sem.at[i, 4 + k], place.x_peer(d))
            )
            copies[-1].start()
        second.append(copies)
        forward(i, 3, far)
        if i < 4:
            doubling.advance()
    for i in range(5):
        for k, d in enumerate((1, 2, 3)):
            first[i][k].wait_recv()
            forward(i, k, place.zhi * 4 + (place.x - d + 4) % 4)
        if i < 4:
            doubling.advance()
    for i in range(5):
        for k, d in enumerate((1, 2, 3)):
            second[i][k].wait_recv()
            forward(i, 4 + k, (1 - place.zhi) * 4 + (place.x - d + 4) % 4)
    total[...] = tile[8]
    for copy in forwards:
        copy.wait_recv()
    for copy in forwards + sum(first, []) + sum(second, []):
        copy.wait_send()
    for copy in locals_:
        copy.wait()
    doubling.drain()


def gather_weights(w_qkv, w_out, w_up, w_down, norms, counted):
    any_space = pl.BlockSpec(memory_space=pl.ANY)
    vmem = pl.BlockSpec(memory_space=pltpu.VMEM)
    tile_norms = jnp.zeros((16, 128), BF16).at[: norms.shape[0], : norms.shape[1]].set(norms)
    count = jnp.broadcast_to(jnp.sum(counted.astype(F32)), (8, 128))
    shards = (w_qkv, w_out, w_up, w_down, tile_norms)
    fq, fo, fu, fd, fn, total = pl.pallas_call(
        gather_kernel,
        out_shape=[jax.ShapeDtypeStruct((8, *w.shape), BF16) for w in shards]
        + [jax.ShapeDtypeStruct((8, 128), F32)],
        in_specs=[any_space] * 5 + [vmem],
        out_specs=[any_space] * 5 + [vmem],
        scratch_shapes=[
            pltpu.VMEM((9, 8, 128), F32),
            pltpu.VMEM((8, 8, 128), F32),
            pltpu.SemaphoreType.DMA((5, 14)),
            pltpu.SemaphoreType.DMA((5, 14)),
            pltpu.SemaphoreType.DMA((5,)),
            pltpu.SemaphoreType.DMA((8,)),
            pltpu.SemaphoreType.DMA((8,)),
        ],
        compiler_params=pltpu.CompilerParams(collective_id=0, has_side_effects=True),
        name="gather_weights",
    )(*shards, count)
    full_norms = fn[:, : norms.shape[0], : norms.shape[1]].transpose(1, 0, 2).reshape(norms.shape[0], -1)
    return (
        fq.reshape(-1, fq.shape[-1]),
        fo.reshape(-1, fo.shape[-1]),
        fu.reshape(-1, fu.shape[-1]),
        fd.reshape(-1, fd.shape[-1]),
        full_norms,
        total[0, 0],
    )


def reduce_kernel(*refs):
    gq, go, gu, gd, small = refs[:5]
    outs, small_out = refs[5:9], refs[9]
    held, from_x, sum_x, from_y, sum_y, from_z = (refs[10 + 4 * k : 14 + 4 * k] for k in range(6))
    tile, slots, send_sem, recv_sem, tile_send, tile_recv = refs[34:]
    grads = (gq, go, gu, gd)
    place = Place()
    near_z = (place.doubling()[5], place.doubling()[6])
    plane = [
        place.at(y=(place.y + d) % 4, core=(place.core + c) % 2)
        for d in range(4)
        for c in range(2)
        if d + c > 0
    ]
    greet(plane + [place.x_peer(d) for d in (1, 2, 3)] + [place.z_far(), *near_z])
    tile[0] = small[...]
    doubling = Doubling(place, tile, slots, tile_send, tile_recv)
    doubling.start()
    sends = []

    def go_on(copy):
        copy.start()
        sends.append(copy)
        return copy

    pair = []
    for i, grad in enumerate(grads):
        width = grad.shape[-1]
        pair.append(
            go_on(
                remote(
                    grad.at[:, :, :, half_of(width, 1 - place.core)], held[i],
                    send_sem.at[i, 0], recv_sem.at[i, 0], place.sibling(),
                )
            )
        )
    doubling.advance()
    across = []
    for i, grad in enumerate(grads):
        width, rows = grad.shape[-1], grad.shape[2]
        pair[i].wait_recv()
        lanes = half_of(width, place.core)

        def add_pair(step, carry, grad=grad, i=i, lanes=lanes, rows=rows):
            block = step // (rows // 48)
            zh, xx = block // 4, block % 4
            part = pl.ds(pl.multiple_of((step % (rows // 48)) * 48, 16), 48)
            mine = grad[zh, xx, part, lanes].astype(F32)
            held[i][zh, xx, part, :] = (mine + held[i][zh, xx, part, :].astype(F32)).astype(BF16)
            return carry

        lax.fori_loop(0, 8 * (rows // 48), add_pair, 0)
        copies = []
        for k, d in enumerate((1, 2, 3)):
            to = (place.x + d) % 4
            copies.append(
                go_on(
                    remote(
                        held[i].at[:, to], from_x[i].at[k],
                        send_sem.at[i, 1 + k], recv_sem.at[i, 1 + k], place.x_peer(d),
                    )
                )
            )
        across.append(copies)
    doubling.advance()
    along = []
    for i, grad in enumerate(grads):
        rows = grad.shape[2]
        for copy in across[i]:
            copy.wait_recv()

        def add_x(step, carry, i=i, rows=rows):
            zh = step // (rows // 48)
            part = pl.ds(pl.multiple_of((step % (rows // 48)) * 48, 16), 48)
            value = held[i][zh, place.x, part, :].astype(F32)
            for k in range(3):
                value = value + from_x[i][k, zh, part, :].astype(F32)
            sum_x[i][zh, part, :] = value.astype(BF16)
            return carry

        lax.fori_loop(0, 2 * (rows // 48), add_x, 0)
        copies = []
        for k, d in enumerate((1, 2, 3)):
            to = (place.y + d) % 4
            part = pl.ds(pl.multiple_of((to % 2) * (rows // 2), 16), rows // 2)
            copies.append(
                go_on(
                    remote(
                        sum_x[i].at[to // 2, part], from_y[i].at[k],
                        send_sem.at[i, 4 + k], recv_sem.at[i, 4 + k], place.y_peer(d),
                    )
                )
            )
        along.append(copies)
        doubling.advance()
    owner = place.y // 2
    side = place.zlo // 2
    here = place.zhi == owner
    mine = jnp.logical_and(here, place.core == side)
    other = jnp.logical_and(here, place.core != side)

    def z_copy(i, k, device):
        return remote(sum_y[i], from_z[i].at[k], send_sem.at[i, 7 + k], recv_sem.at[i, 7 + k], device)

    def add_z(i, k):
        rows = sum_y[i].shape[0]

        def body(step, carry):
            part = pl.ds(pl.multiple_of(step * 48, 16), 48)
            sum_y[i][part, :] = (
                sum_y[i][part, :].astype(F32) + from_z[i][k, part, :].astype(F32)
            ).astype(BF16)
            return carry

        lax.fori_loop(0, rows // 48, body, 0)

    for i, grad in enumerate(grads):
        rows = grad.shape[2]
        for copy in along[i]:
            copy.wait_recv()

        def add_y(step, carry, i=i, rows=rows):
            part = pl.ds(pl.multiple_of((place.y % 2) * (rows // 2) + step * 48, 16), 48)
            value = sum_x[i][owner, part, :].astype(F32)
            there = pl.ds(pl.multiple_of(step * 48, 16), 48)
            for k in range(3):
                value = value + from_y[i][k, there, :].astype(F32)
            sum_y[i][there, :] = value.astype(BF16)
            return carry

        lax.fori_loop(0, rows // 96, add_y, 0)

        @pl.when(jnp.logical_not(here))
        def _(i=i):
            z_copy(i, 0, place.z_far()).start()

    doubling.advance()
    for i in range(4):
        @pl.when(here)
        def _(i=i):
            z_copy(i, 0, place.z_far()).wait_recv()
            add_z(i, 0)

        @pl.when(other)
        def _(i=i):
            z_copy(i, 1, near_z[1]).start()

    doubling.advance()
    for i in range(4):
        @pl.when(mine)
        def _(i=i):
            z_copy(i, 1, near_z[1]).wait_recv()
            add_z(i, 1)
            z_copy(i, 2, near_z[0]).start()

    def cast_copy(i, k, device):
        rows = sum_y[i].shape[0]
        part = pl.ds(pl.multiple_of((place.y % 2) * rows, 16), rows)
        return remote(
            outs[i].at[part], outs[i].at[part],
            send_sem.at[i, 10 + k], recv_sem.at[i, 10 + place.y % 2], device,
        )

    for i in range(4):
        @pl.when(mine)
        def _(i=i):
            copy = z_copy(i, 2, near_z[0])
            copy.wait()
            rows = sum_y[i].shape[0]

            def body(step, carry):
                part = pl.ds(pl.multiple_of(step * 48, 16), 48)
                there = pl.ds(pl.multiple_of((place.y % 2) * rows + step * 48, 16), 48)
                outs[i][there, :] = (
                    sum_y[i][part, :].astype(F32) + from_z[i][2, part, :].astype(F32)
                ).astype(BF16)
                return carry

            lax.fori_loop(0, rows // 48, body, 0)
            for k, device in enumerate(plane):
                cast_copy(i, k, device).start()

    def arrived(i, k):
        rows = sum_y[i].shape[0]
        part = outs[i].at[pl.ds(k * rows, rows)]
        return remote(part, part, send_sem.at[i, 10], recv_sem.at[i, 10 + k], place.sibling())

    for i in range(4):
        for k in range(2):
            @pl.when(jnp.logical_not(jnp.logical_and(mine, place.y % 2 == k)))
            def _(i=i, k=k):
                arrived(i, k).wait_recv()

    small_out[...] = tile[8]
    for i in range(4):
        @pl.when(mine)
        def _(i=i):
            for k, device in enumerate(plane):
                cast_copy(i, k, device).wait_send()

        @pl.when(other)
        def _(i=i):
            z_copy(i, 1, near_z[1]).wait_send()

        @pl.when(jnp.logical_not(here))
        def _(i=i):
            z_copy(i, 0, place.z_far()).wait_send()

    for copy in sends:
        copy.wait_send()
    doubling.drain()


def reduce_grads(grads, small):
    vmem = pl.BlockSpec(memory_space=pltpu.VMEM)
    blocks = [g.reshape(2, 4, g.shape[0] // 8, g.shape[1]) for g in grads]
    rows = [b.shape[2] for b in blocks]
    half = [b.shape[3] // 2 for b in blocks]
    each = lambda shape: [pltpu.VMEM(shape(r, h), BF16) for r, h in zip(rows, half)]
    results = pl.pallas_call(
        reduce_kernel,
        out_shape=[jax.ShapeDtypeStruct((r, h), BF16) for r, h in zip(rows, half)]
        + [jax.ShapeDtypeStruct(small.shape, F32)],
        in_specs=[vmem] * 5,
        out_specs=[vmem] * 5,
        scratch_shapes=each(lambda r, h: (2, 4, r, h))
        + each(lambda r, h: (3, 2, r, h))
        + each(lambda r, h: (2, r, h))
        + each(lambda r, h: (3, r // 2, h))
        + each(lambda r, h: (r // 2, h))
        + each(lambda r, h: (3, r // 2, h))
        + [
            pltpu.VMEM((9, *small.shape), F32),
            pltpu.VMEM((8, *small.shape), F32),
            pltpu.SemaphoreType.DMA((4, 17)),
            pltpu.SemaphoreType.DMA((4, 17)),
            pltpu.SemaphoreType.DMA((8,)),
            pltpu.SemaphoreType.DMA((8,)),
        ],
        compiler_params=pltpu.CompilerParams(
            collective_id=1, has_side_effects=True, vmem_limit_bytes=60 * 2**20
        ),
        name="reduce_grads",
    )(*blocks, small)
    ctx = lax.axis_index("ctx")
    finals = []
    for result in results[:4]:
        width = result.shape[1] // 16
        finals.append(lax.dynamic_slice_in_dim(result, (ctx % 16) * width, width, axis=1).astype(F32))
    return finals, results[4]


def layer_norm(values, gain_row, shift_row):
    row_mean = jnp.mean(values, axis=-1, keepdims=True)
    centered = values - row_mean
    inv_scale = lax.rsqrt(jnp.mean(centered * centered, axis=-1, keepdims=True) + 1e-05)
    normed = centered * inv_scale
    return (normed * gain_row + shift_row, normed, inv_scale)


def norm_back(grad_rows, normed, inv_scale, gain_row):
    weighted = grad_rows * gain_row
    grad_input = inv_scale * (
        weighted
        - jnp.mean(weighted, axis=-1, keepdims=True)
        - normed * jnp.mean(weighted * normed, axis=-1, keepdims=True)
    )
    return (grad_input, jnp.sum(grad_rows * normed, axis=0), jnp.sum(grad_rows, axis=0))


def gelu_exact(values):
    return jax.nn.gelu(values, approximate=False)


def selector(index):
    slot_count = index.shape[1]
    source_iota = jnp.arange(slot_count, dtype=jnp.int32)[None, :, None]
    return (index[:, None, :] == source_iota).astype(jnp.bfloat16)


def permute(array, table):
    return jnp.einsum("hct,hts->hcs", array, table, preferred_element_type=jnp.float32).astype(
        jnp.bfloat16
    )


def take_index(array, index):
    return jnp.take_along_axis(array, index[:, None, :], axis=2)


def cluster_order(labels):
    slot_count = labels.shape[2]
    keys = labels[:, 0, :] * slot_count + jnp.arange(slot_count, dtype=jnp.int32)[None, :]
    order = jnp.argsort(keys, axis=1)
    inverse = jnp.argsort(order, axis=1)
    return (order, inverse)


def as_blocks(array):
    return array.reshape(array.shape[0], array.shape[1], array.shape[2] // CLUSTER, CLUSTER)


def from_blocks(array):
    return array.reshape(array.shape[0], array.shape[1], array.shape[2] * array.shape[3])


def cluster_scores(blocks, seg_blocks, head_size):
    query_rows = blocks[:, :head_size]
    key_rows = blocks[:, head_size : 2 * head_size]
    raw_scores = jnp.einsum(
        "hdgq,hdgk->hgqk", query_rows, key_rows, preferred_element_type=jnp.float32
    ) * head_size ** (-0.5)
    allowed = seg_blocks[:, :, :, None] == seg_blocks[:, :, None, :]
    return (raw_scores, allowed)


def attend_forward(blocks, seg_blocks, head_size):
    raw_scores, allowed = cluster_scores(blocks, seg_blocks, head_size)
    masked = jnp.where(allowed, raw_scores, -1e30)
    row_top = jnp.max(masked, axis=-1, keepdims=True)
    row_total = jnp.sum(jnp.where(allowed, jnp.exp(masked - row_top), 0.0), axis=-1, keepdims=True)
    logsum = row_top + jnp.log(row_total)
    weights = jnp.where(allowed, jnp.exp(raw_scores - logsum), 0.0)
    value_rows = blocks[:, 2 * head_size :]
    attended = jnp.einsum(
        "hgqk,hdgk->hdgq",
        weights.astype(jnp.bfloat16),
        value_rows,
        preferred_element_type=jnp.float32,
    )
    return (attended.astype(jnp.bfloat16), logsum)


def attend_backward(blocks, seg_blocks, logsum, grad_heads, head_size):
    raw_scores, allowed = cluster_scores(blocks, seg_blocks, head_size)
    weights = jnp.where(allowed, jnp.exp(raw_scores - logsum), 0.0)
    query_rows = blocks[:, :head_size]
    key_rows = blocks[:, head_size : 2 * head_size]
    value_rows = blocks[:, 2 * head_size :]
    grad_weights = jnp.einsum(
        "hdgq,hdgk->hgqk", grad_heads, value_rows, preferred_element_type=jnp.float32
    )
    row_delta = jnp.sum(weights * grad_weights, axis=-1, keepdims=True)
    grad_raw = (weights * (grad_weights - row_delta)).astype(jnp.bfloat16)
    factor = head_size ** (-0.5)
    grad_query = (
        jnp.einsum("hgqk,hdgk->hdgq", grad_raw, key_rows, preferred_element_type=jnp.float32)
        * factor
    )
    grad_keys = (
        jnp.einsum("hgqk,hdgq->hdgk", grad_raw, query_rows, preferred_element_type=jnp.float32)
        * factor
    )
    grad_values = jnp.einsum(
        "hgqk,hdgq->hdgk",
        weights.astype(jnp.bfloat16),
        grad_heads,
        preferred_element_type=jnp.float32,
    )
    return jnp.concatenate([grad_query, grad_keys, grad_values], axis=1).astype(jnp.bfloat16)


def local(tokens, teacher, clusters, segments, counted, w_qkv, w_out, w_up, w_down, norms):
    full_qkv, full_out, full_up, full_down, full_norms, total_count = gather_weights(
        w_qkv, w_out, w_up, w_down, norms, counted
    )
    x_rows = tokens[0]
    tok_count, model_dim = x_rows.shape
    head_count = clusters.shape[1]
    head_size = model_dim // head_count
    peer_count = lax.axis_size("ctx")
    share_size = tok_count // peer_count
    per_device = tok_count // CLUSTER
    cluster_ids = clusters[0]
    target_dev = cluster_ids // per_device
    onehot = (target_dev[:, :, None] == jnp.arange(peer_count, dtype=jnp.int32)).astype(jnp.int32)
    within = jnp.sum((jnp.cumsum(onehot, axis=1) - 1) * onehot, axis=2)
    slot_index = target_dev * share_size + within
    head_iota = jnp.arange(head_count, dtype=jnp.int32)[:, None]
    token_iota = jnp.broadcast_to(jnp.arange(tok_count, dtype=jnp.int32)[None, :], slot_index.shape)
    send_order = jnp.zeros_like(slot_index).at[head_iota, slot_index].set(token_iota)
    send_table = selector(send_order)
    home_table = selector(slot_index)
    qkv = jnp.dot(x_rows, full_qkv, preferred_element_type=jnp.float32).astype(jnp.bfloat16)
    packed = (
        qkv.reshape(tok_count, 3, head_count, head_size)
        .transpose(2, 1, 3, 0)
        .reshape(head_count, 3 * head_size, tok_count)
    )
    seg_ids = jnp.broadcast_to(segments[0][None, :], cluster_ids.shape)
    label_pair = jnp.stack([cluster_ids, seg_ids], axis=1)
    sent_qkv = permute(packed, send_table)
    sent_labels = take_index(label_pair, send_order)
    got_qkv, got_labels = (
        lax.all_to_all(sent_qkv, "ctx", split_axis=2, concat_axis=2, tiled=True),
        lax.all_to_all(sent_labels, "ctx", split_axis=2, concat_axis=2, tiled=True),
    )
    order, inverse = cluster_order(got_labels)
    order_table = selector(order)
    inverse_table = selector(inverse)
    qkv_blocks = as_blocks(permute(got_qkv, order_table))
    seg_blocks = as_blocks(take_index(got_labels[:, 1:2, :], order))[:, 0]
    attended, logsum = attend_forward(qkv_blocks, seg_blocks, head_size)
    returned = lax.all_to_all(
        permute(from_blocks(attended), inverse_table),
        "ctx",
        split_axis=2,
        concat_axis=2,
        tiled=True,
    )
    mixed_heads = permute(returned, home_table).transpose(2, 0, 1).reshape(tok_count, model_dim)
    gain_rows = full_norms.astype(jnp.float32)
    first_sum = x_rows.astype(jnp.float32) + jnp.dot(
        mixed_heads, full_out, preferred_element_type=jnp.float32
    )
    normed_one, unit_one, scale_one = layer_norm(first_sum, gain_rows[0], gain_rows[1])
    normed_low = normed_one.astype(jnp.bfloat16)
    upper_rows = jnp.dot(normed_low, full_up, preferred_element_type=jnp.float32)
    active, gelu_back = jax.vjp(gelu_exact, upper_rows)
    active_low = active.astype(jnp.bfloat16)
    second = normed_one + jnp.dot(active_low, full_down, preferred_element_type=jnp.float32)
    result, unit_two, scale_two = layer_norm(second, gain_rows[2], gain_rows[3])
    errors = result - teacher[0].astype(jnp.float32)
    mask_rows = counted[0].astype(jnp.float32)
    partial_value = jnp.sum(mask_rows * jnp.mean(errors * errors, axis=1))
    everyone = tok_count * peer_count * lax.axis_size("wsh")
    grad_result = everyone / total_count * mask_rows[:, None] * errors
    grad_second, grad_gain_two, grad_shift_two = norm_back(
        grad_result, unit_two, scale_two, gain_rows[2]
    )
    grad_branch_two = grad_second.astype(jnp.bfloat16)
    grad_down = jnp.dot(active_low.T, grad_branch_two, preferred_element_type=jnp.float32)
    grad_active = jnp.dot(grad_branch_two, full_down.T, preferred_element_type=jnp.float32)
    (grad_upper,) = gelu_back(grad_active)
    grad_upper_low = grad_upper.astype(jnp.bfloat16)
    grad_up = jnp.dot(normed_low.T, grad_upper_low, preferred_element_type=jnp.float32)
    grad_normed = (
        jnp.dot(grad_upper_low, full_up.T, preferred_element_type=jnp.float32) + grad_second
    )
    grad_first, grad_gain_one, grad_shift_one = norm_back(
        grad_normed, unit_one, scale_one, gain_rows[0]
    )
    grad_branch = grad_first.astype(jnp.bfloat16)
    grad_outw = jnp.dot(mixed_heads.T, grad_branch, preferred_element_type=jnp.float32)
    grad_mixed = jnp.dot(grad_branch, full_out.T, preferred_element_type=jnp.float32).astype(
        jnp.bfloat16
    )
    grad_heads = permute(
        grad_mixed.reshape(tok_count, head_count, head_size).transpose(1, 2, 0), send_table
    )
    grad_got = lax.all_to_all(grad_heads, "ctx", split_axis=2, concat_axis=2, tiled=True)
    back_table = order_table
    back_home = inverse_table
    back_blocks, back_segs = qkv_blocks, seg_blocks
    grad_blocks = as_blocks(permute(grad_got, back_table))
    grad_packed = attend_backward(back_blocks, back_segs, logsum, grad_blocks, head_size)
    grad_home = lax.all_to_all(
        permute(from_blocks(grad_packed), back_home), "ctx", split_axis=2, concat_axis=2, tiled=True
    )
    grad_qkv = (
        permute(grad_home, home_table)
        .reshape(head_count, 3, head_size, tok_count)
        .transpose(3, 1, 0, 2)
        .reshape(tok_count, 3 * model_dim)
    )
    grad_inw = jnp.dot(x_rows.T, grad_qkv, preferred_element_type=jnp.float32)
    grad_tokens = jnp.dot(grad_qkv, full_qkv.T, preferred_element_type=jnp.float32) + grad_first
    grad_norms = jnp.stack([grad_gain_one, grad_shift_one, grad_gain_two, grad_shift_two])
    small = jnp.zeros((8, model_dim), F32).at[:4].set(grad_norms).at[4, 0].set(partial_value)
    (final_qkv, final_out, final_up, final_down), small = reduce_grads(
        [g.astype(BF16) for g in (grad_inw, grad_outw, grad_up, grad_down)], small
    )
    loss_value = small[4, 0] / total_count
    width = model_dim // (peer_count * lax.axis_size("wsh"))
    at = lax.axis_index("ctx") * lax.axis_size("wsh") + lax.axis_index("wsh")
    final_norms = lax.dynamic_slice(small, (0, at * width), (4, width))
    return (
        result.astype(jnp.bfloat16)[None],
        grad_tokens[None],
        loss_value,
        final_qkv,
        final_out,
        final_up,
        final_down,
        final_norms,
    )


def solution(mesh):
    placed = (
        P("wsh", "ctx", None),
        P("wsh", "ctx", None),
        P("wsh", None, "ctx"),
        P("wsh", "ctx"),
        P("wsh", "ctx"),
        P("wsh", None),
        P("wsh", None),
        P("wsh", None),
        P("wsh", None),
        P(None, "wsh"),
    )
    return jax.shard_map(
        local,
        mesh=mesh,
        in_specs=placed,
        out_specs=(
            P("wsh", "ctx", None),
            P("wsh", "ctx", None),
            P(),
            P("wsh", "ctx"),
            P("wsh", "ctx"),
            P("wsh", "ctx"),
            P("wsh", "ctx"),
            P(None, ("ctx", "wsh")),
        ),
        check_vma=False,
    )
```

```python
import functools
import jax
import jax.numpy as jnp
from jax import lax
from jax.experimental import pallas as pl
from jax.experimental.pallas import tpu as pltpu
from jax.sharding import PartitionSpec as P

MESH = pl.DeviceIdType.MESH
BF16 = jnp.bfloat16
F32 = jnp.float32


class Place:
    def __init__(self):
        self.ctx = lax.axis_index("ctx")
        self.wsh = lax.axis_index("wsh")
        self.zlo = self.ctx // 8
        self.y = (self.ctx // 2) % 4
        self.core = self.ctx % 2
        self.zhi = self.wsh // 4
        self.x = self.wsh % 4

    def at(self, zlo=None, y=None, core=None, zhi=None, x=None):
        zlo = self.zlo if zlo is None else zlo
        y = self.y if y is None else y
        core = self.core if core is None else core
        zhi = self.zhi if zhi is None else zhi
        x = self.x if x is None else x
        return (zlo * 8 + y * 2 + core, zhi * 4 + x)

    def sibling(self):
        return self.at(core=1 - self.core)

    def x_peer(self, step):
        return self.at(x=(self.x + step) % 4)

    def y_peer(self, step):
        return self.at(y=(self.y + step) % 4)

    def z_peer(self, step):
        z = (self.zhi * 4 + self.zlo + step + 8) % 8
        return self.at(zlo=z % 4, zhi=z // 4)

    def plane(self):
        return [
            self.at(y=(self.y + d) % 4, core=(self.core + c) % 2)
            for d, c in ((0, 1), (1, 0), (1, 1), (2, 0), (2, 1), (3, 0), (3, 1))
        ]

    def rank(self):
        return self.y * 2 + self.core

    def z_far(self):
        return self.at(zhi=1 - self.zhi)

    def doubling(self):
        return (
            self.sibling(),
            self.at(y=self.y + 1 - 2 * (self.y % 2)),
            self.at(y=(self.y + 2) % 4),
            self.at(x=self.x + 1 - 2 * (self.x % 2)),
            self.at(x=(self.x + 2) % 4),
            self.at(zlo=self.zlo + 1 - 2 * (self.zlo % 2)),
            self.at(zlo=(self.zlo + 2) % 4),
            self.z_far(),
        )


def greet(devices):
    barrier = pltpu.get_barrier_semaphore()
    for device in devices:
        pl.semaphore_signal(barrier, inc=1, device_id=device, device_id_type=MESH)
    pl.semaphore_wait(barrier, len(devices))


def remote(source, target, send_sem, recv_sem, device):
    return pltpu.make_async_remote_copy(
        src_ref=source,
        dst_ref=target,
        send_sem=send_sem,
        recv_sem=recv_sem,
        device_id=device,
        device_id_type=MESH,
    )


def half_of(width, which):
    half = width // 2
    return pl.ds(pl.multiple_of(which * half, 128), half)


class Doubling:
    def __init__(self, place, tile, slots, send_sems, recv_sems):
        self.partners = place.doubling()
        self.tile, self.slots = tile, slots
        self.send_sems, self.recv_sems = send_sems, recv_sems
        self.step = 0
        self.copies = []

    def start(self):
        k = self.step
        copy = remote(
            self.tile.at[k], self.slots.at[k], self.send_sems.at[k], self.recv_sems.at[k], self.partners[k]
        )
        copy.start()
        self.copies.append(copy)

    def advance(self):
        k = self.step
        self.copies[k].wait_recv()
        self.tile[k + 1] = self.tile[k] + self.slots[k]
        self.step = k + 1
        if self.step < 8:
            self.start()

    def drain(self):
        for copy in self.copies:
            copy.wait_send()


NEG = -1e30
NT = (((1,), (1,)), ((), ()))
TN = (((0,), (0,)), ((), ()))


def matmul(left, right, dims=(((1,), (0,)), ((), ()))):
    return lax.dot_general(left, right, dims, preferred_element_type=F32)


class Gather:
    def __init__(self, place, shard, full, send_sems, recv_sems, local_sem):
        self.place, self.shard, self.full = place, shard, full
        self.send_sems, self.recv_sems = send_sems, recv_sems
        self.rows = shard.shape[0]
        self.lanes = half_of(shard.shape[1], place.core)
        self.local = pltpu.make_async_copy(shard, full.at[place.wsh], local_sem)
        self.copies = {}

    def part(self, index, which=None):
        block = self.full.at[index]
        if which is None:
            return block.at[:, self.lanes]
        half = self.rows // 2
        return block.at[which * half : (which + 1) * half, self.lanes]

    def send(self, k, source, target, device):
        copy = remote(source, target, self.send_sems.at[k], self.recv_sems.at[k], device)
        copy.start()
        self.copies[k] = copy

    def own(self, far, step):
        return (far * 4) + (self.place.x + step + 4) % 4

    def start_z(self):
        place = self.place
        self.local.start()
        self.send(2, self.shard.at[:, self.lanes], self.part(place.wsh), place.z_far())

    def start_x(self):
        place = self.place
        self.send(0, self.shard.at[:, self.lanes], self.part(place.wsh), place.x_peer(1))
        self.send(1, self.shard.at[:, self.lanes], self.part(place.wsh), place.x_peer(3))

    def pass_on(self, zh, base):
        place = self.place
        left, right = self.own(zh, -1), self.own(zh, 1)
        self.copies[base].wait_recv()
        self.send(base + 3, self.part(left, 0), self.part(left, 0), place.x_peer(1))
        self.send(base + 5, self.part(left), self.part(left), place.sibling())
        self.copies[base + 1].wait_recv()
        self.send(base + 4, self.part(right, 1), self.part(right, 1), place.x_peer(3))
        self.send(base + 6, self.part(right), self.part(right), place.sibling())

    def opposite(self, zh, base):
        place = self.place
        index = self.own(zh, 2)
        for which in range(2):
            self.copies[base + 3 + which].wait_recv()
            self.send(base + 7 + which, self.part(index, which), self.part(index, which), place.sibling())

    def near(self):
        self.pass_on(self.place.zhi, 0)

    def near_opposite(self):
        self.opposite(self.place.zhi, 0)

    def from_z(self):
        place = self.place
        index = self.own(1 - place.zhi, 0)
        self.copies[2].wait_recv()
        self.send(10, self.part(index), self.part(index), place.x_peer(1))
        self.send(11, self.part(index), self.part(index), place.x_peer(3))
        self.send(9, self.part(index), self.part(index), place.sibling())

    def far(self):
        self.pass_on(1 - self.place.zhi, 10)

    def far_opposite(self):
        self.opposite(1 - self.place.zhi, 10)

    def finish(self):
        self.local.wait()
        for k in (5, 6, 7, 8, 9, 15, 16, 17, 18):
            self.copies[k].wait_recv()

    def drain(self):
        for k in self.copies:
            self.copies[k].wait_send()


def head_mask(which):
    lane = lax.broadcasted_iota(jnp.int32, (1, 128), 1)
    return jnp.where((lane // 64) == which, 1.0, 0.0).astype(BF16)


def to_slots(slot_row, head, count):
    row = slot_row[pl.ds(head, 1), :]
    iota = lax.broadcasted_iota(jnp.int32, (count, count), 0).astype(F32)
    return jnp.where(iota == row, 1.0, 0.0).astype(BF16)


def to_tokens(slot_col, head, count):
    lane = lax.broadcasted_iota(jnp.int32, slot_col.shape, 1)
    column = jnp.sum(jnp.where(lane == head, slot_col[...], 0.0), axis=1, keepdims=True)
    iota = lax.broadcasted_iota(jnp.int32, (count, count), 1).astype(F32)
    return jnp.where(iota == column, 1.0, 0.0).astype(BF16)


def pair_select(first, second):
    lane = lax.broadcasted_iota(jnp.int32, first.shape, 1)
    return jnp.where((lane // 64) % 2 == 0, first, second)


def make_slots(clusters, segments, slot_row, slot_col, labels):
    heads, count = 12, clusters.shape[1]
    groups = lax.shift_right_logical(clusters[...], 2)
    iota = lax.broadcasted_iota(jnp.int32, (32, count), 0)
    before = lax.broadcasted_iota(jnp.int32, (count, count), 0)
    after = lax.broadcasted_iota(jnp.int32, (count, count), 1)
    upper = jnp.where(before <= after, 1.0, 0.0).astype(BF16)
    hot = [jnp.where(groups[h : h + 1, :] == iota, 1.0, 0.0) for h in range(heads)]
    counts = matmul(jnp.concatenate(hot, axis=0).astype(BF16), upper)
    group_f = groups.astype(F32)
    rows = []
    for h in range(heads):
        rank = jnp.sum(counts[32 * h : 32 * h + 32] * hot[h], axis=0, keepdims=True)
        rows.append(group_f[h : h + 1] * 16.0 + rank - 1.0)
    slots = jnp.concatenate(rows + [jnp.zeros((128 - heads, count), F32)], axis=0)
    slot_row[...] = slots[:16]
    slot_col[...] = slots.T
    label = (segments[0:1, :] * 4 + (clusters[...] & 3)).astype(F32)
    labels[...] = jnp.concatenate([label, jnp.zeros((112, count), F32)], axis=0).T.astype(BF16)


def rows16(j):
    return slice(16 * j, 16 * j + 16)


def forward_kernel(
    x, clusters, segments, wq, wo, wu, wd, small,
    mixed, fq, fo, fu, fd, got, before, after, logsum, hot, cold, slot_row, slot_col, total,
    labels, sent_labels, got_labels, before_labels, after_labels, wide_labels, sent, out, back, log_cols,
    tile, slots,
    w_send, w_recv, w_local, t_send, t_recv, a_send, a_recv, a_local, z_send, z_recv, b_send, b_recv, b_local,
):
    place = Place()
    plane, rank = place.plane(), place.rank()
    up, down = place.z_peer(1), place.z_peer(-1)
    partners = place.doubling()
    greet(
        plane + [place.x_peer(1), place.x_peer(2), place.x_peer(3), place.z_far(), up, down, partners[5], partners[6]]
    )
    weights = [
        Gather(place, shard, full, w_send.at[i], w_recv.at[i], w_local.at[i])
        for i, (shard, full) in enumerate(((wq, fq), (wo, fo), (wu, fu), (wd, fd)))
    ]
    first, rest = weights[0], weights[1:]
    first.start_z()
    first.start_x()
    tile[0] = small[...]
    doubling = Doubling(place, tile, slots, t_send, t_recv)
    doubling.start()
    count = x.shape[0]
    make_slots(clusters, segments, slot_row, slot_col, labels)

    sent_labels[...] = jnp.zeros_like(sent_labels)

    def move_labels(head, carry):
        lane = lax.broadcasted_iota(jnp.int32, (count, 128), 1)
        moved = matmul(to_slots(slot_row, head, count), labels[...])
        sent_labels[...] = jnp.where(lane == head, moved, sent_labels[...])
        return carry

    lax.fori_loop(0, 12, move_labels, 0)
    labels[...] = sent_labels[...].astype(BF16)

    def block(which):
        return pl.ds(pl.multiple_of(which * 64, 64), 64)

    def ranks():
        return [dev[0] % 8 for dev in plane]

    label_copies = [
        remote(labels.at[block(to)], got_labels.at[rank], a_send.at[6, k], a_recv.at[6, k], plane[k])
        for k, to in enumerate(ranks())
    ]
    for copy in label_copies:
        copy.start()
    own_labels = pltpu.make_async_copy(labels.at[block(rank)], got_labels.at[rank], a_local.at[6])
    own_labels.start()
    doubling.advance()
    first.near()
    doubling.advance()
    own_labels.wait()
    for copy in label_copies:
        copy.wait_recv()
    label_up = remote(got_labels.at[4:8], before_labels, z_send.at[6, 0], z_recv.at[6, 0], up)
    label_down = remote(got_labels.at[0:4], after_labels, z_send.at[6, 1], z_recv.at[6, 1], down)
    label_up.start()
    label_down.start()
    first.from_z()
    for w in rest:
        w.start_z()
    first.near_opposite()
    doubling.advance()
    label_up.wait_recv()
    label_down.wait_recv()
    for j in range(4):
        wide_labels[j, 0:64] = jnp.where(
            place.zlo == 0, -1.0, before_labels[:, rows16(j), :].reshape(64, 128).astype(F32)
        )
        wide_labels[j, 64:192] = got_labels[:, rows16(j), :].reshape(128, 128).astype(F32)
        wide_labels[j, 192:256] = jnp.where(
            place.zlo == 3, -1.0, after_labels[:, rows16(j), :].reshape(64, 128).astype(F32)
        )

    def make_hot(head, carry):
        lane = lax.broadcasted_iota(jnp.int32, (256, 128), 1)
        for j in range(4):
            column = jnp.sum(jnp.where(lane == head, wide_labels[j], 0.0), axis=1, keepdims=True)
            same = lane.astype(F32) == column
            cold[head * 4 + j] = jnp.where(same, 0.0, NEG).astype(BF16)
            hot[head * 4 + j] = jnp.where(same, 1.0, 0.0)[64:192].astype(BF16)
        return carry

    lax.fori_loop(0, 12, make_hot, 0)
    doubling.advance()
    first.far()
    doubling.advance()
    for w in rest:
        w.start_x()
    first.far_opposite()
    first.finish()

    def send_copies(p, fn):
        for k, to in enumerate(ranks()):
            fn(remote(sent.at[p, block(to)], got.at[p, rank], a_send.at[p, k], a_recv.at[p, k], plane[k]))

    def own_copy(p):
        return pltpu.make_async_copy(sent.at[p, block(rank)], got.at[p, rank], a_local.at[p])

    def project(p, carry):
        parts = []
        for t in range(3):
            lanes = pl.ds(pl.multiple_of(t * 768 + p * 128, 128), 128)
            value = matmul(x[...], fq[:, :, lanes].reshape(768, 128)).astype(BF16)
            parts.append(value * jnp.asarray(0.125, BF16) if t == 0 else value)
        rows = jnp.concatenate(parts, axis=1)
        moved = [matmul(to_slots(slot_row, 2 * p + a, count), rows) for a in range(2)]
        sent[p] = pair_select(moved[0], moved[1]).astype(BF16)
        send_copies(p, lambda copy: copy.start())
        own_copy(p).start()
        return carry

    lax.fori_loop(0, 6, project, 0)
    doubling.advance()

    def halo(p):
        return (
            remote(got.at[p, 4:8, :, 128:384], before.at[p], z_send.at[p, 0], z_recv.at[p, 0], up),
            remote(got.at[p, 0:4, :, 128:384], after.at[p], z_send.at[p, 1], z_recv.at[p, 1], down),
        )

    def back_copies(p, fn):
        for k, to in enumerate(ranks()):
            fn(remote(out.at[p, to], back.at[p, rank], b_send.at[p, k], b_recv.at[p, k], plane[k]))

    def own_back(p):
        return pltpu.make_async_copy(out.at[p, rank], back.at[p, rank], b_local.at[p])

    def arrive(p):
        own_copy(p).wait()
        send_copies(p, lambda copy: copy.wait_recv())
        for copy in halo(p):
            copy.start()

    masks = [head_mask(a) for a in range(2)]

    def attend(p):
        for copy in halo(p):
            copy.wait_recv()
        lane = lax.broadcasted_iota(jnp.int32, (128, 128), 1)
        for j in range(4):
            r = rows16(j)
            query = got[p, :, r, 0:128].reshape(128, 128)
            keys = jnp.concatenate(
                [before[p, :, r, 0:128].reshape(64, 128), got[p, :, r, 128:256].reshape(128, 128),
                 after[p, :, r, 0:128].reshape(64, 128)], axis=0)
            values = jnp.concatenate(
                [before[p, :, r, 128:256].reshape(64, 128), got[p, :, r, 256:384].reshape(128, 128),
                 after[p, :, r, 128:256].reshape(64, 128)], axis=0)
            halves = []
            for a in range(2):
                head = 2 * p + a
                scores = matmul(
                    jnp.concatenate([query * masks[a], hot[head * 4 + j]], axis=1),
                    jnp.concatenate([keys, cold[head * 4 + j]], axis=1), NT)
                top = jnp.max(scores, axis=1, keepdims=True)
                weights_ = jnp.exp(scores - top)
                sums = jnp.sum(weights_, axis=1, keepdims=True)
                halves.append(matmul(weights_.astype(BF16), values) / sums)
                log_cols[j] = jnp.where(lane == head, top + jnp.log(sums), log_cols[j])
            out[p, :, r, :] = pair_select(halves[0], halves[1]).astype(BF16).reshape(8, 16, 128)
        back_copies(p, lambda copy: copy.start())
        own_back(p).start()

    log_cols[...] = jnp.zeros_like(log_cols)
    arrive(0)
    for w in rest:
        w.near()

    def steady(p, carry):
        arrive(p)
        attend(p - 1)
        return carry

    lax.fori_loop(1, 4, steady, 0)
    doubling.advance()
    for w in rest:
        w.from_z()
        w.near_opposite()
    lax.fori_loop(4, 6, steady, 0)
    doubling.advance()
    attend(5)

    def home(p, carry):
        own_back(p).wait()
        back_copies(p, lambda copy: copy.wait_recv())
        rows = back[p].reshape(count, 128)
        moved = [matmul(to_tokens(slot_col, 2 * p + a, count), rows) for a in range(2)]
        mixed[:, pl.ds(pl.multiple_of(p * 128, 128), 128)] = pair_select(moved[0], moved[1]).astype(BF16)
        return carry

    lax.fori_loop(0, 6, home, 0)
    for j in range(4):
        logsum[j] = log_cols[j].T[:16]
    for w in rest:
        w.far()
    for w in rest:
        w.far_opposite()
    for w in rest:
        w.finish()
    total[...] = tile[8]

    def settle(p, carry):
        send_copies(p, lambda copy: copy.wait_send())
        back_copies(p, lambda copy: copy.wait_send())
        for copy in halo(p):
            copy.wait_send()
        return carry

    lax.fori_loop(0, 6, settle, 0)
    for copy in label_copies + [label_up, label_down]:
        copy.wait_send()
    for w in weights:
        w.drain()
    doubling.drain()


ANY = pl.BlockSpec(memory_space=pl.ANY)
VMEM = pl.BlockSpec(memory_space=pltpu.VMEM)


def shaped(*shape, dtype=BF16):
    return jax.ShapeDtypeStruct(shape, dtype)


def forward(x, clusters, segments, shards, small):
    count = x.shape[0]
    dma = pltpu.SemaphoreType.DMA
    return pl.pallas_call(
        forward_kernel,
        out_shape=[
            shaped(*x.shape),
            *[shaped(8, *w.shape) for w in shards],
            shaped(6, 8, 64, 384),
            shaped(6, 4, 64, 256),
            shaped(6, 4, 64, 256),
            shaped(4, 16, 128, dtype=F32),
            shaped(48, 128, 128),
            shaped(48, 256, 128),
            shaped(16, count, dtype=F32),
            shaped(count, 128, dtype=F32),
            shaped(*small.shape, dtype=F32),
        ],
        in_specs=[VMEM] * 3 + [ANY] * 4 + [VMEM],
        out_specs=[VMEM] * 2 + [ANY] * 3 + [VMEM] * 9,
        scratch_shapes=[
            pltpu.VMEM((count, 128), BF16),
            pltpu.VMEM((count, 128), F32),
            pltpu.VMEM((8, 64, 128), BF16),
            pltpu.VMEM((4, 64, 128), BF16),
            pltpu.VMEM((4, 64, 128), BF16),
            pltpu.VMEM((4, 256, 128), F32),
            pltpu.VMEM((6, count, 384), BF16),
            pltpu.VMEM((6, 8, 64, 128), BF16),
            pltpu.VMEM((6, 8, 64, 128), BF16),
            pltpu.VMEM((4, 128, 128), F32),
            pltpu.VMEM((9, *small.shape), F32),
            pltpu.VMEM((8, *small.shape), F32),
            dma((4, 19)), dma((4, 19)), dma((4,)), dma((8,)), dma((8,)),
            dma((7, 7)), dma((7, 7)), dma((7,)), dma((7, 2)), dma((7, 2)),
            dma((6, 7)), dma((6, 7)), dma((6,)),
        ],
        compiler_params=pltpu.CompilerParams(
            collective_id=0, has_side_effects=True, vmem_limit_bytes=60 * 2**20
        ),
        name="forward_attention",
    )(x, clusters, segments, *shards, small)


def backward_kernel(
    grad_mixed, x_turned, grad_first, fq, got, before, after, logsum, hot, cold, slot_row, slot_col,
    grad_x, grad_wq,
    sent, got_grad, grads, to_before, to_after, from_before, from_after, back,
    a_send, a_recv, a_local, z_send, z_recv, b_send, b_recv, b_local,
):
    place = Place()
    plane, rank = place.plane(), place.rank()
    up, down = place.z_peer(1), place.z_peer(-1)
    greet(plane + [up, down])
    count = grad_mixed.shape[0]
    ranks = [dev[0] % 8 for dev in plane]

    def block(which):
        return pl.ds(pl.multiple_of(which * 64, 64), 64)

    def send_copies(p, fn):
        for k, to in enumerate(ranks):
            fn(remote(sent.at[p, block(to)], got_grad.at[p, rank], a_send.at[p, k], a_recv.at[p, k], plane[k]))

    def own_copy(p):
        return pltpu.make_async_copy(sent.at[p, block(rank)], got_grad.at[p, rank], a_local.at[p])

    def leave(p, carry):
        rows = grad_mixed[:, pl.ds(pl.multiple_of(p * 128, 128), 128)]
        moved = [matmul(to_slots(slot_row, 2 * p + a, count), rows) for a in range(2)]
        sent[p] = pair_select(moved[0], moved[1]).astype(BF16)
        send_copies(p, lambda copy: copy.start())
        own_copy(p).start()
        return carry

    lax.fori_loop(0, 6, leave, 0)

    def halo(p):
        return (
            remote(to_after.at[p], from_before.at[p], z_send.at[p, 0], z_recv.at[p, 0], up),
            remote(to_before.at[p], from_after.at[p], z_send.at[p, 1], z_recv.at[p, 1], down),
        )

    def back_copies(p, fn):
        for k, to in enumerate(ranks):
            fn(remote(grads.at[p, to], back.at[p, rank], b_send.at[p, k], b_recv.at[p, k], plane[k]))

    def own_back(p):
        return pltpu.make_async_copy(grads.at[p, rank], back.at[p, rank], b_local.at[p])

    masks = [head_mask(a) for a in range(2)]

    def attend(p):
        own_copy(p).wait()
        send_copies(p, lambda copy: copy.wait_recv())
        for j in range(4):
            r = rows16(j)
            query = got[p, :, r, 0:128].reshape(128, 128)
            keys = jnp.concatenate(
                [before[p, :, r, 0:128].reshape(64, 128), got[p, :, r, 128:256].reshape(128, 128),
                 after[p, :, r, 0:128].reshape(64, 128)], axis=0)
            values = jnp.concatenate(
                [before[p, :, r, 128:256].reshape(64, 128), got[p, :, r, 256:384].reshape(128, 128),
                 after[p, :, r, 128:256].reshape(64, 128)], axis=0)
            grad = got_grad[p, :, r, :].reshape(128, 128)
            dq, dk, dv = [], [], []
            for a in range(2):
                head = 2 * p + a
                scores = matmul(
                    jnp.concatenate([keys, cold[head * 4 + j]], axis=1),
                    jnp.concatenate([query * masks[a], hot[head * 4 + j]], axis=1), NT)
                probs = jnp.exp(scores - logsum[j, pl.ds(head, 1), :])
                grad_probs = matmul(values, grad * masks[a], NT)
                delta = jnp.sum(probs * grad_probs, axis=0, keepdims=True)
                grad_scores = (probs * (grad_probs - delta)).astype(BF16)
                dk.append(matmul(grad_scores, query))
                dv.append(matmul(probs.astype(BF16), grad))
                dq.append(matmul(grad_scores, keys, TN))
            dq = (pair_select(*dq) * 0.125).astype(BF16)
            dk = pair_select(*dk).astype(BF16)
            dv = pair_select(*dv).astype(BF16)
            both = jnp.concatenate([dk, dv], axis=1)
            to_before[p, :, r, :] = both[0:64].reshape(4, 16, 256)
            to_after[p, :, r, :] = both[192:256].reshape(4, 16, 256)
            grads[p, :, r, 0:128] = dq.reshape(8, 16, 128)
            grads[p, :, r, 128:384] = both[64:192].reshape(8, 16, 256)
        for copy in halo(p):
            copy.start()

    def give(p):
        for copy in halo(p):
            copy.wait_recv()
        for part, extra in ((slice(0, 4), from_before), (slice(4, 8), from_after)):
            grads[p, part, :, 128:384] = (
                grads[p, part, :, 128:384].astype(F32) + extra[p].astype(F32)
            ).astype(BF16)
        back_copies(p, lambda copy: copy.start())
        own_back(p).start()

    attend(0)

    def steady(p, carry):
        attend(p)
        give(p - 1)
        return carry

    lax.fori_loop(1, 6, steady, 0)
    give(5)
    grad_x[...] = grad_first[...]

    def home(p, carry):
        own_back(p).wait()
        back_copies(p, lambda copy: copy.wait_recv())
        rows = back[p].reshape(count, 384)
        moved = [matmul(to_tokens(slot_col, 2 * p + a, count), rows) for a in range(2)]
        grad_qkv = pair_select(moved[0], moved[1]).astype(BF16)
        weight = matmul(x_turned[...], grad_qkv).astype(BF16)
        columns = []
        for t in range(3):
            lanes = pl.ds(pl.multiple_of(t * 768 + p * 128, 128), 128)
            grad_wq[:, lanes] = weight[:, t * 128 : t * 128 + 128]
            columns.append(fq[:, :, lanes].reshape(768, 128))
        grad_x[...] += matmul(grad_qkv, jnp.concatenate(columns, axis=1), NT)
        return carry

    lax.fori_loop(0, 6, home, 0)

    def settle(p, carry):
        send_copies(p, lambda copy: copy.wait_send())
        back_copies(p, lambda copy: copy.wait_send())
        for copy in halo(p):
            copy.wait_send()
        return carry

    lax.fori_loop(0, 6, settle, 0)


def backward(grad_mixed, x_turned, grad_first, *kept):
    count = grad_mixed.shape[0]
    dma = pltpu.SemaphoreType.DMA
    return pl.pallas_call(
        backward_kernel,
        out_shape=[shaped(*grad_first.shape, dtype=F32), shaped(768, 2304)],
        in_specs=[VMEM] * 12,
        out_specs=[VMEM] * 2,
        scratch_shapes=[
            pltpu.VMEM((6, count, 128), BF16),
            pltpu.VMEM((6, 8, 64, 128), BF16),
            pltpu.VMEM((6, 8, 64, 384), BF16),
            pltpu.VMEM((6, 4, 64, 256), BF16),
            pltpu.VMEM((6, 4, 64, 256), BF16),
            pltpu.VMEM((6, 4, 64, 256), BF16),
            pltpu.VMEM((6, 4, 64, 256), BF16),
            pltpu.VMEM((6, 8, 64, 384), BF16),
            dma((6, 7)), dma((6, 7)), dma((6,)), dma((6, 2)), dma((6, 2)),
            dma((6, 7)), dma((6, 7)), dma((6,)),
        ],
        compiler_params=pltpu.CompilerParams(
            collective_id=2, has_side_effects=True, vmem_limit_bytes=60 * 2**20
        ),
        name="backward_attention",
    )(grad_mixed, x_turned, grad_first, *kept)


def reduce_kernel(*refs):
    gq, go, gu, gd, small = refs[:5]
    outs, small_out = refs[5:9], refs[9]
    held, from_x, sum_x, from_y, sum_y, from_z = (refs[10 + 4 * k : 14 + 4 * k] for k in range(6))
    tile, slots, send_sem, recv_sem, tile_send, tile_recv = refs[34:]
    grads = (gq, go, gu, gd)
    place = Place()
    near_z = (place.doubling()[5], place.doubling()[6])
    plane = [
        place.at(y=(place.y + d) % 4, core=(place.core + c) % 2)
        for d in range(4)
        for c in range(2)
        if d + c > 0
    ]
    greet(plane + [place.x_peer(d) for d in (1, 2, 3)] + [place.z_far(), *near_z])
    tile[0] = small[...]
    doubling = Doubling(place, tile, slots, tile_send, tile_recv)
    doubling.start()
    sends = []

    def go_on(copy):
        copy.start()
        sends.append(copy)
        return copy

    pair = []
    for i, grad in enumerate(grads):
        width = grad.shape[-1]
        pair.append(
            go_on(
                remote(
                    grad.at[:, :, :, half_of(width, 1 - place.core)], held[i],
                    send_sem.at[i, 0], recv_sem.at[i, 0], place.sibling(),
                )
            )
        )
    doubling.advance()
    across = []
    for i, grad in enumerate(grads):
        width, rows = grad.shape[-1], grad.shape[2]
        pair[i].wait_recv()
        lanes = half_of(width, place.core)

        def add_pair(step, carry, grad=grad, i=i, lanes=lanes, rows=rows):
            block = step // (rows // 48)
            zh, xx = block // 4, block % 4
            part = pl.ds(pl.multiple_of((step % (rows // 48)) * 48, 16), 48)
            mine = grad[zh, xx, part, lanes].astype(F32)
            held[i][zh, xx, part, :] = (mine + held[i][zh, xx, part, :].astype(F32)).astype(BF16)
            return carry

        lax.fori_loop(0, 8 * (rows // 48), add_pair, 0)
        copies = []
        for k, d in enumerate((1, 2, 3)):
            to = (place.x + d) % 4
            copies.append(
                go_on(
                    remote(
                        held[i].at[:, to], from_x[i].at[k],
                        send_sem.at[i, 1 + k], recv_sem.at[i, 1 + k], place.x_peer(d),
                    )
                )
            )
        across.append(copies)
    doubling.advance()
    along = []
    for i, grad in enumerate(grads):
        rows = grad.shape[2]
        for copy in across[i]:
            copy.wait_recv()

        def add_x(step, carry, i=i, rows=rows):
            zh = step // (rows // 48)
            part = pl.ds(pl.multiple_of((step % (rows // 48)) * 48, 16), 48)
            value = held[i][zh, place.x, part, :].astype(F32)
            for k in range(3):
                value = value + from_x[i][k, zh, part, :].astype(F32)
            sum_x[i][zh, part, :] = value.astype(BF16)
            return carry

        lax.fori_loop(0, 2 * (rows // 48), add_x, 0)
        copies = []
        for k, d in enumerate((1, 2, 3)):
            to = (place.y + d) % 4
            part = pl.ds(pl.multiple_of((to % 2) * (rows // 2), 16), rows // 2)
            copies.append(
                go_on(
                    remote(
                        sum_x[i].at[to // 2, part], from_y[i].at[k],
                        send_sem.at[i, 4 + k], recv_sem.at[i, 4 + k], place.y_peer(d),
                    )
                )
            )
        along.append(copies)
        doubling.advance()
    owner = place.y // 2
    side = place.zlo // 2
    here = place.zhi == owner
    mine = jnp.logical_and(here, place.core == side)
    other = jnp.logical_and(here, place.core != side)

    def z_copy(i, k, device):
        return remote(sum_y[i], from_z[i].at[k], send_sem.at[i, 7 + k], recv_sem.at[i, 7 + k], device)

    def add_z(i, k):
        rows = sum_y[i].shape[0]

        def body(step, carry):
            part = pl.ds(pl.multiple_of(step * 48, 16), 48)
            sum_y[i][part, :] = (
                sum_y[i][part, :].astype(F32) + from_z[i][k, part, :].astype(F32)
            ).astype(BF16)
            return carry

        lax.fori_loop(0, rows // 48, body, 0)

    for i, grad in enumerate(grads):
        rows = grad.shape[2]
        for copy in along[i]:
            copy.wait_recv()

        def add_y(step, carry, i=i, rows=rows):
            part = pl.ds(pl.multiple_of((place.y % 2) * (rows // 2) + step * 48, 16), 48)
            value = sum_x[i][owner, part, :].astype(F32)
            there = pl.ds(pl.multiple_of(step * 48, 16), 48)
            for k in range(3):
                value = value + from_y[i][k, there, :].astype(F32)
            sum_y[i][there, :] = value.astype(BF16)
            return carry

        lax.fori_loop(0, rows // 96, add_y, 0)

        @pl.when(jnp.logical_not(here))
        def _(i=i):
            z_copy(i, 0, place.z_far()).start()

    doubling.advance()
    for i in range(4):
        @pl.when(here)
        def _(i=i):
            z_copy(i, 0, place.z_far()).wait_recv()
            add_z(i, 0)

        @pl.when(other)
        def _(i=i):
            z_copy(i, 1, near_z[1]).start()

    doubling.advance()
    for i in range(4):
        @pl.when(mine)
        def _(i=i):
            z_copy(i, 1, near_z[1]).wait_recv()
            add_z(i, 1)
            z_copy(i, 2, near_z[0]).start()

    def cast_copy(i, k, device):
        rows = sum_y[i].shape[0]
        part = pl.ds(pl.multiple_of((place.y % 2) * rows, 16), rows)
        return remote(
            outs[i].at[part], outs[i].at[part],
            send_sem.at[i, 10 + k], recv_sem.at[i, 10 + place.y % 2], device,
        )

    for i in range(4):
        @pl.when(mine)
        def _(i=i):
            copy = z_copy(i, 2, near_z[0])
            copy.wait()
            rows = sum_y[i].shape[0]

            def body(step, carry):
                part = pl.ds(pl.multiple_of(step * 48, 16), 48)
                there = pl.ds(pl.multiple_of((place.y % 2) * rows + step * 48, 16), 48)
                outs[i][there, :] = (
                    sum_y[i][part, :].astype(F32) + from_z[i][2, part, :].astype(F32)
                ).astype(BF16)
                return carry

            lax.fori_loop(0, rows // 48, body, 0)
            for k, device in enumerate(plane):
                cast_copy(i, k, device).start()

    def arrived(i, k):
        rows = sum_y[i].shape[0]
        part = outs[i].at[pl.ds(k * rows, rows)]
        return remote(part, part, send_sem.at[i, 10], recv_sem.at[i, 10 + k], place.sibling())

    for i in range(4):
        for k in range(2):
            @pl.when(jnp.logical_not(jnp.logical_and(mine, place.y % 2 == k)))
            def _(i=i, k=k):
                arrived(i, k).wait_recv()

    small_out[...] = tile[8]
    for i in range(4):
        @pl.when(mine)
        def _(i=i):
            for k, device in enumerate(plane):
                cast_copy(i, k, device).wait_send()

        @pl.when(other)
        def _(i=i):
            z_copy(i, 1, near_z[1]).wait_send()

        @pl.when(jnp.logical_not(here))
        def _(i=i):
            z_copy(i, 0, place.z_far()).wait_send()

    for copy in sends:
        copy.wait_send()
    doubling.drain()


def reduce_grads(grads, small):
    vmem = pl.BlockSpec(memory_space=pltpu.VMEM)
    blocks = [g.reshape(2, 4, g.shape[0] // 8, g.shape[1]) for g in grads]
    rows = [b.shape[2] for b in blocks]
    half = [b.shape[3] // 2 for b in blocks]
    each = lambda shape: [pltpu.VMEM(shape(r, h), BF16) for r, h in zip(rows, half)]
    results = pl.pallas_call(
        reduce_kernel,
        out_shape=[jax.ShapeDtypeStruct((r, h), BF16) for r, h in zip(rows, half)]
        + [jax.ShapeDtypeStruct(small.shape, F32)],
        in_specs=[vmem] * 5,
        out_specs=[vmem] * 5,
        scratch_shapes=each(lambda r, h: (2, 4, r, h))
        + each(lambda r, h: (3, 2, r, h))
        + each(lambda r, h: (2, r, h))
        + each(lambda r, h: (3, r // 2, h))
        + each(lambda r, h: (r // 2, h))
        + each(lambda r, h: (3, r // 2, h))
        + [
            pltpu.VMEM((9, *small.shape), F32),
            pltpu.VMEM((8, *small.shape), F32),
            pltpu.SemaphoreType.DMA((4, 17)),
            pltpu.SemaphoreType.DMA((4, 17)),
            pltpu.SemaphoreType.DMA((8,)),
            pltpu.SemaphoreType.DMA((8,)),
        ],
        compiler_params=pltpu.CompilerParams(
            collective_id=1, has_side_effects=True, vmem_limit_bytes=60 * 2**20
        ),
        name="reduce_grads",
    )(*blocks, small)
    ctx = lax.axis_index("ctx")
    finals = []
    for result in results[:4]:
        width = result.shape[1] // 16
        finals.append(lax.dynamic_slice_in_dim(result, (ctx % 16) * width, width, axis=1).astype(F32))
    return finals, results[4]


def layer_norm(values, gain_row, shift_row):
    row_mean = jnp.mean(values, axis=-1, keepdims=True)
    centered = values - row_mean
    inv_scale = lax.rsqrt(jnp.mean(centered * centered, axis=-1, keepdims=True) + 1e-05)
    normed = centered * inv_scale
    return (normed * gain_row + shift_row, normed, inv_scale)


def norm_back(grad_rows, normed, inv_scale, gain_row):
    weighted = grad_rows * gain_row
    grad_input = inv_scale * (
        weighted
        - jnp.mean(weighted, axis=-1, keepdims=True)
        - normed * jnp.mean(weighted * normed, axis=-1, keepdims=True)
    )
    return (grad_input, jnp.sum(grad_rows * normed, axis=0), jnp.sum(grad_rows, axis=0))


def gelu_exact(values):
    return jax.nn.gelu(values, approximate=False)


def local(tokens, teacher, clusters, segments, counted, w_qkv, w_out, w_up, w_down, norms):
    x_rows = tokens[0]
    tok_count, model_dim = x_rows.shape
    wsh, ctx = lax.axis_index("wsh"), lax.axis_index("ctx")
    mask_rows = counted[0].astype(F32)
    small = lax.dynamic_update_slice(
        jnp.zeros((8, model_dim), F32).at[4, 0].set(jnp.sum(mask_rows)), norms.astype(F32), (0, wsh * norms.shape[1])
    )
    padded = jnp.zeros((16, tok_count), jnp.int32).at[: clusters.shape[1]].set(clusters[0])
    mixed, fq, fo, fu, fd, *kept, small = forward(
        x_rows, padded, segments, (w_qkv, w_out, w_up, w_down), small
    )
    full_out, full_up, full_down = (w.reshape(-1, w.shape[-1]) for w in (fo, fu, fd))
    gain_rows = small[:4] / lax.axis_size("ctx")
    total_count = small[4, 0]
    first_sum = x_rows.astype(F32) + jnp.dot(mixed, full_out, preferred_element_type=F32)
    normed_one, unit_one, scale_one = layer_norm(first_sum, gain_rows[0], gain_rows[1])
    normed_low = normed_one.astype(BF16)
    upper_rows = jnp.dot(normed_low, full_up, preferred_element_type=F32)
    active, gelu_back = jax.vjp(gelu_exact, upper_rows)
    active_low = active.astype(BF16)
    second = normed_one + jnp.dot(active_low, full_down, preferred_element_type=F32)
    result, unit_two, scale_two = layer_norm(second, gain_rows[2], gain_rows[3])
    errors = result - teacher[0].astype(F32)
    partial_value = jnp.sum(mask_rows * jnp.mean(errors * errors, axis=1))
    everyone = tok_count * lax.axis_size("ctx") * lax.axis_size("wsh")
    grad_result = everyone / total_count * mask_rows[:, None] * errors
    grad_second, grad_gain_two, grad_shift_two = norm_back(
        grad_result, unit_two, scale_two, gain_rows[2]
    )
    grad_branch_two = grad_second.astype(BF16)
    grad_down = jnp.dot(active_low.T, grad_branch_two, preferred_element_type=F32)
    grad_active = jnp.dot(grad_branch_two, full_down.T, preferred_element_type=F32)
    (grad_upper,) = gelu_back(grad_active)
    grad_upper_low = grad_upper.astype(BF16)
    grad_up = jnp.dot(normed_low.T, grad_upper_low, preferred_element_type=F32)
    grad_normed = jnp.dot(grad_upper_low, full_up.T, preferred_element_type=F32) + grad_second
    grad_first, grad_gain_one, grad_shift_one = norm_back(
        grad_normed, unit_one, scale_one, gain_rows[0]
    )
    grad_branch = grad_first.astype(BF16)
    grad_outw = jnp.dot(mixed.T, grad_branch, preferred_element_type=F32)
    grad_mixed = jnp.dot(grad_branch, full_out.T, preferred_element_type=F32).astype(BF16)
    grad_tokens, grad_inw = backward(grad_mixed, x_rows.T, grad_first, fq, *kept)
    grad_norms = jnp.stack([grad_gain_one, grad_shift_one, grad_gain_two, grad_shift_two])
    small = jnp.zeros((8, model_dim), F32).at[:4].set(grad_norms).at[4, 0].set(partial_value)
    (final_qkv, final_out, final_up, final_down), small = reduce_grads(
        [grad_inw] + [g.astype(BF16) for g in (grad_outw, grad_up, grad_down)], small
    )
    width = model_dim // (lax.axis_size("ctx") * lax.axis_size("wsh"))
    at = ctx * lax.axis_size("wsh") + wsh
    final_norms = lax.dynamic_slice(small, (0, at * width), (4, width))
    return (
        result.astype(BF16)[None],
        grad_tokens[None],
        small[4, 0] / total_count,
        final_qkv,
        final_out,
        final_up,
        final_down,
        final_norms,
    )


def solution(mesh):
    placed = (
        P("wsh", "ctx", None),
        P("wsh", "ctx", None),
        P("wsh", None, "ctx"),
        P("wsh", "ctx"),
        P("wsh", "ctx"),
        P("wsh", None),
        P("wsh", None),
        P("wsh", None),
        P("wsh", None),
        P(None, "wsh"),
    )
    return jax.shard_map(
        local,
        mesh=mesh,
        in_specs=placed,
        out_specs=(
            P("wsh", "ctx", None),
            P("wsh", "ctx", None),
            P(),
            P("wsh", "ctx"),
            P("wsh", "ctx"),
            P("wsh", "ctx"),
            P("wsh", "ctx"),
            P(None, ("ctx", "wsh")),
        ),
        check_vma=False,
    )
```

```python
import functools
import jax
import jax.numpy as jnp
from jax import lax
from jax.experimental import pallas as pl
from jax.experimental.pallas import tpu as pltpu
from jax.sharding import PartitionSpec as P

MESH = pl.DeviceIdType.MESH
BF16 = jnp.bfloat16
F32 = jnp.float32


class Place:
    def __init__(self):
        self.ctx = lax.axis_index("ctx")
        self.wsh = lax.axis_index("wsh")
        self.zlo = self.ctx // 8
        self.y = (self.ctx // 2) % 4
        self.core = self.ctx % 2
        self.zhi = self.wsh // 4
        self.x = self.wsh % 4

    def at(self, zlo=None, y=None, core=None, zhi=None, x=None):
        zlo = self.zlo if zlo is None else zlo
        y = self.y if y is None else y
        core = self.core if core is None else core
        zhi = self.zhi if zhi is None else zhi
        x = self.x if x is None else x
        return (zlo * 8 + y * 2 + core, zhi * 4 + x)

    def sibling(self):
        return self.at(core=1 - self.core)

    def x_peer(self, step):
        return self.at(x=(self.x + step) % 4)

    def y_peer(self, step):
        return self.at(y=(self.y + step) % 4)

    def z_peer(self, step):
        z = (self.zhi * 4 + self.zlo + step + 8) % 8
        return self.at(zlo=z % 4, zhi=z // 4)

    def plane(self):
        return [
            self.at(y=(self.y + d) % 4, core=(self.core + c) % 2)
            for d, c in ((0, 1), (1, 0), (1, 1), (2, 0), (2, 1), (3, 0), (3, 1))
        ]

    def rank(self):
        return self.y * 2 + self.core

    def z_far(self):
        return self.at(zhi=1 - self.zhi)

    def doubling(self):
        return (
            self.sibling(),
            self.at(y=self.y + 1 - 2 * (self.y % 2)),
            self.at(y=(self.y + 2) % 4),
            self.at(x=self.x + 1 - 2 * (self.x % 2)),
            self.at(x=(self.x + 2) % 4),
            self.at(zlo=self.zlo + 1 - 2 * (self.zlo % 2)),
            self.at(zlo=(self.zlo + 2) % 4),
            self.z_far(),
        )


def greet(devices):
    barrier = pltpu.get_barrier_semaphore()
    for device in devices:
        pl.semaphore_signal(barrier, inc=1, device_id=device, device_id_type=MESH)
    pl.semaphore_wait(barrier, len(devices))


def remote(source, target, send_sem, recv_sem, device):
    return pltpu.make_async_remote_copy(
        src_ref=source,
        dst_ref=target,
        send_sem=send_sem,
        recv_sem=recv_sem,
        device_id=device,
        device_id_type=MESH,
    )


def half_of(width, which):
    half = width // 2
    return pl.ds(pl.multiple_of(which * half, 128), half)


class Doubling:
    def __init__(self, place, tile, slots, send_sems, recv_sems):
        self.partners = place.doubling()
        self.tile, self.slots = tile, slots
        self.send_sems, self.recv_sems = send_sems, recv_sems
        self.step = 0
        self.copies = []

    def start(self):
        k = self.step
        copy = remote(
            self.tile.at[k], self.slots.at[k], self.send_sems.at[k], self.recv_sems.at[k], self.partners[k]
        )
        copy.start()
        self.copies.append(copy)

    def advance(self):
        k = self.step
        self.copies[k].wait_recv()
        self.tile[k + 1] = self.tile[k] + self.slots[k]
        self.step = k + 1
        if self.step < 8:
            self.start()

    def drain(self):
        for copy in self.copies:
            copy.wait_send()


NEG = -1e30
NT = (((1,), (1,)), ((), ()))
TN = (((0,), (0,)), ((), ()))


def matmul(left, right, dims=(((1,), (0,)), ((), ()))):
    return lax.dot_general(left, right, dims, preferred_element_type=F32)


class Gather:
    def __init__(self, place, shard, full, send_sems, recv_sems, local_sem):
        self.place, self.shard, self.full = place, shard, full
        self.send_sems, self.recv_sems = send_sems, recv_sems
        self.rows = shard.shape[0]
        self.lanes = half_of(shard.shape[1], place.core)
        self.local = pltpu.make_async_copy(shard, full.at[place.wsh], local_sem)
        self.copies = {}

    def part(self, index, which=None):
        block = self.full.at[index]
        if which is None:
            return block.at[:, self.lanes]
        half = self.rows // 2
        return block.at[which * half : (which + 1) * half, self.lanes]

    def send(self, k, source, target, device):
        copy = remote(source, target, self.send_sems.at[k], self.recv_sems.at[k], device)
        copy.start()
        self.copies[k] = copy

    def own(self, far, step):
        return (far * 4) + (self.place.x + step + 4) % 4

    def start_z(self):
        place = self.place
        self.local.start()
        self.send(2, self.shard.at[:, self.lanes], self.part(place.wsh), place.z_far())

    def start_x(self):
        place = self.place
        self.send(0, self.shard.at[:, self.lanes], self.part(place.wsh), place.x_peer(1))
        self.send(1, self.shard.at[:, self.lanes], self.part(place.wsh), place.x_peer(3))

    def pass_on(self, zh, base):
        place = self.place
        left, right = self.own(zh, -1), self.own(zh, 1)
        self.copies[base].wait_recv()
        self.send(base + 3, self.part(left, 0), self.part(left, 0), place.x_peer(1))
        self.send(base + 5, self.part(left), self.part(left), place.sibling())
        self.copies[base + 1].wait_recv()
        self.send(base + 4, self.part(right, 1), self.part(right, 1), place.x_peer(3))
        self.send(base + 6, self.part(right), self.part(right), place.sibling())

    def opposite(self, zh, base):
        place = self.place
        index = self.own(zh, 2)
        for which in range(2):
            self.copies[base + 3 + which].wait_recv()
            self.send(base + 7 + which, self.part(index, which), self.part(index, which), place.sibling())

    def near(self):
        self.pass_on(self.place.zhi, 0)

    def near_opposite(self):
        self.opposite(self.place.zhi, 0)

    def from_z(self):
        place = self.place
        index = self.own(1 - place.zhi, 0)
        self.copies[2].wait_recv()
        self.send(10, self.part(index), self.part(index), place.x_peer(1))
        self.send(11, self.part(index), self.part(index), place.x_peer(3))
        self.send(9, self.part(index), self.part(index), place.sibling())

    def far(self):
        self.pass_on(1 - self.place.zhi, 10)

    def far_opposite(self):
        self.opposite(1 - self.place.zhi, 10)

    def finish(self):
        self.local.wait()
        for k in (5, 6, 7, 8, 9, 15, 16, 17, 18):
            self.copies[k].wait_recv()

    def drain(self):
        for k in self.copies:
            self.copies[k].wait_send()


def head_mask(which):
    lane = lax.broadcasted_iota(jnp.int32, (1, 128), 1)
    return jnp.where((lane // 64) == which, 1.0, 0.0).astype(BF16)


def to_slots(slot_row, head, count):
    row = slot_row[pl.ds(head, 1), :]
    iota = lax.broadcasted_iota(jnp.int32, (count, count), 0).astype(F32)
    return jnp.where(iota == row, 1.0, 0.0).astype(BF16)


def to_tokens(slot_col, head, count):
    lane = lax.broadcasted_iota(jnp.int32, slot_col.shape, 1)
    column = jnp.sum(jnp.where(lane == head, slot_col[...], 0.0), axis=1, keepdims=True)
    iota = lax.broadcasted_iota(jnp.int32, (count, count), 1).astype(F32)
    return jnp.where(iota == column, 1.0, 0.0).astype(BF16)


def pair_select(first, second):
    lane = lax.broadcasted_iota(jnp.int32, first.shape, 1)
    return jnp.where((lane // 64) % 2 == 0, first, second)


def make_slots(clusters, segments, slot_row, slot_col, labels):
    heads, count = 12, clusters.shape[1]
    groups = lax.shift_right_logical(clusters[...], 2)
    iota = lax.broadcasted_iota(jnp.int32, (32, count), 0)
    before = lax.broadcasted_iota(jnp.int32, (count, count), 0)
    after = lax.broadcasted_iota(jnp.int32, (count, count), 1)
    upper = jnp.where(before <= after, 1.0, 0.0).astype(BF16)
    hot = [jnp.where(groups[h : h + 1, :] == iota, 1.0, 0.0) for h in range(heads)]
    counts = matmul(jnp.concatenate(hot, axis=0).astype(BF16), upper)
    group_f = groups.astype(F32)
    rows = []
    for h in range(heads):
        rank = jnp.sum(counts[32 * h : 32 * h + 32] * hot[h], axis=0, keepdims=True)
        rows.append(group_f[h : h + 1] * 16.0 + rank - 1.0)
    slots = jnp.concatenate(rows + [jnp.zeros((128 - heads, count), F32)], axis=0)
    slot_row[...] = slots[:16]
    slot_col[...] = slots.T
    label = (segments[0:1, :] * 4 + (clusters[...] & 3)).astype(F32)
    labels[...] = jnp.concatenate([label, jnp.zeros((112, count), F32)], axis=0).T.astype(BF16)


def rows16(j):
    return slice(16 * j, 16 * j + 16)


def forward_kernel(
    x, clusters, segments, wq, wo, wu, wd, small,
    mixed, fq_out, fo, fu, fd, got_out, before_out, after_out, logsum, hot_out, cold_out, slot_row, slot_col, total,
    fq, got, before, after, hot, cold,
    labels, sent_labels, got_labels, before_labels, after_labels, wide_labels, sent, out, back, log_cols,
    tile, slots,
    w_send, w_recv, w_local, t_send, t_recv, a_send, a_recv, a_local, z_send, z_recv, b_send, b_recv, b_local, k_sem,
):
    place = Place()
    plane, rank = place.plane(), place.rank()
    up, down = place.z_peer(1), place.z_peer(-1)
    kept = []

    def keep(source, target):
        copy = pltpu.make_async_copy(source, target, k_sem.at[len(kept)])
        copy.start()
        kept.append(copy)

    partners = place.doubling()
    greet(
        plane + [place.x_peer(1), place.x_peer(2), place.x_peer(3), place.z_far(), up, down, partners[5], partners[6]]
    )
    weights = [
        Gather(place, shard, full, w_send.at[i], w_recv.at[i], w_local.at[i])
        for i, (shard, full) in enumerate(((wq, fq), (wo, fo), (wu, fu), (wd, fd)))
    ]
    first, rest = weights[0], weights[1:]
    first.start_z()
    first.start_x()
    tile[0] = small[...]
    doubling = Doubling(place, tile, slots, t_send, t_recv)
    doubling.start()
    count = x.shape[0]
    make_slots(clusters, segments, slot_row, slot_col, labels)

    sent_labels[...] = jnp.zeros_like(sent_labels)

    def move_labels(head, carry):
        lane = lax.broadcasted_iota(jnp.int32, (count, 128), 1)
        moved = matmul(to_slots(slot_row, head, count), labels[...])
        sent_labels[...] = jnp.where(lane == head, moved, sent_labels[...])
        return carry

    lax.fori_loop(0, 12, move_labels, 0)
    labels[...] = sent_labels[...].astype(BF16)

    def block(which):
        return pl.ds(pl.multiple_of(which * 64, 64), 64)

    def ranks():
        return [dev[0] % 8 for dev in plane]

    label_copies = [
        remote(labels.at[block(to)], got_labels.at[rank], a_send.at[6, k], a_recv.at[6, k], plane[k])
        for k, to in enumerate(ranks())
    ]
    for copy in label_copies:
        copy.start()
    own_labels = pltpu.make_async_copy(labels.at[block(rank)], got_labels.at[rank], a_local.at[6])
    own_labels.start()
    doubling.advance()
    first.near()
    doubling.advance()
    own_labels.wait()
    for copy in label_copies:
        copy.wait_recv()
    label_up = remote(got_labels.at[4:8], before_labels, z_send.at[6, 0], z_recv.at[6, 0], up)
    label_down = remote(got_labels.at[0:4], after_labels, z_send.at[6, 1], z_recv.at[6, 1], down)
    label_up.start()
    label_down.start()
    first.from_z()
    for w in rest:
        w.start_z()
    first.near_opposite()
    doubling.advance()
    label_up.wait_recv()
    label_down.wait_recv()
    for j in range(4):
        wide_labels[j, 0:64] = jnp.where(
            place.zlo == 0, -1.0, before_labels[:, rows16(j), :].reshape(64, 128).astype(F32)
        )
        wide_labels[j, 64:192] = got_labels[:, rows16(j), :].reshape(128, 128).astype(F32)
        wide_labels[j, 192:256] = jnp.where(
            place.zlo == 3, -1.0, after_labels[:, rows16(j), :].reshape(64, 128).astype(F32)
        )

    def make_hot(head, carry):
        lane = lax.broadcasted_iota(jnp.int32, (256, 128), 1)
        for j in range(4):
            column = jnp.sum(jnp.where(lane == head, wide_labels[j], 0.0), axis=1, keepdims=True)
            same = lane.astype(F32) == column
            cold[head * 4 + j] = jnp.where(same, 0.0, NEG).astype(BF16)
            hot[head * 4 + j] = jnp.where(same, 1.0, 0.0)[64:192].astype(BF16)
        return carry

    lax.fori_loop(0, 12, make_hot, 0)
    keep(hot, hot_out)
    keep(cold, cold_out)
    doubling.advance()
    first.far()
    doubling.advance()
    for w in rest:
        w.start_x()
    first.far_opposite()
    first.finish()
    keep(fq, fq_out)

    def send_copies(p, fn):
        for k, to in enumerate(ranks()):
            fn(remote(sent.at[p, block(to)], got.at[p, rank], a_send.at[p, k], a_recv.at[p, k], plane[k]))

    def own_copy(p):
        return pltpu.make_async_copy(sent.at[p, block(rank)], got.at[p, rank], a_local.at[p])

    def project(p, carry):
        parts = []
        for t in range(3):
            lanes = pl.ds(pl.multiple_of(t * 768 + p * 128, 128), 128)
            value = matmul(x[...], fq[:, :, lanes].reshape(768, 128)).astype(BF16)
            parts.append(value * jnp.asarray(0.125, BF16) if t == 0 else value)
        rows = jnp.concatenate(parts, axis=1)
        moved = [matmul(to_slots(slot_row, 2 * p + a, count), rows) for a in range(2)]
        sent[p] = pair_select(moved[0], moved[1]).astype(BF16)
        send_copies(p, lambda copy: copy.start())
        own_copy(p).start()
        return carry

    lax.fori_loop(0, 6, project, 0)
    doubling.advance()

    def halo(p):
        return (
            remote(got.at[p, 4:8, :, 128:384], before.at[p], z_send.at[p, 0], z_recv.at[p, 0], up),
            remote(got.at[p, 0:4, :, 128:384], after.at[p], z_send.at[p, 1], z_recv.at[p, 1], down),
        )

    def back_copies(p, fn):
        for k, to in enumerate(ranks()):
            fn(remote(out.at[p, to], back.at[p, rank], b_send.at[p, k], b_recv.at[p, k], plane[k]))

    def own_back(p):
        return pltpu.make_async_copy(out.at[p, rank], back.at[p, rank], b_local.at[p])

    def arrive(p):
        own_copy(p).wait()
        send_copies(p, lambda copy: copy.wait_recv())
        for copy in halo(p):
            copy.start()

    masks = [head_mask(a) for a in range(2)]

    def attend(p):
        for copy in halo(p):
            copy.wait_recv()
        lane = lax.broadcasted_iota(jnp.int32, (128, 128), 1)
        for j in range(4):
            r = rows16(j)
            query = got[p, :, r, 0:128].reshape(128, 128)
            keys = jnp.concatenate(
                [before[p, :, r, 0:128].reshape(64, 128), got[p, :, r, 128:256].reshape(128, 128),
                 after[p, :, r, 0:128].reshape(64, 128)], axis=0)
            values = jnp.concatenate(
                [before[p, :, r, 128:256].reshape(64, 128), got[p, :, r, 256:384].reshape(128, 128),
                 after[p, :, r, 128:256].reshape(64, 128)], axis=0)
            halves = []
            for a in range(2):
                head = 2 * p + a
                scores = matmul(
                    jnp.concatenate([query * masks[a], hot[head * 4 + j]], axis=1),
                    jnp.concatenate([keys, cold[head * 4 + j]], axis=1), NT)
                top = jnp.max(scores, axis=1, keepdims=True)
                weights_ = jnp.exp(scores - top)
                sums = jnp.sum(weights_, axis=1, keepdims=True)
                halves.append(matmul(weights_.astype(BF16), values) / sums)
                log_cols[j] = jnp.where(lane == head, top + jnp.log(sums), log_cols[j])
            out[p, :, r, :] = pair_select(halves[0], halves[1]).astype(BF16).reshape(8, 16, 128)
        back_copies(p, lambda copy: copy.start())
        own_back(p).start()

    log_cols[...] = jnp.zeros_like(log_cols)
    arrive(0)
    for w in rest:
        w.near()

    def steady(p, carry):
        arrive(p)
        attend(p - 1)
        return carry

    lax.fori_loop(1, 4, steady, 0)
    doubling.advance()
    for w in rest:
        w.from_z()
        w.near_opposite()
    lax.fori_loop(4, 6, steady, 0)
    doubling.advance()
    attend(5)
    keep(got, got_out)
    keep(before, before_out)
    keep(after, after_out)

    def home(p, carry):
        own_back(p).wait()
        back_copies(p, lambda copy: copy.wait_recv())
        rows = back[p].reshape(count, 128)
        moved = [matmul(to_tokens(slot_col, 2 * p + a, count), rows) for a in range(2)]
        mixed[:, pl.ds(pl.multiple_of(p * 128, 128), 128)] = pair_select(moved[0], moved[1]).astype(BF16)
        return carry

    lax.fori_loop(0, 6, home, 0)
    for j in range(4):
        logsum[j] = log_cols[j].T[:16]
    for w in rest:
        w.far()
    for w in rest:
        w.far_opposite()
    for w in rest:
        w.finish()
    total[...] = tile[8]

    def settle(p, carry):
        send_copies(p, lambda copy: copy.wait_send())
        back_copies(p, lambda copy: copy.wait_send())
        for copy in halo(p):
            copy.wait_send()
        return carry

    lax.fori_loop(0, 6, settle, 0)
    for copy in label_copies + [label_up, label_down]:
        copy.wait_send()
    for w in weights:
        w.drain()
    for copy in kept:
        copy.wait()
    doubling.drain()


ANY = pl.BlockSpec(memory_space=pl.ANY)
VMEM = pl.BlockSpec(memory_space=pltpu.VMEM)


def shaped(*shape, dtype=BF16):
    return jax.ShapeDtypeStruct(shape, dtype)


def forward(x, clusters, segments, shards, small):
    count = x.shape[0]
    dma = pltpu.SemaphoreType.DMA
    return pl.pallas_call(
        forward_kernel,
        out_shape=[
            shaped(*x.shape),
            *[shaped(8, *w.shape) for w in shards],
            shaped(6, 8, 64, 384),
            shaped(6, 4, 64, 256),
            shaped(6, 4, 64, 256),
            shaped(4, 16, 128, dtype=F32),
            shaped(48, 128, 128),
            shaped(48, 256, 128),
            shaped(16, count, dtype=F32),
            shaped(count, 128, dtype=F32),
            shaped(*small.shape, dtype=F32),
        ],
        in_specs=[VMEM] * 3 + [ANY] * 4 + [VMEM],
        out_specs=[VMEM] + [ANY] * 7 + [VMEM] + [ANY] * 2 + [VMEM] * 3,
        scratch_shapes=[
            pltpu.VMEM((8, *shards[0].shape), BF16),
            pltpu.VMEM((6, 8, 64, 384), BF16),
            pltpu.VMEM((6, 4, 64, 256), BF16),
            pltpu.VMEM((6, 4, 64, 256), BF16),
            pltpu.VMEM((48, 128, 128), BF16),
            pltpu.VMEM((48, 256, 128), BF16),
            pltpu.VMEM((count, 128), BF16),
            pltpu.VMEM((count, 128), F32),
            pltpu.VMEM((8, 64, 128), BF16),
            pltpu.VMEM((4, 64, 128), BF16),
            pltpu.VMEM((4, 64, 128), BF16),
            pltpu.VMEM((4, 256, 128), F32),
            pltpu.VMEM((6, count, 384), BF16),
            pltpu.VMEM((6, 8, 64, 128), BF16),
            pltpu.VMEM((6, 8, 64, 128), BF16),
            pltpu.VMEM((4, 128, 128), F32),
            pltpu.VMEM((9, *small.shape), F32),
            pltpu.VMEM((8, *small.shape), F32),
            dma((4, 19)), dma((4, 19)), dma((4,)), dma((8,)), dma((8,)),
            dma((7, 7)), dma((7, 7)), dma((7,)), dma((7, 2)), dma((7, 2)),
            dma((6, 7)), dma((6, 7)), dma((6,)), dma((6,)),
        ],
        compiler_params=pltpu.CompilerParams(
            collective_id=0, has_side_effects=True, vmem_limit_bytes=60 * 2**20
        ),
        name="forward_attention",
    )(x, clusters, segments, *shards, small)


class Reduce:
    def __init__(self, place, grad, mine, held, near, far, sum_x, from_y, sum_y, from_z, out, send_sems, recv_sems, load_sem):
        self.place, self.grad, self.mine, self.held = place, grad, mine, held
        self.near, self.far, self.sum_x, self.from_y = near, far, sum_x, from_y
        self.sum_y, self.from_z, self.out = sum_y, from_z, out
        self.send_sems, self.recv_sems, self.load_sem = send_sems, recv_sems, load_sem
        self.rows, self.width = grad.shape[2], grad.shape[3]
        self.owner, self.side = place.y // 2, place.zlo // 2
        self.here = place.zhi == self.owner
        self.final = jnp.logical_and(self.here, place.core == self.side)
        self.other = jnp.logical_and(self.here, place.core != self.side)
        self.copies = {}

    def send(self, k, source, target, device):
        copy = remote(source, target, self.send_sems.at[k], self.recv_sems.at[k], device)
        copy.start()
        self.copies[k] = copy

    def each(self, count, body):
        def step(i, carry):
            body(pl.ds(pl.multiple_of(i * 48, 16), 48))
            return carry

        lax.fori_loop(0, count // 48, step, 0)

    def after(self, rows, offset):
        return pl.ds(pl.multiple_of(rows.start + offset, 16), rows.size)

    def start(self):
        place = self.place
        self.send(0, self.grad.at[:, :, :, half_of(self.width, 1 - place.core)], self.held, place.sibling())
        if self.load_sem is not None:
            self.load = pltpu.make_async_copy(
                self.grad.at[:, :, :, half_of(self.width, place.core)], self.mine, self.load_sem
            )
            self.load.start()

    def own(self, zh, xx, rows):
        if self.load_sem is not None:
            return self.mine[zh, xx, rows, :]
        return self.grad[zh, xx, rows, half_of(self.width, self.place.core)]

    def add_pair(self, xx):
        def block(zh, carry):
            self.each(self.rows, lambda rows: self.add_rows(zh, xx, rows))
            return carry

        lax.fori_loop(0, 2, block, 0)

    def add_rows(self, zh, xx, rows):
        self.held[zh, xx, rows, :] = (
            self.own(zh, xx, rows).astype(F32) + self.held[zh, xx, rows, :].astype(F32)
        ).astype(BF16)

    def to_opposite(self):
        place = self.place
        self.copies[0].wait_recv()
        if self.load_sem is not None:
            self.load.wait()
        half = self.rows // 2
        opposite = (place.x + 2) % 4
        self.add_pair(opposite)
        self.send(1, self.held.at[:, opposite, 0:half], self.near.at[0], place.x_peer(1))
        self.send(2, self.held.at[:, opposite, half : self.rows], self.near.at[1], place.x_peer(3))
        for step in (1, 3, 0):
            self.add_pair((place.x + step) % 4)

    def to_near(self):
        place = self.place
        half = self.rows // 2
        for k, step in enumerate((1, 3)):
            to = (place.x + step) % 4
            self.copies[1 + k].wait_recv()

            def block(zh, carry, k=k, to=to):
                def body(rows):
                    there = self.after(rows, k * half)
                    self.held[zh, to, there, :] = (
                        self.held[zh, to, there, :].astype(F32) + self.near[k, zh, rows, :].astype(F32)
                    ).astype(BF16)

                self.each(half, body)
                return carry

            lax.fori_loop(0, 2, block, 0)
            self.send(3 + k, self.held.at[:, to], self.far.at[k], place.x_peer(step))

    def to_y(self):
        place = self.place
        half = self.rows // 2
        for k in range(2):
            self.copies[3 + k].wait_recv()

        def block(zh, carry):
            def body(rows):
                value = self.held[zh, place.x, rows, :].astype(F32)
                value = value + self.far[0, zh, rows, :].astype(F32) + self.far[1, zh, rows, :].astype(F32)
                self.sum_x[zh, rows, :] = value.astype(BF16)

            self.each(self.rows, body)
            return carry

        lax.fori_loop(0, 2, block, 0)
        for k, d in enumerate((1, 2, 3)):
            to = (place.y + d) % 4
            part = pl.ds(pl.multiple_of((to % 2) * half, 16), half)
            self.send(5 + k, self.sum_x.at[to // 2, part], self.from_y.at[k], place.y_peer(d))

    def z_copy(self, k):
        partners = self.place.doubling()
        device = (partners[7], partners[6], partners[5])[k]
        return remote(self.sum_y, self.from_z.at[k], self.send_sems.at[8 + k], self.recv_sems.at[8 + k], device)

    def to_far_z(self):
        place = self.place
        half = self.rows // 2
        for k in range(3):
            self.copies[5 + k].wait_recv()

        def body(rows):
            value = self.sum_x[self.owner, self.after(rows, (place.y % 2) * half), :].astype(F32)
            for k in range(3):
                value = value + self.from_y[k, rows, :].astype(F32)
            self.sum_y[rows, :] = value.astype(BF16)

        self.each(half, body)

        @pl.when(jnp.logical_not(self.here))
        def _():
            self.z_copy(0).start()

    def add_z(self, k):
        self.z_copy(k).wait_recv()

        def body(rows):
            self.sum_y[rows, :] = (self.sum_y[rows, :].astype(F32) + self.from_z[k, rows, :].astype(F32)).astype(BF16)

        self.each(self.rows // 2, body)

    def to_near_z(self):
        @pl.when(self.here)
        def _():
            self.add_z(0)

        @pl.when(self.other)
        def _():
            self.z_copy(1).start()

    def to_next_z(self):
        @pl.when(self.final)
        def _():
            self.add_z(1)
            self.z_copy(2).start()

    def spread_copy(self, k, device):
        half = self.rows // 2
        part = self.out.at[pl.ds(pl.multiple_of((self.place.y % 2) * half, 16), half)]
        return remote(part, part, self.send_sems.at[11 + k], self.recv_sems.at[11 + self.place.y % 2], device)

    def spread(self):
        half = self.rows // 2

        @pl.when(self.final)
        def _():
            self.z_copy(2).wait()

            def body(rows):
                there = self.after(rows, (self.place.y % 2) * half)
                self.out[there, :] = (
                    self.sum_y[rows, :].astype(F32) + self.from_z[2, rows, :].astype(F32)
                ).astype(BF16)

            self.each(half, body)
            for k, device in enumerate(self.place.plane()):
                self.spread_copy(k, device).start()

    def finish(self):
        half = self.rows // 2
        for k in range(2):
            part = self.out.at[k * half : (k + 1) * half]

            @pl.when(jnp.logical_not(jnp.logical_and(self.final, self.place.y % 2 == k)))
            def _(k=k, part=part):
                remote(part, part, self.send_sems.at[11], self.recv_sems.at[11 + k], self.place.sibling()).wait_recv()

    def drain(self):
        for k in self.copies:
            self.copies[k].wait_send()

        @pl.when(self.final)
        def _():
            for k, device in enumerate(self.place.plane()):
                self.spread_copy(k, device).wait_send()

        @pl.when(self.other)
        def _():
            self.z_copy(1).wait_send()

        @pl.when(jnp.logical_not(self.here))
        def _():
            self.z_copy(0).wait_send()


def reduce_scratch(rows, half):
    return [
        pltpu.VMEM((2, 4, rows, half), BF16),
        pltpu.VMEM((2, 2, rows // 2, half), BF16),
        pltpu.VMEM((2, 2, rows, half), BF16),
        pltpu.VMEM((2, rows, half), BF16),
        pltpu.VMEM((3, rows // 2, half), BF16),
        pltpu.VMEM((rows // 2, half), BF16),
        pltpu.VMEM((3, rows // 2, half), BF16),
    ]


def backward_kernel(*refs):
    (grad_mixed, grad_first, logsum, slot_row, slot_col, small, x_hbm, fq_hbm, got_hbm, before_hbm, after_hbm,
     hot_hbm, cold_hbm, go, gu, gd) = refs[:16]
    grad_x, out_q, out_o, out_u, out_d, small_out = refs[16:22]
    x_turned, fq, got, before, after, hot, cold, gq = refs[22:30]
    sent, got_grad, grads, to_before, to_after, from_before, from_after, back = refs[30:38]
    mine = (None, *refs[38:41])
    reduce_refs = [refs[41 + 7 * i : 48 + 7 * i] for i in range(4)]
    (tile, slots, a_send, a_recv, a_local, z_send, z_recv, b_send, b_recv, b_local,
     t_send, t_recv, r_send, r_recv, r_load, l_sem) = refs[69:]
    place = Place()
    plane, rank = place.plane(), place.rank()
    up, down = place.z_peer(1), place.z_peer(-1)
    partners = place.doubling()
    greet(
        plane + [place.x_peer(1), place.x_peer(2), place.x_peer(3), place.z_far(), up, down, partners[5], partners[6]]
    )
    loads = [
        pltpu.make_async_copy(source, target, l_sem.at[i])
        for i, (source, target) in enumerate(
            ((got_hbm, got), (before_hbm, before), (after_hbm, after), (hot_hbm, hot), (cold_hbm, cold),
             (fq_hbm, fq), (x_hbm, x_turned))
        )
    ]
    for copy in loads:
        copy.start()
    sums = [
        Reduce(place, grad, mine[i], *reduce_refs[i], out, r_send.at[i], r_recv.at[i], r_load.at[i] if i else None)
        for i, (grad, out) in enumerate(((gq, out_q), (go, out_o), (gu, out_u), (gd, out_d)))
    ]
    query_sum, rest = sums[0], sums[1:]
    for r in rest:
        r.start()
    tile[0] = small[...]
    doubling = Doubling(place, tile, slots, t_send, t_recv)
    doubling.start()
    count = grad_mixed.shape[0]
    ranks = [dev[0] % 8 for dev in plane]

    def block(which):
        return pl.ds(pl.multiple_of(which * 64, 64), 64)

    def send_copies(p, fn):
        for k, to in enumerate(ranks):
            fn(remote(sent.at[p, block(to)], got_grad.at[p, rank], a_send.at[p, k], a_recv.at[p, k], plane[k]))

    def own_copy(p):
        return pltpu.make_async_copy(sent.at[p, block(rank)], got_grad.at[p, rank], a_local.at[p])

    def leave(p, carry):
        rows = grad_mixed[:, pl.ds(pl.multiple_of(p * 128, 128), 128)]
        moved = [matmul(to_slots(slot_row, 2 * p + a, count), rows) for a in range(2)]
        sent[p] = pair_select(moved[0], moved[1]).astype(BF16)
        send_copies(p, lambda copy: copy.start())
        own_copy(p).start()
        return carry

    lax.fori_loop(0, 6, leave, 0)
    for r in rest:
        r.to_opposite()
    for copy in loads[:5]:
        copy.wait()
    doubling.advance()

    def halo(p):
        return (
            remote(to_after.at[p], from_before.at[p], z_send.at[p, 0], z_recv.at[p, 0], up),
            remote(to_before.at[p], from_after.at[p], z_send.at[p, 1], z_recv.at[p, 1], down),
        )

    def back_copies(p, fn):
        for k, to in enumerate(ranks):
            fn(remote(grads.at[p, to], back.at[p, rank], b_send.at[p, k], b_recv.at[p, k], plane[k]))

    def own_back(p):
        return pltpu.make_async_copy(grads.at[p, rank], back.at[p, rank], b_local.at[p])

    masks = [head_mask(a) for a in range(2)]

    def attend(p):
        own_copy(p).wait()
        send_copies(p, lambda copy: copy.wait_recv())
        for j in range(4):
            r = rows16(j)
            query = got[p, :, r, 0:128].reshape(128, 128)
            keys = jnp.concatenate(
                [before[p, :, r, 0:128].reshape(64, 128), got[p, :, r, 128:256].reshape(128, 128),
                 after[p, :, r, 0:128].reshape(64, 128)], axis=0)
            values = jnp.concatenate(
                [before[p, :, r, 128:256].reshape(64, 128), got[p, :, r, 256:384].reshape(128, 128),
                 after[p, :, r, 128:256].reshape(64, 128)], axis=0)
            grad = got_grad[p, :, r, :].reshape(128, 128)
            dq, dk, dv = [], [], []
            for a in range(2):
                head = 2 * p + a
                scores = matmul(
                    jnp.concatenate([keys, cold[head * 4 + j]], axis=1),
                    jnp.concatenate([query * masks[a], hot[head * 4 + j]], axis=1), NT)
                probs = jnp.exp(scores - logsum[j, pl.ds(head, 1), :])
                grad_probs = matmul(values, grad * masks[a], NT)
                delta = jnp.sum(probs * grad_probs, axis=0, keepdims=True)
                grad_scores = (probs * (grad_probs - delta)).astype(BF16)
                dk.append(matmul(grad_scores, query))
                dv.append(matmul(probs.astype(BF16), grad))
                dq.append(matmul(grad_scores, keys, TN))
            dq = (pair_select(*dq) * 0.125).astype(BF16)
            dk = pair_select(*dk).astype(BF16)
            dv = pair_select(*dv).astype(BF16)
            both = jnp.concatenate([dk, dv], axis=1)
            to_before[p, :, r, :] = both[0:64].reshape(4, 16, 256)
            to_after[p, :, r, :] = both[192:256].reshape(4, 16, 256)
            grads[p, :, r, 0:128] = dq.reshape(8, 16, 128)
            grads[p, :, r, 128:384] = both[64:192].reshape(8, 16, 256)
        for copy in halo(p):
            copy.start()

    def give(p):
        for copy in halo(p):
            copy.wait_recv()
        for part, extra in ((slice(0, 4), from_before), (slice(4, 8), from_after)):
            grads[p, part, :, 128:384] = (
                grads[p, part, :, 128:384].astype(F32) + extra[p].astype(F32)
            ).astype(BF16)
        back_copies(p, lambda copy: copy.start())
        own_back(p).start()

    attend(0)
    doubling.advance()

    def steady(p, carry):
        attend(p)
        give(p - 1)
        return carry

    lax.fori_loop(1, 3, steady, 0)
    for r in rest:
        r.to_near()
    doubling.advance()
    lax.fori_loop(3, 6, steady, 0)
    give(5)
    for copy in loads[5:]:
        copy.wait()
    doubling.advance()
    for r in rest:
        r.to_y()
    doubling.advance()
    grad_x[...] = grad_first[...]

    def home(p, carry):
        own_back(p).wait()
        back_copies(p, lambda copy: copy.wait_recv())
        rows = back[p].reshape(count, 384)
        moved = [matmul(to_tokens(slot_col, 2 * p + a, count), rows) for a in range(2)]
        grad_qkv = pair_select(moved[0], moved[1]).astype(BF16)
        weight = matmul(x_turned[...], grad_qkv).astype(BF16)
        columns = []
        for t in range(3):
            lanes = pl.ds(pl.multiple_of(t * 768 + p * 128, 128), 128)
            gq[:, :, :, lanes] = weight[:, t * 128 : t * 128 + 128].reshape(2, 4, 96, 128)
            columns.append(fq[:, :, lanes].reshape(768, 128))
        grad_x[...] += matmul(grad_qkv, jnp.concatenate(columns, axis=1), NT)
        return carry

    lax.fori_loop(0, 6, home, 0)
    query_sum.start()
    for r in rest:
        r.to_far_z()
    doubling.advance()
    query_sum.to_opposite()
    for r in rest:
        r.to_near_z()
    query_sum.to_near()
    doubling.advance()
    for r in rest:
        r.to_next_z()
    query_sum.to_y()
    doubling.advance()
    for r in rest:
        r.spread()
    query_sum.to_far_z()
    query_sum.to_near_z()
    query_sum.to_next_z()
    query_sum.spread()
    small_out[...] = tile[8]

    def settle(p, carry):
        send_copies(p, lambda copy: copy.wait_send())
        back_copies(p, lambda copy: copy.wait_send())
        for copy in halo(p):
            copy.wait_send()
        return carry

    lax.fori_loop(0, 6, settle, 0)
    for r in rest + [query_sum]:
        r.finish()
    for r in sums:
        r.drain()
    doubling.drain()


def backward(grad_mixed, grad_first, small, x_turned, fq, kept, grads):
    got, before, after, logsum, hot, cold, slot_row, slot_col = kept
    count = grad_mixed.shape[0]
    dma = pltpu.SemaphoreType.DMA
    blocks = [g.reshape(2, 4, g.shape[0] // 8, g.shape[1]) for g in grads]
    shapes = [(96, 2304)] + [b.shape[2:] for b in blocks]
    like = lambda array: pltpu.VMEM(array.shape, array.dtype)
    reduce_refs = []
    for rows, width in shapes:
        reduce_refs += reduce_scratch(rows, width // 2)
    loaded = (x_turned, fq, got, before, after, hot, cold)
    results = pl.pallas_call(
        backward_kernel,
        out_shape=[shaped(*grad_first.shape, dtype=F32)]
        + [shaped(rows, width // 2) for rows, width in shapes]
        + [shaped(*small.shape, dtype=F32)],
        in_specs=[VMEM] * 6 + [ANY] * 10,
        out_specs=[VMEM] * 6,
        scratch_shapes=[like(array) for array in loaded]
        + [
            pltpu.VMEM((2, 4, 96, 2304), BF16),
            pltpu.VMEM((6, count, 128), BF16),
            pltpu.VMEM((6, 8, 64, 128), BF16),
            pltpu.VMEM((6, 8, 64, 384), BF16),
            pltpu.VMEM((6, 4, 64, 256), BF16),
            pltpu.VMEM((6, 4, 64, 256), BF16),
            pltpu.VMEM((6, 4, 64, 256), BF16),
            pltpu.VMEM((6, 4, 64, 256), BF16),
            pltpu.VMEM((6, 8, 64, 384), BF16),
        ]
        + [pltpu.VMEM((2, 4, rows, width // 2), BF16) for rows, width in shapes[1:]]
        + reduce_refs
        + [
            pltpu.VMEM((9, *small.shape), F32),
            pltpu.VMEM((8, *small.shape), F32),
            dma((6, 7)), dma((6, 7)), dma((6,)), dma((6, 2)), dma((6, 2)),
            dma((6, 7)), dma((6, 7)), dma((6,)),
            dma((8,)), dma((8,)), dma((4, 18)), dma((4, 18)), dma((4,)), dma((7,)),
        ],
        compiler_params=pltpu.CompilerParams(
            collective_id=1, has_side_effects=True, vmem_limit_bytes=62 * 2**20
        ),
        name="backward_attention",
    )(grad_mixed, grad_first, logsum, slot_row, slot_col, small, *loaded, *blocks)
    ctx = lax.axis_index("ctx")
    finals = []
    for result in results[1:5]:
        width = result.shape[1] // 16
        finals.append(lax.dynamic_slice_in_dim(result, (ctx % 16) * width, width, axis=1).astype(F32))
    return results[0], finals, results[5]


def layer_norm(values, gain_row, shift_row):
    row_mean = jnp.mean(values, axis=-1, keepdims=True)
    centered = values - row_mean
    inv_scale = lax.rsqrt(jnp.mean(centered * centered, axis=-1, keepdims=True) + 1e-05)
    normed = centered * inv_scale
    return (normed * gain_row + shift_row, normed, inv_scale)


def norm_back(grad_rows, normed, inv_scale, gain_row):
    weighted = grad_rows * gain_row
    grad_input = inv_scale * (
        weighted
        - jnp.mean(weighted, axis=-1, keepdims=True)
        - normed * jnp.mean(weighted * normed, axis=-1, keepdims=True)
    )
    return (grad_input, jnp.sum(grad_rows * normed, axis=0), jnp.sum(grad_rows, axis=0))


def gelu_exact(values):
    return jax.nn.gelu(values, approximate=False)


def local(tokens, teacher, clusters, segments, counted, w_qkv, w_out, w_up, w_down, norms):
    x_rows = tokens[0]
    tok_count, model_dim = x_rows.shape
    wsh, ctx = lax.axis_index("wsh"), lax.axis_index("ctx")
    mask_rows = counted[0].astype(F32)
    small = lax.dynamic_update_slice(
        jnp.zeros((8, model_dim), F32).at[4, 0].set(jnp.sum(mask_rows)), norms.astype(F32), (0, wsh * norms.shape[1])
    )
    padded = jnp.zeros((16, tok_count), jnp.int32).at[: clusters.shape[1]].set(clusters[0])
    mixed, fq, fo, fu, fd, *kept, small = forward(
        x_rows, padded, segments, (w_qkv, w_out, w_up, w_down), small
    )
    full_out, full_up, full_down = (w.reshape(-1, w.shape[-1]) for w in (fo, fu, fd))
    gain_rows = small[:4] / lax.axis_size("ctx")
    total_count = small[4, 0]
    first_sum = x_rows.astype(F32) + jnp.dot(mixed, full_out, preferred_element_type=F32)
    normed_one, unit_one, scale_one = layer_norm(first_sum, gain_rows[0], gain_rows[1])
    normed_low = normed_one.astype(BF16)
    upper_rows = jnp.dot(normed_low, full_up, preferred_element_type=F32)
    active, gelu_back = jax.vjp(gelu_exact, upper_rows)
    active_low = active.astype(BF16)
    second = normed_one + jnp.dot(active_low, full_down, preferred_element_type=F32)
    result, unit_two, scale_two = layer_norm(second, gain_rows[2], gain_rows[3])
    errors = result - teacher[0].astype(F32)
    partial_value = jnp.sum(mask_rows * jnp.mean(errors * errors, axis=1))
    everyone = tok_count * lax.axis_size("ctx") * lax.axis_size("wsh")
    grad_result = everyone / total_count * mask_rows[:, None] * errors
    grad_second, grad_gain_two, grad_shift_two = norm_back(
        grad_result, unit_two, scale_two, gain_rows[2]
    )
    grad_branch_two = grad_second.astype(BF16)
    grad_down = jnp.dot(active_low.T, grad_branch_two, preferred_element_type=F32)
    grad_active = jnp.dot(grad_branch_two, full_down.T, preferred_element_type=F32)
    (grad_upper,) = gelu_back(grad_active)
    grad_upper_low = grad_upper.astype(BF16)
    grad_up = jnp.dot(normed_low.T, grad_upper_low, preferred_element_type=F32)
    grad_normed = jnp.dot(grad_upper_low, full_up.T, preferred_element_type=F32) + grad_second
    grad_first, grad_gain_one, grad_shift_one = norm_back(
        grad_normed, unit_one, scale_one, gain_rows[0]
    )
    grad_branch = grad_first.astype(BF16)
    grad_outw = jnp.dot(mixed.T, grad_branch, preferred_element_type=F32)
    grad_mixed = jnp.dot(grad_branch, full_out.T, preferred_element_type=F32).astype(BF16)
    grad_norms = jnp.stack([grad_gain_one, grad_shift_one, grad_gain_two, grad_shift_two])
    small = jnp.zeros((8, model_dim), F32).at[:4].set(grad_norms).at[4, 0].set(partial_value)
    grad_tokens, (final_qkv, final_out, final_up, final_down), small = backward(
        grad_mixed, grad_first, small, x_rows.T, fq, kept, [g.astype(BF16) for g in (grad_outw, grad_up, grad_down)]
    )
    width = model_dim // (lax.axis_size("ctx") * lax.axis_size("wsh"))
    at = ctx * lax.axis_size("wsh") + wsh
    final_norms = lax.dynamic_slice(small, (0, at * width), (4, width))
    return (
        result.astype(BF16)[None],
        grad_tokens[None],
        small[4, 0] / total_count,
        final_qkv,
        final_out,
        final_up,
        final_down,
        final_norms,
    )


def solution(mesh):
    placed = (
        P("wsh", "ctx", None),
        P("wsh", "ctx", None),
        P("wsh", None, "ctx"),
        P("wsh", "ctx"),
        P("wsh", "ctx"),
        P("wsh", None),
        P("wsh", None),
        P("wsh", None),
        P("wsh", None),
        P(None, "wsh"),
    )
    return jax.shard_map(
        local,
        mesh=mesh,
        in_specs=placed,
        out_specs=(
            P("wsh", "ctx", None),
            P("wsh", "ctx", None),
            P(),
            P("wsh", "ctx"),
            P("wsh", "ctx"),
            P("wsh", "ctx"),
            P("wsh", "ctx"),
            P(None, ("ctx", "wsh")),
        ),
        check_vma=False,
    )
```

```python
import functools
import jax
import jax.numpy as jnp
from jax import lax
from jax.experimental import pallas as pl
from jax.experimental.pallas import tpu as pltpu
from jax.sharding import PartitionSpec as P

MESH = pl.DeviceIdType.MESH
BF16 = jnp.bfloat16
F32 = jnp.float32


class Place:
    def __init__(self):
        self.ctx = lax.axis_index("ctx")
        self.wsh = lax.axis_index("wsh")
        self.zlo = self.ctx // 8
        self.y = (self.ctx // 2) % 4
        self.core = self.ctx % 2
        self.zhi = self.wsh // 4
        self.x = self.wsh % 4

    def at(self, zlo=None, y=None, core=None, zhi=None, x=None):
        zlo = self.zlo if zlo is None else zlo
        y = self.y if y is None else y
        core = self.core if core is None else core
        zhi = self.zhi if zhi is None else zhi
        x = self.x if x is None else x
        return (zlo * 8 + y * 2 + core, zhi * 4 + x)

    def sibling(self):
        return self.at(core=1 - self.core)

    def x_peer(self, step):
        return self.at(x=(self.x + step) % 4)

    def y_peer(self, step):
        return self.at(y=(self.y + step) % 4)

    def z_peer(self, step):
        z = (self.zhi * 4 + self.zlo + step + 8) % 8
        return self.at(zlo=z % 4, zhi=z // 4)

    def plane(self):
        return [
            self.at(y=(self.y + d) % 4, core=(self.core + c) % 2)
            for d, c in ((0, 1), (1, 0), (1, 1), (2, 0), (2, 1), (3, 0), (3, 1))
        ]

    def rank(self):
        return self.y * 2 + self.core

    def z_far(self):
        return self.at(zhi=1 - self.zhi)

    def doubling(self):
        return (
            self.sibling(),
            self.at(y=self.y + 1 - 2 * (self.y % 2)),
            self.at(y=(self.y + 2) % 4),
            self.at(x=self.x + 1 - 2 * (self.x % 2)),
            self.at(x=(self.x + 2) % 4),
            self.at(zlo=self.zlo + 1 - 2 * (self.zlo % 2)),
            self.at(zlo=(self.zlo + 2) % 4),
            self.z_far(),
        )


def greet(devices):
    barrier = pltpu.get_barrier_semaphore()
    for device in devices:
        pl.semaphore_signal(barrier, inc=1, device_id=device, device_id_type=MESH)
    pl.semaphore_wait(barrier, len(devices))


def remote(source, target, send_sem, recv_sem, device):
    return pltpu.make_async_remote_copy(
        src_ref=source,
        dst_ref=target,
        send_sem=send_sem,
        recv_sem=recv_sem,
        device_id=device,
        device_id_type=MESH,
    )


def half_of(width, which):
    half = width // 2
    return pl.ds(pl.multiple_of(which * half, 128), half)


class Doubling:
    def __init__(self, place, tile, slots, send_sems, recv_sems):
        self.partners = place.doubling()
        self.tile, self.slots = tile, slots
        self.send_sems, self.recv_sems = send_sems, recv_sems
        self.step = 0
        self.copies = []

    def start(self):
        k = self.step
        copy = remote(
            self.tile.at[k], self.slots.at[k], self.send_sems.at[k], self.recv_sems.at[k], self.partners[k]
        )
        copy.start()
        self.copies.append(copy)

    def advance(self):
        k = self.step
        self.copies[k].wait_recv()
        self.tile[k + 1] = self.tile[k] + self.slots[k]
        self.step = k + 1
        if self.step < 8:
            self.start()

    def drain(self):
        for copy in self.copies:
            copy.wait_send()


NEG = -1e30
NT = (((1,), (1,)), ((), ()))
TN = (((0,), (0,)), ((), ()))


def matmul(left, right, dims=(((1,), (0,)), ((), ()))):
    return lax.dot_general(left, right, dims, preferred_element_type=F32)


class Gather:
    def __init__(self, place, shard, full, send_sems, recv_sems, local_sem):
        self.place, self.shard, self.full = place, shard, full
        self.send_sems, self.recv_sems = send_sems, recv_sems
        self.rows = shard.shape[0]
        self.lanes = half_of(shard.shape[1], place.core)
        self.local = pltpu.make_async_copy(shard, full.at[place.wsh], local_sem)
        self.copies = {}

    def part(self, index, which=None):
        block = self.full.at[index]
        if which is None:
            return block.at[:, self.lanes]
        half = self.rows // 2
        return block.at[which * half : (which + 1) * half, self.lanes]

    def send(self, k, source, target, device):
        copy = remote(source, target, self.send_sems.at[k], self.recv_sems.at[k], device)
        copy.start()
        self.copies[k] = copy

    def own(self, far, step):
        return (far * 4) + (self.place.x + step + 4) % 4

    def start_z(self):
        place = self.place
        self.local.start()
        self.send(2, self.shard.at[:, self.lanes], self.part(place.wsh), place.z_far())

    def start_x(self):
        place = self.place
        self.send(0, self.shard.at[:, self.lanes], self.part(place.wsh), place.x_peer(1))
        self.send(1, self.shard.at[:, self.lanes], self.part(place.wsh), place.x_peer(3))

    def pass_on(self, zh, base):
        place = self.place
        left, right = self.own(zh, -1), self.own(zh, 1)
        self.copies[base].wait_recv()
        self.send(base + 3, self.part(left, 0), self.part(left, 0), place.x_peer(1))
        self.send(base + 5, self.part(left), self.part(left), place.sibling())
        self.copies[base + 1].wait_recv()
        self.send(base + 4, self.part(right, 1), self.part(right, 1), place.x_peer(3))
        self.send(base + 6, self.part(right), self.part(right), place.sibling())

    def opposite(self, zh, base):
        place = self.place
        index = self.own(zh, 2)
        for which in range(2):
            self.copies[base + 3 + which].wait_recv()
            self.send(base + 7 + which, self.part(index, which), self.part(index, which), place.sibling())

    def near(self):
        self.pass_on(self.place.zhi, 0)

    def near_opposite(self):
        self.opposite(self.place.zhi, 0)

    def from_z(self):
        place = self.place
        index = self.own(1 - place.zhi, 0)
        self.copies[2].wait_recv()
        self.send(10, self.part(index), self.part(index), place.x_peer(1))
        self.send(11, self.part(index), self.part(index), place.x_peer(3))
        self.send(9, self.part(index), self.part(index), place.sibling())

    def far(self):
        self.pass_on(1 - self.place.zhi, 10)

    def far_opposite(self):
        self.opposite(1 - self.place.zhi, 10)

    def finish(self):
        self.local.wait()
        for k in (5, 6, 7, 8, 9, 15, 16, 17, 18):
            self.copies[k].wait_recv()

    def drain(self):
        for k in self.copies:
            self.copies[k].wait_send()


def head_mask(which):
    lane = lax.broadcasted_iota(jnp.int32, (1, 128), 1)
    return jnp.where((lane // 64) == which, 1.0, 0.0).astype(BF16)


def to_slots(slot_row, head, count):
    row = slot_row[pl.ds(head, 1), :]
    iota = lax.broadcasted_iota(jnp.int32, (count, count), 0).astype(F32)
    return jnp.where(iota == row, 1.0, 0.0).astype(BF16)


def to_tokens(slot_col, head, count):
    lane = lax.broadcasted_iota(jnp.int32, slot_col.shape, 1)
    column = jnp.sum(jnp.where(lane == head, slot_col[...], 0.0), axis=1, keepdims=True)
    iota = lax.broadcasted_iota(jnp.int32, (count, count), 1).astype(F32)
    return jnp.where(iota == column, 1.0, 0.0).astype(BF16)


def pair_select(first, second):
    lane = lax.broadcasted_iota(jnp.int32, first.shape, 1)
    return jnp.where((lane // 64) % 2 == 0, first, second)


def make_slots(clusters, segments, counted, slot_row, slot_col, labels):
    heads, count = clusters.shape
    groups = lax.shift_right_logical(clusters[...], 2)
    iota = lax.broadcasted_iota(jnp.int32, (32, count), 0)
    before = lax.broadcasted_iota(jnp.int32, (count, count), 0)
    after = lax.broadcasted_iota(jnp.int32, (count, count), 1)
    upper = jnp.where(before <= after, 1.0, 0.0).astype(BF16)
    hot = [jnp.where(groups[h : h + 1, :] == iota, 1.0, 0.0) for h in range(heads)]
    counts = matmul(jnp.concatenate(hot, axis=0).astype(BF16), upper)
    group_f = groups.astype(F32)
    rows = []
    for h in range(heads):
        rank = jnp.sum(counts[32 * h : 32 * h + 32] * hot[h], axis=0, keepdims=True)
        rows.append(group_f[h : h + 1] * 16.0 + rank - 1.0)
    slots = jnp.concatenate(rows + [counted[...].astype(F32), jnp.zeros((127 - heads, count), F32)], axis=0)
    slot_row[...] = slots[:16]
    slot_col[...] = slots.T
    label = (segments[0:1, :] * 4 + (clusters[...] & 3)).astype(F32)
    labels[...] = jnp.concatenate([label, jnp.zeros((128 - heads, count), F32)], axis=0).T.astype(BF16)


def rows16(j):
    return slice(16 * j, 16 * j + 16)


def forward_kernel(
    x, clusters, segments, counted, norms, wq, wo, wu, wd,
    mixed, x_turned, fq_out, fo, fu, fd, got_out, before_out, after_out, logsum, hot_out, cold_out, slot_row, slot_col, total,
    fq, got, before, after, hot, cold,
    labels, sent_labels, got_labels, before_labels, after_labels, wide_labels, sent, out, back, log_cols,
    tile, slots,
    w_send, w_recv, w_local, t_send, t_recv, a_send, a_recv, a_local, z_send, z_recv, b_send, b_recv, b_local, k_sem,
):
    place = Place()
    plane, rank = place.plane(), place.rank()
    up, down = place.z_peer(1), place.z_peer(-1)
    kept = []

    def keep(source, target):
        copy = pltpu.make_async_copy(source, target, k_sem.at[len(kept)])
        copy.start()
        kept.append(copy)

    partners = place.doubling()
    greet(
        plane + [place.x_peer(1), place.x_peer(2), place.x_peer(3), place.z_far(), up, down, partners[5], partners[6]]
    )
    weights = [
        Gather(place, shard, full, w_send.at[i], w_recv.at[i], w_local.at[i])
        for i, (shard, full) in enumerate(((wq, fq), (wo, fo), (wu, fu), (wd, fd)))
    ]
    first, rest = weights[0], weights[1:]
    first.start_z()
    first.start_x()
    tile[0] = jnp.zeros_like(tile[0])
    tile[0, 0:4, 0 : norms.shape[1]] = norms[...].astype(F32)
    tile[0] = pltpu.roll(tile[0], place.wsh * norms.shape[1], 1)
    lane_zero = lax.broadcasted_iota(jnp.int32, (1, tile.shape[2]), 1) == 0
    tile[0, 4:5, :] = jnp.where(lane_zero, jnp.sum(counted[...].astype(F32), axis=1, keepdims=True), 0.0)
    doubling = Doubling(place, tile, slots, t_send, t_recv)
    doubling.start()
    count = x.shape[0]
    make_slots(clusters, segments, counted, slot_row, slot_col, labels)

    sent_labels[...] = jnp.zeros_like(sent_labels)

    def move_labels(head, carry):
        lane = lax.broadcasted_iota(jnp.int32, (count, 128), 1)
        moved = matmul(to_slots(slot_row, head, count), labels[...])
        sent_labels[...] = jnp.where(lane == head, moved, sent_labels[...])
        return carry

    lax.fori_loop(0, 12, move_labels, 0)
    labels[...] = sent_labels[...].astype(BF16)

    def block(which):
        return pl.ds(pl.multiple_of(which * 64, 64), 64)

    def ranks():
        return [dev[0] % 8 for dev in plane]

    label_copies = [
        remote(labels.at[block(to)], got_labels.at[rank], a_send.at[6, k], a_recv.at[6, k], plane[k])
        for k, to in enumerate(ranks())
    ]
    for copy in label_copies:
        copy.start()
    own_labels = pltpu.make_async_copy(labels.at[block(rank)], got_labels.at[rank], a_local.at[6])
    own_labels.start()
    doubling.advance()
    first.near()
    x_turned[...] = x[...].astype(F32).T.astype(BF16)
    doubling.advance()
    own_labels.wait()
    for copy in label_copies:
        copy.wait_recv()
    label_up = remote(got_labels.at[4:8], before_labels, z_send.at[6, 0], z_recv.at[6, 0], up)
    label_down = remote(got_labels.at[0:4], after_labels, z_send.at[6, 1], z_recv.at[6, 1], down)
    label_up.start()
    label_down.start()
    first.from_z()
    for w in rest:
        w.start_z()
    first.near_opposite()
    doubling.advance()
    label_up.wait_recv()
    label_down.wait_recv()
    for j in range(4):
        wide_labels[j, 0:64] = jnp.where(
            place.zlo == 0, -1.0, before_labels[:, rows16(j), :].reshape(64, 128).astype(F32)
        )
        wide_labels[j, 64:192] = got_labels[:, rows16(j), :].reshape(128, 128).astype(F32)
        wide_labels[j, 192:256] = jnp.where(
            place.zlo == 3, -1.0, after_labels[:, rows16(j), :].reshape(64, 128).astype(F32)
        )

    def make_hot(head, carry):
        lane = lax.broadcasted_iota(jnp.int32, (256, 128), 1)
        for j in range(4):
            column = jnp.sum(jnp.where(lane == head, wide_labels[j], 0.0), axis=1, keepdims=True)
            same = lane.astype(F32) == column
            cold[head * 4 + j] = jnp.where(same, 0.0, NEG).astype(BF16)
            hot[head * 4 + j] = jnp.where(same, 1.0, 0.0)[64:192].astype(BF16)
        return carry

    lax.fori_loop(0, 12, make_hot, 0)
    keep(hot, hot_out)
    keep(cold, cold_out)
    doubling.advance()
    first.far()
    doubling.advance()
    for w in rest:
        w.start_x()
    first.far_opposite()
    first.finish()
    keep(fq, fq_out)

    def send_copies(p, fn):
        for k, to in enumerate(ranks()):
            fn(remote(sent.at[p, block(to)], got.at[p, rank], a_send.at[p, k], a_recv.at[p, k], plane[k]))

    def own_copy(p):
        return pltpu.make_async_copy(sent.at[p, block(rank)], got.at[p, rank], a_local.at[p])

    def project(p, carry):
        parts = []
        for t in range(3):
            lanes = pl.ds(pl.multiple_of(t * 768 + p * 128, 128), 128)
            value = matmul(x[...], fq[:, :, lanes].reshape(768, 128)).astype(BF16)
            parts.append(value * jnp.asarray(0.125, BF16) if t == 0 else value)
        rows = jnp.concatenate(parts, axis=1)
        moved = [matmul(to_slots(slot_row, 2 * p + a, count), rows) for a in range(2)]
        sent[p] = pair_select(moved[0], moved[1]).astype(BF16)
        send_copies(p, lambda copy: copy.start())
        own_copy(p).start()
        return carry

    w_out, w_up, w_down = rest
    lax.fori_loop(0, 6, project, 0)
    doubling.advance()
    w_out.near()
    w_out.from_z()
    w_up.near()

    def halo(p):
        return (
            remote(got.at[p, 4:8, :, 128:384], before.at[p], z_send.at[p, 0], z_recv.at[p, 0], up),
            remote(got.at[p, 0:4, :, 128:384], after.at[p], z_send.at[p, 1], z_recv.at[p, 1], down),
        )

    def back_copies(p, fn):
        for k, to in enumerate(ranks()):
            fn(remote(out.at[p, to], back.at[p, rank], b_send.at[p, k], b_recv.at[p, k], plane[k]))

    def own_back(p):
        return pltpu.make_async_copy(out.at[p, rank], back.at[p, rank], b_local.at[p])

    def arrive(p):
        own_copy(p).wait()
        send_copies(p, lambda copy: copy.wait_recv())
        for copy in halo(p):
            copy.start()

    masks = [head_mask(a) for a in range(2)]

    def attend(p):
        for copy in halo(p):
            copy.wait_recv()
        lane = lax.broadcasted_iota(jnp.int32, (128, 128), 1)
        for j in range(4):
            r = rows16(j)
            query = got[p, :, r, 0:128].reshape(128, 128)
            keys = jnp.concatenate(
                [before[p, :, r, 0:128].reshape(64, 128), got[p, :, r, 128:256].reshape(128, 128),
                 after[p, :, r, 0:128].reshape(64, 128)], axis=0)
            values = jnp.concatenate(
                [before[p, :, r, 128:256].reshape(64, 128), got[p, :, r, 256:384].reshape(128, 128),
                 after[p, :, r, 128:256].reshape(64, 128)], axis=0)
            halves = []
            for a in range(2):
                head = 2 * p + a
                scores = matmul(
                    jnp.concatenate([query * masks[a], hot[head * 4 + j]], axis=1),
                    jnp.concatenate([keys, cold[head * 4 + j]], axis=1), NT)
                top = jnp.max(scores, axis=1, keepdims=True)
                weights_ = jnp.exp(scores - top)
                sums = jnp.sum(weights_, axis=1, keepdims=True)
                halves.append(matmul(weights_.astype(BF16), values) / sums)
                log_cols[j] = jnp.where(lane == head, top + jnp.log(sums), log_cols[j])
            out[p, :, r, :] = pair_select(halves[0], halves[1]).astype(BF16).reshape(8, 16, 128)
        back_copies(p, lambda copy: copy.start())
        own_back(p).start()

    log_cols[...] = jnp.zeros_like(log_cols)
    arrive(0)
    arrive(1)
    w_up.from_z()
    w_down.near()
    attend(0)
    w_out.near_opposite()
    w_out.far()
    arrive(2)
    attend(1)
    w_up.near_opposite()
    doubling.advance()
    arrive(3)
    attend(2)
    w_down.from_z()
    w_down.near_opposite()
    w_out.far_opposite()
    arrive(4)
    attend(3)
    w_up.far()
    doubling.advance()
    arrive(5)
    attend(4)
    w_down.far()
    attend(5)
    w_up.far_opposite()
    keep(got, got_out)
    keep(before, before_out)
    keep(after, after_out)

    def home(p, carry):
        own_back(p).wait()
        back_copies(p, lambda copy: copy.wait_recv())
        rows = back[p].reshape(count, 128)
        moved = [matmul(to_tokens(slot_col, 2 * p + a, count), rows) for a in range(2)]
        mixed[:, pl.ds(pl.multiple_of(p * 128, 128), 128)] = pair_select(moved[0], moved[1]).astype(BF16)
        return carry

    lax.fori_loop(0, 6, home, 0)
    for j in range(4):
        logsum[j] = log_cols[j].T[:16]
    w_down.far_opposite()
    for w in rest:
        w.finish()
    total[...] = tile[8]

    def settle(p, carry):
        send_copies(p, lambda copy: copy.wait_send())
        back_copies(p, lambda copy: copy.wait_send())
        for copy in halo(p):
            copy.wait_send()
        return carry

    lax.fori_loop(0, 6, settle, 0)
    for copy in label_copies + [label_up, label_down]:
        copy.wait_send()
    for w in weights:
        w.drain()
    for copy in kept:
        copy.wait()
    doubling.drain()


ANY = pl.BlockSpec(memory_space=pl.ANY)
VMEM = pl.BlockSpec(memory_space=pltpu.VMEM)


def shaped(*shape, dtype=BF16):
    return jax.ShapeDtypeStruct(shape, dtype)


def forward(x, clusters, segments, counted, norms, shards):
    count, width = x.shape
    dma = pltpu.SemaphoreType.DMA
    return pl.pallas_call(
        forward_kernel,
        out_shape=[
            shaped(*x.shape),
            shaped(width, count),
            *[shaped(8, *w.shape) for w in shards],
            shaped(6, 8, 64, 384),
            shaped(6, 4, 64, 256),
            shaped(6, 4, 64, 256),
            shaped(4, 16, 128, dtype=F32),
            shaped(48, 128, 128),
            shaped(48, 256, 128),
            shaped(16, count, dtype=F32),
            shaped(count, 128, dtype=F32),
            shaped(8, width, dtype=F32),
        ],
        in_specs=[VMEM] * 5 + [ANY] * 4,
        out_specs=[VMEM] * 2 + [ANY] * 7 + [VMEM] + [ANY] * 2 + [VMEM] * 3,
        scratch_shapes=[
            pltpu.VMEM((8, *shards[0].shape), BF16),
            pltpu.VMEM((6, 8, 64, 384), BF16),
            pltpu.VMEM((6, 4, 64, 256), BF16),
            pltpu.VMEM((6, 4, 64, 256), BF16),
            pltpu.VMEM((48, 128, 128), BF16),
            pltpu.VMEM((48, 256, 128), BF16),
            pltpu.VMEM((count, 128), BF16),
            pltpu.VMEM((count, 128), F32),
            pltpu.VMEM((8, 64, 128), BF16),
            pltpu.VMEM((4, 64, 128), BF16),
            pltpu.VMEM((4, 64, 128), BF16),
            pltpu.VMEM((4, 256, 128), F32),
            pltpu.VMEM((6, count, 384), BF16),
            pltpu.VMEM((6, 8, 64, 128), BF16),
            pltpu.VMEM((6, 8, 64, 128), BF16),
            pltpu.VMEM((4, 128, 128), F32),
            pltpu.VMEM((9, 8, width), F32),
            pltpu.VMEM((8, 8, width), F32),
            dma((4, 19)), dma((4, 19)), dma((4,)), dma((8,)), dma((8,)),
            dma((7, 7)), dma((7, 7)), dma((7,)), dma((7, 2)), dma((7, 2)),
            dma((6, 7)), dma((6, 7)), dma((6,)), dma((6,)),
        ],
        compiler_params=pltpu.CompilerParams(
            collective_id=0, has_side_effects=True, vmem_limit_bytes=60 * 2**20
        ),
        name="forward_attention",
    )(x, clusters, segments, counted, norms, *shards)


class Reduce:
    def __init__(self, place, grad, mine, held, near, far, sum_x, from_y, sum_y, from_z, out, send_sems, recv_sems, load_sem):
        self.place, self.grad, self.mine, self.held = place, grad, mine, held
        self.near, self.far, self.sum_x, self.from_y = near, far, sum_x, from_y
        self.sum_y, self.from_z, self.out = sum_y, from_z, out
        self.send_sems, self.recv_sems, self.load_sem = send_sems, recv_sems, load_sem
        self.rows, self.width = grad.shape[2], grad.shape[3]
        self.owner, self.side = place.y // 2, place.zlo // 2
        self.here = place.zhi == self.owner
        self.final = jnp.logical_and(self.here, place.core == self.side)
        self.other = jnp.logical_and(self.here, place.core != self.side)
        self.copies = {}

    def send(self, k, source, target, device):
        copy = remote(source, target, self.send_sems.at[k], self.recv_sems.at[k], device)
        copy.start()
        self.copies[k] = copy

    def each(self, count, body):
        def step(i, carry):
            body(pl.ds(pl.multiple_of(i * 48, 16), 48))
            return carry

        lax.fori_loop(0, count // 48, step, 0)

    def after(self, rows, offset):
        return pl.ds(pl.multiple_of(rows.start + offset, 16), rows.size)

    def start(self):
        place = self.place
        self.send(0, self.grad.at[:, :, :, half_of(self.width, 1 - place.core)], self.held, place.sibling())
        if self.load_sem is not None:
            self.load = pltpu.make_async_copy(
                self.grad.at[:, :, :, half_of(self.width, place.core)], self.mine, self.load_sem
            )
            self.load.start()

    def own(self, zh, xx, rows):
        if self.load_sem is not None:
            return self.mine[zh, xx, rows, :]
        return self.grad[zh, xx, rows, half_of(self.width, self.place.core)]

    def add_pair(self, xx):
        def block(zh, carry):
            self.each(self.rows, lambda rows: self.add_rows(zh, xx, rows))
            return carry

        lax.fori_loop(0, 2, block, 0)

    def add_rows(self, zh, xx, rows):
        self.held[zh, xx, rows, :] = (
            self.own(zh, xx, rows).astype(F32) + self.held[zh, xx, rows, :].astype(F32)
        ).astype(BF16)

    def to_opposite(self):
        place = self.place
        self.copies[0].wait_recv()
        if self.load_sem is not None:
            self.load.wait()
        half = self.rows // 2
        opposite = (place.x + 2) % 4
        self.add_pair(opposite)
        self.send(1, self.held.at[:, opposite, 0:half], self.near.at[0], place.x_peer(1))
        self.send(2, self.held.at[:, opposite, half : self.rows], self.near.at[1], place.x_peer(3))
        for step in (1, 3, 0):
            self.add_pair((place.x + step) % 4)

    def to_near(self):
        place = self.place
        half = self.rows // 2
        for k, step in enumerate((1, 3)):
            to = (place.x + step) % 4
            self.copies[1 + k].wait_recv()

            def block(zh, carry, k=k, to=to):
                def body(rows):
                    there = self.after(rows, k * half)
                    self.held[zh, to, there, :] = (
                        self.held[zh, to, there, :].astype(F32) + self.near[k, zh, rows, :].astype(F32)
                    ).astype(BF16)

                self.each(half, body)
                return carry

            lax.fori_loop(0, 2, block, 0)
            self.send(3 + k, self.held.at[:, to], self.far.at[k], place.x_peer(step))

    def to_y(self):
        place = self.place
        half = self.rows // 2
        for k in range(2):
            self.copies[3 + k].wait_recv()

        def block(zh, carry):
            def body(rows):
                value = self.held[zh, place.x, rows, :].astype(F32)
                value = value + self.far[0, zh, rows, :].astype(F32) + self.far[1, zh, rows, :].astype(F32)
                self.sum_x[zh, rows, :] = value.astype(BF16)

            self.each(self.rows, body)
            return carry

        lax.fori_loop(0, 2, block, 0)
        for k, d in enumerate((1, 2, 3)):
            to = (place.y + d) % 4
            part = pl.ds(pl.multiple_of((to % 2) * half, 16), half)
            self.send(5 + k, self.sum_x.at[to // 2, part], self.from_y.at[k], place.y_peer(d))

    def z_copy(self, k):
        partners = self.place.doubling()
        device = (partners[7], partners[6], partners[5])[k]
        return remote(self.sum_y, self.from_z.at[k], self.send_sems.at[8 + k], self.recv_sems.at[8 + k], device)

    def to_far_z(self):
        place = self.place
        half = self.rows // 2
        for k in range(3):
            self.copies[5 + k].wait_recv()

        def body(rows):
            value = self.sum_x[self.owner, self.after(rows, (place.y % 2) * half), :].astype(F32)
            for k in range(3):
                value = value + self.from_y[k, rows, :].astype(F32)
            self.sum_y[rows, :] = value.astype(BF16)

        self.each(half, body)

        @pl.when(jnp.logical_not(self.here))
        def _():
            self.z_copy(0).start()

    def add_z(self, k):
        self.z_copy(k).wait_recv()

        def body(rows):
            self.sum_y[rows, :] = (self.sum_y[rows, :].astype(F32) + self.from_z[k, rows, :].astype(F32)).astype(BF16)

        self.each(self.rows // 2, body)

    def to_near_z(self):
        @pl.when(self.here)
        def _():
            self.add_z(0)

        @pl.when(self.other)
        def _():
            self.z_copy(1).start()

    def to_next_z(self):
        @pl.when(self.final)
        def _():
            self.add_z(1)
            self.z_copy(2).start()

    def spread_copy(self, k, device):
        half = self.rows // 2
        part = self.out.at[pl.ds(pl.multiple_of((self.place.y % 2) * half, 16), half)]
        return remote(part, part, self.send_sems.at[11 + k], self.recv_sems.at[11 + self.place.y % 2], device)

    def spread(self):
        half = self.rows // 2

        @pl.when(self.final)
        def _():
            self.z_copy(2).wait()

            def body(rows):
                there = self.after(rows, (self.place.y % 2) * half)
                self.out[there, :] = (
                    self.sum_y[rows, :].astype(F32) + self.from_z[2, rows, :].astype(F32)
                ).astype(BF16)

            self.each(half, body)
            for k, device in enumerate(self.place.plane()):
                self.spread_copy(k, device).start()

    def finish(self):
        half = self.rows // 2
        for k in range(2):
            part = self.out.at[k * half : (k + 1) * half]

            @pl.when(jnp.logical_not(jnp.logical_and(self.final, self.place.y % 2 == k)))
            def _(k=k, part=part):
                remote(part, part, self.send_sems.at[11], self.recv_sems.at[11 + k], self.place.sibling()).wait_recv()

    def drain(self):
        for k in self.copies:
            self.copies[k].wait_send()

        @pl.when(self.final)
        def _():
            for k, device in enumerate(self.place.plane()):
                self.spread_copy(k, device).wait_send()

        @pl.when(self.other)
        def _():
            self.z_copy(1).wait_send()

        @pl.when(jnp.logical_not(self.here))
        def _():
            self.z_copy(0).wait_send()


def reduce_scratch(rows, half):
    return [
        pltpu.VMEM((2, 4, rows, half), BF16),
        pltpu.VMEM((2, 2, rows // 2, half), BF16),
        pltpu.VMEM((2, 2, rows, half), BF16),
        pltpu.VMEM((2, rows, half), BF16),
        pltpu.VMEM((3, rows // 2, half), BF16),
        pltpu.VMEM((rows // 2, half), BF16),
        pltpu.VMEM((3, rows // 2, half), BF16),
    ]


def backward_kernel(*refs):
    (grad_mixed, grad_first, logsum, slot_row, slot_col, small, x_hbm, fq_hbm, got_hbm, before_hbm, after_hbm,
     hot_hbm, cold_hbm, go, gu, gd) = refs[:16]
    grad_x, out_q, out_o, out_u, out_d, small_out = refs[16:22]
    x_turned, fq, got, before, after, hot, cold, gq = refs[22:30]
    sent, got_grad, grads, to_before, to_after, from_before, from_after, back = refs[30:38]
    mine = (None, *refs[38:41])
    reduce_refs = [refs[41 + 7 * i : 48 + 7 * i] for i in range(4)]
    (tile, slots, a_send, a_recv, a_local, z_send, z_recv, b_send, b_recv, b_local,
     t_send, t_recv, r_send, r_recv, r_load, l_sem) = refs[69:]
    place = Place()
    plane, rank = place.plane(), place.rank()
    up, down = place.z_peer(1), place.z_peer(-1)
    partners = place.doubling()
    greet(
        plane + [place.x_peer(1), place.x_peer(2), place.x_peer(3), place.z_far(), up, down, partners[5], partners[6]]
    )
    loads = [
        pltpu.make_async_copy(source, target, l_sem.at[i])
        for i, (source, target) in enumerate(
            ((got_hbm, got), (before_hbm, before), (after_hbm, after), (hot_hbm, hot), (cold_hbm, cold),
             (fq_hbm, fq), (x_hbm, x_turned))
        )
    ]
    for copy in loads:
        copy.start()
    sums = [
        Reduce(place, grad, mine[i], *reduce_refs[i], out, r_send.at[i], r_recv.at[i], r_load.at[i] if i else None)
        for i, (grad, out) in enumerate(((gq, out_q), (go, out_o), (gu, out_u), (gd, out_d)))
    ]
    query_sum, rest = sums[0], sums[1:]
    for r in rest:
        r.start()
    tile[0] = small[...]
    doubling = Doubling(place, tile, slots, t_send, t_recv)
    doubling.start()
    count = grad_mixed.shape[0]
    ranks = [dev[0] % 8 for dev in plane]

    def block(which):
        return pl.ds(pl.multiple_of(which * 64, 64), 64)

    def send_copies(p, fn):
        for k, to in enumerate(ranks):
            fn(remote(sent.at[p, block(to)], got_grad.at[p, rank], a_send.at[p, k], a_recv.at[p, k], plane[k]))

    def own_copy(p):
        return pltpu.make_async_copy(sent.at[p, block(rank)], got_grad.at[p, rank], a_local.at[p])

    def leave(p, carry):
        rows = grad_mixed[:, pl.ds(pl.multiple_of(p * 128, 128), 128)]
        moved = [matmul(to_slots(slot_row, 2 * p + a, count), rows) for a in range(2)]
        sent[p] = pair_select(moved[0], moved[1]).astype(BF16)
        send_copies(p, lambda copy: copy.start())
        own_copy(p).start()
        return carry

    lax.fori_loop(0, 6, leave, 0)
    for r in rest:
        r.to_opposite()
    for copy in loads[:5]:
        copy.wait()
    doubling.advance()

    def halo(p):
        return (
            remote(to_after.at[p], from_before.at[p], z_send.at[p, 0], z_recv.at[p, 0], up),
            remote(to_before.at[p], from_after.at[p], z_send.at[p, 1], z_recv.at[p, 1], down),
        )

    def back_copies(p, fn):
        for k, to in enumerate(ranks):
            fn(remote(grads.at[p, to], back.at[p, rank], b_send.at[p, k], b_recv.at[p, k], plane[k]))

    def own_back(p):
        return pltpu.make_async_copy(grads.at[p, rank], back.at[p, rank], b_local.at[p])

    masks = [head_mask(a) for a in range(2)]

    def attend(p):
        own_copy(p).wait()
        send_copies(p, lambda copy: copy.wait_recv())
        for j in range(4):
            r = rows16(j)
            query = got[p, :, r, 0:128].reshape(128, 128)
            keys = jnp.concatenate(
                [before[p, :, r, 0:128].reshape(64, 128), got[p, :, r, 128:256].reshape(128, 128),
                 after[p, :, r, 0:128].reshape(64, 128)], axis=0)
            values = jnp.concatenate(
                [before[p, :, r, 128:256].reshape(64, 128), got[p, :, r, 256:384].reshape(128, 128),
                 after[p, :, r, 128:256].reshape(64, 128)], axis=0)
            grad = got_grad[p, :, r, :].reshape(128, 128)
            dq, dk, dv = [], [], []
            for a in range(2):
                head = 2 * p + a
                scores = matmul(
                    jnp.concatenate([keys, cold[head * 4 + j]], axis=1),
                    jnp.concatenate([query * masks[a], hot[head * 4 + j]], axis=1), NT)
                probs = jnp.exp(scores - logsum[j, pl.ds(head, 1), :])
                grad_probs = matmul(values, grad * masks[a], NT)
                delta = jnp.sum(probs * grad_probs, axis=0, keepdims=True)
                grad_scores = (probs * (grad_probs - delta)).astype(BF16)
                dk.append(matmul(grad_scores, query))
                dv.append(matmul(probs.astype(BF16), grad))
                dq.append(matmul(grad_scores, keys, TN))
            dq = (pair_select(*dq) * 0.125).astype(BF16)
            dk = pair_select(*dk).astype(BF16)
            dv = pair_select(*dv).astype(BF16)
            both = jnp.concatenate([dk, dv], axis=1)
            to_before[p, :, r, :] = both[0:64].reshape(4, 16, 256)
            to_after[p, :, r, :] = both[192:256].reshape(4, 16, 256)
            grads[p, :, r, 0:128] = dq.reshape(8, 16, 128)
            grads[p, :, r, 128:384] = both[64:192].reshape(8, 16, 256)
        for copy in halo(p):
            copy.start()

    def give(p):
        for copy in halo(p):
            copy.wait_recv()
        for part, extra in ((slice(0, 4), from_before), (slice(4, 8), from_after)):
            grads[p, part, :, 128:384] = (
                grads[p, part, :, 128:384].astype(F32) + extra[p].astype(F32)
            ).astype(BF16)
        back_copies(p, lambda copy: copy.start())
        own_back(p).start()

    attend(0)
    doubling.advance()

    def steady(p, carry):
        attend(p)
        give(p - 1)
        return carry

    lax.fori_loop(1, 3, steady, 0)
    for r in rest:
        r.to_near()
    doubling.advance()
    lax.fori_loop(3, 6, steady, 0)
    give(5)
    for copy in loads[5:]:
        copy.wait()
    doubling.advance()
    for r in rest:
        r.to_y()
    doubling.advance()
    grad_x[...] = grad_first[...]

    def home(p, carry):
        own_back(p).wait()
        back_copies(p, lambda copy: copy.wait_recv())
        rows = back[p].reshape(count, 384)
        moved = [matmul(to_tokens(slot_col, 2 * p + a, count), rows) for a in range(2)]
        grad_qkv = pair_select(moved[0], moved[1]).astype(BF16)
        weight = matmul(x_turned[...], grad_qkv).astype(BF16)
        columns = []
        for t in range(3):
            lanes = pl.ds(pl.multiple_of(t * 768 + p * 128, 128), 128)
            gq[:, :, :, lanes] = weight[:, t * 128 : t * 128 + 128].reshape(2, 4, 96, 128)
            columns.append(fq[:, :, lanes].reshape(768, 128))
        grad_x[...] += matmul(grad_qkv, jnp.concatenate(columns, axis=1), NT)
        return carry

    lax.fori_loop(0, 6, home, 0)
    query_sum.start()
    for r in rest:
        r.to_far_z()
    doubling.advance()
    query_sum.to_opposite()
    for r in rest:
        r.to_near_z()
    query_sum.to_near()
    doubling.advance()
    for r in rest:
        r.to_next_z()
    query_sum.to_y()
    doubling.advance()
    for r in rest:
        r.spread()
    query_sum.to_far_z()
    query_sum.to_near_z()
    query_sum.to_next_z()
    query_sum.spread()
    small_out[...] = tile[8]

    def settle(p, carry):
        send_copies(p, lambda copy: copy.wait_send())
        back_copies(p, lambda copy: copy.wait_send())
        for copy in halo(p):
            copy.wait_send()
        return carry

    lax.fori_loop(0, 6, settle, 0)
    for r in rest + [query_sum]:
        r.finish()
    for r in sums:
        r.drain()
    doubling.drain()


def backward(grad_mixed, grad_first, small, x_turned, fq, kept, grads):
    got, before, after, logsum, hot, cold, slot_row, slot_col = kept
    count = grad_mixed.shape[0]
    dma = pltpu.SemaphoreType.DMA
    blocks = [g.reshape(2, 4, g.shape[0] // 8, g.shape[1]) for g in grads]
    shapes = [(96, 2304)] + [b.shape[2:] for b in blocks]
    like = lambda array: pltpu.VMEM(array.shape, array.dtype)
    reduce_refs = []
    for rows, width in shapes:
        reduce_refs += reduce_scratch(rows, width // 2)
    loaded = (x_turned, fq, got, before, after, hot, cold)
    results = pl.pallas_call(
        backward_kernel,
        out_shape=[shaped(*grad_first.shape, dtype=F32)]
        + [shaped(rows, width // 2) for rows, width in shapes]
        + [shaped(*small.shape, dtype=F32)],
        in_specs=[VMEM] * 6 + [ANY] * 10,
        out_specs=[VMEM] * 6,
        scratch_shapes=[like(array) for array in loaded]
        + [
            pltpu.VMEM((2, 4, 96, 2304), BF16),
            pltpu.VMEM((6, count, 128), BF16),
            pltpu.VMEM((6, 8, 64, 128), BF16),
            pltpu.VMEM((6, 8, 64, 384), BF16),
            pltpu.VMEM((6, 4, 64, 256), BF16),
            pltpu.VMEM((6, 4, 64, 256), BF16),
            pltpu.VMEM((6, 4, 64, 256), BF16),
            pltpu.VMEM((6, 4, 64, 256), BF16),
            pltpu.VMEM((6, 8, 64, 384), BF16),
        ]
        + [pltpu.VMEM((2, 4, rows, width // 2), BF16) for rows, width in shapes[1:]]
        + reduce_refs
        + [
            pltpu.VMEM((9, *small.shape), F32),
            pltpu.VMEM((8, *small.shape), F32),
            dma((6, 7)), dma((6, 7)), dma((6,)), dma((6, 2)), dma((6, 2)),
            dma((6, 7)), dma((6, 7)), dma((6,)),
            dma((8,)), dma((8,)), dma((4, 18)), dma((4, 18)), dma((4,)), dma((7,)),
        ],
        compiler_params=pltpu.CompilerParams(
            collective_id=1, has_side_effects=True, vmem_limit_bytes=62 * 2**20
        ),
        name="backward_attention",
    )(grad_mixed, grad_first, logsum, slot_row, slot_col, small, *loaded, *blocks)
    ctx = lax.axis_index("ctx")
    finals = []
    for result in results[1:5]:
        width = result.shape[1] // 16
        finals.append(lax.dynamic_slice_in_dim(result, (ctx % 16) * width, width, axis=1).astype(F32))
    return results[0], finals, results[5]


CHUNK = 512


def norm_rows(values):
    centered = values - jnp.mean(values, axis=-1, keepdims=True)
    scale = lax.rsqrt(jnp.mean(centered * centered, axis=-1, keepdims=True) + 1e-05)
    return centered * scale, scale


def norm_rows_back(grad, normed, scale, gain):
    weighted = grad * gain
    return scale * (
        weighted
        - jnp.mean(weighted, axis=-1, keepdims=True)
        - normed * jnp.mean(weighted * normed, axis=-1, keepdims=True)
    )


def middle_kernel(
    everyone, ctx_size,
    mixed, x, teacher, slot_col, total, wo_hbm, wu_hbm, wd_hbm,
    result, grad_first, grad_mixed, small, go_hbm, gu_hbm, gd_hbm,
    wo, wu, wd, active, slope, normed, unit, scale, low, low_turned, acc, branch, grad_upper, go, gu, gd,
    in_sem, out_sem,
):
    loads = [
        pltpu.make_async_copy(source, target, in_sem.at[i])
        for i, (source, target) in enumerate(((wo_hbm, wo), (wu_hbm, wu), (wd_hbm, wd)))
    ]
    for copy in loads:
        copy.start()
    count, width = x.shape
    tile = 128
    chunks = wd.shape[0] // CHUNK
    gains = total[0:4] / ctx_size
    small[...] = jnp.zeros_like(small)

    def rows_of(i):
        return pl.ds(pl.multiple_of(i * tile, tile), tile)

    def lanes_of(c):
        return pl.ds(pl.multiple_of(c * CHUNK, CHUNK), CHUNK)

    loads[0].wait()
    for i in range(2):
        rows = slice(i * 256, i * 256 + 256)
        acc[rows, :] = matmul(mixed[rows, :], wo[...])

    def first_norm(i, carry):
        rows = rows_of(i)
        unit_rows, scale_rows = norm_rows(x[rows, :].astype(F32) + acc[rows, :])
        unit[rows, :] = unit_rows
        scale[rows, :] = scale_rows
        value = unit_rows * gains[0:1] + gains[1:2]
        normed[rows, :] = value
        low[rows, :] = value.astype(BF16)
        acc[rows, :] = value
        return carry

    lax.fori_loop(0, count // tile, first_norm, 0)
    loads[1].wait()
    loads[2].wait()

    def expand(c, carry):
        lanes = lanes_of(c)
        up = wu[:, :, lanes].reshape(width, CHUNK)
        down = wd[lanes, :]
        for i in range(2):
            rows = slice(i * 256, i * 256 + 256)
            upper = matmul(low[rows, :], up)
            share = 0.5 + 0.5 * lax.erf(upper * 0.7071067811865476)
            density = jnp.exp(upper * upper * -0.5) * 0.3989422804014327
            value = (upper * share).astype(BF16)
            active[rows, lanes] = value
            slope[rows, lanes] = share + upper * density
            acc[rows, :] += matmul(value, down)
        return carry

    lax.fori_loop(0, chunks, expand, 0)
    low_turned[...] = normed[...].T.astype(BF16)

    def second_norm(i, carry):
        rows = rows_of(i)
        unit_rows, scale_rows = norm_rows(acc[rows, :])
        value = unit_rows * gains[2:3] + gains[3:4]
        result[rows, :] = value.astype(BF16)
        error = value - teacher[rows, :].astype(F32)
        mask = slot_col[rows, 12:13]
        losses = mask * jnp.mean(error * error, axis=-1, keepdims=True)
        grad = (everyone / total[4:5, 0:1]) * mask * error
        small[2:3, :] += jnp.sum(grad * unit_rows, axis=0, keepdims=True)
        small[3:4, :] += jnp.sum(grad, axis=0, keepdims=True)
        small[4:5, 0:1] += jnp.sum(losses, axis=0, keepdims=True)
        back = norm_rows_back(grad, unit_rows, scale_rows, gains[2:3])
        acc[rows, :] = back
        branch[rows, :] = back.astype(BF16)
        return carry

    lax.fori_loop(0, count // tile, second_norm, 0)

    def outs(c):
        lanes = lanes_of(c)
        return (
            pltpu.make_async_copy(gd.at[lanes], gd_hbm.at[lanes], out_sem.at[c, 0]),
            pltpu.make_async_copy(gu.at[:, :, lanes], gu_hbm.at[:, :, lanes], out_sem.at[c, 1]),
        )

    def contract(c, carry):
        lanes = lanes_of(c)
        up = wu[:, :, lanes].reshape(width, CHUNK)
        down = wd[lanes, :]
        for i in range(2):
            rows = slice(i * 256, i * 256 + 256)
            value = (matmul(branch[rows, :], down, NT) * slope[rows, lanes]).astype(BF16)
            grad_upper[rows, :] = value
            acc[rows, :] += matmul(value, up, NT)
        gd[lanes, :] = matmul(active[:, lanes], branch[...], TN).astype(BF16)
        gu[:, :, lanes] = matmul(low_turned[...], grad_upper[...]).astype(BF16).reshape(8, width // 8, CHUNK)
        for copy in outs(c):
            copy.start()
        return carry

    lax.fori_loop(0, chunks, contract, 0)

    def first_back(i, carry):
        rows = rows_of(i)
        grad = acc[rows, :]
        small[0:1, :] += jnp.sum(grad * unit[rows, :], axis=0, keepdims=True)
        small[1:2, :] += jnp.sum(grad, axis=0, keepdims=True)
        back = norm_rows_back(grad, unit[rows, :], scale[rows, :], gains[0:1])
        grad_first[rows, :] = back
        branch[rows, :] = back.astype(BF16)
        return carry

    lax.fori_loop(0, count // tile, first_back, 0)
    go[...] = matmul(mixed[...], branch[...], TN).astype(BF16)
    last = pltpu.make_async_copy(go, go_hbm, in_sem.at[0])
    last.start()
    for i in range(2):
        rows = slice(i * 256, i * 256 + 256)
        grad_mixed[rows, :] = matmul(branch[rows, :], wo[...], NT).astype(BF16)

    def settle(c, carry):
        for copy in outs(c):
            copy.wait()
        return carry

    lax.fori_loop(0, chunks, settle, 0)
    last.wait()


def middle(everyone, ctx_size, mixed, x, teacher, slot_col, total, wo, wu, wd):
    count, width = x.shape
    hidden = wd.shape[0]
    dma = pltpu.SemaphoreType.DMA
    vm = pltpu.VMEM
    return pl.pallas_call(
        functools.partial(middle_kernel, everyone, ctx_size),
        out_shape=[
            shaped(count, width),
            shaped(count, width, dtype=F32),
            shaped(count, width),
            shaped(8, width, dtype=F32),
            shaped(*wo.shape),
            shaped(*wu.shape),
            shaped(*wd.shape),
        ],
        in_specs=[VMEM] * 5 + [ANY] * 3,
        out_specs=[VMEM] * 4 + [ANY] * 3,
        scratch_shapes=[
            vm(wo.shape, BF16), vm(wu.shape, BF16), vm(wd.shape, BF16),
            vm((count, hidden), BF16), vm((count, hidden), F32),
            vm((count, width), F32), vm((count, width), F32), vm((count, 1), F32),
            vm((count, width), BF16), vm((width, count), BF16), vm((count, width), F32),
            vm((count, width), BF16), vm((count, CHUNK), BF16),
            vm(wo.shape, BF16), vm(wu.shape, BF16), vm(wd.shape, BF16),
            dma((3,)), dma((hidden // CHUNK, 2)),
        ],
        compiler_params=pltpu.CompilerParams(vmem_limit_bytes=60 * 2**20),
        name="dense_middle",
    )(mixed, x, teacher, slot_col, total, wo, wu, wd)


def local(tokens, teacher, clusters, segments, counted, w_qkv, w_out, w_up, w_down, norms):
    x_rows = tokens[0]
    tok_count, model_dim = x_rows.shape
    wsh, ctx = lax.axis_index("wsh"), lax.axis_index("ctx")
    ctx_size, wsh_size = lax.axis_size("ctx"), lax.axis_size("wsh")
    mixed, x_turned, fq, fo, fu, fd, *kept, total = forward(
        x_rows, clusters[0], segments, counted, norms, (w_qkv, w_out, w_up, w_down)
    )
    everyone = float(tok_count * ctx_size * wsh_size)
    result, grad_first, grad_mixed, small, *grads = middle(
        everyone, float(ctx_size), mixed, x_rows, teacher[0], kept[-1], total,
        fo.reshape(-1, model_dim), fu, fd.reshape(-1, model_dim),
    )
    grad_tokens, (final_qkv, final_out, final_up, final_down), small = backward(
        grad_mixed, grad_first, small, x_turned, fq, kept, [g.reshape(-1, g.shape[-1]) for g in grads]
    )
    width = model_dim // (ctx_size * wsh_size)
    at = ctx * wsh_size + wsh
    final_norms = lax.dynamic_slice(small, (0, at * width), (4, width))
    return (
        result[None],
        grad_tokens[None],
        small[4, 0] / total[4, 0],
        final_qkv,
        final_out,
        final_up,
        final_down,
        final_norms,
    )


def solution(mesh):
    placed = (
        P("wsh", "ctx", None),
        P("wsh", "ctx", None),
        P("wsh", None, "ctx"),
        P("wsh", "ctx"),
        P("wsh", "ctx"),
        P("wsh", None),
        P("wsh", None),
        P("wsh", None),
        P("wsh", None),
        P(None, "wsh"),
    )
    return jax.shard_map(
        local,
        mesh=mesh,
        in_specs=placed,
        out_specs=(
            P("wsh", "ctx", None),
            P("wsh", "ctx", None),
            P(),
            P("wsh", "ctx"),
            P("wsh", "ctx"),
            P("wsh", "ctx"),
            P("wsh", "ctx"),
            P(None, ("ctx", "wsh")),
        ),
        check_vma=False,
    )
```

```python
import functools
import jax
import jax.numpy as jnp
from jax import lax
from jax.experimental import pallas as pl
from jax.experimental.pallas import tpu as pltpu
from jax.sharding import PartitionSpec as P

MESH = pl.DeviceIdType.MESH
BF16 = jnp.bfloat16
F32 = jnp.float32


class Place:
    def __init__(self):
        self.ctx = lax.axis_index("ctx")
        self.wsh = lax.axis_index("wsh")
        self.zlo = self.ctx // 8
        self.y = (self.ctx // 2) % 4
        self.core = self.ctx % 2
        self.zhi = self.wsh // 4
        self.x = self.wsh % 4

    def at(self, zlo=None, y=None, core=None, zhi=None, x=None):
        zlo = self.zlo if zlo is None else zlo
        y = self.y if y is None else y
        core = self.core if core is None else core
        zhi = self.zhi if zhi is None else zhi
        x = self.x if x is None else x
        return (zlo * 8 + y * 2 + core, zhi * 4 + x)

    def sibling(self):
        return self.at(core=1 - self.core)

    def x_peer(self, step):
        return self.at(x=(self.x + step) % 4)

    def y_peer(self, step):
        return self.at(y=(self.y + step) % 4)

    def z_peer(self, step):
        z = (self.zhi * 4 + self.zlo + step + 8) % 8
        return self.at(zlo=z % 4, zhi=z // 4)

    def plane(self):
        return [
            self.at(y=(self.y + d) % 4, core=(self.core + c) % 2)
            for d, c in ((0, 1), (1, 0), (1, 1), (2, 0), (2, 1), (3, 0), (3, 1))
        ]

    def rank(self):
        return self.y * 2 + self.core

    def z_far(self):
        return self.at(zhi=1 - self.zhi)

    def doubling(self):
        return (
            self.sibling(),
            self.at(y=self.y + 1 - 2 * (self.y % 2)),
            self.at(y=(self.y + 2) % 4),
            self.at(x=self.x + 1 - 2 * (self.x % 2)),
            self.at(x=(self.x + 2) % 4),
            self.at(zlo=self.zlo + 1 - 2 * (self.zlo % 2)),
            self.at(zlo=(self.zlo + 2) % 4),
            self.z_far(),
        )


def greet(devices):
    barrier = pltpu.get_barrier_semaphore()
    for device in devices:
        pl.semaphore_signal(barrier, inc=1, device_id=device, device_id_type=MESH)
    pl.semaphore_wait(barrier, len(devices))


def remote(source, target, send_sem, recv_sem, device):
    return pltpu.make_async_remote_copy(
        src_ref=source,
        dst_ref=target,
        send_sem=send_sem,
        recv_sem=recv_sem,
        device_id=device,
        device_id_type=MESH,
    )


def half_of(width, which):
    half = width // 2
    return pl.ds(pl.multiple_of(which * half, 128), half)


class Doubling:
    def __init__(self, place, tile, slots, send_sems, recv_sems):
        self.partners = place.doubling()
        self.tile, self.slots = tile, slots
        self.send_sems, self.recv_sems = send_sems, recv_sems
        self.step = 0
        self.copies = []

    def start(self):
        k = self.step
        copy = remote(
            self.tile.at[k], self.slots.at[k], self.send_sems.at[k], self.recv_sems.at[k], self.partners[k]
        )
        copy.start()
        self.copies.append(copy)

    def advance(self):
        k = self.step
        self.copies[k].wait_recv()
        self.tile[k + 1] = self.tile[k] + self.slots[k]
        self.step = k + 1
        if self.step < 8:
            self.start()

    def drain(self):
        for copy in self.copies:
            copy.wait_send()


NEG = -1e30
NT = (((1,), (1,)), ((), ()))
TN = (((0,), (0,)), ((), ()))


def matmul(left, right, dims=(((1,), (0,)), ((), ()))):
    return lax.dot_general(left, right, dims, preferred_element_type=F32)


class Gather:
    def __init__(self, place, shard, full, send_sems, recv_sems, local_sem):
        self.place, self.shard, self.full = place, shard, full
        self.send_sems, self.recv_sems = send_sems, recv_sems
        self.rows = shard.shape[0]
        self.lanes = half_of(shard.shape[1], place.core)
        self.local = pltpu.make_async_copy(shard, full.at[place.wsh], local_sem)
        self.copies = {}

    def part(self, index, which=None):
        block = self.full.at[index]
        if which is None:
            return block.at[:, self.lanes]
        half = self.rows // 2
        return block.at[which * half : (which + 1) * half, self.lanes]

    def send(self, k, source, target, device):
        copy = remote(source, target, self.send_sems.at[k], self.recv_sems.at[k], device)
        copy.start()
        self.copies[k] = copy

    def own(self, far, step):
        return (far * 4) + (self.place.x + step + 4) % 4

    def start_z(self):
        place = self.place
        self.local.start()
        self.send(2, self.shard.at[:, self.lanes], self.part(place.wsh), place.z_far())

    def start_x(self):
        place = self.place
        self.send(0, self.shard.at[:, self.lanes], self.part(place.wsh), place.x_peer(1))
        self.send(1, self.shard.at[:, self.lanes], self.part(place.wsh), place.x_peer(3))

    def pass_on(self, zh, base):
        place = self.place
        left, right = self.own(zh, -1), self.own(zh, 1)
        self.copies[base].wait_recv()
        self.send(base + 3, self.part(left, 0), self.part(left, 0), place.x_peer(1))
        self.send(base + 5, self.part(left), self.part(left), place.sibling())
        self.copies[base + 1].wait_recv()
        self.send(base + 4, self.part(right, 1), self.part(right, 1), place.x_peer(3))
        self.send(base + 6, self.part(right), self.part(right), place.sibling())

    def opposite(self, zh, base):
        place = self.place
        index = self.own(zh, 2)
        for which in range(2):
            self.copies[base + 3 + which].wait_recv()
            self.send(base + 7 + which, self.part(index, which), self.part(index, which), place.sibling())

    def near(self):
        self.pass_on(self.place.zhi, 0)

    def near_opposite(self):
        self.opposite(self.place.zhi, 0)

    def from_z(self):
        place = self.place
        index = self.own(1 - place.zhi, 0)
        self.copies[2].wait_recv()
        self.send(10, self.part(index), self.part(index), place.x_peer(1))
        self.send(11, self.part(index), self.part(index), place.x_peer(3))
        self.send(9, self.part(index), self.part(index), place.sibling())

    def far(self):
        self.pass_on(1 - self.place.zhi, 10)

    def far_opposite(self):
        self.opposite(1 - self.place.zhi, 10)

    def finish(self):
        self.local.wait()
        for k in (5, 6, 7, 8, 9, 15, 16, 17, 18):
            self.copies[k].wait_recv()

    def drain(self):
        for k in self.copies:
            self.copies[k].wait_send()


def head_mask(which):
    lane = lax.broadcasted_iota(jnp.int32, (1, 128), 1)
    return jnp.where((lane // 64) == which, 1.0, 0.0).astype(BF16)


def to_slots(slot_row, head, count):
    row = slot_row[pl.ds(head, 1), :]
    iota = lax.broadcasted_iota(jnp.int32, (count, count), 0).astype(F32)
    return jnp.where(iota == row, 1.0, 0.0).astype(BF16)


def to_tokens(slot_col, head, count):
    lane = lax.broadcasted_iota(jnp.int32, slot_col.shape, 1)
    column = jnp.sum(jnp.where(lane == head, slot_col[...], 0.0), axis=1, keepdims=True)
    iota = lax.broadcasted_iota(jnp.int32, (count, count), 1).astype(F32)
    return jnp.where(iota == column, 1.0, 0.0).astype(BF16)


def pair_select(first, second):
    lane = lax.broadcasted_iota(jnp.int32, first.shape, 1)
    return jnp.where((lane // 64) % 2 == 0, first, second)


def heads_home(turned):
    return jnp.concatenate([turned[0:64, 0:128], turned[64:128, 128:256]], axis=0).T


def make_slots(clusters, segments, counted, slot_row, slot_col, labels):
    heads, count = clusters.shape
    groups = lax.shift_right_logical(clusters[...], 2)
    iota = lax.broadcasted_iota(jnp.int32, (32, count), 0)
    before = lax.broadcasted_iota(jnp.int32, (count, count), 0)
    after = lax.broadcasted_iota(jnp.int32, (count, count), 1)
    upper = jnp.where(before <= after, 1.0, 0.0).astype(BF16)
    hot = [jnp.where(groups[h : h + 1, :] == iota, 1.0, 0.0) for h in range(heads)]
    counts = matmul(jnp.concatenate(hot, axis=0).astype(BF16), upper)
    group_f = groups.astype(F32)
    rows = []
    for h in range(heads):
        rank = jnp.sum(counts[32 * h : 32 * h + 32] * hot[h], axis=0, keepdims=True)
        rows.append(group_f[h : h + 1] * 16.0 + rank - 1.0)
    slots = jnp.concatenate(rows + [counted[...].astype(F32), jnp.zeros((127 - heads, count), F32)], axis=0)
    slot_row[...] = slots[:16]
    slot_col[...] = slots.T
    label = (segments[0:1, :] * 4 + (clusters[...] & 3)).astype(F32)
    labels[...] = jnp.concatenate([label, jnp.zeros((128 - heads, count), F32)], axis=0).T.astype(BF16)


def rows16(j):
    return slice(16 * j, 16 * j + 16)


def forward_kernel(
    x, clusters, segments, counted, norms, wq, wo, wu, wd,
    mixed, x_turned, fq_out, fo, fu, fd, got_out, before_out, after_out, logsum, hot_out, cold_out, slot_row, slot_col, total,
    fq, got, before, after, hot, cold,
    labels, sent_labels, got_labels, before_labels, after_labels, wide_labels, sent, out, back,
    tile, slots,
    w_send, w_recv, w_local, t_send, t_recv, a_send, a_recv, a_local, z_send, z_recv, b_send, b_recv, b_local, k_sem,
):
    place = Place()
    plane, rank = place.plane(), place.rank()
    up, down = place.z_peer(1), place.z_peer(-1)
    kept = []

    def keep(source, target):
        copy = pltpu.make_async_copy(source, target, k_sem.at[len(kept)])
        copy.start()
        kept.append(copy)

    partners = place.doubling()
    greet(
        plane + [place.x_peer(1), place.x_peer(2), place.x_peer(3), place.z_far(), up, down, partners[5], partners[6]]
    )
    weights = [
        Gather(place, shard, full, w_send.at[i], w_recv.at[i], w_local.at[i])
        for i, (shard, full) in enumerate(((wq, fq), (wo, fo), (wu, fu), (wd, fd)))
    ]
    first, rest = weights[0], weights[1:]
    first.start_z()
    first.start_x()
    tile[0] = jnp.zeros_like(tile[0])
    tile[0, 0:4, 0 : norms.shape[1]] = norms[...].astype(F32)
    tile[0] = pltpu.roll(tile[0], place.wsh * norms.shape[1], 1)
    lane_zero = lax.broadcasted_iota(jnp.int32, (1, tile.shape[2]), 1) == 0
    tile[0, 4:5, :] = jnp.where(lane_zero, jnp.sum(counted[...].astype(F32), axis=1, keepdims=True), 0.0)
    doubling = Doubling(place, tile, slots, t_send, t_recv)
    doubling.start()
    count = x.shape[0]
    make_slots(clusters, segments, counted, slot_row, slot_col, labels)

    sent_labels[...] = jnp.zeros_like(sent_labels)

    def move_labels(head, carry):
        lane = lax.broadcasted_iota(jnp.int32, (count, 128), 1)
        moved = matmul(to_slots(slot_row, head, count), labels[...])
        sent_labels[...] = jnp.where(lane == head, moved, sent_labels[...])
        return carry

    lax.fori_loop(0, 12, move_labels, 0)
    labels[...] = sent_labels[...].astype(BF16)

    def block(which):
        return pl.ds(pl.multiple_of(which * 64, 64), 64)

    def ranks():
        return [dev[0] % 8 for dev in plane]

    label_copies = [
        remote(labels.at[block(to)], got_labels.at[rank], a_send.at[6, k], a_recv.at[6, k], plane[k])
        for k, to in enumerate(ranks())
    ]
    for copy in label_copies:
        copy.start()
    own_labels = pltpu.make_async_copy(labels.at[block(rank)], got_labels.at[rank], a_local.at[6])
    own_labels.start()
    doubling.advance()
    first.near()
    x_turned[...] = x[...].astype(F32).T.astype(BF16)
    doubling.advance()
    own_labels.wait()
    for copy in label_copies:
        copy.wait_recv()
    label_up = remote(got_labels.at[4:8], before_labels, z_send.at[6, 0], z_recv.at[6, 0], up)
    label_down = remote(got_labels.at[0:4], after_labels, z_send.at[6, 1], z_recv.at[6, 1], down)
    label_up.start()
    label_down.start()
    first.from_z()
    for w in rest:
        w.start_z()
    first.near_opposite()
    doubling.advance()
    label_up.wait_recv()
    label_down.wait_recv()
    for j in range(4):
        wide_labels[j, 0:64] = jnp.where(
            place.zlo == 0, -1.0, before_labels[:, rows16(j), :].reshape(64, 128).astype(F32)
        )
        wide_labels[j, 64:192] = got_labels[:, rows16(j), :].reshape(128, 128).astype(F32)
        wide_labels[j, 192:256] = jnp.where(
            place.zlo == 3, -1.0, after_labels[:, rows16(j), :].reshape(64, 128).astype(F32)
        )

    def make_hot(head, carry):
        lane = lax.broadcasted_iota(jnp.int32, (256, 128), 1)
        for j in range(4):
            column = jnp.sum(jnp.where(lane == head, wide_labels[j], 0.0), axis=1, keepdims=True)
            same = lane.astype(F32) == column
            cold[head * 4 + j] = jnp.where(same, 0.0, NEG).astype(BF16)
            hot[head * 4 + j] = jnp.where(same, 1.0, 0.0)[64:192].astype(BF16)
        return carry

    lax.fori_loop(0, 12, make_hot, 0)
    keep(hot, hot_out)
    keep(cold, cold_out)
    doubling.advance()
    first.far()
    doubling.advance()
    for w in rest:
        w.start_x()
    first.far_opposite()
    first.finish()
    keep(fq, fq_out)

    def send_copies(p, fn):
        for k, to in enumerate(ranks()):
            fn(remote(sent.at[p, block(to)], got.at[p, rank], a_send.at[p, k], a_recv.at[p, k], plane[k]))

    def own_copy(p):
        return pltpu.make_async_copy(sent.at[p, block(rank)], got.at[p, rank], a_local.at[p])

    def project(i, carry):
        parts = []
        for t in range(3):
            lanes = pl.ds(pl.multiple_of(t * 768 + i * 256, 128), 256)
            value = matmul(x[...], fq[:, :, lanes].reshape(768, 256)).astype(BF16)
            parts.append(value * jnp.asarray(0.125, BF16) if t == 0 else value)
        for b in range(2):
            p = 2 * i + b
            rows = jnp.concatenate([part[:, b * 128 : b * 128 + 128] for part in parts], axis=1)
            moved = [matmul(to_slots(slot_row, 2 * p + a, count), rows) for a in range(2)]
            sent[p] = pair_select(moved[0], moved[1]).astype(BF16)
            send_copies(p, lambda copy: copy.start())
            own_copy(p).start()
        return carry

    w_out, w_up, w_down = rest
    lax.fori_loop(0, 3, project, 0)
    doubling.advance()
    w_out.near()
    w_out.from_z()
    w_up.near()

    def halo(p):
        return (
            remote(got.at[p, 4:8, :, 128:384], before.at[p], z_send.at[p, 0], z_recv.at[p, 0], up),
            remote(got.at[p, 0:4, :, 128:384], after.at[p], z_send.at[p, 1], z_recv.at[p, 1], down),
        )

    def back_copies(p, fn):
        for k, to in enumerate(ranks()):
            fn(remote(out.at[p, to], back.at[p, rank], b_send.at[p, k], b_recv.at[p, k], plane[k]))

    def own_back(p):
        return pltpu.make_async_copy(out.at[p, rank], back.at[p, rank], b_local.at[p])

    def arrive(p):
        own_copy(p).wait()
        send_copies(p, lambda copy: copy.wait_recv())
        for copy in halo(p):
            copy.start()

    masks = [head_mask(a) for a in range(2)]

    def attend(p):
        for copy in halo(p):
            copy.wait_recv()
        for j in range(4):
            r = rows16(j)
            query = got[p, :, r, 0:128].reshape(128, 128)
            keys = jnp.concatenate(
                [before[p, :, r, 0:128].reshape(64, 128), got[p, :, r, 128:256].reshape(128, 128),
                 after[p, :, r, 0:128].reshape(64, 128)], axis=0)
            values = jnp.concatenate(
                [before[p, :, r, 128:256].reshape(64, 128), got[p, :, r, 256:384].reshape(128, 128),
                 after[p, :, r, 128:256].reshape(64, 128)], axis=0)
            probs = []
            for a in range(2):
                head = 2 * p + a
                scores = matmul(
                    jnp.concatenate([keys, cold[head * 4 + j]], axis=1),
                    jnp.concatenate([query * masks[a], hot[head * 4 + j]], axis=1), NT)
                top = jnp.max(scores, axis=0, keepdims=True)
                raised = jnp.exp(scores - top)
                sums = jnp.sum(raised, axis=0, keepdims=True)
                probs.append((raised * (1.0 / sums)).astype(BF16))
                logsum[j, pl.ds(head, 1), :] = top + jnp.log(sums)
            out[p, :, r, :] = heads_home(matmul(values, jnp.concatenate(probs, axis=1), TN)).astype(BF16).reshape(8, 16, 128)
        back_copies(p, lambda copy: copy.start())
        own_back(p).start()

    arrive(0)
    arrive(1)
    w_up.from_z()
    w_down.near()
    attend(0)
    w_out.near_opposite()
    w_out.far()
    arrive(2)
    attend(1)
    w_up.near_opposite()
    doubling.advance()
    arrive(3)
    attend(2)
    w_down.from_z()
    w_down.near_opposite()
    w_out.far_opposite()
    arrive(4)
    attend(3)
    w_up.far()
    doubling.advance()
    arrive(5)
    attend(4)
    w_down.far()
    attend(5)
    w_up.far_opposite()
    keep(got, got_out)
    keep(before, before_out)
    keep(after, after_out)

    def home(p, carry):
        own_back(p).wait()
        back_copies(p, lambda copy: copy.wait_recv())
        rows = back[p].reshape(count, 128)
        moved = [matmul(to_tokens(slot_col, 2 * p + a, count), rows) for a in range(2)]
        mixed[:, pl.ds(pl.multiple_of(p * 128, 128), 128)] = pair_select(moved[0], moved[1]).astype(BF16)
        return carry

    lax.fori_loop(0, 6, home, 0)
    w_down.far_opposite()
    for w in rest:
        w.finish()
    total[...] = tile[8]

    def settle(p, carry):
        send_copies(p, lambda copy: copy.wait_send())
        back_copies(p, lambda copy: copy.wait_send())
        for copy in halo(p):
            copy.wait_send()
        return carry

    lax.fori_loop(0, 6, settle, 0)
    for copy in label_copies + [label_up, label_down]:
        copy.wait_send()
    for w in weights:
        w.drain()
    for copy in kept:
        copy.wait()
    doubling.drain()


ANY = pl.BlockSpec(memory_space=pl.ANY)
VMEM = pl.BlockSpec(memory_space=pltpu.VMEM)


def shaped(*shape, dtype=BF16):
    return jax.ShapeDtypeStruct(shape, dtype)


def forward(x, clusters, segments, counted, norms, shards):
    count, width = x.shape
    dma = pltpu.SemaphoreType.DMA
    return pl.pallas_call(
        forward_kernel,
        out_shape=[
            shaped(*x.shape),
            shaped(width, count),
            *[shaped(8, *w.shape) for w in shards],
            shaped(6, 8, 64, 384),
            shaped(6, 4, 64, 256),
            shaped(6, 4, 64, 256),
            shaped(4, 16, 128, dtype=F32),
            shaped(48, 128, 128),
            shaped(48, 256, 128),
            shaped(16, count, dtype=F32),
            shaped(count, 128, dtype=F32),
            shaped(8, width, dtype=F32),
        ],
        in_specs=[VMEM] * 5 + [ANY] * 4,
        out_specs=[VMEM] * 2 + [ANY] * 7 + [VMEM] + [ANY] * 2 + [VMEM] * 3,
        scratch_shapes=[
            pltpu.VMEM((8, *shards[0].shape), BF16),
            pltpu.VMEM((6, 8, 64, 384), BF16),
            pltpu.VMEM((6, 4, 64, 256), BF16),
            pltpu.VMEM((6, 4, 64, 256), BF16),
            pltpu.VMEM((48, 128, 128), BF16),
            pltpu.VMEM((48, 256, 128), BF16),
            pltpu.VMEM((count, 128), BF16),
            pltpu.VMEM((count, 128), F32),
            pltpu.VMEM((8, 64, 128), BF16),
            pltpu.VMEM((4, 64, 128), BF16),
            pltpu.VMEM((4, 64, 128), BF16),
            pltpu.VMEM((4, 256, 128), F32),
            pltpu.VMEM((6, count, 384), BF16),
            pltpu.VMEM((6, 8, 64, 128), BF16),
            pltpu.VMEM((6, 8, 64, 128), BF16),
            pltpu.VMEM((9, 8, width), F32),
            pltpu.VMEM((8, 8, width), F32),
            dma((4, 19)), dma((4, 19)), dma((4,)), dma((8,)), dma((8,)),
            dma((7, 7)), dma((7, 7)), dma((7,)), dma((7, 2)), dma((7, 2)),
            dma((6, 7)), dma((6, 7)), dma((6,)), dma((6,)),
        ],
        compiler_params=pltpu.CompilerParams(
            collective_id=0, has_side_effects=True, vmem_limit_bytes=60 * 2**20
        ),
        name="forward_attention",
    )(x, clusters, segments, counted, norms, *shards)


class Reduce:
    def __init__(self, place, held, near, far, sum_x, from_y, sum_y, from_z, out, send_sems, recv_sems, grad=None, source=None, load_sem=None):
        self.place, self.held, self.grad = place, held, grad
        self.near, self.far, self.sum_x, self.from_y = near, far, sum_x, from_y
        self.sum_y, self.from_z, self.out = sum_y, from_z, out
        self.send_sems, self.recv_sems = send_sems, recv_sems
        self.rows, self.half = held.shape[2], held.shape[3]
        self.window = out.shape[1]
        self.owner = place.y // 2
        self.z = place.zhi * 4 + place.zlo
        self.final = jnp.logical_and(place.zhi == self.owner, place.core == place.zlo // 2)
        self.copies = {}
        if source is not None:
            self.load = pltpu.make_async_copy(source, held, load_sem)

    def send(self, k, source, target, device):
        copy = remote(source, target, self.send_sems.at[k], self.recv_sems.at[k], device)
        copy.start()
        self.copies[k] = copy

    def each(self, count, body):
        def step(i, carry):
            body(pl.ds(pl.multiple_of(i * 48, 16), 48))
            return carry

        lax.fori_loop(0, count // 48, step, 0)

    def after(self, rows, offset):
        return pl.ds(pl.multiple_of(rows.start + offset, 16), rows.size)

    def blocks(self, body):
        def step(zh, carry):
            body(zh)
            return carry

        lax.fori_loop(0, 2, step, 0)

    def start(self):
        place = self.place
        self.send(0, self.grad.at[:, :, :, half_of(2 * self.half, 1 - place.core)], self.held, place.sibling())

    def add_pair(self, xx):
        mine = half_of(2 * self.half, self.place.core)

        def block(zh):
            def body(rows):
                self.held[zh, xx, rows, :] = (
                    self.grad[zh, xx, rows, mine].astype(F32) + self.held[zh, xx, rows, :].astype(F32)
                ).astype(BF16)

            self.each(self.rows, body)

        self.blocks(block)

    def to_opposite(self):
        place = self.place
        half = self.rows // 2
        opposite = (place.x + 2) % 4
        if self.grad is None:
            self.load.wait()
        else:
            self.copies[0].wait_recv()
            self.add_pair(opposite)
        self.send(1, self.held.at[:, opposite, 0:half], self.near.at[0], place.x_peer(1))
        self.send(2, self.held.at[:, opposite, half : self.rows], self.near.at[1], place.x_peer(3))
        if self.grad is not None:
            for step in (1, 3, 0):
                self.add_pair((place.x + step) % 4)

    def to_near(self):
        place = self.place
        half = self.rows // 2
        for k, step in enumerate((1, 3)):
            to = (place.x + step) % 4
            self.copies[1 + k].wait_recv()

            def block(zh, k=k, to=to):
                def body(rows):
                    there = self.after(rows, k * half)
                    self.held[zh, to, there, :] = (
                        self.held[zh, to, there, :].astype(F32) + self.near[k, zh, rows, :].astype(F32)
                    ).astype(BF16)

                self.each(half, body)

            self.blocks(block)
            self.send(3 + k, self.held.at[:, to], self.far.at[k], place.x_peer(step))

    def to_y(self):
        place = self.place
        half = self.rows // 2
        for k in range(2):
            self.copies[3 + k].wait_recv()

        def block(zh):
            def body(rows):
                value = self.held[zh, place.x, rows, :].astype(F32)
                value = value + self.far[0, zh, rows, :].astype(F32) + self.far[1, zh, rows, :].astype(F32)
                self.sum_x[zh, rows, :] = value.astype(BF16)

            self.each(self.rows, body)

        self.blocks(block)
        for k, d in enumerate((1, 2, 3)):
            to = (place.y + d) % 4
            part = pl.ds(pl.multiple_of((to % 2) * half, 16), half)
            self.send(5 + k, self.sum_x.at[to // 2, part], self.from_y.at[k], place.y_peer(d))

    def lanes(self, zlo):
        offset = (zlo % 2) * (self.half - self.window)
        return pl.ds(pl.multiple_of(offset, 128), self.window)

    def z_copy(self, k):
        place = self.place
        zlo = 2 * place.core + k
        return remote(
            self.sum_y.at[:, self.lanes(zlo)], self.from_z.at[self.z],
            self.send_sems.at[8 + k], self.recv_sems.at[8 + self.z], place.at(zlo=zlo, zhi=self.owner),
        )

    def is_target(self, k):
        place = self.place
        return jnp.logical_and(place.zhi == self.owner, place.zlo == 2 * place.core + k)

    def to_z(self):
        place = self.place
        half = self.rows // 2
        for k in range(3):
            self.copies[5 + k].wait_recv()

        def body(rows):
            value = self.sum_x[self.owner, self.after(rows, (place.y % 2) * half), :].astype(F32)
            for k in range(3):
                value = value + self.from_y[k, rows, :].astype(F32)
            self.sum_y[rows, :] = value.astype(BF16)

        self.each(half, body)
        for k in range(2):
            @pl.when(jnp.logical_not(self.is_target(k)))
            def _(k=k):
                self.z_copy(k).start()

    def spread_copy(self, k, device):
        half = self.rows // 2
        part = self.out.at[pl.ds(pl.multiple_of((self.place.y % 2) * half, 16), half)]
        return remote(part, part, self.send_sems.at[10 + k], self.recv_sems.at[16 + self.place.y % 2], device)

    def spread(self):
        half = self.rows // 2

        @pl.when(self.final)
        def _():
            self.from_z[self.z] = self.sum_y[:, self.lanes(self.place.zlo)]
            for z in range(8):
                @pl.when(self.z != z)
                def _(z=z):
                    part = self.from_z.at[z]
                    remote(part, part, self.send_sems.at[8], self.recv_sems.at[8 + z], self.place.sibling()).wait_recv()

            def body(rows):
                there = self.after(rows, (self.place.y % 2) * half)
                value = self.from_z[0, rows, :].astype(F32)
                for z in range(1, 8):
                    value = value + self.from_z[z, rows, :].astype(F32)
                self.out[there, :] = value.astype(BF16)

            self.each(half, body)
            for k, device in enumerate(self.place.plane()):
                self.spread_copy(k, device).start()

    def finish(self):
        half = self.rows // 2
        for k in range(2):
            part = self.out.at[k * half : (k + 1) * half]

            @pl.when(jnp.logical_not(jnp.logical_and(self.final, self.place.y % 2 == k)))
            def _(k=k, part=part):
                remote(part, part, self.send_sems.at[10], self.recv_sems.at[16 + k], self.place.sibling()).wait_recv()

    def drain(self):
        for k in self.copies:
            self.copies[k].wait_send()
        for k in range(2):
            @pl.when(jnp.logical_not(self.is_target(k)))
            def _(k=k):
                self.z_copy(k).wait_send()

        @pl.when(self.final)
        def _():
            for k, device in enumerate(self.place.plane()):
                self.spread_copy(k, device).wait_send()


def reduce_scratch(rows, half, window):
    return [
        pltpu.VMEM((2, 4, rows, half), BF16),
        pltpu.VMEM((2, 2, rows // 2, half), BF16),
        pltpu.VMEM((2, 2, rows, half), BF16),
        pltpu.VMEM((2, rows, half), BF16),
        pltpu.VMEM((3, rows // 2, half), BF16),
        pltpu.VMEM((rows // 2, half), BF16),
        pltpu.VMEM((8, rows // 2, window), BF16),
        pltpu.VMEM((rows, window), BF16),
    ]


def cut(value, offset, target):
    width = value.shape[1]
    target[...] = pltpu.roll(value, (width - offset) % width, 1)[:, : target.shape[1]]


ORDER = (0, 3, 1, 4, 2, 5)


def backward_kernel(*refs):
    (grad_mixed, grad_first, logsum, slot_row, slot_col, small, x_hbm, fq_hbm, got_hbm, before_hbm, after_hbm,
     hot_hbm, cold_hbm, go, gu, gd) = refs[:16]
    grad_x, out_q, out_o, out_u, out_d, small_out = refs[16:22]
    x_turned, fq, got, before, after, hot, cold = refs[22:29]
    sent, got_grad, grads, to_before, to_after, from_before, from_after, back = refs[29:37]
    grads_q = refs[37:40]
    reduce_refs = [refs[40 + 8 * i : 48 + 8 * i] for i in range(6)]
    (tile, slots, a_send, a_recv, a_local, z_send, z_recv, b_send, b_recv, b_local,
     t_send, t_recv, r_send, r_recv, r_load, l_sem) = refs[88:]
    place = Place()
    plane, rank = place.plane(), place.rank()
    up, down = place.z_peer(1), place.z_peer(-1)
    loads = [
        pltpu.make_async_copy(source, target, l_sem.at[i])
        for i, (source, target) in enumerate(
            ((got_hbm, got), (before_hbm, before), (after_hbm, after), (hot_hbm, hot), (cold_hbm, cold),
             (fq_hbm, fq), (x_hbm, x_turned))
        )
    ]
    rest = [
        Reduce(place, *reduce_refs[i], r_send.at[i], r_recv.at[i], source=source, load_sem=r_load.at[i])
        for i, source in enumerate((go, gu, gd))
    ]
    by_group = [
        Reduce(place, *reduce_refs[3 + i], r_send.at[3 + i], r_recv.at[3 + i], grad=grads_q[i]) for i in range(3)
    ]
    for r in rest:
        r.load.start()
    for copy in loads:
        copy.start()
    greet(plane + [place.x_peer(d) for d in (1, 2, 3)] + [place.z_peer(d) for d in range(1, 8)])
    sum_o, sum_u, sum_d = rest
    for r in (sum_d, sum_u, sum_o):
        r.to_opposite()
    tile[0] = small[...]
    doubling = Doubling(place, tile, slots, t_send, t_recv)
    doubling.start()
    count = grad_mixed.shape[0]
    ranks = [dev[0] % 8 for dev in plane]

    def block(which):
        return pl.ds(pl.multiple_of(which * 64, 64), 64)

    def send_copies(p, fn):
        for k, to in enumerate(ranks):
            fn(remote(sent.at[p, block(to)], got_grad.at[p, rank], a_send.at[p, k], a_recv.at[p, k], plane[k]))

    def own_copy(p):
        return pltpu.make_async_copy(sent.at[p, block(rank)], got_grad.at[p, rank], a_local.at[p])

    def leave(i, carry):
        p = i // 2 + 3 * (i % 2)
        rows = grad_mixed[:, pl.ds(pl.multiple_of(p * 128, 128), 128)]
        moved = [matmul(to_slots(slot_row, 2 * p + a, count), rows) for a in range(2)]
        sent[p] = pair_select(moved[0], moved[1]).astype(BF16)
        send_copies(p, lambda copy: copy.start())
        own_copy(p).start()
        return carry

    lax.fori_loop(0, 6, leave, 0)
    for copy in loads[:5]:
        copy.wait()

    def halo(p):
        return (
            remote(to_after.at[p], from_before.at[p], z_send.at[p, 0], z_recv.at[p, 0], up),
            remote(to_before.at[p], from_after.at[p], z_send.at[p, 1], z_recv.at[p, 1], down),
        )

    def back_copies(p, fn):
        for k, to in enumerate(ranks):
            fn(remote(grads.at[p, to], back.at[p, rank], b_send.at[p, k], b_recv.at[p, k], plane[k]))

    def own_back(p):
        return pltpu.make_async_copy(grads.at[p, rank], back.at[p, rank], b_local.at[p])

    masks = [head_mask(a) for a in range(2)]

    def attend(p):
        own_copy(p).wait()
        send_copies(p, lambda copy: copy.wait_recv())
        for j in range(4):
            r = rows16(j)
            query = got[p, :, r, 0:128].reshape(128, 128)
            keys = jnp.concatenate(
                [before[p, :, r, 0:128].reshape(64, 128), got[p, :, r, 128:256].reshape(128, 128),
                 after[p, :, r, 0:128].reshape(64, 128)], axis=0)
            values = jnp.concatenate(
                [before[p, :, r, 128:256].reshape(64, 128), got[p, :, r, 256:384].reshape(128, 128),
                 after[p, :, r, 128:256].reshape(64, 128)], axis=0)
            grad = got_grad[p, :, r, :].reshape(128, 128)
            queries = [query * masks[a] for a in range(2)]
            grad_both = jnp.concatenate([grad * masks[a] for a in range(2)], axis=0)
            grad_probs = matmul(values, grad_both, NT)
            probs, grad_scores = [], []
            for a in range(2):
                head = 2 * p + a
                scores = matmul(
                    jnp.concatenate([keys, cold[head * 4 + j]], axis=1),
                    jnp.concatenate([queries[a], hot[head * 4 + j]], axis=1), NT)
                prob = jnp.exp(scores - logsum[j, pl.ds(head, 1), :])
                own = grad_probs[:, a * 128 : a * 128 + 128]
                delta = jnp.sum(prob * own, axis=0, keepdims=True)
                probs.append(prob.astype(BF16))
                grad_scores.append((prob * (own - delta)).astype(BF16))
            grad_scores = jnp.concatenate(grad_scores, axis=1)
            dk = matmul(grad_scores, jnp.concatenate(queries, axis=0))
            dv = matmul(jnp.concatenate(probs, axis=1), grad_both)
            dq = heads_home(matmul(keys, grad_scores, TN)) * 0.125
            both = jnp.concatenate([dk, dv], axis=1).astype(BF16)
            to_before[p, :, r, :] = both[0:64].reshape(4, 16, 256)
            to_after[p, :, r, :] = both[192:256].reshape(4, 16, 256)
            grads[p, :, r, 0:128] = dq.astype(BF16).reshape(8, 16, 128)
            grads[p, :, r, 128:384] = both[64:192].reshape(8, 16, 256)
        for copy in halo(p):
            copy.start()

    def give(p):
        for copy in halo(p):
            copy.wait_recv()
        for part, extra in ((slice(0, 4), from_before), (slice(4, 8), from_after)):
            grads[p, part, :, 128:384] = (
                grads[p, part, :, 128:384].astype(F32) + extra[p].astype(F32)
            ).astype(BF16)
        back_copies(p, lambda copy: copy.start())
        own_back(p).start()

    def home(p):
        own_back(p).wait()
        back_copies(p, lambda copy: copy.wait_recv())
        rows = back[p].reshape(count, 384)
        moved = [matmul(to_tokens(slot_col, 2 * p + a, count), rows) for a in range(2)]
        grad_qkv = pair_select(moved[0], moved[1]).astype(BF16)
        back[p] = grad_qkv.reshape(8, 64, 384)
        weight = matmul(x_turned[...], grad_qkv).astype(BF16)
        group, late = p % 3, p // 3
        for t, lane in enumerate((late, 2 + late, 4 + late)):
            grads_q[group][:, :, :, lane * 128 : lane * 128 + 128] = weight[:, t * 128 : t * 128 + 128].reshape(2, 4, 96, 128)

    def turn_back(i):
        rows = slice(i * 128, i * 128 + 128)
        parts = [
            back[p, 2 * i : 2 * i + 2, :, t * 128 : t * 128 + 128].reshape(128, 128) for t in range(3) for p in range(6)
        ]
        grad_x[rows, :] = grad_first[rows, :] + matmul(jnp.concatenate(parts, axis=1), fq[...].reshape(768, 2304), NT)

    attend(0)
    doubling.advance()
    attend(3)
    give(0)
    sum_d.to_near()
    attend(1)
    give(3)
    sum_u.to_near()
    sum_o.to_near()
    attend(4)
    give(1)
    doubling.advance()
    attend(2)
    give(4)
    attend(5)
    give(2)
    sum_d.to_y()
    give(5)
    for copy in loads[5:]:
        copy.wait()
    home(0)
    doubling.advance()
    home(3)
    by_group[0].start()
    sum_u.to_y()
    sum_d.to_z()
    home(1)
    by_group[0].to_opposite()
    home(4)
    by_group[1].start()
    sum_o.to_y()
    by_group[0].to_near()
    doubling.advance()
    home(2)
    by_group[1].to_opposite()
    sum_u.to_z()
    home(5)
    by_group[2].start()
    by_group[0].to_y()
    by_group[1].to_near()
    doubling.advance()
    by_group[2].to_opposite()
    sum_o.to_z()
    turn_back(0)
    by_group[1].to_y()
    by_group[0].to_z()
    by_group[2].to_near()
    doubling.advance()
    sum_d.spread()
    turn_back(1)
    by_group[1].to_z()
    by_group[2].to_y()
    doubling.advance()
    sum_u.spread()
    sum_o.spread()
    by_group[0].spread()
    turn_back(2)
    by_group[2].to_z()
    doubling.advance()
    by_group[1].spread()
    turn_back(3)
    by_group[2].spread()
    small_out[...] = tile[8]

    def settle(p, carry):
        send_copies(p, lambda copy: copy.wait_send())
        back_copies(p, lambda copy: copy.wait_send())
        for copy in halo(p):
            copy.wait_send()
        return carry

    lax.fori_loop(0, 6, settle, 0)
    seat = place.y * 2 + place.core
    for r, target in zip((sum_d, sum_u, sum_o), (out_d, out_u, out_o)):
        r.finish()
        width = target.shape[1]
        offset = (place.zlo % 2) * (8 * width - (r.half - r.window)) + seat * width
        cut(r.out[...].astype(F32), offset, target)
    for r in by_group:
        r.finish()
    tiles = [by_group[g].out[:, i * 128 : i * 128 + 128].astype(F32) for i in range(3) for g in range(3)]
    width = out_q.shape[1]
    cut(jnp.concatenate(tiles, axis=1), (place.zlo % 2) * 8 * width + seat * width, out_q)
    for r in rest + by_group:
        r.drain()
    doubling.drain()


def backward(grad_mixed, grad_first, small, x_turned, fq, kept, halves):
    got, before, after, logsum, hot, cold, slot_row, slot_col = kept
    count = grad_mixed.shape[0]
    dma = pltpu.SemaphoreType.DMA
    vm = pltpu.VMEM
    rows_in = (halves[2].shape[2],)
    shapes = [(96, 384, 256), (96, 1536, 768), (rows_in[0], 384, 256)] + [(96, 384, 384)] * 3
    reduce_refs = []
    for shape in shapes:
        reduce_refs += reduce_scratch(*shape)
    loaded = (x_turned, fq, got, before, after, hot, cold)
    results = pl.pallas_call(
        backward_kernel,
        out_shape=[
            shaped(*grad_first.shape, dtype=F32),
            shaped(96, 72, dtype=F32),
            shaped(96, 24, dtype=F32),
            shaped(96, 96, dtype=F32),
            shaped(384, 24, dtype=F32),
            shaped(*small.shape, dtype=F32),
        ],
        in_specs=[VMEM] * 6 + [ANY] * 10,
        out_specs=[VMEM] * 6,
        scratch_shapes=[vm(array.shape, array.dtype) for array in loaded]
        + [
            vm((6, count, 128), BF16),
            vm((6, 8, 64, 128), BF16),
            vm((6, 8, 64, 384), BF16),
            vm((6, 4, 64, 256), BF16),
            vm((6, 4, 64, 256), BF16),
            vm((6, 4, 64, 256), BF16),
            vm((6, 4, 64, 256), BF16),
            vm((6, 8, 64, 384), BF16),
        ]
        + [vm((2, 4, 96, 768), BF16)] * 3
        + reduce_refs
        + [
            vm((9, *small.shape), F32),
            vm((8, *small.shape), F32),
            dma((6, 7)), dma((6, 7)), dma((6,)), dma((6, 2)), dma((6, 2)),
            dma((6, 7)), dma((6, 7)), dma((6,)),
            dma((8,)), dma((8,)), dma((6, 17)), dma((6, 18)), dma((3,)), dma((7,)),
        ],
        compiler_params=pltpu.CompilerParams(
            collective_id=1, has_side_effects=True, vmem_limit_bytes=62 * 2**20
        ),
        name="backward_attention",
    )(grad_mixed, grad_first, logsum, slot_row, slot_col, small, *loaded, *halves)
    return results[0], results[1:5], results[5]


CHUNK = 512


def norm_rows(values):
    centered = values - jnp.mean(values, axis=-1, keepdims=True)
    scale = lax.rsqrt(jnp.mean(centered * centered, axis=-1, keepdims=True) + 1e-05)
    return centered * scale, scale


def norm_rows_back(grad, normed, scale, gain):
    weighted = grad * gain
    return scale * (
        weighted
        - jnp.mean(weighted, axis=-1, keepdims=True)
        - normed * jnp.mean(weighted * normed, axis=-1, keepdims=True)
    )


def middle_kernel(
    everyone, ctx_size,
    mixed, x, teacher, slot_col, total, wo_hbm, wu_hbm, wd_hbm,
    result, grad_first, grad_mixed, small, go_hbm, gu_hbm, gd_hbm,
    wo, wu, wd, active, slope, normed, unit, scale, low, low_turned, acc, branch, grad_upper, go, gu, gd,
    held_o, held_u, held_d, in_sem, out_sem, send_sem, recv_sem,
):
    place = Place()
    core, sibling = place.core, place.sibling()
    loads = [
        pltpu.make_async_copy(source, target, in_sem.at[i])
        for i, (source, target) in enumerate(((wo_hbm, wo), (wu_hbm, wu), (wd_hbm, wd)))
    ]
    for copy in loads:
        copy.start()
    greet([sibling])
    count, width = x.shape
    tile = 128
    chunks = wd.shape[0] // CHUNK
    gains = total[0:4] / ctx_size
    small[...] = jnp.zeros_like(small)

    def rows_of(i):
        return pl.ds(pl.multiple_of(i * tile, tile), tile)

    def lanes_of(c):
        return pl.ds(pl.multiple_of(c * CHUNK, CHUNK), CHUNK)

    loads[0].wait()
    for i in range(2):
        rows = slice(i * 256, i * 256 + 256)
        acc[rows, :] = matmul(mixed[rows, :], wo[...])

    def first_norm(i, carry):
        rows = rows_of(i)
        unit_rows, scale_rows = norm_rows(x[rows, :].astype(F32) + acc[rows, :])
        unit[rows, :] = unit_rows
        scale[rows, :] = scale_rows
        value = unit_rows * gains[0:1] + gains[1:2]
        normed[rows, :] = value
        low[rows, :] = value.astype(BF16)
        acc[rows, :] = value
        return carry

    lax.fori_loop(0, count // tile, first_norm, 0)
    loads[1].wait()
    loads[2].wait()

    def expand(c, carry):
        lanes = lanes_of(c)
        up = wu[:, :, lanes].reshape(width, CHUNK)
        down = wd[lanes, :]
        for i in range(2):
            rows = slice(i * 256, i * 256 + 256)
            upper = matmul(low[rows, :], up)
            share = 0.5 + 0.5 * lax.erf(upper * 0.7071067811865476)
            density = jnp.exp(upper * upper * -0.5) * 0.3989422804014327
            value = (upper * share).astype(BF16)
            active[rows, lanes] = value
            slope[rows, lanes] = share + upper * density
            acc[rows, :] += matmul(value, down)
        return carry

    lax.fori_loop(0, chunks, expand, 0)
    low_turned[...] = normed[...].T.astype(BF16)

    def second_norm(i, carry):
        rows = rows_of(i)
        unit_rows, scale_rows = norm_rows(acc[rows, :])
        value = unit_rows * gains[2:3] + gains[3:4]
        result[rows, :] = value.astype(BF16)
        error = value - teacher[rows, :].astype(F32)
        mask = slot_col[rows, 12:13]
        losses = mask * jnp.mean(error * error, axis=-1, keepdims=True)
        grad = (everyone / total[4:5, 0:1]) * mask * error
        small[2:3, :] += jnp.sum(grad * unit_rows, axis=0, keepdims=True)
        small[3:4, :] += jnp.sum(grad, axis=0, keepdims=True)
        small[4:5, 0:1] += jnp.sum(losses, axis=0, keepdims=True)
        back = norm_rows_back(grad, unit_rows, scale_rows, gains[2:3])
        acc[rows, :] = back
        branch[rows, :] = back.astype(BF16)
        return carry

    lax.fori_loop(0, count // tile, second_norm, 0)

    half = chunks // 2
    theirs, ours = half_of(width, 1 - core), half_of(width, core)

    def down_copy(c):
        lanes = lanes_of(c)
        return remote(gd.at[lanes, theirs], held_d.at[lanes], send_sem.at[c], recv_sem.at[c], sibling)

    def up_copy(i):
        return remote(gu.at[i], held_u.at[i], send_sem.at[chunks + i], recv_sem.at[chunks + i], sibling)

    def up_out(i):
        return pltpu.make_async_copy(held_u.at[i], gu_hbm.at[:, :, lanes_of(i)], out_sem.at[chunks + i])

    def contract(c):
        lanes = lanes_of(c)
        up = wu[:, :, lanes].reshape(width, CHUNK)
        down = wd[lanes, :]
        for i in range(2):
            rows = slice(i * 256, i * 256 + 256)
            value = (matmul(branch[rows, :], down, NT) * slope[rows, lanes]).astype(BF16)
            grad_upper[rows, :] = value
            acc[rows, :] += matmul(value, up, NT)
        gd[lanes, :] = matmul(active[:, lanes], branch[...], TN).astype(BF16)
        down_copy(c).start()
        return matmul(low_turned[...], grad_upper[...]).reshape(8, width // 8, CHUNK)

    def for_sibling(i, carry):
        gu[i] = contract((1 - core) * half + i).astype(BF16)
        up_copy(i).start()
        return carry

    def for_own(i, carry):
        value = contract(core * half + i)
        up_copy(i).wait_recv()
        held_u[i] = (value + held_u[i].astype(F32)).astype(BF16)
        up_out(i).start()
        return carry

    lax.fori_loop(0, half, for_sibling, 0)
    lax.fori_loop(0, half, for_own, 0)

    def first_back(i, carry):
        rows = rows_of(i)
        grad = acc[rows, :]
        small[0:1, :] += jnp.sum(grad * unit[rows, :], axis=0, keepdims=True)
        small[1:2, :] += jnp.sum(grad, axis=0, keepdims=True)
        back = norm_rows_back(grad, unit[rows, :], scale[rows, :], gains[0:1])
        grad_first[rows, :] = back
        branch[rows, :] = back.astype(BF16)
        return carry

    lax.fori_loop(0, count // tile, first_back, 0)
    go[...] = matmul(mixed[...], branch[...], TN).astype(BF16)
    last = remote(go.at[:, theirs], held_o, send_sem.at[chunks + half], recv_sem.at[chunks + half], sibling)
    last.start()
    for i in range(2):
        rows = slice(i * 256, i * 256 + 256)
        grad_mixed[rows, :] = matmul(branch[rows, :], wo[...], NT).astype(BF16)

    def down_out(c):
        lanes = lanes_of(c)
        return pltpu.make_async_copy(held_d.at[lanes], gd_hbm.at[lanes], out_sem.at[c])

    def add_down(c, carry):
        lanes = lanes_of(c)
        down_copy(c).wait_recv()
        held_d[lanes, :] = (gd[lanes, ours].astype(F32) + held_d[lanes, :].astype(F32)).astype(BF16)
        down_out(c).start()
        return carry

    lax.fori_loop(0, chunks, add_down, 0)
    last.wait_recv()
    held_o[...] = (go[:, ours].astype(F32) + held_o[...].astype(F32)).astype(BF16)
    out = pltpu.make_async_copy(held_o, go_hbm, in_sem.at[0])
    out.start()

    def settle_down(c, carry):
        down_copy(c).wait_send()
        down_out(c).wait()
        return carry

    def settle_up(i, carry):
        up_copy(i).wait_send()
        up_out(i).wait()
        return carry

    lax.fori_loop(0, chunks, settle_down, 0)
    lax.fori_loop(0, half, settle_up, 0)
    last.wait_send()
    out.wait()


def middle(everyone, ctx_size, mixed, x, teacher, slot_col, total, wo, wu, wd):
    count, width = x.shape
    hidden = wd.shape[0]
    chunks = hidden // CHUNK
    dma = pltpu.SemaphoreType.DMA
    vm = pltpu.VMEM
    return pl.pallas_call(
        functools.partial(middle_kernel, everyone, ctx_size),
        out_shape=[
            shaped(count, width),
            shaped(count, width, dtype=F32),
            shaped(count, width),
            shaped(8, width, dtype=F32),
            shaped(width, width // 2),
            shaped(8, width // 8, hidden // 2),
            shaped(hidden, width // 2),
        ],
        in_specs=[VMEM] * 5 + [ANY] * 3,
        out_specs=[VMEM] * 4 + [ANY] * 3,
        scratch_shapes=[
            vm(wo.shape, BF16), vm(wu.shape, BF16), vm(wd.shape, BF16),
            vm((count, hidden), BF16), vm((count, hidden), F32),
            vm((count, width), F32), vm((count, width), F32), vm((count, 1), F32),
            vm((count, width), BF16), vm((width, count), BF16), vm((count, width), F32),
            vm((count, width), BF16), vm((count, CHUNK), BF16),
            vm(wo.shape, BF16), vm((chunks // 2, 8, width // 8, CHUNK), BF16), vm(wd.shape, BF16),
            vm((width, width // 2), BF16), vm((chunks // 2, 8, width // 8, CHUNK), BF16), vm((hidden, width // 2), BF16),
            dma((3,)), dma((chunks + chunks // 2,)), dma((chunks + chunks // 2 + 1,)), dma((chunks + chunks // 2 + 1,)),
        ],
        compiler_params=pltpu.CompilerParams(
            collective_id=2, has_side_effects=True, vmem_limit_bytes=62 * 2**20
        ),
        name="dense_middle",
    )(mixed, x, teacher, slot_col, total, wo, wu, wd)


def local(tokens, teacher, clusters, segments, counted, w_qkv, w_out, w_up, w_down, norms):
    x_rows = tokens[0]
    tok_count, model_dim = x_rows.shape
    wsh, ctx = lax.axis_index("wsh"), lax.axis_index("ctx")
    ctx_size, wsh_size = lax.axis_size("ctx"), lax.axis_size("wsh")
    mixed, x_turned, fq, fo, fu, fd, *kept, total = forward(
        x_rows, clusters[0], segments, counted, norms, (w_qkv, w_out, w_up, w_down)
    )
    everyone = float(tok_count * ctx_size * wsh_size)
    result, grad_first, grad_mixed, small, *grads = middle(
        everyone, float(ctx_size), mixed, x_rows, teacher[0], kept[-1], total,
        fo.reshape(-1, model_dim), fu, fd.reshape(-1, model_dim),
    )
    grad_tokens, (final_qkv, final_out, final_up, final_down), small = backward(
        grad_mixed, grad_first, small, x_turned, fq, kept,
        [g.reshape(2, 4, -1, g.shape[-1]) for g in grads]
    )
    width = model_dim // (ctx_size * wsh_size)
    at = ctx * wsh_size + wsh
    final_norms = lax.dynamic_slice(small, (0, at * width), (4, width))
    return (
        result[None],
        grad_tokens[None],
        small[4, 0] / total[4, 0],
        final_qkv,
        final_out,
        final_up,
        final_down,
        final_norms,
    )


def solution(mesh):
    placed = (
        P("wsh", "ctx", None),
        P("wsh", "ctx", None),
        P("wsh", None, "ctx"),
        P("wsh", "ctx"),
        P("wsh", "ctx"),
        P("wsh", None),
        P("wsh", None),
        P("wsh", None),
        P("wsh", None),
        P(None, "wsh"),
    )
    return jax.shard_map(
        local,
        mesh=mesh,
        in_specs=placed,
        out_specs=(
            P("wsh", "ctx", None),
            P("wsh", "ctx", None),
            P(),
            P("wsh", "ctx"),
            P("wsh", "ctx"),
            P("wsh", "ctx"),
            P("wsh", "ctx"),
            P(None, ("ctx", "wsh")),
        ),
        check_vma=False,
    )
```

```python
import functools
import jax
import jax.numpy as jnp
from jax import lax
from jax.experimental import pallas as pl
from jax.experimental.pallas import tpu as pltpu
from jax.sharding import PartitionSpec as P

MESH = pl.DeviceIdType.MESH
BF16 = jnp.bfloat16
F32 = jnp.float32


class Place:
    def __init__(self):
        self.ctx = lax.axis_index("ctx")
        self.wsh = lax.axis_index("wsh")
        self.zlo = self.ctx // 8
        self.y = (self.ctx // 2) % 4
        self.core = self.ctx % 2
        self.zhi = self.wsh // 4
        self.x = self.wsh % 4

    def at(self, zlo=None, y=None, core=None, zhi=None, x=None):
        zlo = self.zlo if zlo is None else zlo
        y = self.y if y is None else y
        core = self.core if core is None else core
        zhi = self.zhi if zhi is None else zhi
        x = self.x if x is None else x
        return (zlo * 8 + y * 2 + core, zhi * 4 + x)

    def sibling(self):
        return self.at(core=1 - self.core)

    def x_peer(self, step):
        return self.at(x=(self.x + step) % 4)

    def y_peer(self, step):
        return self.at(y=(self.y + step) % 4)

    def z_peer(self, step):
        z = (self.zhi * 4 + self.zlo + step + 8) % 8
        return self.at(zlo=z % 4, zhi=z // 4)

    def plane(self):
        return [
            self.at(y=(self.y + d) % 4, core=(self.core + c) % 2)
            for d, c in ((0, 1), (1, 0), (1, 1), (2, 0), (2, 1), (3, 0), (3, 1))
        ]

    def rank(self):
        return self.y * 2 + self.core

    def z_far(self):
        return self.at(zhi=1 - self.zhi)

    def doubling(self):
        return (
            self.z_far(),
            self.sibling(),
            self.at(y=self.y + 1 - 2 * (self.y % 2)),
            self.at(y=(self.y + 2) % 4),
            self.at(x=self.x + 1 - 2 * (self.x % 2)),
            self.at(x=(self.x + 2) % 4),
            self.at(zlo=self.zlo + 1 - 2 * (self.zlo % 2)),
            self.at(zlo=(self.zlo + 2) % 4),
        )


def greet(devices):
    barrier = pltpu.get_barrier_semaphore()
    for device in devices:
        pl.semaphore_signal(barrier, inc=1, device_id=device, device_id_type=MESH)
    pl.semaphore_wait(barrier, len(devices))


def remote(source, target, send_sem, recv_sem, device):
    return pltpu.make_async_remote_copy(
        src_ref=source,
        dst_ref=target,
        send_sem=send_sem,
        recv_sem=recv_sem,
        device_id=device,
        device_id_type=MESH,
    )


def half_of(width, which):
    half = width // 2
    return pl.ds(pl.multiple_of(which * half, 128), half)


class Doubling:
    def __init__(self, place, tile, slots, send_sems, recv_sems):
        self.partners = place.doubling()
        self.tile, self.slots = tile, slots
        self.send_sems, self.recv_sems = send_sems, recv_sems
        self.step = 0
        self.copies = []

    def start(self):
        k = self.step
        copy = remote(
            self.tile.at[k], self.slots.at[k], self.send_sems.at[k], self.recv_sems.at[k], self.partners[k]
        )
        copy.start()
        self.copies.append(copy)

    def advance(self):
        k = self.step
        self.copies[k].wait_recv()
        self.tile[k + 1] = self.tile[k] + self.slots[k]
        self.step = k + 1
        if self.step < 8:
            self.start()

    def drain(self):
        for copy in self.copies:
            copy.wait_send()


NEG = -1e30
NT = (((1,), (1,)), ((), ()))
TN = (((0,), (0,)), ((), ()))


def matmul(left, right, dims=(((1,), (0,)), ((), ()))):
    return lax.dot_general(left, right, dims, preferred_element_type=F32)


class Gather:
    def __init__(self, place, shard, full, send_sems, recv_sems, local_sem):
        self.place, self.shard, self.full = place, shard, full
        self.send_sems, self.recv_sems = send_sems, recv_sems
        self.rows = shard.shape[0]
        self.lanes = half_of(shard.shape[1], place.core)
        self.local = pltpu.make_async_copy(shard, full.at[place.wsh], local_sem)
        self.copies = {}

    def part(self, index, which=None):
        block = self.full.at[index]
        if which is None:
            return block.at[:, self.lanes]
        half = self.rows // 2
        return block.at[which * half : (which + 1) * half, self.lanes]

    def send(self, k, source, target, device):
        copy = remote(source, target, self.send_sems.at[k], self.recv_sems.at[k], device)
        copy.start()
        self.copies[k] = copy

    def own(self, far, step):
        return (far * 4) + (self.place.x + step + 4) % 4

    def start_z(self):
        place = self.place
        self.local.start()
        self.send(2, self.shard.at[:, self.lanes], self.part(place.wsh), place.z_far())

    def start_x(self):
        place = self.place
        self.send(0, self.shard.at[:, self.lanes], self.part(place.wsh), place.x_peer(1))
        self.send(1, self.shard.at[:, self.lanes], self.part(place.wsh), place.x_peer(3))

    def pass_on(self, zh, base):
        place = self.place
        left, right = self.own(zh, -1), self.own(zh, 1)
        self.copies[base].wait_recv()
        self.send(base + 3, self.part(left, 0), self.part(left, 0), place.x_peer(1))
        self.send(base + 5, self.part(left), self.part(left), place.sibling())
        self.copies[base + 1].wait_recv()
        self.send(base + 4, self.part(right, 1), self.part(right, 1), place.x_peer(3))
        self.send(base + 6, self.part(right), self.part(right), place.sibling())

    def opposite(self, zh, base):
        place = self.place
        index = self.own(zh, 2)
        for which in range(2):
            self.copies[base + 3 + which].wait_recv()
            self.send(base + 7 + which, self.part(index, which), self.part(index, which), place.sibling())

    def near(self):
        self.pass_on(self.place.zhi, 0)

    def near_opposite(self):
        self.opposite(self.place.zhi, 0)

    def from_z(self):
        place = self.place
        index = self.own(1 - place.zhi, 0)
        self.copies[2].wait_recv()
        self.send(10, self.part(index), self.part(index), place.x_peer(1))
        self.send(11, self.part(index), self.part(index), place.x_peer(3))
        self.send(9, self.part(index), self.part(index), place.sibling())

    def far(self):
        self.pass_on(1 - self.place.zhi, 10)

    def far_opposite(self):
        self.opposite(1 - self.place.zhi, 10)

    def finish(self):
        self.local.wait()
        for k in (5, 6, 7, 8, 9, 15, 16, 17, 18):
            self.copies[k].wait_recv()

    def drain(self):
        for k in self.copies:
            self.copies[k].wait_send()


def head_mask(which):
    lane = lax.broadcasted_iota(jnp.int32, (1, 128), 1)
    return jnp.where((lane // 64) == which, 1.0, 0.0).astype(BF16)


def to_slots(slot_row, head, count):
    row = slot_row[pl.ds(head, 1), :]
    iota = lax.broadcasted_iota(jnp.int32, (count, count), 0).astype(F32)
    return jnp.where(iota == row, 1.0, 0.0).astype(BF16)


def to_tokens(slot_col, head, count):
    lane = lax.broadcasted_iota(jnp.int32, slot_col.shape, 1)
    column = jnp.sum(jnp.where(lane == head, slot_col[...], 0.0), axis=1, keepdims=True)
    iota = lax.broadcasted_iota(jnp.int32, (count, count), 1).astype(F32)
    return jnp.where(iota == column, 1.0, 0.0).astype(BF16)


def pair_select(first, second):
    lane = lax.broadcasted_iota(jnp.int32, first.shape, 1)
    return jnp.where((lane // 64) % 2 == 0, first, second)


def heads_home(turned):
    return jnp.concatenate([turned[0:64, 0:128], turned[64:128, 128:256]], axis=0).T


def make_slots(clusters, segments, counted, slot_row, slot_col, labels):
    heads, count = clusters.shape
    groups = lax.shift_right_logical(clusters[...], 2)
    iota = lax.broadcasted_iota(jnp.int32, (32, count), 0)
    before = lax.broadcasted_iota(jnp.int32, (count, count), 0)
    after = lax.broadcasted_iota(jnp.int32, (count, count), 1)
    upper = jnp.where(before <= after, 1.0, 0.0).astype(BF16)
    hot = [jnp.where(groups[h : h + 1, :] == iota, 1.0, 0.0) for h in range(heads)]
    counts = matmul(jnp.concatenate(hot, axis=0).astype(BF16), upper)
    group_f = groups.astype(F32)
    rows = []
    for h in range(heads):
        rank = jnp.sum(counts[32 * h : 32 * h + 32] * hot[h], axis=0, keepdims=True)
        rows.append(group_f[h : h + 1] * 16.0 + rank - 1.0)
    slots = jnp.concatenate(rows + [counted[...].astype(F32), jnp.zeros((127 - heads, count), F32)], axis=0)
    slot_row[...] = slots[:16]
    slot_col[...] = slots.T
    label = (segments[0:1, :] * 4 + (clusters[...] & 3)).astype(F32)
    labels[...] = jnp.concatenate([label, jnp.zeros((128 - heads, count), F32)], axis=0).T.astype(BF16)


def rows16(j):
    return slice(16 * j, 16 * j + 16)


def forward_kernel(
    x, clusters, segments, counted, norms, wq, wo, wu, wd,
    mixed, x_turned, fq_out, fo, fu, fd, got_out, before_out, after_out, logsum, hot_out, cold_out, slot_row, slot_col, total,
    pieces, fq, got, before, after, hot, cold,
    labels, sent_labels, got_labels, before_labels, after_labels, wide_labels, sent, out, back,
    tile, slots,
    w_send, w_recv, w_local, t_send, t_recv, a_send, a_recv, a_local, z_send, z_recv, b_send, b_recv, b_local, k_sem,
):
    place = Place()
    plane, rank = place.plane(), place.rank()
    up, down = place.z_peer(1), place.z_peer(-1)
    kept = []

    def keep(source, target):
        copy = pltpu.make_async_copy(source, target, k_sem.at[len(kept)])
        copy.start()
        kept.append(copy)

    partners = place.doubling()
    for g in range(3):
        for b in range(2):
            for t in range(3):
                lane = t * 768 + (2 * g + b) * 128
                pieces[g, :, b * 384 + t * 128 : b * 384 + t * 128 + 128] = wq[:, lane : lane + 128]
    greet(
        plane + [place.x_peer(1), place.x_peer(2), place.x_peer(3), place.z_far(), up, down, partners[6], partners[7]]
    )
    weights = [
        Gather(place, shard, full, w_send.at[i], w_recv.at[i], w_local.at[i])
        for i, (shard, full) in enumerate(
            [(pieces.at[g], fq.at[g]) for g in range(3)] + [(wo, fo), (wu, fu), (wd, fd)]
        )
    ]
    first, second, third, w_out, w_up, w_down = weights
    rest = (w_out, w_up, w_down)
    tile[0] = jnp.zeros_like(tile[0])
    tile[0, 0:4, 0 : norms.shape[1]] = norms[...].astype(F32)
    tile[0] = pltpu.roll(tile[0], place.wsh * norms.shape[1], 1)
    lane_zero = lax.broadcasted_iota(jnp.int32, (1, tile.shape[2]), 1) == 0
    tile[0, 4:5, :] = jnp.where(lane_zero, jnp.sum(counted[...].astype(F32), axis=1, keepdims=True), 0.0)
    doubling = Doubling(place, tile, slots, t_send, t_recv)
    doubling.start()
    first.start_z()
    first.start_x()
    count = x.shape[0]
    make_slots(clusters, segments, counted, slot_row, slot_col, labels)

    second.start_z()
    second.start_x()
    sent_labels[...] = jnp.zeros_like(sent_labels)

    def move_labels(head, carry):
        lane = lax.broadcasted_iota(jnp.int32, (count, 128), 1)
        moved = matmul(to_slots(slot_row, head, count), labels[...])
        sent_labels[...] = jnp.where(lane == head, moved, sent_labels[...])
        return carry

    lax.fori_loop(0, 6, move_labels, 0)
    first.near()
    third.start_z()
    third.start_x()
    lax.fori_loop(6, 12, move_labels, 0)
    labels[...] = sent_labels[...].astype(BF16)

    def block(which):
        return pl.ds(pl.multiple_of(which * 64, 64), 64)

    def ranks():
        return [dev[0] % 8 for dev in plane]

    label_copies = [
        remote(labels.at[block(to)], got_labels.at[rank], a_send.at[6, k], a_recv.at[6, k], plane[k])
        for k, to in enumerate(ranks())
    ]
    for copy in label_copies:
        copy.start()
    own_labels = pltpu.make_async_copy(labels.at[block(rank)], got_labels.at[rank], a_local.at[6])
    own_labels.start()
    first.from_z()
    second.near()
    first.near_opposite()
    doubling.advance()
    x_turned[...] = x[...].astype(F32).T.astype(BF16)
    doubling.advance()
    second.from_z()
    first.far()
    third.near()
    second.near_opposite()
    doubling.advance()
    third.from_z()
    own_labels.wait()
    for copy in label_copies:
        copy.wait_recv()
    label_up = remote(got_labels.at[4:8], before_labels, z_send.at[6, 0], z_recv.at[6, 0], up)
    label_down = remote(got_labels.at[0:4], after_labels, z_send.at[6, 1], z_recv.at[6, 1], down)
    label_up.start()
    label_down.start()
    for w in rest:
        w.start_z()
    first.far_opposite()
    first.finish()

    def make_hot(head, carry):
        lane = lax.broadcasted_iota(jnp.int32, (256, 128), 1)
        for j in range(4):
            column = jnp.sum(jnp.where(lane == head, wide_labels[j], 0.0), axis=1, keepdims=True)
            same = lane.astype(F32) == column
            cold[head * 4 + j] = jnp.where(same, 0.0, NEG).astype(BF16)
            hot[head * 4 + j] = jnp.where(same, 1.0, 0.0)[64:192].astype(BF16)
        return carry

    def send_copies(p, fn):
        for k, to in enumerate(ranks()):
            fn(remote(sent.at[p, block(to)], got.at[p, rank], a_send.at[p, k], a_recv.at[p, k], plane[k]))

    def own_copy(p):
        return pltpu.make_async_copy(sent.at[p, block(rank)], got.at[p, rank], a_local.at[p])

    def project(g):
        value = matmul(x[...], fq[g].reshape(768, 768))
        lane = lax.broadcasted_iota(jnp.int32, (1, 384), 1)
        scale = jnp.where(lane < 128, 0.125, 1.0)
        for b in range(2):
            p = 2 * g + b
            rows = (value[:, b * 384 : b * 384 + 384] * scale).astype(BF16)
            moved = [matmul(to_slots(slot_row, 2 * p + a, count), rows) for a in range(2)]
            sent[p] = pair_select(moved[0], moved[1]).astype(BF16)
            send_copies(p, lambda copy: copy.start())
            own_copy(p).start()

    project(0)
    second.far()
    third.near_opposite()
    third.far()
    second.far_opposite()
    second.finish()
    doubling.advance()
    for w in rest:
        w.start_x()
    project(1)
    third.far_opposite()
    third.finish()
    project(2)
    keep(fq, fq_out)
    label_up.wait_recv()
    label_down.wait_recv()
    for j in range(4):
        wide_labels[j, 0:64] = jnp.where(
            place.zlo == 0, -1.0, before_labels[:, rows16(j), :].reshape(64, 128).astype(F32)
        )
        wide_labels[j, 64:192] = got_labels[:, rows16(j), :].reshape(128, 128).astype(F32)
        wide_labels[j, 192:256] = jnp.where(
            place.zlo == 3, -1.0, after_labels[:, rows16(j), :].reshape(64, 128).astype(F32)
        )
    lax.fori_loop(0, 12, make_hot, 0)
    keep(hot, hot_out)
    keep(cold, cold_out)
    w_out.near()
    w_out.from_z()
    w_up.near()
    doubling.advance()

    def halo(p):
        return (
            remote(got.at[p, 4:8, :, 128:384], before.at[p], z_send.at[p, 0], z_recv.at[p, 0], up),
            remote(got.at[p, 0:4, :, 128:384], after.at[p], z_send.at[p, 1], z_recv.at[p, 1], down),
        )

    def back_copies(p, fn):
        for k, to in enumerate(ranks()):
            fn(remote(out.at[p, to], back.at[p, rank], b_send.at[p, k], b_recv.at[p, k], plane[k]))

    def own_back(p):
        return pltpu.make_async_copy(out.at[p, rank], back.at[p, rank], b_local.at[p])

    def arrive(p):
        own_copy(p).wait()
        send_copies(p, lambda copy: copy.wait_recv())
        for copy in halo(p):
            copy.start()

    masks = [head_mask(a) for a in range(2)]

    def attend(p):
        for copy in halo(p):
            copy.wait_recv()
        for j in range(4):
            r = rows16(j)
            query = got[p, :, r, 0:128].reshape(128, 128)
            keys = jnp.concatenate(
                [before[p, :, r, 0:128].reshape(64, 128), got[p, :, r, 128:256].reshape(128, 128),
                 after[p, :, r, 0:128].reshape(64, 128)], axis=0)
            values = jnp.concatenate(
                [before[p, :, r, 128:256].reshape(64, 128), got[p, :, r, 256:384].reshape(128, 128),
                 after[p, :, r, 128:256].reshape(64, 128)], axis=0)
            probs = []
            for a in range(2):
                head = 2 * p + a
                scores = matmul(
                    jnp.concatenate([keys, cold[head * 4 + j]], axis=1),
                    jnp.concatenate([query * masks[a], hot[head * 4 + j]], axis=1), NT)
                top = jnp.max(scores, axis=0, keepdims=True)
                raised = jnp.exp(scores - top)
                sums = jnp.sum(raised, axis=0, keepdims=True)
                probs.append((raised * (1.0 / sums)).astype(BF16))
                logsum[j, pl.ds(head, 1), :] = top + jnp.log(sums)
            out[p, :, r, :] = heads_home(matmul(values, jnp.concatenate(probs, axis=1), TN)).astype(BF16).reshape(8, 16, 128)
        back_copies(p, lambda copy: copy.start())
        own_back(p).start()

    def home(p):
        own_back(p).wait()
        back_copies(p, lambda copy: copy.wait_recv())
        rows = back[p].reshape(count, 128)
        moved = [matmul(to_tokens(slot_col, 2 * p + a, count), rows) for a in range(2)]
        mixed[:, p * 128 : p * 128 + 128] = pair_select(moved[0], moved[1]).astype(BF16)

    arrive(0)
    w_up.from_z()
    arrive(1)
    attend(0)
    w_down.near()
    w_out.near_opposite()
    arrive(2)
    attend(1)
    w_down.from_z()
    w_up.near_opposite()
    doubling.advance()
    arrive(3)
    attend(2)
    home(0)
    w_out.far()
    arrive(4)
    attend(3)
    home(1)
    w_up.far()
    w_down.near_opposite()
    arrive(5)
    attend(4)
    home(2)
    home(3)
    doubling.advance()

    def settle_out(p, carry):
        send_copies(p, lambda copy: copy.wait_send())
        return carry

    def settle_back(p, carry):
        back_copies(p, lambda copy: copy.wait_send())
        for copy in halo(p):
            copy.wait_send()
        return carry

    lax.fori_loop(0, 6, settle_out, 0)
    for copy in label_copies + [label_up, label_down]:
        copy.wait_send()
    for w in (first, second, third):
        w.drain()
    w_down.far()
    attend(5)
    keep(got, got_out)
    keep(before, before_out)
    keep(after, after_out)
    w_out.far_opposite()
    w_up.far_opposite()
    home(4)
    lax.fori_loop(0, 5, settle_back, 0)
    w_down.far_opposite()
    home(5)
    doubling.advance()
    for w in rest:
        w.finish()
    total[...] = tile[8]
    settle_back(5, 0)
    for w in rest:
        w.drain()
    for copy in kept:
        copy.wait()
    doubling.drain()


ANY = pl.BlockSpec(memory_space=pl.ANY)
VMEM = pl.BlockSpec(memory_space=pltpu.VMEM)


def shaped(*shape, dtype=BF16):
    return jax.ShapeDtypeStruct(shape, dtype)


def forward(x, clusters, segments, counted, norms, shards):
    count, width = x.shape
    dma = pltpu.SemaphoreType.DMA
    return pl.pallas_call(
        forward_kernel,
        out_shape=[
            shaped(*x.shape),
            shaped(width, count),
            shaped(3, 8, shards[0].shape[0], 768),
            *[shaped(8, *w.shape) for w in shards[1:]],
            shaped(6, 8, 64, 384),
            shaped(6, 4, 64, 256),
            shaped(6, 4, 64, 256),
            shaped(4, 16, 128, dtype=F32),
            shaped(48, 128, 128),
            shaped(48, 256, 128),
            shaped(16, count, dtype=F32),
            shaped(count, 128, dtype=F32),
            shaped(8, width, dtype=F32),
        ],
        in_specs=[VMEM] * 9,
        out_specs=[VMEM] * 2 + [ANY] * 7 + [VMEM] + [ANY] * 2 + [VMEM] * 3,
        scratch_shapes=[
            pltpu.VMEM((3, shards[0].shape[0], 768), BF16),
            pltpu.VMEM((3, 8, shards[0].shape[0], 768), BF16),
            pltpu.VMEM((6, 8, 64, 384), BF16),
            pltpu.VMEM((6, 4, 64, 256), BF16),
            pltpu.VMEM((6, 4, 64, 256), BF16),
            pltpu.VMEM((48, 128, 128), BF16),
            pltpu.VMEM((48, 256, 128), BF16),
            pltpu.VMEM((count, 128), BF16),
            pltpu.VMEM((count, 128), F32),
            pltpu.VMEM((8, 64, 128), BF16),
            pltpu.VMEM((4, 64, 128), BF16),
            pltpu.VMEM((4, 64, 128), BF16),
            pltpu.VMEM((4, 256, 128), F32),
            pltpu.VMEM((6, count, 384), BF16),
            pltpu.VMEM((6, 8, 64, 128), BF16),
            pltpu.VMEM((6, 8, 64, 128), BF16),
            pltpu.VMEM((9, 8, width), F32),
            pltpu.VMEM((8, 8, width), F32),
            dma((6, 19)), dma((6, 19)), dma((6,)), dma((8,)), dma((8,)),
            dma((7, 7)), dma((7, 7)), dma((7,)), dma((7, 2)), dma((7, 2)),
            dma((6, 7)), dma((6, 7)), dma((6,)), dma((6,)),
        ],
        compiler_params=pltpu.CompilerParams(
            collective_id=0, has_side_effects=True, vmem_limit_bytes=60 * 2**20
        ),
        name="forward_attention",
    )(x, clusters, segments, counted, norms, *shards)


class Reduce:
    def __init__(self, place, held, near, far, sum_x, from_y, sum_y, from_z, out, send_sems, recv_sems, grad=None, source=None, load_sem=None):
        self.place, self.held, self.grad = place, held, grad
        self.near, self.far, self.sum_x, self.from_y = near, far, sum_x, from_y
        self.sum_y, self.from_z, self.out = sum_y, from_z, out
        self.send_sems, self.recv_sems = send_sems, recv_sems
        self.rows, self.half = held.shape[2], held.shape[3]
        self.window = out.shape[1]
        self.owner = place.y // 2
        self.z = place.zhi * 4 + place.zlo
        self.final = jnp.logical_and(place.zhi == self.owner, place.core == place.zlo // 2)
        self.copies = {}
        if source is not None:
            self.load = pltpu.make_async_copy(source, held, load_sem)

    def send(self, k, source, target, device):
        copy = remote(source, target, self.send_sems.at[k], self.recv_sems.at[k], device)
        copy.start()
        self.copies[k] = copy

    def each(self, count, body):
        def step(i, carry):
            body(pl.ds(pl.multiple_of(i * 48, 16), 48))
            return carry

        lax.fori_loop(0, count // 48, step, 0)

    def after(self, rows, offset):
        return pl.ds(pl.multiple_of(rows.start + offset, 16), rows.size)

    def blocks(self, body):
        def step(zh, carry):
            body(zh)
            return carry

        lax.fori_loop(0, 2, step, 0)

    def start(self):
        place = self.place
        self.send(0, self.grad.at[:, :, :, half_of(2 * self.half, 1 - place.core)], self.held, place.sibling())

    def add_pair(self, xx):
        mine = half_of(2 * self.half, self.place.core)

        def block(zh):
            def body(rows):
                self.held[zh, xx, rows, :] = (
                    self.grad[zh, xx, rows, mine].astype(F32) + self.held[zh, xx, rows, :].astype(F32)
                ).astype(BF16)

            self.each(self.rows, body)

        self.blocks(block)

    def to_opposite(self):
        place = self.place
        half = self.rows // 2
        opposite = (place.x + 2) % 4
        if self.grad is None:
            self.load.wait()
        else:
            self.copies[0].wait_recv()
            self.add_pair(opposite)
        self.send(1, self.held.at[:, opposite, 0:half], self.near.at[0], place.x_peer(1))
        self.send(2, self.held.at[:, opposite, half : self.rows], self.near.at[1], place.x_peer(3))
        if self.grad is not None:
            for step in (1, 3, 0):
                self.add_pair((place.x + step) % 4)

    def to_near(self):
        place = self.place
        half = self.rows // 2
        for k, step in enumerate((1, 3)):
            to = (place.x + step) % 4
            self.copies[1 + k].wait_recv()

            def block(zh, k=k, to=to):
                def body(rows):
                    there = self.after(rows, k * half)
                    self.held[zh, to, there, :] = (
                        self.held[zh, to, there, :].astype(F32) + self.near[k, zh, rows, :].astype(F32)
                    ).astype(BF16)

                self.each(half, body)

            self.blocks(block)
            self.send(3 + k, self.held.at[:, to], self.far.at[k], place.x_peer(step))

    def to_y(self):
        place = self.place
        half = self.rows // 2
        for k in range(2):
            self.copies[3 + k].wait_recv()

        def block(zh):
            def body(rows):
                value = self.held[zh, place.x, rows, :].astype(F32)
                value = value + self.far[0, zh, rows, :].astype(F32) + self.far[1, zh, rows, :].astype(F32)
                self.sum_x[zh, rows, :] = value.astype(BF16)

            self.each(self.rows, body)

        self.blocks(block)
        for k, d in enumerate((1, 2, 3)):
            to = (place.y + d) % 4
            part = pl.ds(pl.multiple_of((to % 2) * half, 16), half)
            self.send(5 + k, self.sum_x.at[to // 2, part], self.from_y.at[k], place.y_peer(d))

    def lanes(self, zlo):
        offset = (zlo % 2) * (self.half - self.window)
        return pl.ds(pl.multiple_of(offset, 128), self.window)

    def z_copy(self, k):
        place = self.place
        zlo = 2 * place.core + k
        return remote(
            self.sum_y.at[:, self.lanes(zlo)], self.from_z.at[self.z],
            self.send_sems.at[8 + k], self.recv_sems.at[8 + self.z], place.at(zlo=zlo, zhi=self.owner),
        )

    def is_target(self, k):
        place = self.place
        return jnp.logical_and(place.zhi == self.owner, place.zlo == 2 * place.core + k)

    def to_z(self):
        place = self.place
        half = self.rows // 2
        for k in range(3):
            self.copies[5 + k].wait_recv()

        def body(rows):
            value = self.sum_x[self.owner, self.after(rows, (place.y % 2) * half), :].astype(F32)
            for k in range(3):
                value = value + self.from_y[k, rows, :].astype(F32)
            self.sum_y[rows, :] = value.astype(BF16)

        self.each(half, body)
        for k in range(2):
            @pl.when(jnp.logical_not(self.is_target(k)))
            def _(k=k):
                self.z_copy(k).start()

    def spread_copy(self, k, device):
        half = self.rows // 2
        part = self.out.at[pl.ds(pl.multiple_of((self.place.y % 2) * half, 16), half)]
        return remote(part, part, self.send_sems.at[10 + k], self.recv_sems.at[16 + self.place.y % 2], device)

    def spread(self):
        half = self.rows // 2

        @pl.when(self.final)
        def _():
            self.from_z[self.z] = self.sum_y[:, self.lanes(self.place.zlo)]
            for z in range(8):
                @pl.when(self.z != z)
                def _(z=z):
                    part = self.from_z.at[z]
                    remote(part, part, self.send_sems.at[8], self.recv_sems.at[8 + z], self.place.sibling()).wait_recv()

            def body(rows):
                there = self.after(rows, (self.place.y % 2) * half)
                value = self.from_z[0, rows, :].astype(F32)
                for z in range(1, 8):
                    value = value + self.from_z[z, rows, :].astype(F32)
                self.out[there, :] = value.astype(BF16)

            self.each(half, body)
            for k, device in enumerate(self.place.plane()):
                self.spread_copy(k, device).start()

    def finish(self):
        half = self.rows // 2
        for k in range(2):
            part = self.out.at[k * half : (k + 1) * half]

            @pl.when(jnp.logical_not(jnp.logical_and(self.final, self.place.y % 2 == k)))
            def _(k=k, part=part):
                remote(part, part, self.send_sems.at[10], self.recv_sems.at[16 + k], self.place.sibling()).wait_recv()

    def drain(self):
        for k in self.copies:
            self.copies[k].wait_send()
        for k in range(2):
            @pl.when(jnp.logical_not(self.is_target(k)))
            def _(k=k):
                self.z_copy(k).wait_send()

        @pl.when(self.final)
        def _():
            for k, device in enumerate(self.place.plane()):
                self.spread_copy(k, device).wait_send()


def reduce_scratch(rows, half, window):
    return [
        pltpu.VMEM((2, 4, rows, half), BF16),
        pltpu.VMEM((2, 2, rows // 2, half), BF16),
        pltpu.VMEM((2, 2, rows, half), BF16),
        pltpu.VMEM((2, rows, half), BF16),
        pltpu.VMEM((3, rows // 2, half), BF16),
        pltpu.VMEM((rows // 2, half), BF16),
        pltpu.VMEM((8, rows // 2, window), BF16),
        pltpu.VMEM((rows, window), BF16),
    ]


def cut(value, offset, target):
    rows, width = value.shape
    first = pltpu.roll(value, (width - offset) % width, 1)[:, 0:128]
    if target.shape[0] == rows:
        target[...] = first[:, : target.shape[1]]
        return
    if rows % 128:
        first = jnp.concatenate([first, jnp.zeros((128 - rows % 128, 128), F32)], axis=0)
    target[...] = first.T[: target.shape[0], :rows]


ORDER = (0, 3, 1, 4, 2, 5)


def backward_kernel(*refs):
    (grad_mixed, grad_first, logsum, slot_row, slot_col, small, x_hbm, fq_hbm, got_hbm, before_hbm, after_hbm,
     hot_hbm, cold_hbm, go, gu, gd) = refs[:16]
    grad_x, out_q, out_o, out_u, out_d, norms_out, loss_out = refs[16:23]
    x_turned, fq, got, before, after, hot, cold = refs[23:30]
    sent, got_grad, grads, to_before, to_after, from_before, from_after, back = refs[30:38]
    grads_q = refs[38:41]
    reduce_refs = [refs[41 + 8 * i : 49 + 8 * i] for i in range(6)]
    (tile, slots, a_send, a_recv, a_local, z_send, z_recv, b_send, b_recv, b_local,
     t_send, t_recv, r_send, r_recv, r_load, l_sem) = refs[89:]
    place = Place()
    plane, rank = place.plane(), place.rank()
    up, down = place.z_peer(1), place.z_peer(-1)
    loads = [
        pltpu.make_async_copy(source, target, l_sem.at[i])
        for i, (source, target) in enumerate(
            ((got_hbm, got), (before_hbm, before), (after_hbm, after), (hot_hbm, hot), (cold_hbm, cold),
             (fq_hbm, fq), (x_hbm, x_turned))
        )
    ]
    rest = [
        Reduce(place, *reduce_refs[i], r_send.at[i], r_recv.at[i], source=source, load_sem=r_load.at[i])
        for i, source in enumerate((go, gu, gd))
    ]
    by_group = [
        Reduce(place, *reduce_refs[3 + i], r_send.at[3 + i], r_recv.at[3 + i], grad=grads_q[i]) for i in range(3)
    ]
    for r in rest:
        r.load.start()
    for copy in loads:
        copy.start()
    greet(plane + [place.x_peer(d) for d in (1, 2, 3)] + [place.z_peer(d) for d in range(1, 8)])
    sum_o, sum_u, sum_d = rest
    for r in (sum_d, sum_u, sum_o):
        r.to_opposite()
    tile[0] = small[...]
    doubling = Doubling(place, tile, slots, t_send, t_recv)
    doubling.start()
    count = grad_mixed.shape[0]
    ranks = [dev[0] % 8 for dev in plane]

    def block(which):
        return pl.ds(pl.multiple_of(which * 64, 64), 64)

    def send_copies(p, fn):
        for k, to in enumerate(ranks):
            fn(remote(sent.at[p, block(to)], got_grad.at[p, rank], a_send.at[p, k], a_recv.at[p, k], plane[k]))

    def own_copy(p):
        return pltpu.make_async_copy(sent.at[p, block(rank)], got_grad.at[p, rank], a_local.at[p])

    def leave(i, carry):
        p = i // 2 + 3 * (i % 2)
        rows = grad_mixed[:, pl.ds(pl.multiple_of(p * 128, 128), 128)]
        moved = [matmul(to_slots(slot_row, 2 * p + a, count), rows) for a in range(2)]
        sent[p] = pair_select(moved[0], moved[1]).astype(BF16)
        send_copies(p, lambda copy: copy.start())
        own_copy(p).start()
        return carry

    lax.fori_loop(0, 6, leave, 0)
    for copy in loads[:5]:
        copy.wait()

    def halo(p):
        return (
            remote(to_after.at[p], from_before.at[p], z_send.at[p, 0], z_recv.at[p, 0], up),
            remote(to_before.at[p], from_after.at[p], z_send.at[p, 1], z_recv.at[p, 1], down),
        )

    def back_copies(p, fn):
        for k, to in enumerate(ranks):
            fn(remote(grads.at[p, to], back.at[p, rank], b_send.at[p, k], b_recv.at[p, k], plane[k]))

    def own_back(p):
        return pltpu.make_async_copy(grads.at[p, rank], back.at[p, rank], b_local.at[p])

    masks = [head_mask(a) for a in range(2)]

    def attend(p):
        own_copy(p).wait()
        send_copies(p, lambda copy: copy.wait_recv())
        for j in range(4):
            r = rows16(j)
            query = got[p, :, r, 0:128].reshape(128, 128)
            keys = jnp.concatenate(
                [before[p, :, r, 0:128].reshape(64, 128), got[p, :, r, 128:256].reshape(128, 128),
                 after[p, :, r, 0:128].reshape(64, 128)], axis=0)
            values = jnp.concatenate(
                [before[p, :, r, 128:256].reshape(64, 128), got[p, :, r, 256:384].reshape(128, 128),
                 after[p, :, r, 128:256].reshape(64, 128)], axis=0)
            grad = got_grad[p, :, r, :].reshape(128, 128)
            queries = [query * masks[a] for a in range(2)]
            grad_both = jnp.concatenate([grad * masks[a] for a in range(2)], axis=0)
            grad_probs = matmul(values, grad_both, NT)
            probs, grad_scores = [], []
            for a in range(2):
                head = 2 * p + a
                scores = matmul(
                    jnp.concatenate([keys, cold[head * 4 + j]], axis=1),
                    jnp.concatenate([queries[a], hot[head * 4 + j]], axis=1), NT)
                prob = jnp.exp(scores - logsum[j, pl.ds(head, 1), :])
                own = grad_probs[:, a * 128 : a * 128 + 128]
                delta = jnp.sum(prob * own, axis=0, keepdims=True)
                probs.append(prob.astype(BF16))
                grad_scores.append((prob * (own - delta)).astype(BF16))
            grad_scores = jnp.concatenate(grad_scores, axis=1)
            dk = matmul(grad_scores, jnp.concatenate(queries, axis=0))
            dv = matmul(jnp.concatenate(probs, axis=1), grad_both)
            dq = heads_home(matmul(keys, grad_scores, TN)) * 0.125
            both = jnp.concatenate([dk, dv], axis=1).astype(BF16)
            to_before[p, :, r, :] = both[0:64].reshape(4, 16, 256)
            to_after[p, :, r, :] = both[192:256].reshape(4, 16, 256)
            grads[p, :, r, 0:128] = dq.astype(BF16).reshape(8, 16, 128)
            grads[p, :, r, 128:384] = both[64:192].reshape(8, 16, 256)
        for copy in halo(p):
            copy.start()

    def give(p):
        for copy in halo(p):
            copy.wait_recv()
        for part, extra in ((slice(0, 4), from_before), (slice(4, 8), from_after)):
            grads[p, part, :, 128:384] = (
                grads[p, part, :, 128:384].astype(F32) + extra[p].astype(F32)
            ).astype(BF16)
        back_copies(p, lambda copy: copy.start())
        own_back(p).start()

    def home(p):
        own_back(p).wait()
        back_copies(p, lambda copy: copy.wait_recv())
        rows = back[p].reshape(count, 384)
        moved = [matmul(to_tokens(slot_col, 2 * p + a, count), rows) for a in range(2)]
        grad_qkv = pair_select(moved[0], moved[1]).astype(BF16)
        back[p] = grad_qkv.reshape(8, 64, 384)
        weight = matmul(x_turned[...], grad_qkv).astype(BF16)
        group, late = p % 3, p // 3
        for t, lane in enumerate((late, 2 + late, 4 + late)):
            grads_q[group][:, :, :, lane * 128 : lane * 128 + 128] = weight[:, t * 128 : t * 128 + 128].reshape(2, 4, 96, 128)

    def turn_back(i):
        rows = slice(i * 128, i * 128 + 128)
        value = grad_first[rows, :]
        for g in range(3):
            pair = [back[2 * g + b, 2 * i : 2 * i + 2].reshape(128, 384) for b in range(2)]
            value = value + matmul(jnp.concatenate(pair, axis=1), fq[g].reshape(768, 768), NT)
        grad_x[rows, :] = value

    attend(0)
    doubling.advance()
    attend(3)
    sum_d.to_near()
    attend(1)
    give(0)
    give(3)
    sum_u.to_near()
    sum_o.to_near()
    attend(4)
    give(1)
    doubling.advance()
    attend(2)
    give(4)
    attend(5)
    give(2)
    sum_d.to_y()
    give(5)
    for copy in loads[5:]:
        copy.wait()
    home(0)
    doubling.advance()
    home(3)
    by_group[0].start()
    sum_u.to_y()
    sum_d.to_z()
    home(1)
    by_group[0].to_opposite()
    home(4)
    by_group[1].start()
    sum_o.to_y()
    by_group[0].to_near()
    doubling.advance()
    home(2)
    by_group[1].to_opposite()
    sum_u.to_z()
    home(5)
    by_group[2].start()
    by_group[0].to_y()
    by_group[1].to_near()
    doubling.advance()
    by_group[2].to_opposite()
    sum_o.to_z()
    turn_back(0)
    by_group[1].to_y()
    by_group[0].to_z()
    by_group[2].to_near()
    doubling.advance()
    sum_d.spread()
    turn_back(1)
    by_group[1].to_z()
    by_group[2].to_y()
    doubling.advance()
    sum_u.spread()
    sum_o.spread()
    by_group[0].spread()
    turn_back(2)
    by_group[2].to_z()
    doubling.advance()
    by_group[1].spread()

    def settle(p, carry):
        send_copies(p, lambda copy: copy.wait_send())
        back_copies(p, lambda copy: copy.wait_send())
        for copy in halo(p):
            copy.wait_send()
        return carry

    lax.fori_loop(0, 6, settle, 0)
    seat = place.y * 2 + place.core
    for r, target in zip((sum_d, sum_u, sum_o), (out_d, out_u, out_o)):
        r.finish()
        width = r.half // 16
        offset = (place.zlo % 2) * (8 * width - (r.half - r.window)) + seat * width
        cut(r.out[...].astype(F32), offset, target)
    turn_back(3)
    by_group[2].spread()
    total = tile[8]
    loss_out[...] = total[4:5, 0:1]
    all_width = total.shape[1]
    shift = (all_width - (place.ctx * 8 + place.wsh) * norms_out.shape[1]) % all_width
    norms_out[...] = pltpu.roll(total, shift, 1)[0:4, 0 : norms_out.shape[1]]
    for r in rest:
        r.drain()
    for r in by_group:
        r.finish()
    tiles = [by_group[g].out[:, i * 128 : i * 128 + 128].astype(F32) for i in range(3) for g in range(3)]
    width = 72
    cut(jnp.concatenate(tiles, axis=1), (place.zlo % 2) * 8 * width + seat * width, out_q)
    for r in by_group:
        r.drain()
    doubling.drain()


def backward(grad_mixed, grad_first, small, x_turned, fq, kept, halves):
    got, before, after, logsum, hot, cold, slot_row, slot_col = kept
    count = grad_mixed.shape[0]
    dma = pltpu.SemaphoreType.DMA
    vm = pltpu.VMEM
    rows_in = (halves[2].shape[2],)
    shapes = [(96, 384, 256), (96, 1536, 768), (rows_in[0], 384, 256)] + [(96, 384, 384)] * 3
    reduce_refs = []
    for shape in shapes:
        reduce_refs += reduce_scratch(*shape)
    loaded = (x_turned, fq, got, before, after, hot, cold)
    results = pl.pallas_call(
        backward_kernel,
        out_shape=[
            shaped(*grad_first.shape, dtype=F32),
            shaped(72, 96, dtype=F32),
            shaped(24, 96, dtype=F32),
            shaped(96, 96, dtype=F32),
            shaped(24, 384, dtype=F32),
            shaped(4, small.shape[1] // 256, dtype=F32),
            shaped(1, 1, dtype=F32),
        ],
        in_specs=[VMEM] * 6 + [ANY] * 10,
        out_specs=[VMEM] * 7,
        scratch_shapes=[vm(array.shape, array.dtype) for array in loaded]
        + [
            vm((6, count, 128), BF16),
            vm((6, 8, 64, 128), BF16),
            vm((6, 8, 64, 384), BF16),
            vm((6, 4, 64, 256), BF16),
            vm((6, 4, 64, 256), BF16),
            vm((6, 4, 64, 256), BF16),
            vm((6, 4, 64, 256), BF16),
            vm((6, 8, 64, 384), BF16),
        ]
        + [vm((2, 4, 96, 768), BF16)] * 3
        + reduce_refs
        + [
            vm((9, *small.shape), F32),
            vm((8, *small.shape), F32),
            dma((6, 7)), dma((6, 7)), dma((6,)), dma((6, 2)), dma((6, 2)),
            dma((6, 7)), dma((6, 7)), dma((6,)),
            dma((8,)), dma((8,)), dma((6, 17)), dma((6, 18)), dma((3,)), dma((7,)),
        ],
        compiler_params=pltpu.CompilerParams(
            collective_id=1, has_side_effects=True, vmem_limit_bytes=62 * 2**20
        ),
        name="backward_attention",
    )(grad_mixed, grad_first, logsum, slot_row, slot_col, small, *loaded, *halves)
    return results


CHUNK = 512


def norm_rows(values):
    centered = values - jnp.mean(values, axis=-1, keepdims=True)
    scale = lax.rsqrt(jnp.mean(centered * centered, axis=-1, keepdims=True) + 1e-05)
    return centered * scale, scale


def norm_rows_back(grad, normed, scale, gain):
    weighted = grad * gain
    return scale * (
        weighted
        - jnp.mean(weighted, axis=-1, keepdims=True)
        - normed * jnp.mean(weighted * normed, axis=-1, keepdims=True)
    )


def middle_kernel(
    everyone, ctx_size,
    mixed, x, teacher, slot_col, total, wo_hbm, wu_hbm, wd_hbm,
    result, grad_first, grad_mixed, small, go_hbm, gu_hbm, gd_hbm,
    wo, wu, wd, active, slope, normed, unit, scale, low, low_turned, acc, branch, grad_upper, go, gu, gd,
    held_o, held_u, held_d, in_sem, out_sem, send_sem, recv_sem,
):
    place = Place()
    core, sibling = place.core, place.sibling()
    loads = [
        pltpu.make_async_copy(source, target, in_sem.at[i])
        for i, (source, target) in enumerate(((wo_hbm, wo), (wu_hbm, wu), (wd_hbm, wd)))
    ]
    for copy in loads:
        copy.start()
    greet([sibling])
    count, width = x.shape
    tile = 128
    chunks = wd.shape[0] // CHUNK
    gains = total[0:4] / ctx_size
    small[...] = jnp.zeros_like(small)

    def rows_of(i):
        return pl.ds(pl.multiple_of(i * tile, tile), tile)

    def lanes_of(c):
        return pl.ds(pl.multiple_of(c * CHUNK, CHUNK), CHUNK)

    loads[0].wait()
    for i in range(2):
        rows = slice(i * 256, i * 256 + 256)
        acc[rows, :] = matmul(mixed[rows, :], wo[...])

    def first_norm(i, carry):
        rows = rows_of(i)
        unit_rows, scale_rows = norm_rows(x[rows, :].astype(F32) + acc[rows, :])
        unit[rows, :] = unit_rows
        scale[rows, :] = scale_rows
        value = unit_rows * gains[0:1] + gains[1:2]
        normed[rows, :] = value
        low[rows, :] = value.astype(BF16)
        acc[rows, :] = value
        return carry

    lax.fori_loop(0, count // tile, first_norm, 0)
    loads[1].wait()
    loads[2].wait()

    def expand(c, carry):
        lanes = lanes_of(c)
        up = wu[:, :, lanes].reshape(width, CHUNK)
        down = wd[lanes, :]
        for i in range(2):
            rows = slice(i * 256, i * 256 + 256)
            upper = matmul(low[rows, :], up)
            share = 0.5 + 0.5 * lax.erf(upper * 0.7071067811865476)
            density = jnp.exp(upper * upper * -0.5) * 0.3989422804014327
            value = (upper * share).astype(BF16)
            active[rows, lanes] = value
            slope[rows, lanes] = share + upper * density
            acc[rows, :] += matmul(value, down)
        return carry

    lax.fori_loop(0, chunks, expand, 0)
    low_turned[...] = normed[...].T.astype(BF16)

    def second_norm(i, carry):
        rows = rows_of(i)
        unit_rows, scale_rows = norm_rows(acc[rows, :])
        value = unit_rows * gains[2:3] + gains[3:4]
        result[rows, :] = value.astype(BF16)
        error = value - teacher[rows, :].astype(F32)
        mask = slot_col[rows, 12:13]
        losses = mask * jnp.mean(error * error, axis=-1, keepdims=True)
        grad = (everyone / total[4:5, 0:1]) * mask * error
        small[2:3, :] += jnp.sum(grad * unit_rows, axis=0, keepdims=True)
        small[3:4, :] += jnp.sum(grad, axis=0, keepdims=True)
        small[4:5, 0:1] += jnp.sum(losses, axis=0, keepdims=True) / total[4:5, 0:1]
        back = norm_rows_back(grad, unit_rows, scale_rows, gains[2:3])
        acc[rows, :] = back
        branch[rows, :] = back.astype(BF16)
        return carry

    lax.fori_loop(0, count // tile, second_norm, 0)

    half = chunks // 2
    theirs, ours = half_of(width, 1 - core), half_of(width, core)

    def down_copy(c):
        lanes = lanes_of(c)
        return remote(gd.at[lanes, theirs], held_d.at[lanes], send_sem.at[c], recv_sem.at[c], sibling)

    def up_copy(i):
        return remote(gu.at[i], held_u.at[i], send_sem.at[chunks + i], recv_sem.at[chunks + i], sibling)

    def up_out(i):
        return pltpu.make_async_copy(held_u.at[i], gu_hbm.at[:, :, lanes_of(i)], out_sem.at[chunks + i])

    def contract(c):
        lanes = lanes_of(c)
        up = wu[:, :, lanes].reshape(width, CHUNK)
        down = wd[lanes, :]
        for i in range(2):
            rows = slice(i * 256, i * 256 + 256)
            value = (matmul(branch[rows, :], down, NT) * slope[rows, lanes]).astype(BF16)
            grad_upper[rows, :] = value
            acc[rows, :] += matmul(value, up, NT)
        gd[lanes, :] = matmul(active[:, lanes], branch[...], TN).astype(BF16)
        down_copy(c).start()
        return matmul(low_turned[...], grad_upper[...]).reshape(8, width // 8, CHUNK)

    def for_sibling(i, carry):
        gu[i] = contract((1 - core) * half + i).astype(BF16)
        up_copy(i).start()
        return carry

    def for_own(i, carry):
        value = contract(core * half + i)
        up_copy(i).wait_recv()
        held_u[i] = (value + held_u[i].astype(F32)).astype(BF16)
        up_out(i).start()
        return carry

    lax.fori_loop(0, half, for_sibling, 0)
    lax.fori_loop(0, half, for_own, 0)

    def first_back(i, carry):
        rows = rows_of(i)
        grad = acc[rows, :]
        small[0:1, :] += jnp.sum(grad * unit[rows, :], axis=0, keepdims=True)
        small[1:2, :] += jnp.sum(grad, axis=0, keepdims=True)
        back = norm_rows_back(grad, unit[rows, :], scale[rows, :], gains[0:1])
        grad_first[rows, :] = back
        branch[rows, :] = back.astype(BF16)
        return carry

    lax.fori_loop(0, count // tile, first_back, 0)
    go[...] = matmul(mixed[...], branch[...], TN).astype(BF16)
    last = remote(go.at[:, theirs], held_o, send_sem.at[chunks + half], recv_sem.at[chunks + half], sibling)
    last.start()
    for i in range(2):
        rows = slice(i * 256, i * 256 + 256)
        grad_mixed[rows, :] = matmul(branch[rows, :], wo[...], NT).astype(BF16)

    def down_out(c):
        lanes = lanes_of(c)
        return pltpu.make_async_copy(held_d.at[lanes], gd_hbm.at[lanes], out_sem.at[c])

    def add_down(c, carry):
        lanes = lanes_of(c)
        down_copy(c).wait_recv()
        held_d[lanes, :] = (gd[lanes, ours].astype(F32) + held_d[lanes, :].astype(F32)).astype(BF16)
        down_out(c).start()
        return carry

    lax.fori_loop(0, chunks, add_down, 0)
    last.wait_recv()
    held_o[...] = (go[:, ours].astype(F32) + held_o[...].astype(F32)).astype(BF16)
    out = pltpu.make_async_copy(held_o, go_hbm, in_sem.at[0])
    out.start()

    def settle_down(c, carry):
        down_copy(c).wait_send()
        down_out(c).wait()
        return carry

    def settle_up(i, carry):
        up_copy(i).wait_send()
        up_out(i).wait()
        return carry

    lax.fori_loop(0, chunks, settle_down, 0)
    lax.fori_loop(0, half, settle_up, 0)
    last.wait_send()
    out.wait()


def middle(everyone, ctx_size, mixed, x, teacher, slot_col, total, wo, wu, wd):
    count, width = x.shape
    hidden = wd.shape[0]
    chunks = hidden // CHUNK
    dma = pltpu.SemaphoreType.DMA
    vm = pltpu.VMEM
    return pl.pallas_call(
        functools.partial(middle_kernel, everyone, ctx_size),
        out_shape=[
            shaped(count, width),
            shaped(count, width, dtype=F32),
            shaped(count, width),
            shaped(8, width, dtype=F32),
            shaped(width, width // 2),
            shaped(8, width // 8, hidden // 2),
            shaped(hidden, width // 2),
        ],
        in_specs=[VMEM] * 5 + [ANY] * 3,
        out_specs=[VMEM] * 4 + [ANY] * 3,
        scratch_shapes=[
            vm(wo.shape, BF16), vm(wu.shape, BF16), vm(wd.shape, BF16),
            vm((count, hidden), BF16), vm((count, hidden), F32),
            vm((count, width), F32), vm((count, width), F32), vm((count, 1), F32),
            vm((count, width), BF16), vm((width, count), BF16), vm((count, width), F32),
            vm((count, width), BF16), vm((count, CHUNK), BF16),
            vm(wo.shape, BF16), vm((chunks // 2, 8, width // 8, CHUNK), BF16), vm(wd.shape, BF16),
            vm((width, width // 2), BF16), vm((chunks // 2, 8, width // 8, CHUNK), BF16), vm((hidden, width // 2), BF16),
            dma((3,)), dma((chunks + chunks // 2,)), dma((chunks + chunks // 2 + 1,)), dma((chunks + chunks // 2 + 1,)),
        ],
        compiler_params=pltpu.CompilerParams(
            collective_id=2, has_side_effects=True, vmem_limit_bytes=62 * 2**20
        ),
        name="dense_middle",
    )(mixed, x, teacher, slot_col, total, wo, wu, wd)


def local(tokens, teacher, clusters, segments, counted, w_qkv, w_out, w_up, w_down, norms):
    x_rows = tokens[0]
    tok_count, model_dim = x_rows.shape
    ctx_size, wsh_size = lax.axis_size("ctx"), lax.axis_size("wsh")
    mixed, x_turned, fq, fo, fu, fd, *kept, total = forward(
        x_rows, clusters[0], segments, counted, norms, (w_qkv, w_out, w_up, w_down)
    )
    everyone = float(tok_count * ctx_size * wsh_size)
    result, grad_first, grad_mixed, small, *grads = middle(
        everyone, float(ctx_size), mixed, x_rows, teacher[0], kept[-1], total,
        fo.reshape(-1, model_dim), fu, fd.reshape(-1, model_dim),
    )
    grad_tokens, final_qkv, final_out, final_up, final_down, final_norms, loss = backward(
        grad_mixed, grad_first, small, x_turned, fq, kept,
        [g.reshape(2, 4, -1, g.shape[-1]) for g in grads]
    )
    return (
        result[None],
        grad_tokens[None],
        loss.reshape(()),
        final_qkv.T,
        final_out.T,
        final_up,
        final_down.T,
        final_norms,
    )


def solution(mesh):
    placed = (
        P("wsh", "ctx", None),
        P("wsh", "ctx", None),
        P("wsh", None, "ctx"),
        P("wsh", "ctx"),
        P("wsh", "ctx"),
        P("wsh", None),
        P("wsh", None),
        P("wsh", None),
        P("wsh", None),
        P(None, "wsh"),
    )
    return jax.shard_map(
        local,
        mesh=mesh,
        in_specs=placed,
        out_specs=(
            P("wsh", "ctx", None),
            P("wsh", "ctx", None),
            P(),
            P("wsh", "ctx"),
            P("wsh", "ctx"),
            P("wsh", "ctx"),
            P("wsh", "ctx"),
            P(None, ("ctx", "wsh")),
        ),
        check_vma=False,
    )
```

```python
import functools
import jax
import jax.numpy as jnp
from jax import lax
from jax.experimental import pallas as pl
from jax.experimental.pallas import tpu as pltpu
from jax.sharding import PartitionSpec as P

MESH = pl.DeviceIdType.MESH
BF16 = jnp.bfloat16
F32 = jnp.float32


class Place:
    def __init__(self):
        self.ctx = lax.axis_index("ctx")
        self.wsh = lax.axis_index("wsh")
        self.zlo = self.ctx // 8
        self.y = (self.ctx // 2) % 4
        self.core = self.ctx % 2
        self.zhi = self.wsh // 4
        self.x = self.wsh % 4

    def at(self, zlo=None, y=None, core=None, zhi=None, x=None):
        zlo = self.zlo if zlo is None else zlo
        y = self.y if y is None else y
        core = self.core if core is None else core
        zhi = self.zhi if zhi is None else zhi
        x = self.x if x is None else x
        return (zlo * 8 + y * 2 + core, zhi * 4 + x)

    def sibling(self):
        return self.at(core=1 - self.core)

    def x_peer(self, step):
        return self.at(x=(self.x + step) % 4)

    def y_peer(self, step):
        return self.at(y=(self.y + step) % 4)

    def z_peer(self, step):
        z = (self.zhi * 4 + self.zlo + step + 8) % 8
        return self.at(zlo=z % 4, zhi=z // 4)

    def plane(self):
        return [
            self.at(y=(self.y + d) % 4, core=(self.core + c) % 2)
            for d, c in ((0, 1), (1, 0), (1, 1), (2, 0), (2, 1), (3, 0), (3, 1))
        ]

    def rank(self):
        return self.y * 2 + self.core

    def z_far(self):
        return self.at(zhi=1 - self.zhi)

    def doubling(self):
        return (
            self.z_far(),
            self.sibling(),
            self.at(y=self.y + 1 - 2 * (self.y % 2)),
            self.at(y=(self.y + 2) % 4),
            self.at(x=self.x + 1 - 2 * (self.x % 2)),
            self.at(x=(self.x + 2) % 4),
            self.at(zlo=self.zlo + 1 - 2 * (self.zlo % 2)),
            self.at(zlo=(self.zlo + 2) % 4),
        )


def greet(devices):
    barrier = pltpu.get_barrier_semaphore()
    for device in devices:
        pl.semaphore_signal(barrier, inc=1, device_id=device, device_id_type=MESH)
    pl.semaphore_wait(barrier, len(devices))


def remote(source, target, send_sem, recv_sem, device):
    return pltpu.make_async_remote_copy(
        src_ref=source,
        dst_ref=target,
        send_sem=send_sem,
        recv_sem=recv_sem,
        device_id=device,
        device_id_type=MESH,
    )


def half_of(width, which):
    half = width // 2
    return pl.ds(pl.multiple_of(which * half, 128), half)


class Doubling:
    def __init__(self, place, tile, slots, send_sems, recv_sems):
        self.partners = place.doubling()
        self.tile, self.slots = tile, slots
        self.send_sems, self.recv_sems = send_sems, recv_sems
        self.step = 0
        self.copies = []

    def start(self):
        k = self.step
        copy = remote(
            self.tile.at[k], self.slots.at[k], self.send_sems.at[k], self.recv_sems.at[k], self.partners[k]
        )
        copy.start()
        self.copies.append(copy)

    def advance(self):
        k = self.step
        self.copies[k].wait_recv()
        self.tile[k + 1] = self.tile[k] + self.slots[k]
        self.step = k + 1
        if self.step < 8:
            self.start()

    def drain(self):
        for copy in self.copies:
            copy.wait_send()


NEG = -1e30
NT = (((1,), (1,)), ((), ()))
TN = (((0,), (0,)), ((), ()))


def matmul(left, right, dims=(((1,), (0,)), ((), ()))):
    return lax.dot_general(left, right, dims, preferred_element_type=F32)


class Gather:
    def __init__(self, place, shard, full, send_sems, recv_sems, local_sem):
        self.place, self.shard, self.full = place, shard, full
        self.send_sems, self.recv_sems = send_sems, recv_sems
        self.rows = shard.shape[0]
        self.lanes = half_of(shard.shape[1], place.core)
        self.local = pltpu.make_async_copy(shard, full.at[place.wsh], local_sem)
        self.copies = {}

    def part(self, index, which=None):
        block = self.full.at[index]
        if which is None:
            return block.at[:, self.lanes]
        half = self.rows // 2
        return block.at[which * half : (which + 1) * half, self.lanes]

    def send(self, k, source, target, device):
        copy = remote(source, target, self.send_sems.at[k], self.recv_sems.at[k], device)
        copy.start()
        self.copies[k] = copy

    def own(self, far, step):
        return (far * 4) + (self.place.x + step + 4) % 4

    def start_z(self):
        place = self.place
        self.local.start()
        self.send(2, self.shard.at[:, self.lanes], self.part(place.wsh), place.z_far())

    def start_x(self):
        place = self.place
        self.send(0, self.shard.at[:, self.lanes], self.part(place.wsh), place.x_peer(1))
        self.send(1, self.shard.at[:, self.lanes], self.part(place.wsh), place.x_peer(3))

    def pass_on(self, zh, base):
        place = self.place
        left, right = self.own(zh, -1), self.own(zh, 1)
        self.copies[base].wait_recv()
        self.send(base + 3, self.part(left, 0), self.part(left, 0), place.x_peer(1))
        self.send(base + 5, self.part(left), self.part(left), place.sibling())
        self.copies[base + 1].wait_recv()
        self.send(base + 4, self.part(right, 1), self.part(right, 1), place.x_peer(3))
        self.send(base + 6, self.part(right), self.part(right), place.sibling())

    def opposite(self, zh, base):
        place = self.place
        index = self.own(zh, 2)
        for which in range(2):
            self.copies[base + 3 + which].wait_recv()
            self.send(base + 7 + which, self.part(index, which), self.part(index, which), place.sibling())

    def near(self):
        self.pass_on(self.place.zhi, 0)

    def near_opposite(self):
        self.opposite(self.place.zhi, 0)

    def from_z(self):
        place = self.place
        index = self.own(1 - place.zhi, 0)
        self.copies[2].wait_recv()
        self.send(10, self.part(index), self.part(index), place.x_peer(1))
        self.send(11, self.part(index), self.part(index), place.x_peer(3))
        self.send(9, self.part(index), self.part(index), place.sibling())

    def far(self):
        self.pass_on(1 - self.place.zhi, 10)

    def far_opposite(self):
        self.opposite(1 - self.place.zhi, 10)

    def finish(self):
        self.local.wait()
        for k in (5, 6, 7, 8, 9, 15, 16, 17, 18):
            self.copies[k].wait_recv()

    def drain(self):
        for k in self.copies:
            self.copies[k].wait_send()


def head_mask(which):
    lane = lax.broadcasted_iota(jnp.int32, (1, 128), 1)
    return jnp.where((lane // 64) == which, 1.0, 0.0).astype(BF16)


def to_slots(slot_row, head, count):
    row = slot_row[pl.ds(head, 1), :]
    iota = lax.broadcasted_iota(jnp.int32, (count, count), 0).astype(F32)
    return jnp.where(iota == row, 1.0, 0.0).astype(BF16)


def to_tokens(slot_col, head, count):
    lane = lax.broadcasted_iota(jnp.int32, slot_col.shape, 1)
    column = jnp.sum(jnp.where(lane == head, slot_col[...], 0.0), axis=1, keepdims=True)
    iota = lax.broadcasted_iota(jnp.int32, (count, count), 1).astype(F32)
    return jnp.where(iota == column, 1.0, 0.0).astype(BF16)


def pair_select(first, second):
    lane = lax.broadcasted_iota(jnp.int32, first.shape, 1)
    return jnp.where((lane // 64) % 2 == 0, first, second)


def heads_home(turned):
    return jnp.concatenate([turned[0:64, 0:128], turned[64:128, 128:256]], axis=0).T


def make_slots(clusters, segments, counted, slot_row, slot_col, labels):
    heads, count = clusters.shape
    groups = lax.shift_right_logical(clusters[...], 2)
    iota = lax.broadcasted_iota(jnp.int32, (32, count), 0)
    before = lax.broadcasted_iota(jnp.int32, (count, count), 0)
    after = lax.broadcasted_iota(jnp.int32, (count, count), 1)
    upper = jnp.where(before <= after, 1.0, 0.0).astype(BF16)
    hot = [jnp.where(groups[h : h + 1, :] == iota, 1.0, 0.0) for h in range(heads)]
    counts = matmul(jnp.concatenate(hot, axis=0).astype(BF16), upper)
    group_f = groups.astype(F32)
    rows = []
    for h in range(heads):
        rank = jnp.sum(counts[32 * h : 32 * h + 32] * hot[h], axis=0, keepdims=True)
        rows.append(group_f[h : h + 1] * 16.0 + rank - 1.0)
    slots = jnp.concatenate(rows + [counted[...].astype(F32), jnp.zeros((127 - heads, count), F32)], axis=0)
    slot_row[...] = slots[:16]
    slot_col[...] = slots.T
    label = (segments[0:1, :] * 4 + (clusters[...] & 3)).astype(F32)
    labels[...] = jnp.concatenate([label, jnp.zeros((128 - heads, count), F32)], axis=0).T.astype(BF16)


def rows16(j):
    return slice(16 * j, 16 * j + 16)


def forward_kernel(
    x, clusters, segments, counted, norms, wq, wo, wu, wd,
    mixed, x_turned, fq_out, fo, fu, fd, got_out, before_out, after_out, logsum, hot_out, cold_out, slot_row, slot_col, total,
    pieces, fq, got, before, after, hot, cold,
    labels, sent_labels, got_labels, before_labels, after_labels, wide_labels, sent, out, back,
    tile, slots,
    w_send, w_recv, w_local, t_send, t_recv, a_send, a_recv, a_local, z_send, z_recv, b_send, b_recv, b_local, k_sem,
):
    place = Place()
    plane, rank = place.plane(), place.rank()
    up, down = place.z_peer(1), place.z_peer(-1)
    kept = []

    def keep(source, target):
        copy = pltpu.make_async_copy(source, target, k_sem.at[len(kept)])
        copy.start()
        kept.append(copy)

    partners = place.doubling()
    for g in range(3):
        for b in range(2):
            for t in range(3):
                lane = t * 768 + (2 * g + b) * 128
                pieces[g, :, b * 384 + t * 128 : b * 384 + t * 128 + 128] = wq[:, lane : lane + 128]
    greet(
        plane + [place.x_peer(1), place.x_peer(2), place.x_peer(3), place.z_far(), up, down, partners[6], partners[7]]
    )
    weights = [
        Gather(place, shard, full, w_send.at[i], w_recv.at[i], w_local.at[i])
        for i, (shard, full) in enumerate(
            [(pieces.at[g], fq.at[g]) for g in range(3)] + [(wo, fo), (wu, fu), (wd, fd)]
        )
    ]
    first, second, third, w_out, w_up, w_down = weights
    rest = (w_out, w_up, w_down)
    tile[0] = jnp.zeros_like(tile[0])
    tile[0, 0:4, 0 : norms.shape[1]] = norms[...].astype(F32)
    tile[0] = pltpu.roll(tile[0], place.wsh * norms.shape[1], 1)
    lane_zero = lax.broadcasted_iota(jnp.int32, (1, tile.shape[2]), 1) == 0
    tile[0, 4:5, :] = jnp.where(lane_zero, jnp.sum(counted[...].astype(F32), axis=1, keepdims=True), 0.0)
    doubling = Doubling(place, tile, slots, t_send, t_recv)
    doubling.start()
    first.start_z()
    first.start_x()
    count = x.shape[0]
    make_slots(clusters, segments, counted, slot_row, slot_col, labels)

    second.start_z()
    second.start_x()
    sent_labels[...] = jnp.zeros_like(sent_labels)

    def move_labels(head, carry):
        lane = lax.broadcasted_iota(jnp.int32, (count, 128), 1)
        moved = matmul(to_slots(slot_row, head, count), labels[...])
        sent_labels[...] = jnp.where(lane == head, moved, sent_labels[...])
        return carry

    lax.fori_loop(0, 6, move_labels, 0)
    first.near()
    third.start_z()
    third.start_x()
    lax.fori_loop(6, 12, move_labels, 0)
    labels[...] = sent_labels[...].astype(BF16)

    def block(which):
        return pl.ds(pl.multiple_of(which * 64, 64), 64)

    def ranks():
        return [dev[0] % 8 for dev in plane]

    label_copies = [
        remote(labels.at[block(to)], got_labels.at[rank], a_send.at[6, k], a_recv.at[6, k], plane[k])
        for k, to in enumerate(ranks())
    ]
    for copy in label_copies:
        copy.start()
    own_labels = pltpu.make_async_copy(labels.at[block(rank)], got_labels.at[rank], a_local.at[6])
    own_labels.start()
    first.from_z()
    second.near()
    first.near_opposite()
    doubling.advance()
    x_turned[...] = x[...].astype(F32).T.astype(BF16)
    doubling.advance()
    second.from_z()
    first.far()
    third.near()
    second.near_opposite()
    doubling.advance()
    third.from_z()
    own_labels.wait()
    for copy in label_copies:
        copy.wait_recv()
    label_up = remote(got_labels.at[4:8], before_labels, z_send.at[6, 0], z_recv.at[6, 0], up)
    label_down = remote(got_labels.at[0:4], after_labels, z_send.at[6, 1], z_recv.at[6, 1], down)
    label_up.start()
    label_down.start()
    for w in rest:
        w.start_z()
    first.far_opposite()
    first.finish()

    def make_hot(head, carry):
        lane = lax.broadcasted_iota(jnp.int32, (256, 128), 1)
        for j in range(4):
            column = jnp.sum(jnp.where(lane == head, wide_labels[j], 0.0), axis=1, keepdims=True)
            same = lane.astype(F32) == column
            cold[head * 4 + j] = jnp.where(same, 0.0, NEG).astype(BF16)
            hot[head * 4 + j] = jnp.where(same, 1.0, 0.0)[64:192].astype(BF16)
        return carry

    def send_copies(p, fn):
        for k, to in enumerate(ranks()):
            fn(remote(sent.at[p, block(to)], got.at[p, rank], a_send.at[p, k], a_recv.at[p, k], plane[k]))

    def own_copy(p):
        return pltpu.make_async_copy(sent.at[p, block(rank)], got.at[p, rank], a_local.at[p])

    def project(g):
        value = matmul(x[...], fq[g].reshape(768, 768))
        lane = lax.broadcasted_iota(jnp.int32, (1, 384), 1)
        scale = jnp.where(lane < 128, 0.125, 1.0)
        for b in range(2):
            p = 2 * g + b
            rows = (value[:, b * 384 : b * 384 + 384] * scale).astype(BF16)
            moved = [matmul(to_slots(slot_row, 2 * p + a, count), rows) for a in range(2)]
            sent[p] = pair_select(moved[0], moved[1]).astype(BF16)
            send_copies(p, lambda copy: copy.start())
            own_copy(p).start()

    project(0)
    second.far()
    third.near_opposite()
    third.far()
    second.far_opposite()
    second.finish()
    doubling.advance()
    for w in rest:
        w.start_x()
    project(1)
    third.far_opposite()
    third.finish()
    project(2)
    keep(fq, fq_out)
    label_up.wait_recv()
    label_down.wait_recv()
    for j in range(4):
        wide_labels[j, 0:64] = jnp.where(
            place.zlo == 0, -1.0, before_labels[:, rows16(j), :].reshape(64, 128).astype(F32)
        )
        wide_labels[j, 64:192] = got_labels[:, rows16(j), :].reshape(128, 128).astype(F32)
        wide_labels[j, 192:256] = jnp.where(
            place.zlo == 3, -1.0, after_labels[:, rows16(j), :].reshape(64, 128).astype(F32)
        )
    lax.fori_loop(0, 12, make_hot, 0)
    keep(hot, hot_out)
    keep(cold, cold_out)
    w_out.near()
    w_out.from_z()
    w_up.near()
    doubling.advance()

    def halo(p):
        return (
            remote(got.at[p, 4:8, :, 128:384], before.at[p], z_send.at[p, 0], z_recv.at[p, 0], up),
            remote(got.at[p, 0:4, :, 128:384], after.at[p], z_send.at[p, 1], z_recv.at[p, 1], down),
        )

    def back_copies(p, fn):
        for k, to in enumerate(ranks()):
            fn(remote(out.at[p, to], back.at[p, rank], b_send.at[p, k], b_recv.at[p, k], plane[k]))

    def own_back(p):
        return pltpu.make_async_copy(out.at[p, rank], back.at[p, rank], b_local.at[p])

    def arrive(p):
        own_copy(p).wait()
        send_copies(p, lambda copy: copy.wait_recv())
        for copy in halo(p):
            copy.start()

    masks = [head_mask(a) for a in range(2)]

    def attend(p):
        for copy in halo(p):
            copy.wait_recv()
        for j in range(4):
            r = rows16(j)
            query = got[p, :, r, 0:128].reshape(128, 128)
            keys = jnp.concatenate(
                [before[p, :, r, 0:128].reshape(64, 128), got[p, :, r, 128:256].reshape(128, 128),
                 after[p, :, r, 0:128].reshape(64, 128)], axis=0)
            values = jnp.concatenate(
                [before[p, :, r, 128:256].reshape(64, 128), got[p, :, r, 256:384].reshape(128, 128),
                 after[p, :, r, 128:256].reshape(64, 128)], axis=0)
            probs = []
            for a in range(2):
                head = 2 * p + a
                scores = matmul(
                    jnp.concatenate([keys, cold[head * 4 + j]], axis=1),
                    jnp.concatenate([query * masks[a], hot[head * 4 + j]], axis=1), NT)
                top = jnp.max(scores, axis=0, keepdims=True)
                raised = jnp.exp(scores - top)
                sums = jnp.sum(raised, axis=0, keepdims=True)
                probs.append((raised * (1.0 / sums)).astype(BF16))
                logsum[j, pl.ds(head, 1), :] = top + jnp.log(sums)
            out[p, :, r, :] = heads_home(matmul(values, jnp.concatenate(probs, axis=1), TN)).astype(BF16).reshape(8, 16, 128)
        back_copies(p, lambda copy: copy.start())
        own_back(p).start()

    def home(p):
        own_back(p).wait()
        back_copies(p, lambda copy: copy.wait_recv())
        rows = back[p].reshape(count, 128)
        moved = [matmul(to_tokens(slot_col, 2 * p + a, count), rows) for a in range(2)]
        mixed[:, p * 128 : p * 128 + 128] = pair_select(moved[0], moved[1]).astype(BF16)

    arrive(0)
    w_up.from_z()
    arrive(1)
    attend(0)
    w_down.near()
    w_out.near_opposite()
    arrive(2)
    attend(1)
    w_down.from_z()
    w_up.near_opposite()
    doubling.advance()
    arrive(3)
    attend(2)
    home(0)
    w_out.far()
    arrive(4)
    attend(3)
    home(1)
    w_up.far()
    w_down.near_opposite()
    arrive(5)
    attend(4)
    home(2)
    home(3)
    doubling.advance()

    def settle_out(p, carry):
        send_copies(p, lambda copy: copy.wait_send())
        return carry

    def settle_back(p, carry):
        back_copies(p, lambda copy: copy.wait_send())
        for copy in halo(p):
            copy.wait_send()
        return carry

    lax.fori_loop(0, 6, settle_out, 0)
    for copy in label_copies + [label_up, label_down]:
        copy.wait_send()
    for w in (first, second, third):
        w.drain()
    w_down.far()
    attend(5)
    keep(got, got_out)
    keep(before, before_out)
    keep(after, after_out)
    w_out.far_opposite()
    w_up.far_opposite()
    home(4)
    lax.fori_loop(0, 5, settle_back, 0)
    w_down.far_opposite()
    home(5)
    doubling.advance()
    for w in rest:
        w.finish()
    total[...] = tile[8]
    settle_back(5, 0)
    for w in rest:
        w.drain()
    for copy in kept:
        copy.wait()
    doubling.drain()


ANY = pl.BlockSpec(memory_space=pl.ANY)
VMEM = pl.BlockSpec(memory_space=pltpu.VMEM)


def shaped(*shape, dtype=BF16):
    return jax.ShapeDtypeStruct(shape, dtype)


def forward(x, clusters, segments, counted, norms, shards):
    count, width = x.shape
    dma = pltpu.SemaphoreType.DMA
    return pl.pallas_call(
        forward_kernel,
        out_shape=[
            shaped(*x.shape),
            shaped(width, count),
            shaped(3, 8, shards[0].shape[0], 768),
            *[shaped(8, *w.shape) for w in shards[1:]],
            shaped(6, 8, 64, 384),
            shaped(6, 4, 64, 256),
            shaped(6, 4, 64, 256),
            shaped(4, 16, 128, dtype=F32),
            shaped(48, 128, 128),
            shaped(48, 256, 128),
            shaped(16, count, dtype=F32),
            shaped(count, 128, dtype=F32),
            shaped(8, width, dtype=F32),
        ],
        in_specs=[VMEM] * 9,
        out_specs=[VMEM] * 2 + [ANY] * 7 + [VMEM] + [ANY] * 2 + [VMEM] * 3,
        scratch_shapes=[
            pltpu.VMEM((3, shards[0].shape[0], 768), BF16),
            pltpu.VMEM((3, 8, shards[0].shape[0], 768), BF16),
            pltpu.VMEM((6, 8, 64, 384), BF16),
            pltpu.VMEM((6, 4, 64, 256), BF16),
            pltpu.VMEM((6, 4, 64, 256), BF16),
            pltpu.VMEM((48, 128, 128), BF16),
            pltpu.VMEM((48, 256, 128), BF16),
            pltpu.VMEM((count, 128), BF16),
            pltpu.VMEM((count, 128), F32),
            pltpu.VMEM((8, 64, 128), BF16),
            pltpu.VMEM((4, 64, 128), BF16),
            pltpu.VMEM((4, 64, 128), BF16),
            pltpu.VMEM((4, 256, 128), F32),
            pltpu.VMEM((6, count, 384), BF16),
            pltpu.VMEM((6, 8, 64, 128), BF16),
            pltpu.VMEM((6, 8, 64, 128), BF16),
            pltpu.VMEM((9, 8, width), F32),
            pltpu.VMEM((8, 8, width), F32),
            dma((6, 19)), dma((6, 19)), dma((6,)), dma((8,)), dma((8,)),
            dma((7, 7)), dma((7, 7)), dma((7,)), dma((7, 2)), dma((7, 2)),
            dma((6, 7)), dma((6, 7)), dma((6,)), dma((6,)),
        ],
        compiler_params=pltpu.CompilerParams(
            collective_id=0, has_side_effects=True, vmem_limit_bytes=60 * 2**20
        ),
        name="forward_attention",
    )(x, clusters, segments, counted, norms, *shards)


class Reduce:
    def __init__(self, place, held, near, far, sum_x, from_y, sum_y, from_z, out, send_sems, recv_sems, grad=None, source=None, near_source=None, load_sems=None):
        self.place, self.held, self.grad = place, held, grad
        self.near, self.far, self.sum_x, self.from_y = near, far, sum_x, from_y
        self.sum_y, self.from_z, self.out = sum_y, from_z, out
        self.send_sems, self.recv_sems = send_sems, recv_sems
        self.rows, self.half = held.shape[2], held.shape[3]
        self.window = out.shape[1]
        self.owner = place.y // 2
        self.z = place.zhi * 4 + place.zlo
        self.final = jnp.logical_and(place.zhi == self.owner, place.core == place.zlo // 2)
        self.copies = {}
        if source is not None:
            self.loads = [pltpu.make_async_copy(source, held, load_sems.at[0])]
        self.begun = near_source is not None
        if self.begun:
            self.loads.append(pltpu.make_async_copy(near_source, near, load_sems.at[1]))

    def send(self, k, source, target, device):
        copy = remote(source, target, self.send_sems.at[k], self.recv_sems.at[k], device)
        copy.start()
        self.copies[k] = copy

    def each(self, count, body):
        def step(i, carry):
            body(pl.ds(pl.multiple_of(i * 48, 16), 48))
            return carry

        lax.fori_loop(0, count // 48, step, 0)

    def after(self, rows, offset):
        return pl.ds(pl.multiple_of(rows.start + offset, 16), rows.size)

    def blocks(self, body):
        def step(zh, carry):
            body(zh)
            return carry

        lax.fori_loop(0, 2, step, 0)

    def start(self):
        place = self.place
        self.send(0, self.grad.at[:, :, :, half_of(2 * self.half, 1 - place.core)], self.held, place.sibling())

    def add_pair(self, xx):
        mine = half_of(2 * self.half, self.place.core)

        def block(zh):
            def body(rows):
                self.held[zh, xx, rows, :] = (
                    self.grad[zh, xx, rows, mine].astype(F32) + self.held[zh, xx, rows, :].astype(F32)
                ).astype(BF16)

            self.each(self.rows, body)

        self.blocks(block)

    def to_opposite(self):
        place = self.place
        half = self.rows // 2
        opposite = (place.x + 2) % 4
        if self.grad is None:
            self.loads[0].wait()
        else:
            self.copies[0].wait_recv()
            self.add_pair(opposite)
        self.send(1, self.held.at[:, opposite, 0:half], self.near.at[0], place.x_peer(1))
        self.send(2, self.held.at[:, opposite, half : self.rows], self.near.at[1], place.x_peer(3))
        if self.grad is not None:
            for step in (1, 3, 0):
                self.add_pair((place.x + step) % 4)

    def to_near(self):
        place = self.place
        half = self.rows // 2
        if self.begun:
            for copy in self.loads:
                copy.wait()
        for k, step in enumerate((1, 3)):
            to = (place.x + step) % 4
            if not self.begun:
                self.copies[1 + k].wait_recv()

            def block(zh, k=k, to=to):
                def body(rows):
                    there = self.after(rows, k * half)
                    self.held[zh, to, there, :] = (
                        self.held[zh, to, there, :].astype(F32) + self.near[k, zh, rows, :].astype(F32)
                    ).astype(BF16)

                self.each(half, body)

            self.blocks(block)
            self.send(3 + k, self.held.at[:, to], self.far.at[k], place.x_peer(step))

    def to_y(self):
        place = self.place
        half = self.rows // 2
        for k in range(2):
            self.copies[3 + k].wait_recv()

        def block(zh):
            def body(rows):
                value = self.held[zh, place.x, rows, :].astype(F32)
                value = value + self.far[0, zh, rows, :].astype(F32) + self.far[1, zh, rows, :].astype(F32)
                self.sum_x[zh, rows, :] = value.astype(BF16)

            self.each(self.rows, body)

        self.blocks(block)
        for k, d in enumerate((1, 2, 3)):
            to = (place.y + d) % 4
            part = pl.ds(pl.multiple_of((to % 2) * half, 16), half)
            self.send(5 + k, self.sum_x.at[to // 2, part], self.from_y.at[k], place.y_peer(d))

    def lanes(self, zlo):
        offset = (zlo % 2) * (self.half - self.window)
        return pl.ds(pl.multiple_of(offset, 128), self.window)

    def z_copy(self, k):
        place = self.place
        zlo = 2 * place.core + k
        return remote(
            self.sum_y.at[:, self.lanes(zlo)], self.from_z.at[self.z],
            self.send_sems.at[8 + k], self.recv_sems.at[8 + self.z], place.at(zlo=zlo, zhi=self.owner),
        )

    def is_target(self, k):
        place = self.place
        return jnp.logical_and(place.zhi == self.owner, place.zlo == 2 * place.core + k)

    def to_z(self):
        place = self.place
        half = self.rows // 2
        for k in range(3):
            self.copies[5 + k].wait_recv()

        def body(rows):
            value = self.sum_x[self.owner, self.after(rows, (place.y % 2) * half), :].astype(F32)
            for k in range(3):
                value = value + self.from_y[k, rows, :].astype(F32)
            self.sum_y[rows, :] = value.astype(BF16)

        self.each(half, body)
        for k in range(2):
            @pl.when(jnp.logical_not(self.is_target(k)))
            def _(k=k):
                self.z_copy(k).start()

    def spread_copy(self, k, device):
        half = self.rows // 2
        part = self.out.at[pl.ds(pl.multiple_of((self.place.y % 2) * half, 16), half)]
        return remote(part, part, self.send_sems.at[10 + k], self.recv_sems.at[16 + self.place.y % 2], device)

    def spread(self):
        half = self.rows // 2

        @pl.when(self.final)
        def _():
            self.from_z[self.z] = self.sum_y[:, self.lanes(self.place.zlo)]
            for z in range(8):
                @pl.when(self.z != z)
                def _(z=z):
                    part = self.from_z.at[z]
                    remote(part, part, self.send_sems.at[8], self.recv_sems.at[8 + z], self.place.sibling()).wait_recv()

            def body(rows):
                there = self.after(rows, (self.place.y % 2) * half)
                value = self.from_z[0, rows, :].astype(F32)
                for z in range(1, 8):
                    value = value + self.from_z[z, rows, :].astype(F32)
                self.out[there, :] = value.astype(BF16)

            self.each(half, body)
            for k, device in enumerate(self.place.plane()):
                self.spread_copy(k, device).start()

    def finish(self):
        half = self.rows // 2
        for k in range(2):
            part = self.out.at[k * half : (k + 1) * half]

            @pl.when(jnp.logical_not(jnp.logical_and(self.final, self.place.y % 2 == k)))
            def _(k=k, part=part):
                remote(part, part, self.send_sems.at[10], self.recv_sems.at[16 + k], self.place.sibling()).wait_recv()

    def drain(self):
        for k in self.copies:
            self.copies[k].wait_send()
        for k in range(2):
            @pl.when(jnp.logical_not(self.is_target(k)))
            def _(k=k):
                self.z_copy(k).wait_send()

        @pl.when(self.final)
        def _():
            for k, device in enumerate(self.place.plane()):
                self.spread_copy(k, device).wait_send()


def reduce_scratch(rows, half, window):
    return [
        pltpu.VMEM((2, 4, rows, half), BF16),
        pltpu.VMEM((2, 2, rows // 2, half), BF16),
        pltpu.VMEM((2, 2, rows, half), BF16),
        pltpu.VMEM((2, rows, half), BF16),
        pltpu.VMEM((3, rows // 2, half), BF16),
        pltpu.VMEM((rows // 2, half), BF16),
        pltpu.VMEM((8, rows // 2, window), BF16),
        pltpu.VMEM((rows, window), BF16),
    ]


def cut(value, offset, target):
    rows, width = value.shape
    first = pltpu.roll(value, (width - offset) % width, 1)[:, 0:128]
    if target.shape[0] == rows:
        target[...] = first[:, : target.shape[1]]
        return
    if rows % 128:
        first = jnp.concatenate([first, jnp.zeros((128 - rows % 128, 128), F32)], axis=0)
    target[...] = first.T[: target.shape[0], :rows]


ORDER = (0, 3, 1, 4, 2, 5)


def backward_kernel(*refs):
    (grad_mixed, grad_first, logsum, slot_row, slot_col, small, x_hbm, fq_hbm, got_hbm, before_hbm, after_hbm,
     hot_hbm, cold_hbm, go, gu, gd, near_u, near_d) = refs[:18]
    refs = refs[2:]
    grad_x, out_q, out_o, out_u, out_d, norms_out, loss_out = refs[16:23]
    x_turned, fq, got, before, after, hot, cold = refs[23:30]
    sent, got_grad, grads, to_before, to_after, from_before, from_after, back = refs[30:38]
    grads_q = refs[38:41]
    reduce_refs = [refs[41 + 8 * i : 49 + 8 * i] for i in range(6)]
    (tile, slots, a_send, a_recv, a_local, z_send, z_recv, b_send, b_recv, b_local,
     t_send, t_recv, r_send, r_recv, r_load, l_sem) = refs[89:]
    place = Place()
    plane, rank = place.plane(), place.rank()
    up, down = place.z_peer(1), place.z_peer(-1)
    loads = [
        pltpu.make_async_copy(source, target, l_sem.at[i])
        for i, (source, target) in enumerate(
            ((got_hbm, got), (before_hbm, before), (after_hbm, after), (hot_hbm, hot), (cold_hbm, cold),
             (fq_hbm, fq), (x_hbm, x_turned))
        )
    ]
    rest = [
        Reduce(
            place, *reduce_refs[i], r_send.at[i], r_recv.at[i], source=source, near_source=near, load_sems=r_load.at[i]
        )
        for i, (source, near) in enumerate(((go, None), (gu, near_u), (gd, near_d)))
    ]
    by_group = [
        Reduce(place, *reduce_refs[3 + i], r_send.at[3 + i], r_recv.at[3 + i], grad=grads_q[i]) for i in range(3)
    ]
    for r in (rest[2], rest[1], rest[0]):
        for copy in r.loads:
            copy.start()
    for copy in loads:
        copy.start()
    greet(plane + [place.x_peer(d) for d in (1, 2, 3)] + [place.z_peer(d) for d in range(1, 8)])
    sum_o, sum_u, sum_d = rest
    sum_o.to_opposite()
    tile[0] = small[...]
    doubling = Doubling(place, tile, slots, t_send, t_recv)
    doubling.start()
    count = grad_mixed.shape[0]
    ranks = [dev[0] % 8 for dev in plane]

    def block(which):
        return pl.ds(pl.multiple_of(which * 64, 64), 64)

    def send_copies(p, fn):
        for k, to in enumerate(ranks):
            fn(remote(sent.at[p, block(to)], got_grad.at[p, rank], a_send.at[p, k], a_recv.at[p, k], plane[k]))

    def own_copy(p):
        return pltpu.make_async_copy(sent.at[p, block(rank)], got_grad.at[p, rank], a_local.at[p])

    def leave(i, carry):
        p = i // 2 + 3 * (i % 2)
        rows = grad_mixed[:, pl.ds(pl.multiple_of(p * 128, 128), 128)]
        moved = [matmul(to_slots(slot_row, 2 * p + a, count), rows) for a in range(2)]
        sent[p] = pair_select(moved[0], moved[1]).astype(BF16)
        send_copies(p, lambda copy: copy.start())
        own_copy(p).start()
        return carry

    lax.fori_loop(0, 6, leave, 0)
    doubling.advance()
    sum_d.to_near()
    sum_u.to_near()
    for copy in loads[:5]:
        copy.wait()

    def halo(p):
        return (
            remote(to_after.at[p], from_before.at[p], z_send.at[p, 0], z_recv.at[p, 0], up),
            remote(to_before.at[p], from_after.at[p], z_send.at[p, 1], z_recv.at[p, 1], down),
        )

    def back_copies(p, fn):
        for k, to in enumerate(ranks):
            fn(remote(grads.at[p, to], back.at[p, rank], b_send.at[p, k], b_recv.at[p, k], plane[k]))

    def own_back(p):
        return pltpu.make_async_copy(grads.at[p, rank], back.at[p, rank], b_local.at[p])

    masks = [head_mask(a) for a in range(2)]

    def attend(p):
        own_copy(p).wait()
        send_copies(p, lambda copy: copy.wait_recv())
        for j in range(4):
            r = rows16(j)
            query = got[p, :, r, 0:128].reshape(128, 128)
            keys = jnp.concatenate(
                [before[p, :, r, 0:128].reshape(64, 128), got[p, :, r, 128:256].reshape(128, 128),
                 after[p, :, r, 0:128].reshape(64, 128)], axis=0)
            values = jnp.concatenate(
                [before[p, :, r, 128:256].reshape(64, 128), got[p, :, r, 256:384].reshape(128, 128),
                 after[p, :, r, 128:256].reshape(64, 128)], axis=0)
            grad = got_grad[p, :, r, :].reshape(128, 128)
            queries = [query * masks[a] for a in range(2)]
            grad_both = jnp.concatenate([grad * masks[a] for a in range(2)], axis=0)
            grad_probs = matmul(values, grad_both, NT)
            probs, grad_scores = [], []
            for a in range(2):
                head = 2 * p + a
                scores = matmul(
                    jnp.concatenate([keys, cold[head * 4 + j]], axis=1),
                    jnp.concatenate([queries[a], hot[head * 4 + j]], axis=1), NT)
                prob = jnp.exp(scores - logsum[j, pl.ds(head, 1), :])
                own = grad_probs[:, a * 128 : a * 128 + 128]
                delta = jnp.sum(prob * own, axis=0, keepdims=True)
                probs.append(prob.astype(BF16))
                grad_scores.append((prob * (own - delta)).astype(BF16))
            grad_scores = jnp.concatenate(grad_scores, axis=1)
            dk = matmul(grad_scores, jnp.concatenate(queries, axis=0))
            dv = matmul(jnp.concatenate(probs, axis=1), grad_both)
            dq = heads_home(matmul(keys, grad_scores, TN)) * 0.125
            both = jnp.concatenate([dk, dv], axis=1).astype(BF16)
            to_before[p, :, r, :] = both[0:64].reshape(4, 16, 256)
            to_after[p, :, r, :] = both[192:256].reshape(4, 16, 256)
            grads[p, :, r, 0:128] = dq.astype(BF16).reshape(8, 16, 128)
            grads[p, :, r, 128:384] = both[64:192].reshape(8, 16, 256)
        for copy in halo(p):
            copy.start()

    def give(p):
        for copy in halo(p):
            copy.wait_recv()
        for part, extra in ((slice(0, 4), from_before), (slice(4, 8), from_after)):
            grads[p, part, :, 128:384] = (
                grads[p, part, :, 128:384].astype(F32) + extra[p].astype(F32)
            ).astype(BF16)
        back_copies(p, lambda copy: copy.start())
        own_back(p).start()

    def home(p):
        own_back(p).wait()
        back_copies(p, lambda copy: copy.wait_recv())
        rows = back[p].reshape(count, 384)
        moved = [matmul(to_tokens(slot_col, 2 * p + a, count), rows) for a in range(2)]
        grad_qkv = pair_select(moved[0], moved[1]).astype(BF16)
        back[p] = grad_qkv.reshape(8, 64, 384)
        weight = matmul(x_turned[...], grad_qkv).astype(BF16)
        group, late = p % 3, p // 3
        for t, lane in enumerate((late, 2 + late, 4 + late)):
            grads_q[group][:, :, :, lane * 128 : lane * 128 + 128] = weight[:, t * 128 : t * 128 + 128].reshape(2, 4, 96, 128)

    def turn_back(i):
        rows = slice(i * 128, i * 128 + 128)
        value = grad_first[rows, :]
        for g in range(3):
            pair = [back[2 * g + b, 2 * i : 2 * i + 2].reshape(128, 384) for b in range(2)]
            value = value + matmul(jnp.concatenate(pair, axis=1), fq[g].reshape(768, 768), NT)
        grad_x[rows, :] = value

    attend(0)
    doubling.advance()
    attend(3)
    sum_o.to_near()
    attend(1)
    give(0)
    give(3)
    attend(4)
    give(1)
    doubling.advance()
    attend(2)
    give(4)
    sum_d.to_y()
    attend(5)
    give(2)
    give(5)
    for copy in loads[5:]:
        copy.wait()
    home(0)
    home(3)
    by_group[0].start()
    sum_u.to_y()
    home(1)
    doubling.advance()
    by_group[0].to_opposite()
    sum_o.to_y()
    home(4)
    by_group[1].start()
    sum_d.to_z()
    by_group[0].to_near()
    home(2)
    doubling.advance()
    by_group[1].to_opposite()
    home(5)
    by_group[2].start()
    doubling.advance()
    sum_u.to_z()
    by_group[0].to_y()
    by_group[1].to_near()
    by_group[2].to_opposite()
    sum_o.to_z()
    turn_back(0)
    doubling.advance()
    by_group[1].to_y()
    by_group[0].to_z()
    by_group[2].to_near()
    sum_d.spread()
    turn_back(1)
    by_group[1].to_z()
    by_group[2].to_y()
    sum_u.spread()
    sum_o.spread()
    by_group[0].spread()
    turn_back(2)
    by_group[2].to_z()
    doubling.advance()
    by_group[1].spread()

    def settle(p, carry):
        send_copies(p, lambda copy: copy.wait_send())
        back_copies(p, lambda copy: copy.wait_send())
        for copy in halo(p):
            copy.wait_send()
        return carry

    lax.fori_loop(0, 6, settle, 0)
    seat = place.y * 2 + place.core
    for r, target in zip((sum_d, sum_u, sum_o), (out_d, out_u, out_o)):
        r.finish()
        width = r.half // 16
        offset = (place.zlo % 2) * (8 * width - (r.half - r.window)) + seat * width
        cut(r.out[...].astype(F32), offset, target)
    turn_back(3)
    by_group[2].spread()
    total = tile[8]
    loss_out[...] = total[4:5, 0:1]
    all_width = total.shape[1]
    shift = (all_width - (place.ctx * 8 + place.wsh) * norms_out.shape[1]) % all_width
    norms_out[...] = pltpu.roll(total, shift, 1)[0:4, 0 : norms_out.shape[1]]
    for r in rest:
        r.drain()
    for r in by_group:
        r.finish()
    tiles = [by_group[g].out[:, i * 128 : i * 128 + 128].astype(F32) for i in range(3) for g in range(3)]
    width = 72
    cut(jnp.concatenate(tiles, axis=1), (place.zlo % 2) * 8 * width + seat * width, out_q)
    for r in by_group:
        r.drain()
    doubling.drain()


def backward(grad_mixed, grad_first, small, x_turned, fq, kept, halves, nears):
    got, before, after, logsum, hot, cold, slot_row, slot_col = kept
    count = grad_mixed.shape[0]
    dma = pltpu.SemaphoreType.DMA
    vm = pltpu.VMEM
    rows_in = (halves[2].shape[2],)
    shapes = [(96, 384, 256), (96, 1536, 768), (rows_in[0], 384, 256)] + [(96, 384, 384)] * 3
    reduce_refs = []
    for shape in shapes:
        reduce_refs += reduce_scratch(*shape)
    loaded = (x_turned, fq, got, before, after, hot, cold)
    results = pl.pallas_call(
        backward_kernel,
        out_shape=[
            shaped(*grad_first.shape, dtype=F32),
            shaped(72, 96, dtype=F32),
            shaped(24, 96, dtype=F32),
            shaped(96, 96, dtype=F32),
            shaped(24, 384, dtype=F32),
            shaped(4, small.shape[1] // 256, dtype=F32),
            shaped(1, 1, dtype=F32),
        ],
        in_specs=[VMEM] * 6 + [ANY] * 12,
        out_specs=[VMEM] * 7,
        scratch_shapes=[vm(array.shape, array.dtype) for array in loaded]
        + [
            vm((6, count, 128), BF16),
            vm((6, 8, 64, 128), BF16),
            vm((6, 8, 64, 384), BF16),
            vm((6, 4, 64, 256), BF16),
            vm((6, 4, 64, 256), BF16),
            vm((6, 4, 64, 256), BF16),
            vm((6, 4, 64, 256), BF16),
            vm((6, 8, 64, 384), BF16),
        ]
        + [vm((2, 4, 96, 768), BF16)] * 3
        + reduce_refs
        + [
            vm((9, *small.shape), F32),
            vm((8, *small.shape), F32),
            dma((6, 7)), dma((6, 7)), dma((6,)), dma((6, 2)), dma((6, 2)),
            dma((6, 7)), dma((6, 7)), dma((6,)),
            dma((8,)), dma((8,)), dma((6, 17)), dma((6, 18)), dma((3, 2)), dma((7,)),
        ],
        compiler_params=pltpu.CompilerParams(
            collective_id=1, has_side_effects=True, vmem_limit_bytes=62 * 2**20
        ),
        name="backward_attention",
    )(grad_mixed, grad_first, logsum, slot_row, slot_col, small, *loaded, *halves, *nears)
    return results


CHUNK = 512


def norm_rows(values):
    centered = values - jnp.mean(values, axis=-1, keepdims=True)
    scale = lax.rsqrt(jnp.mean(centered * centered, axis=-1, keepdims=True) + 1e-05)
    return centered * scale, scale


def norm_rows_back(grad, normed, scale, gain):
    weighted = grad * gain
    return scale * (
        weighted
        - jnp.mean(weighted, axis=-1, keepdims=True)
        - normed * jnp.mean(weighted * normed, axis=-1, keepdims=True)
    )


def middle_kernel(
    everyone, ctx_size,
    mixed, x, teacher, slot_col, total, wo_hbm, wu_hbm, wd_hbm,
    result, grad_first, grad_mixed, small, go_hbm, gu_hbm, gd_hbm, near_u, near_d,
    wo, wu, wd, active, slope, normed, unit, scale, low, low_turned, acc, branch, grad_upper, go, gu, gd,
    held_o, held_u, held_d, in_sem, out_sem, send_sem, recv_sem, x_send, x_recv,
):
    place = Place()
    core, sibling = place.core, place.sibling()
    loads = [
        pltpu.make_async_copy(source, target, in_sem.at[i])
        for i, (source, target) in enumerate(((wo_hbm, wo), (wu_hbm, wu), (wd_hbm, wd)))
    ]
    for copy in loads:
        copy.start()
    greet([sibling, place.x_peer(1), place.x_peer(3)])
    count, width = x.shape
    tile = 128
    chunks = wd.shape[0] // CHUNK
    gains = total[0:4] / ctx_size
    small[...] = jnp.zeros_like(small)

    def rows_of(i):
        return pl.ds(pl.multiple_of(i * tile, tile), tile)

    def lanes_of(c):
        return pl.ds(pl.multiple_of(c * CHUNK, CHUNK), CHUNK)

    loads[0].wait()
    for i in range(2):
        rows = slice(i * 256, i * 256 + 256)
        acc[rows, :] = matmul(mixed[rows, :], wo[...])

    def first_norm(i, carry):
        rows = rows_of(i)
        unit_rows, scale_rows = norm_rows(x[rows, :].astype(F32) + acc[rows, :])
        unit[rows, :] = unit_rows
        scale[rows, :] = scale_rows
        value = unit_rows * gains[0:1] + gains[1:2]
        normed[rows, :] = value
        low[rows, :] = value.astype(BF16)
        acc[rows, :] = value
        return carry

    lax.fori_loop(0, count // tile, first_norm, 0)
    loads[1].wait()
    loads[2].wait()

    def expand(c, carry):
        lanes = lanes_of(c)
        up = wu[:, :, lanes].reshape(width, CHUNK)
        down = wd[lanes, :]
        for i in range(2):
            rows = slice(i * 256, i * 256 + 256)
            upper = matmul(low[rows, :], up)
            share = 0.5 + 0.5 * lax.erf(upper * 0.7071067811865476)
            density = jnp.exp(upper * upper * -0.5) * 0.3989422804014327
            value = (upper * share).astype(BF16)
            active[rows, lanes] = value
            slope[rows, lanes] = share + upper * density
            acc[rows, :] += matmul(value, down)
        return carry

    lax.fori_loop(0, chunks, expand, 0)
    low_turned[...] = normed[...].T.astype(BF16)

    def second_norm(i, carry):
        rows = rows_of(i)
        unit_rows, scale_rows = norm_rows(acc[rows, :])
        value = unit_rows * gains[2:3] + gains[3:4]
        result[rows, :] = value.astype(BF16)
        error = value - teacher[rows, :].astype(F32)
        mask = slot_col[rows, 12:13]
        losses = mask * jnp.mean(error * error, axis=-1, keepdims=True)
        grad = (everyone / total[4:5, 0:1]) * mask * error
        small[2:3, :] += jnp.sum(grad * unit_rows, axis=0, keepdims=True)
        small[3:4, :] += jnp.sum(grad, axis=0, keepdims=True)
        small[4:5, 0:1] += jnp.sum(losses, axis=0, keepdims=True) / total[4:5, 0:1]
        back = norm_rows_back(grad, unit_rows, scale_rows, gains[2:3])
        acc[rows, :] = back
        branch[rows, :] = back.astype(BF16)
        return carry

    lax.fori_loop(0, count // tile, second_norm, 0)

    half = chunks // 2
    theirs, ours = half_of(width, 1 - core), half_of(width, core)

    def down_copy(c):
        lanes = lanes_of(c)
        return remote(gd.at[lanes, theirs], held_d.at[lanes], send_sem.at[c], recv_sem.at[c], sibling)

    def up_copy(i):
        return remote(gu.at[i], held_u.at[i], send_sem.at[chunks + i], recv_sem.at[chunks + i], sibling)

    def up_out(i):
        return pltpu.make_async_copy(held_u.at[i], gu_hbm.at[:, :, lanes_of(i)], out_sem.at[chunks + i])

    deep = wd.shape[0] // 16
    shallow = width // 16

    def opposite(zh):
        return zh * 4 + (place.x + 2) % 4

    def down_across(k, zh):
        part = pl.ds(pl.multiple_of(opposite(zh) * 2 * deep + k * deep, 16), deep)
        return remote(
            held_d.at[part], near_d.at[k, zh], x_send.at[2 * k + zh], x_recv.at[2 * k + zh], place.x_peer(1 + 2 * k)
        )

    def up_across(i, k, zh):
        n = 4 + i * 4 + 2 * k + zh
        return remote(
            held_u.at[i, opposite(zh), k * shallow : (k + 1) * shallow], near_u.at[k, zh, :, lanes_of(i)],
            x_send.at[n], x_recv.at[n], place.x_peer(1 + 2 * k),
        )

    def make_down(c, carry):
        lanes = lanes_of(c)
        gd[lanes, :] = matmul(active[:, lanes], branch[...], TN).astype(BF16)
        down_copy(c).start()
        return carry

    lax.fori_loop(0, chunks, make_down, 0)

    def contract(c):
        lanes = lanes_of(c)
        up = wu[:, :, lanes].reshape(width, CHUNK)
        down = wd[lanes, :]
        for i in range(2):
            rows = slice(i * 256, i * 256 + 256)
            value = (matmul(branch[rows, :], down, NT) * slope[rows, lanes]).astype(BF16)
            grad_upper[rows, :] = value
            acc[rows, :] += matmul(value, up, NT)
        return matmul(low_turned[...], grad_upper[...]).reshape(8, width // 8, CHUNK)

    def for_sibling(i, carry):
        gu[i] = contract((1 - core) * half + i).astype(BF16)
        up_copy(i).start()
        return carry

    def for_own(i, carry):
        value = contract(core * half + i)
        up_copy(i).wait_recv()
        held_u[i] = (value + held_u[i].astype(F32)).astype(BF16)
        up_out(i).start()
        for k in range(2):
            for zh in range(2):
                up_across(i, k, zh).start()
        return carry

    def down_out(c):
        lanes = lanes_of(c)
        return pltpu.make_async_copy(held_d.at[lanes], gd_hbm.at[lanes], out_sem.at[c])

    def add_down(c, carry):
        lanes = lanes_of(c)
        down_copy(c).wait_recv()
        held_d[lanes, :] = (gd[lanes, ours].astype(F32) + held_d[lanes, :].astype(F32)).astype(BF16)
        down_out(c).start()
        return carry

    lax.fori_loop(0, chunks, add_down, 0)
    for k in range(2):
        for zh in range(2):
            down_across(k, zh).start()
    lax.fori_loop(0, half, for_sibling, 0)
    lax.fori_loop(0, half, for_own, 0)

    def first_back(i, carry):
        rows = rows_of(i)
        grad = acc[rows, :]
        small[0:1, :] += jnp.sum(grad * unit[rows, :], axis=0, keepdims=True)
        small[1:2, :] += jnp.sum(grad, axis=0, keepdims=True)
        back = norm_rows_back(grad, unit[rows, :], scale[rows, :], gains[0:1])
        grad_first[rows, :] = back
        branch[rows, :] = back.astype(BF16)
        return carry

    lax.fori_loop(0, count // tile, first_back, 0)
    go[...] = matmul(mixed[...], branch[...], TN).astype(BF16)
    last = remote(go.at[:, theirs], held_o, send_sem.at[chunks + half], recv_sem.at[chunks + half], sibling)
    last.start()
    for i in range(2):
        rows = slice(i * 256, i * 256 + 256)
        grad_mixed[rows, :] = matmul(branch[rows, :], wo[...], NT).astype(BF16)

    last.wait_recv()
    held_o[...] = (go[:, ours].astype(F32) + held_o[...].astype(F32)).astype(BF16)
    out = pltpu.make_async_copy(held_o, go_hbm, in_sem.at[0])
    out.start()

    def settle_down(c, carry):
        down_copy(c).wait_send()
        down_out(c).wait()
        return carry

    def settle_up(i, carry):
        up_copy(i).wait_send()
        up_out(i).wait()
        return carry

    lax.fori_loop(0, chunks, settle_down, 0)
    lax.fori_loop(0, half, settle_up, 0)
    last.wait_send()
    for k in range(2):
        for zh in range(2):
            down_across(k, zh).wait()
            for i in range(half):
                up_across(i, k, zh).wait()
    out.wait()


def middle(everyone, ctx_size, mixed, x, teacher, slot_col, total, wo, wu, wd):
    count, width = x.shape
    hidden = wd.shape[0]
    chunks = hidden // CHUNK
    dma = pltpu.SemaphoreType.DMA
    vm = pltpu.VMEM
    return pl.pallas_call(
        functools.partial(middle_kernel, everyone, ctx_size),
        out_shape=[
            shaped(count, width),
            shaped(count, width, dtype=F32),
            shaped(count, width),
            shaped(8, width, dtype=F32),
            shaped(width, width // 2),
            shaped(8, width // 8, hidden // 2),
            shaped(hidden, width // 2),
            shaped(2, 2, width // 16, hidden // 2),
            shaped(2, 2, hidden // 16, width // 2),
        ],
        in_specs=[VMEM] * 5 + [ANY] * 3,
        out_specs=[VMEM] * 4 + [ANY] * 5,
        scratch_shapes=[
            vm(wo.shape, BF16), vm(wu.shape, BF16), vm(wd.shape, BF16),
            vm((count, hidden), BF16), vm((count, hidden), F32),
            vm((count, width), F32), vm((count, width), F32), vm((count, 1), F32),
            vm((count, width), BF16), vm((width, count), BF16), vm((count, width), F32),
            vm((count, width), BF16), vm((count, CHUNK), BF16),
            vm(wo.shape, BF16), vm((chunks // 2, 8, width // 8, CHUNK), BF16), vm(wd.shape, BF16),
            vm((width, width // 2), BF16), vm((chunks // 2, 8, width // 8, CHUNK), BF16), vm((hidden, width // 2), BF16),
            dma((3,)), dma((chunks + chunks // 2,)), dma((chunks + chunks // 2 + 1,)), dma((chunks + chunks // 2 + 1,)),
            dma((4 + 2 * chunks,)), dma((4 + 2 * chunks,)),
        ],
        compiler_params=pltpu.CompilerParams(
            collective_id=2, has_side_effects=True, vmem_limit_bytes=62 * 2**20
        ),
        name="dense_middle",
    )(mixed, x, teacher, slot_col, total, wo, wu, wd)


def local(tokens, teacher, clusters, segments, counted, w_qkv, w_out, w_up, w_down, norms):
    x_rows = tokens[0]
    tok_count, model_dim = x_rows.shape
    ctx_size, wsh_size = lax.axis_size("ctx"), lax.axis_size("wsh")
    mixed, x_turned, fq, fo, fu, fd, *kept, total = forward(
        x_rows, clusters[0], segments, counted, norms, (w_qkv, w_out, w_up, w_down)
    )
    everyone = float(tok_count * ctx_size * wsh_size)
    result, grad_first, grad_mixed, small, go, gu, gd, *nears = middle(
        everyone, float(ctx_size), mixed, x_rows, teacher[0], kept[-1], total,
        fo.reshape(-1, model_dim), fu, fd.reshape(-1, model_dim),
    )
    grad_tokens, final_qkv, final_out, final_up, final_down, final_norms, loss = backward(
        grad_mixed, grad_first, small, x_turned, fq, kept,
        [g.reshape(2, 4, -1, g.shape[-1]) for g in (go, gu, gd)], nears,
    )
    return (
        result[None],
        grad_tokens[None],
        loss.reshape(()),
        final_qkv.T,
        final_out.T,
        final_up,
        final_down.T,
        final_norms,
    )


def solution(mesh):
    placed = (
        P("wsh", "ctx", None),
        P("wsh", "ctx", None),
        P("wsh", None, "ctx"),
        P("wsh", "ctx"),
        P("wsh", "ctx"),
        P("wsh", None),
        P("wsh", None),
        P("wsh", None),
        P("wsh", None),
        P(None, "wsh"),
    )
    return jax.shard_map(
        local,
        mesh=mesh,
        in_specs=placed,
        out_specs=(
            P("wsh", "ctx", None),
            P("wsh", "ctx", None),
            P(),
            P("wsh", "ctx"),
            P("wsh", "ctx"),
            P("wsh", "ctx"),
            P("wsh", "ctx"),
            P(None, ("ctx", "wsh")),
        ),
        check_vma=False,
    )
```

```python
import functools
import jax
import jax.numpy as jnp
from jax import lax
from jax.experimental import pallas as pl
from jax.experimental.pallas import tpu as pltpu
from jax.sharding import PartitionSpec as P

MESH = pl.DeviceIdType.MESH
BF16 = jnp.bfloat16
F32 = jnp.float32


class Place:
    def __init__(self):
        self.ctx = lax.axis_index("ctx")
        self.wsh = lax.axis_index("wsh")
        self.zlo = self.ctx // 8
        self.y = (self.ctx // 2) % 4
        self.core = self.ctx % 2
        self.zhi = self.wsh // 4
        self.x = self.wsh % 4

    def at(self, zlo=None, y=None, core=None, zhi=None, x=None):
        zlo = self.zlo if zlo is None else zlo
        y = self.y if y is None else y
        core = self.core if core is None else core
        zhi = self.zhi if zhi is None else zhi
        x = self.x if x is None else x
        return (zlo * 8 + y * 2 + core, zhi * 4 + x)

    def sibling(self):
        return self.at(core=1 - self.core)

    def x_peer(self, step):
        return self.at(x=(self.x + step) % 4)

    def y_peer(self, step):
        return self.at(y=(self.y + step) % 4)

    def z_peer(self, step):
        z = (self.zhi * 4 + self.zlo + step + 8) % 8
        return self.at(zlo=z % 4, zhi=z // 4)

    def plane(self):
        return [
            self.at(y=(self.y + d) % 4, core=(self.core + c) % 2)
            for d, c in ((0, 1), (1, 0), (1, 1), (2, 0), (2, 1), (3, 0), (3, 1))
        ]

    def rank(self):
        return self.y * 2 + self.core

    def z_far(self):
        return self.at(zhi=1 - self.zhi)

    def doubling(self):
        return (
            self.z_far(),
            self.sibling(),
            self.at(y=self.y + 1 - 2 * (self.y % 2)),
            self.at(y=(self.y + 2) % 4),
            self.at(x=self.x + 1 - 2 * (self.x % 2)),
            self.at(x=(self.x + 2) % 4),
            self.at(zlo=self.zlo + 1 - 2 * (self.zlo % 2)),
            self.at(zlo=(self.zlo + 2) % 4),
        )


def greet(devices):
    barrier = pltpu.get_barrier_semaphore()
    for device in devices:
        pl.semaphore_signal(barrier, inc=1, device_id=device, device_id_type=MESH)
    pl.semaphore_wait(barrier, len(devices))


def remote(source, target, send_sem, recv_sem, device):
    return pltpu.make_async_remote_copy(
        src_ref=source,
        dst_ref=target,
        send_sem=send_sem,
        recv_sem=recv_sem,
        device_id=device,
        device_id_type=MESH,
    )


def half_of(width, which):
    half = width // 2
    return pl.ds(pl.multiple_of(which * half, 128), half)


class Doubling:
    def __init__(self, place, tile, slots, send_sems, recv_sems):
        self.partners = place.doubling()
        self.tile, self.slots = tile, slots
        self.send_sems, self.recv_sems = send_sems, recv_sems
        self.step = 0
        self.copies = []

    def start(self):
        k = self.step
        copy = remote(
            self.tile.at[k], self.slots.at[k], self.send_sems.at[k], self.recv_sems.at[k], self.partners[k]
        )
        copy.start()
        self.copies.append(copy)

    def advance(self):
        k = self.step
        self.copies[k].wait_recv()
        self.tile[k + 1] = self.tile[k] + self.slots[k]
        self.step = k + 1
        if self.step < 8:
            self.start()

    def drain(self):
        for copy in self.copies:
            copy.wait_send()


NEG = -1e30
NT = (((1,), (1,)), ((), ()))
TN = (((0,), (0,)), ((), ()))


def matmul(left, right, dims=(((1,), (0,)), ((), ()))):
    return lax.dot_general(left, right, dims, preferred_element_type=F32)


class Gather:
    def __init__(self, place, shard, full, send_sems, recv_sems, local_sem):
        self.place, self.shard, self.full = place, shard, full
        self.send_sems, self.recv_sems = send_sems, recv_sems
        self.rows = shard.shape[0]
        self.lanes = half_of(shard.shape[1], place.core)
        self.local = pltpu.make_async_copy(shard, full.at[place.wsh], local_sem)
        self.copies = {}

    def part(self, index, which=None):
        block = self.full.at[index]
        if which is None:
            return block.at[:, self.lanes]
        half = self.rows // 2
        return block.at[which * half : (which + 1) * half, self.lanes]

    def send(self, k, source, target, device):
        copy = remote(source, target, self.send_sems.at[k], self.recv_sems.at[k], device)
        copy.start()
        self.copies[k] = copy

    def own(self, far, step):
        return (far * 4) + (self.place.x + step + 4) % 4

    def start_z(self):
        place = self.place
        self.local.start()
        self.send(2, self.shard.at[:, self.lanes], self.part(place.wsh), place.z_far())

    def step_z(self, k, source, block, step):
        part = self.part(block)
        return remote(
            part if source is None else source, part, self.send_sems.at[2 + 17 * k], self.recv_sems.at[2],
            self.place.z_peer(step),
        )

    def start_run(self):
        self.local.start()
        own = self.shard.at[:, self.lanes]
        for end, step in ((3, 1), (0, -1)):
            @pl.when(self.place.zlo == end)
            def _(step=step):
                self.step_z(0, own, self.place.wsh, step).start()

    def pass_run(self):
        far = self.own(1 - self.place.zhi, 0)
        for end, step in ((0, 1), (3, -1)):
            @pl.when(self.place.zlo == end)
            def _(step=step):
                copy = self.step_z(1, None, far, step)
                copy.wait_recv()
                copy.start()

    def from_run(self):
        place = self.place
        index = self.own(1 - place.zhi, 0)

        @pl.when(jnp.logical_or(place.zlo == 1, place.zlo == 2))
        def _():
            self.step_z(0, None, index, 1).wait_recv()

        self.send(10, self.part(index), self.part(index), place.x_peer(1))
        self.send(11, self.part(index), self.part(index), place.x_peer(3))
        self.send(9, self.part(index), self.part(index), place.sibling())

    def drain_run(self):
        @pl.when(jnp.logical_or(self.place.zlo == 0, self.place.zlo == 3))
        def _():
            for k in range(2):
                self.step_z(k, None, self.place.wsh, 1).wait_send()

    def start_x(self):
        place = self.place
        self.send(0, self.shard.at[:, self.lanes], self.part(place.wsh), place.x_peer(1))
        self.send(1, self.shard.at[:, self.lanes], self.part(place.wsh), place.x_peer(3))

    def pass_on(self, zh, base):
        place = self.place
        left, right = self.own(zh, -1), self.own(zh, 1)
        self.copies[base].wait_recv()
        self.send(base + 3, self.part(left, 0), self.part(left, 0), place.x_peer(1))
        self.send(base + 5, self.part(left), self.part(left), place.sibling())
        self.copies[base + 1].wait_recv()
        self.send(base + 4, self.part(right, 1), self.part(right, 1), place.x_peer(3))
        self.send(base + 6, self.part(right), self.part(right), place.sibling())

    def opposite(self, zh, base):
        place = self.place
        index = self.own(zh, 2)
        for which in range(2):
            self.copies[base + 3 + which].wait_recv()
            self.send(base + 7 + which, self.part(index, which), self.part(index, which), place.sibling())

    def near(self):
        self.pass_on(self.place.zhi, 0)

    def near_opposite(self):
        self.opposite(self.place.zhi, 0)

    def from_z(self):
        place = self.place
        index = self.own(1 - place.zhi, 0)
        self.copies[2].wait_recv()
        self.send(10, self.part(index), self.part(index), place.x_peer(1))
        self.send(11, self.part(index), self.part(index), place.x_peer(3))
        self.send(9, self.part(index), self.part(index), place.sibling())

    def far(self):
        self.pass_on(1 - self.place.zhi, 10)

    def far_opposite(self):
        self.opposite(1 - self.place.zhi, 10)

    def finish(self):
        self.local.wait()
        for k in (5, 6, 7, 8, 9, 15, 16, 17, 18):
            self.copies[k].wait_recv()

    def drain(self):
        for k in self.copies:
            self.copies[k].wait_send()


def head_mask(which):
    lane = lax.broadcasted_iota(jnp.int32, (1, 128), 1)
    return jnp.where((lane // 64) == which, 1.0, 0.0).astype(BF16)


def to_slots(slot_row, head, count):
    row = slot_row[pl.ds(head, 1), :]
    iota = lax.broadcasted_iota(jnp.int32, (count, count), 0).astype(F32)
    return jnp.where(iota == row, 1.0, 0.0).astype(BF16)


def to_tokens(slot_col, head, count):
    lane = lax.broadcasted_iota(jnp.int32, slot_col.shape, 1)
    column = jnp.sum(jnp.where(lane == head, slot_col[...], 0.0), axis=1, keepdims=True)
    iota = lax.broadcasted_iota(jnp.int32, (count, count), 1).astype(F32)
    return jnp.where(iota == column, 1.0, 0.0).astype(BF16)


def pair_select(first, second):
    lane = lax.broadcasted_iota(jnp.int32, first.shape, 1)
    return jnp.where((lane // 64) % 2 == 0, first, second)


def heads_home(turned):
    return jnp.concatenate([turned[0:64, 0:128], turned[64:128, 128:256]], axis=0).T


def make_slots(clusters, segments, counted, slot_row, slot_col, labels):
    heads, count = clusters.shape
    groups = lax.shift_right_logical(clusters[...], 2)
    iota = lax.broadcasted_iota(jnp.int32, (32, count), 0)
    before = lax.broadcasted_iota(jnp.int32, (count, count), 0)
    after = lax.broadcasted_iota(jnp.int32, (count, count), 1)
    upper = jnp.where(before <= after, 1.0, 0.0).astype(BF16)
    hot = [jnp.where(groups[h : h + 1, :] == iota, 1.0, 0.0) for h in range(heads)]
    counts = matmul(jnp.concatenate(hot, axis=0).astype(BF16), upper)
    group_f = groups.astype(F32)
    rows = []
    for h in range(heads):
        rank = jnp.sum(counts[32 * h : 32 * h + 32] * hot[h], axis=0, keepdims=True)
        rows.append(group_f[h : h + 1] * 16.0 + rank - 1.0)
    slots = jnp.concatenate(rows + [counted[...].astype(F32), jnp.zeros((127 - heads, count), F32)], axis=0)
    slot_row[...] = slots[:16]
    slot_col[...] = slots.T
    label = (segments[0:1, :] * 4 + (clusters[...] & 3)).astype(F32)
    labels[...] = jnp.concatenate([label, jnp.zeros((128 - heads, count), F32)], axis=0).T.astype(BF16)


def rows16(j):
    return slice(16 * j, 16 * j + 16)


def forward_kernel(
    x, clusters, segments, counted, norms, wq, wo, wu, wd,
    mixed, x_turned, fq_out, fo, fu, fd, got_out, before_out, after_out, logsum, hot_out, cold_out, slot_row, slot_col, total,
    pieces, fq, got, before, after, hot, cold,
    labels, sent_labels, got_labels, before_labels, after_labels, wide_labels, sent, out, back,
    tile, slots,
    w_send, w_recv, w_local, t_send, t_recv, a_send, a_recv, a_local, z_send, z_recv, b_send, b_recv, b_local, k_sem,
):
    place = Place()
    plane, rank = place.plane(), place.rank()
    up, down = place.z_peer(1), place.z_peer(-1)
    kept = []

    def keep(source, target):
        copy = pltpu.make_async_copy(source, target, k_sem.at[len(kept)])
        copy.start()
        kept.append(copy)

    partners = place.doubling()
    for g in range(3):
        for b in range(2):
            for t in range(3):
                lane = t * 768 + (2 * g + b) * 128
                pieces[g, :, b * 384 + t * 128 : b * 384 + t * 128 + 128] = wq[:, lane : lane + 128]
    greet(
        plane + [place.x_peer(1), place.x_peer(2), place.x_peer(3), place.z_far(), up, down, partners[6], partners[7]]
    )
    weights = [
        Gather(place, shard, full, w_send.at[i], w_recv.at[i], w_local.at[i])
        for i, (shard, full) in enumerate(
            [(pieces.at[g], fq.at[g]) for g in range(3)] + [(wo, fo), (wu, fu), (wd, fd)]
        )
    ]
    first, second, third, w_out, w_up, w_down = weights
    rest = (w_out, w_up, w_down)
    tile[0] = jnp.zeros_like(tile[0])
    tile[0, 0:4, 0 : norms.shape[1]] = norms[...].astype(F32)
    tile[0] = pltpu.roll(tile[0], place.wsh * norms.shape[1], 1)
    lane_zero = lax.broadcasted_iota(jnp.int32, (1, tile.shape[2]), 1) == 0
    tile[0, 4:5, :] = jnp.where(lane_zero, jnp.sum(counted[...].astype(F32), axis=1, keepdims=True), 0.0)
    doubling = Doubling(place, tile, slots, t_send, t_recv)
    doubling.start()
    first.start_z()
    first.start_x()
    count = x.shape[0]
    make_slots(clusters, segments, counted, slot_row, slot_col, labels)

    second.start_z()
    second.start_x()
    sent_labels[...] = jnp.zeros_like(sent_labels)

    def move_labels(head, carry):
        lane = lax.broadcasted_iota(jnp.int32, (count, 128), 1)
        moved = matmul(to_slots(slot_row, head, count), labels[...])
        sent_labels[...] = jnp.where(lane == head, moved, sent_labels[...])
        return carry

    lax.fori_loop(0, 6, move_labels, 0)
    first.near()
    third.start_z()
    third.start_x()
    lax.fori_loop(6, 12, move_labels, 0)
    labels[...] = sent_labels[...].astype(BF16)

    def block(which):
        return pl.ds(pl.multiple_of(which * 64, 64), 64)

    def ranks():
        return [dev[0] % 8 for dev in plane]

    label_copies = [
        remote(labels.at[block(to)], got_labels.at[rank], a_send.at[6, k], a_recv.at[6, k], plane[k])
        for k, to in enumerate(ranks())
    ]
    for copy in label_copies:
        copy.start()
    own_labels = pltpu.make_async_copy(labels.at[block(rank)], got_labels.at[rank], a_local.at[6])
    own_labels.start()
    first.from_z()
    second.near()
    first.near_opposite()
    doubling.advance()
    x_turned[...] = x[...].astype(F32).T.astype(BF16)
    doubling.advance()
    second.from_z()
    first.far()
    third.near()
    second.near_opposite()
    doubling.advance()
    third.from_z()
    own_labels.wait()
    for copy in label_copies:
        copy.wait_recv()
    label_up = remote(got_labels.at[4:8], before_labels, z_send.at[6, 0], z_recv.at[6, 0], up)
    label_down = remote(got_labels.at[0:4], after_labels, z_send.at[6, 1], z_recv.at[6, 1], down)
    label_up.start()
    label_down.start()
    for w in rest:
        w.start_run()
    first.far_opposite()
    first.finish()

    def make_hot(head, carry):
        lane = lax.broadcasted_iota(jnp.int32, (256, 128), 1)
        for j in range(4):
            column = jnp.sum(jnp.where(lane == head, wide_labels[j], 0.0), axis=1, keepdims=True)
            same = lane.astype(F32) == column
            cold[head * 4 + j] = jnp.where(same, 0.0, NEG).astype(BF16)
            hot[head * 4 + j] = jnp.where(same, 1.0, 0.0)[64:192].astype(BF16)
        return carry

    def send_copies(p, fn):
        for k, to in enumerate(ranks()):
            fn(remote(sent.at[p, block(to)], got.at[p, rank], a_send.at[p, k], a_recv.at[p, k], plane[k]))

    def own_copy(p):
        return pltpu.make_async_copy(sent.at[p, block(rank)], got.at[p, rank], a_local.at[p])

    def project(g):
        value = matmul(x[...], fq[g].reshape(768, 768))
        lane = lax.broadcasted_iota(jnp.int32, (1, 384), 1)
        scale = jnp.where(lane < 128, 0.125, 1.0)
        for b in range(2):
            p = 2 * g + b
            rows = (value[:, b * 384 : b * 384 + 384] * scale).astype(BF16)
            moved = [matmul(to_slots(slot_row, 2 * p + a, count), rows) for a in range(2)]
            sent[p] = pair_select(moved[0], moved[1]).astype(BF16)
            send_copies(p, lambda copy: copy.start())
            own_copy(p).start()

    project(0)
    second.far()
    third.near_opposite()
    third.far()
    second.far_opposite()
    second.finish()
    doubling.advance()
    for w in rest:
        w.start_x()
    project(1)
    w_out.pass_run()
    w_up.pass_run()
    third.far_opposite()
    third.finish()
    project(2)
    w_down.pass_run()
    keep(fq, fq_out)
    label_up.wait_recv()
    label_down.wait_recv()
    for j in range(4):
        wide_labels[j, 0:64] = jnp.where(
            place.zlo == 0, -1.0, before_labels[:, rows16(j), :].reshape(64, 128).astype(F32)
        )
        wide_labels[j, 64:192] = got_labels[:, rows16(j), :].reshape(128, 128).astype(F32)
        wide_labels[j, 192:256] = jnp.where(
            place.zlo == 3, -1.0, after_labels[:, rows16(j), :].reshape(64, 128).astype(F32)
        )
    lax.fori_loop(0, 12, make_hot, 0)
    keep(hot, hot_out)
    keep(cold, cold_out)
    w_out.near()
    w_out.from_run()
    w_up.near()
    doubling.advance()

    def halo(p):
        return (
            remote(got.at[p, 4:8, :, 128:384], before.at[p], z_send.at[p, 0], z_recv.at[p, 0], up),
            remote(got.at[p, 0:4, :, 128:384], after.at[p], z_send.at[p, 1], z_recv.at[p, 1], down),
        )

    def back_copies(p, fn):
        for k, to in enumerate(ranks()):
            fn(remote(out.at[p, to], back.at[p, rank], b_send.at[p, k], b_recv.at[p, k], plane[k]))

    def own_back(p):
        return pltpu.make_async_copy(out.at[p, rank], back.at[p, rank], b_local.at[p])

    def arrive(p):
        own_copy(p).wait()
        send_copies(p, lambda copy: copy.wait_recv())
        for copy in halo(p):
            copy.start()

    masks = [head_mask(a) for a in range(2)]

    def attend(p):
        for copy in halo(p):
            copy.wait_recv()
        for j in range(4):
            r = rows16(j)
            query = got[p, :, r, 0:128].reshape(128, 128)
            keys = jnp.concatenate(
                [before[p, :, r, 0:128].reshape(64, 128), got[p, :, r, 128:256].reshape(128, 128),
                 after[p, :, r, 0:128].reshape(64, 128)], axis=0)
            values = jnp.concatenate(
                [before[p, :, r, 128:256].reshape(64, 128), got[p, :, r, 256:384].reshape(128, 128),
                 after[p, :, r, 128:256].reshape(64, 128)], axis=0)
            probs = []
            for a in range(2):
                head = 2 * p + a
                scores = matmul(
                    jnp.concatenate([keys, cold[head * 4 + j]], axis=1),
                    jnp.concatenate([query * masks[a], hot[head * 4 + j]], axis=1), NT)
                top = jnp.max(scores, axis=0, keepdims=True)
                raised = jnp.exp(scores - top)
                sums = jnp.sum(raised, axis=0, keepdims=True)
                probs.append((raised * (1.0 / sums)).astype(BF16))
                logsum[j, pl.ds(head, 1), :] = top + jnp.log(sums)
            out[p, :, r, :] = heads_home(matmul(values, jnp.concatenate(probs, axis=1), TN)).astype(BF16).reshape(8, 16, 128)
        back_copies(p, lambda copy: copy.start())
        own_back(p).start()

    def home(p):
        own_back(p).wait()
        back_copies(p, lambda copy: copy.wait_recv())
        rows = back[p].reshape(count, 128)
        moved = [matmul(to_tokens(slot_col, 2 * p + a, count), rows) for a in range(2)]
        mixed[:, p * 128 : p * 128 + 128] = pair_select(moved[0], moved[1]).astype(BF16)

    arrive(0)
    w_up.from_run()
    arrive(1)
    attend(0)
    w_down.near()
    w_out.near_opposite()
    arrive(2)
    attend(1)
    w_down.from_run()
    w_up.near_opposite()
    doubling.advance()
    arrive(3)
    attend(2)
    home(0)
    w_out.far()
    arrive(4)
    attend(3)
    home(1)
    w_up.far()
    w_down.near_opposite()
    arrive(5)
    attend(4)
    home(2)
    home(3)
    doubling.advance()

    def settle_out(p, carry):
        send_copies(p, lambda copy: copy.wait_send())
        return carry

    def settle_back(p, carry):
        back_copies(p, lambda copy: copy.wait_send())
        for copy in halo(p):
            copy.wait_send()
        return carry

    lax.fori_loop(0, 6, settle_out, 0)
    for copy in label_copies + [label_up, label_down]:
        copy.wait_send()
    for w in (first, second, third):
        w.drain()
    w_down.far()
    attend(5)
    keep(got, got_out)
    keep(before, before_out)
    keep(after, after_out)
    w_out.far_opposite()
    w_up.far_opposite()
    home(4)
    lax.fori_loop(0, 5, settle_back, 0)
    w_down.far_opposite()
    home(5)
    doubling.advance()
    for w in rest:
        w.finish()
    total[...] = tile[8]
    settle_back(5, 0)
    for w in rest:
        w.drain()
        w.drain_run()
    for copy in kept:
        copy.wait()
    doubling.drain()


ANY = pl.BlockSpec(memory_space=pl.ANY)
VMEM = pl.BlockSpec(memory_space=pltpu.VMEM)


def shaped(*shape, dtype=BF16):
    return jax.ShapeDtypeStruct(shape, dtype)


def forward(x, clusters, segments, counted, norms, shards):
    count, width = x.shape
    dma = pltpu.SemaphoreType.DMA
    return pl.pallas_call(
        forward_kernel,
        out_shape=[
            shaped(*x.shape),
            shaped(width, count),
            shaped(3, 8, shards[0].shape[0], 768),
            *[shaped(8, *w.shape) for w in shards[1:]],
            shaped(6, 8, 64, 384),
            shaped(6, 4, 64, 256),
            shaped(6, 4, 64, 256),
            shaped(4, 16, 128, dtype=F32),
            shaped(48, 128, 128),
            shaped(48, 256, 128),
            shaped(16, count, dtype=F32),
            shaped(count, 128, dtype=F32),
            shaped(8, width, dtype=F32),
        ],
        in_specs=[VMEM] * 9,
        out_specs=[VMEM] * 2 + [ANY] * 7 + [VMEM] + [ANY] * 2 + [VMEM] * 3,
        scratch_shapes=[
            pltpu.VMEM((3, shards[0].shape[0], 768), BF16),
            pltpu.VMEM((3, 8, shards[0].shape[0], 768), BF16),
            pltpu.VMEM((6, 8, 64, 384), BF16),
            pltpu.VMEM((6, 4, 64, 256), BF16),
            pltpu.VMEM((6, 4, 64, 256), BF16),
            pltpu.VMEM((48, 128, 128), BF16),
            pltpu.VMEM((48, 256, 128), BF16),
            pltpu.VMEM((count, 128), BF16),
            pltpu.VMEM((count, 128), F32),
            pltpu.VMEM((8, 64, 128), BF16),
            pltpu.VMEM((4, 64, 128), BF16),
            pltpu.VMEM((4, 64, 128), BF16),
            pltpu.VMEM((4, 256, 128), F32),
            pltpu.VMEM((6, count, 384), BF16),
            pltpu.VMEM((6, 8, 64, 128), BF16),
            pltpu.VMEM((6, 8, 64, 128), BF16),
            pltpu.VMEM((9, 8, width), F32),
            pltpu.VMEM((8, 8, width), F32),
            dma((6, 20)), dma((6, 19)), dma((6,)), dma((8,)), dma((8,)),
            dma((7, 7)), dma((7, 7)), dma((7,)), dma((7, 2)), dma((7, 2)),
            dma((6, 7)), dma((6, 7)), dma((6,)), dma((6,)),
        ],
        compiler_params=pltpu.CompilerParams(
            collective_id=0, has_side_effects=True, vmem_limit_bytes=60 * 2**20
        ),
        name="forward_attention",
    )(x, clusters, segments, counted, norms, *shards)


class Reduce:
    def __init__(self, place, held, near, far, sum_x, from_y, sum_y, from_z, out, send_sems, recv_sems, grad=None, source=None, near_source=None, load_sems=None):
        self.place, self.held, self.grad = place, held, grad
        self.near, self.far, self.sum_x, self.from_y = near, far, sum_x, from_y
        self.sum_y, self.from_z, self.out = sum_y, from_z, out
        self.send_sems, self.recv_sems = send_sems, recv_sems
        self.rows, self.half = held.shape[2], held.shape[3]
        self.window = out.shape[1]
        self.owner = place.y // 2
        self.z = place.zhi * 4 + place.zlo
        self.final = jnp.logical_and(place.zhi == self.owner, place.core == place.zlo // 2)
        self.copies = {}
        if source is not None:
            self.loads = [pltpu.make_async_copy(source, held, load_sems.at[0])]
        self.begun = near_source is not None
        if self.begun:
            self.loads.append(pltpu.make_async_copy(near_source, near, load_sems.at[1]))

    def send(self, k, source, target, device):
        copy = remote(source, target, self.send_sems.at[k], self.recv_sems.at[k], device)
        copy.start()
        self.copies[k] = copy

    def each(self, count, body):
        def step(i, carry):
            body(pl.ds(pl.multiple_of(i * 48, 16), 48))
            return carry

        lax.fori_loop(0, count // 48, step, 0)

    def after(self, rows, offset):
        return pl.ds(pl.multiple_of(rows.start + offset, 16), rows.size)

    def blocks(self, body):
        def step(zh, carry):
            body(zh)
            return carry

        lax.fori_loop(0, 2, step, 0)

    def start(self):
        place = self.place
        self.send(0, self.grad.at[:, :, :, half_of(2 * self.half, 1 - place.core)], self.held, place.sibling())

    def add_pair(self, xx):
        mine = half_of(2 * self.half, self.place.core)

        def block(zh):
            def body(rows):
                self.held[zh, xx, rows, :] = (
                    self.grad[zh, xx, rows, mine].astype(F32) + self.held[zh, xx, rows, :].astype(F32)
                ).astype(BF16)

            self.each(self.rows, body)

        self.blocks(block)

    def to_opposite(self):
        place = self.place
        half = self.rows // 2
        opposite = (place.x + 2) % 4
        if self.grad is None:
            self.loads[0].wait()
        else:
            self.copies[0].wait_recv()
            self.add_pair(opposite)
        self.send(1, self.held.at[:, opposite, 0:half], self.near.at[0], place.x_peer(1))
        self.send(2, self.held.at[:, opposite, half : self.rows], self.near.at[1], place.x_peer(3))
        if self.grad is not None:
            for step in (1, 3, 0):
                self.add_pair((place.x + step) % 4)

    def to_near(self):
        place = self.place
        half = self.rows // 2
        if self.begun:
            for copy in self.loads:
                copy.wait()
        for k, step in enumerate((1, 3)):
            to = (place.x + step) % 4
            if not self.begun:
                self.copies[1 + k].wait_recv()

            def block(zh, k=k, to=to):
                def body(rows):
                    there = self.after(rows, k * half)
                    self.held[zh, to, there, :] = (
                        self.held[zh, to, there, :].astype(F32) + self.near[k, zh, rows, :].astype(F32)
                    ).astype(BF16)

                self.each(half, body)

            self.blocks(block)
            self.send(3 + k, self.held.at[:, to], self.far.at[k], place.x_peer(step))

    def to_y(self):
        place = self.place
        half = self.rows // 2
        for k in range(2):
            self.copies[3 + k].wait_recv()

        def block(zh):
            def body(rows):
                value = self.held[zh, place.x, rows, :].astype(F32)
                value = value + self.far[0, zh, rows, :].astype(F32) + self.far[1, zh, rows, :].astype(F32)
                self.sum_x[zh, rows, :] = value.astype(BF16)

            self.each(self.rows, body)

        self.blocks(block)
        for k, d in enumerate((1, 2, 3)):
            to = (place.y + d) % 4
            part = pl.ds(pl.multiple_of((to % 2) * half, 16), half)
            self.send(5 + k, self.sum_x.at[to // 2, part], self.from_y.at[k], place.y_peer(d))

    def lanes(self, zlo):
        offset = (zlo % 2) * (self.half - self.window)
        return pl.ds(pl.multiple_of(offset, 128), self.window)

    def z_copy(self, k):
        place = self.place
        zlo = 2 * place.core + k
        return remote(
            self.sum_y.at[:, self.lanes(zlo)], self.from_z.at[self.z],
            self.send_sems.at[8 + k], self.recv_sems.at[8 + self.z], place.at(zlo=zlo, zhi=self.owner),
        )

    def is_target(self, k):
        place = self.place
        return jnp.logical_and(place.zhi == self.owner, place.zlo == 2 * place.core + k)

    def to_z(self):
        place = self.place
        half = self.rows // 2
        for k in range(3):
            self.copies[5 + k].wait_recv()

        def body(rows):
            value = self.sum_x[self.owner, self.after(rows, (place.y % 2) * half), :].astype(F32)
            for k in range(3):
                value = value + self.from_y[k, rows, :].astype(F32)
            self.sum_y[rows, :] = value.astype(BF16)

        self.each(half, body)
        for k in range(2):
            @pl.when(jnp.logical_not(self.is_target(k)))
            def _(k=k):
                self.z_copy(k).start()

    def spread_copy(self, k, device):
        half = self.rows // 2
        part = self.out.at[pl.ds(pl.multiple_of((self.place.y % 2) * half, 16), half)]
        return remote(part, part, self.send_sems.at[10 + k], self.recv_sems.at[16 + self.place.y % 2], device)

    def spread(self):
        half = self.rows // 2

        @pl.when(self.final)
        def _():
            self.from_z[self.z] = self.sum_y[:, self.lanes(self.place.zlo)]
            for z in range(8):
                @pl.when(self.z != z)
                def _(z=z):
                    part = self.from_z.at[z]
                    remote(part, part, self.send_sems.at[8], self.recv_sems.at[8 + z], self.place.sibling()).wait_recv()

            def body(rows):
                there = self.after(rows, (self.place.y % 2) * half)
                value = self.from_z[0, rows, :].astype(F32)
                for z in range(1, 8):
                    value = value + self.from_z[z, rows, :].astype(F32)
                self.out[there, :] = value.astype(BF16)

            self.each(half, body)
            for k, device in enumerate(self.place.plane()):
                self.spread_copy(k, device).start()

    def finish(self):
        half = self.rows // 2
        for k in range(2):
            part = self.out.at[k * half : (k + 1) * half]

            @pl.when(jnp.logical_not(jnp.logical_and(self.final, self.place.y % 2 == k)))
            def _(k=k, part=part):
                remote(part, part, self.send_sems.at[10], self.recv_sems.at[16 + k], self.place.sibling()).wait_recv()

    def drain(self):
        for k in self.copies:
            self.copies[k].wait_send()
        for k in range(2):
            @pl.when(jnp.logical_not(self.is_target(k)))
            def _(k=k):
                self.z_copy(k).wait_send()

        @pl.when(self.final)
        def _():
            for k, device in enumerate(self.place.plane()):
                self.spread_copy(k, device).wait_send()


def reduce_scratch(rows, half, window):
    return [
        pltpu.VMEM((2, 4, rows, half), BF16),
        pltpu.VMEM((2, 2, rows // 2, half), BF16),
        pltpu.VMEM((2, 2, rows, half), BF16),
        pltpu.VMEM((2, rows, half), BF16),
        pltpu.VMEM((3, rows // 2, half), BF16),
        pltpu.VMEM((rows // 2, half), BF16),
        pltpu.VMEM((8, rows // 2, window), BF16),
        pltpu.VMEM((rows, window), BF16),
    ]


def cut(value, offset, target):
    rows, width = value.shape
    first = pltpu.roll(value, (width - offset) % width, 1)[:, 0:128]
    if target.shape[0] == rows:
        target[...] = first[:, : target.shape[1]]
        return
    if rows % 128:
        first = jnp.concatenate([first, jnp.zeros((128 - rows % 128, 128), F32)], axis=0)
    target[...] = first.T[: target.shape[0], :rows]


ORDER = (0, 3, 1, 4, 2, 5)


def backward_kernel(*refs):
    (grad_mixed, grad_first, logsum, slot_row, slot_col, small, x_hbm, fq_hbm, got_hbm, before_hbm, after_hbm,
     hot_hbm, cold_hbm, go, gu, gd, near_u, near_d) = refs[:18]
    refs = refs[2:]
    grad_x, out_q, out_o, out_u, out_d, norms_out, loss_out = refs[16:23]
    x_turned, fq, got, before, after, hot, cold = refs[23:30]
    sent, got_grad, grads, to_before, to_after, from_before, from_after, back = refs[30:38]
    grads_q = refs[38:41]
    reduce_refs = [refs[41 + 8 * i : 49 + 8 * i] for i in range(6)]
    (tile, slots, a_send, a_recv, a_local, z_send, z_recv, b_send, b_recv, b_local,
     t_send, t_recv, r_send, r_recv, r_load, l_sem) = refs[89:]
    place = Place()
    plane, rank = place.plane(), place.rank()
    up, down = place.z_peer(1), place.z_peer(-1)
    loads = [
        pltpu.make_async_copy(source, target, l_sem.at[i])
        for i, (source, target) in enumerate(
            ((got_hbm, got), (before_hbm, before), (after_hbm, after), (hot_hbm, hot), (cold_hbm, cold),
             (fq_hbm, fq), (x_hbm, x_turned))
        )
    ]
    rest = [
        Reduce(
            place, *reduce_refs[i], r_send.at[i], r_recv.at[i], source=source, near_source=near, load_sems=r_load.at[i]
        )
        for i, (source, near) in enumerate(((go, None), (gu, near_u), (gd, near_d)))
    ]
    by_group = [
        Reduce(place, *reduce_refs[3 + i], r_send.at[3 + i], r_recv.at[3 + i], grad=grads_q[i]) for i in range(3)
    ]
    for r in (rest[2], rest[1], rest[0]):
        for copy in r.loads:
            copy.start()
    for copy in loads:
        copy.start()
    greet(plane + [place.x_peer(d) for d in (1, 2, 3)] + [place.z_peer(d) for d in range(1, 8)])
    sum_o, sum_u, sum_d = rest
    sum_o.to_opposite()
    tile[0] = small[...]
    doubling = Doubling(place, tile, slots, t_send, t_recv)
    doubling.start()
    count = grad_mixed.shape[0]
    ranks = [dev[0] % 8 for dev in plane]

    def block(which):
        return pl.ds(pl.multiple_of(which * 64, 64), 64)

    def send_copies(p, fn):
        for k, to in enumerate(ranks):
            fn(remote(sent.at[p, block(to)], got_grad.at[p, rank], a_send.at[p, k], a_recv.at[p, k], plane[k]))

    def own_copy(p):
        return pltpu.make_async_copy(sent.at[p, block(rank)], got_grad.at[p, rank], a_local.at[p])

    def leave(i, carry):
        p = i // 2 + 3 * (i % 2)
        rows = grad_mixed[:, pl.ds(pl.multiple_of(p * 128, 128), 128)]
        moved = [matmul(to_slots(slot_row, 2 * p + a, count), rows) for a in range(2)]
        sent[p] = pair_select(moved[0], moved[1]).astype(BF16)
        send_copies(p, lambda copy: copy.start())
        own_copy(p).start()
        return carry

    lax.fori_loop(0, 6, leave, 0)
    doubling.advance()
    sum_d.to_near()
    sum_u.to_near()
    for copy in loads[:5]:
        copy.wait()

    def halo(p):
        return (
            remote(to_after.at[p], from_before.at[p], z_send.at[p, 0], z_recv.at[p, 0], up),
            remote(to_before.at[p], from_after.at[p], z_send.at[p, 1], z_recv.at[p, 1], down),
        )

    def back_copies(p, fn):
        for k, to in enumerate(ranks):
            fn(remote(grads.at[p, to], back.at[p, rank], b_send.at[p, k], b_recv.at[p, k], plane[k]))

    def own_back(p):
        return pltpu.make_async_copy(grads.at[p, rank], back.at[p, rank], b_local.at[p])

    masks = [head_mask(a) for a in range(2)]

    def attend(p):
        own_copy(p).wait()
        send_copies(p, lambda copy: copy.wait_recv())
        for j in range(4):
            r = rows16(j)
            query = got[p, :, r, 0:128].reshape(128, 128)
            keys = jnp.concatenate(
                [before[p, :, r, 0:128].reshape(64, 128), got[p, :, r, 128:256].reshape(128, 128),
                 after[p, :, r, 0:128].reshape(64, 128)], axis=0)
            values = jnp.concatenate(
                [before[p, :, r, 128:256].reshape(64, 128), got[p, :, r, 256:384].reshape(128, 128),
                 after[p, :, r, 128:256].reshape(64, 128)], axis=0)
            grad = got_grad[p, :, r, :].reshape(128, 128)
            queries = [query * masks[a] for a in range(2)]
            grad_both = jnp.concatenate([grad * masks[a] for a in range(2)], axis=0)
            grad_probs = matmul(values, grad_both, NT)
            probs, grad_scores = [], []
            for a in range(2):
                head = 2 * p + a
                scores = matmul(
                    jnp.concatenate([keys, cold[head * 4 + j]], axis=1),
                    jnp.concatenate([queries[a], hot[head * 4 + j]], axis=1), NT)
                prob = jnp.exp(scores - logsum[j, pl.ds(head, 1), :])
                own = grad_probs[:, a * 128 : a * 128 + 128]
                delta = jnp.sum(prob * own, axis=0, keepdims=True)
                probs.append(prob.astype(BF16))
                grad_scores.append((prob * (own - delta)).astype(BF16))
            grad_scores = jnp.concatenate(grad_scores, axis=1)
            dk = matmul(grad_scores, jnp.concatenate(queries, axis=0))
            dv = matmul(jnp.concatenate(probs, axis=1), grad_both)
            dq = heads_home(matmul(keys, grad_scores, TN)) * 0.125
            both = jnp.concatenate([dk, dv], axis=1).astype(BF16)
            to_before[p, :, r, :] = both[0:64].reshape(4, 16, 256)
            to_after[p, :, r, :] = both[192:256].reshape(4, 16, 256)
            grads[p, :, r, 0:128] = dq.astype(BF16).reshape(8, 16, 128)
            grads[p, :, r, 128:384] = both[64:192].reshape(8, 16, 256)
        for copy in halo(p):
            copy.start()

    def give(p):
        for copy in halo(p):
            copy.wait_recv()
        for part, extra in ((slice(0, 4), from_before), (slice(4, 8), from_after)):
            grads[p, part, :, 128:384] = (
                grads[p, part, :, 128:384].astype(F32) + extra[p].astype(F32)
            ).astype(BF16)
        back_copies(p, lambda copy: copy.start())
        own_back(p).start()

    def home(p):
        own_back(p).wait()
        back_copies(p, lambda copy: copy.wait_recv())
        rows = back[p].reshape(count, 384)
        moved = [matmul(to_tokens(slot_col, 2 * p + a, count), rows) for a in range(2)]
        grad_qkv = pair_select(moved[0], moved[1]).astype(BF16)
        back[p] = grad_qkv.reshape(8, 64, 384)
        weight = matmul(x_turned[...], grad_qkv).astype(BF16)
        group, late = p % 3, p // 3
        for t, lane in enumerate((late, 2 + late, 4 + late)):
            grads_q[group][:, :, :, lane * 128 : lane * 128 + 128] = weight[:, t * 128 : t * 128 + 128].reshape(2, 4, 96, 128)

    def turn_back(i):
        rows = slice(i * 128, i * 128 + 128)
        value = grad_first[rows, :]
        for g in range(3):
            pair = [back[2 * g + b, 2 * i : 2 * i + 2].reshape(128, 384) for b in range(2)]
            value = value + matmul(jnp.concatenate(pair, axis=1), fq[g].reshape(768, 768), NT)
        grad_x[rows, :] = value

    attend(0)
    doubling.advance()
    attend(3)
    sum_o.to_near()
    attend(1)
    give(0)
    give(3)
    attend(4)
    give(1)
    doubling.advance()
    attend(2)
    give(4)
    sum_d.to_y()
    attend(5)
    give(2)
    give(5)
    for copy in loads[5:]:
        copy.wait()
    home(0)
    home(3)
    by_group[0].start()
    sum_u.to_y()
    home(1)
    doubling.advance()
    by_group[0].to_opposite()
    sum_o.to_y()
    home(4)
    by_group[1].start()
    sum_d.to_z()
    by_group[0].to_near()
    home(2)
    doubling.advance()
    by_group[1].to_opposite()
    home(5)
    by_group[2].start()
    doubling.advance()
    by_group[0].to_y()
    by_group[1].to_near()
    by_group[2].to_opposite()
    turn_back(0)
    sum_u.to_z()
    by_group[1].to_y()
    by_group[0].to_z()
    by_group[2].to_near()
    doubling.advance()
    sum_o.to_z()
    turn_back(1)
    sum_d.spread()
    by_group[1].to_z()
    turn_back(2)
    by_group[2].to_y()
    sum_u.spread()
    by_group[0].spread()
    sum_o.spread()
    by_group[2].to_z()
    by_group[1].spread()

    def settle(p, carry):
        send_copies(p, lambda copy: copy.wait_send())
        back_copies(p, lambda copy: copy.wait_send())
        for copy in halo(p):
            copy.wait_send()
        return carry

    lax.fori_loop(0, 6, settle, 0)
    seat = place.y * 2 + place.core
    for r, target in zip((sum_d, sum_u, sum_o), (out_d, out_u, out_o)):
        r.finish()
        width = r.half // 16
        offset = (place.zlo % 2) * (8 * width - (r.half - r.window)) + seat * width
        cut(r.out[...].astype(F32), offset, target)
    turn_back(3)
    doubling.advance()
    by_group[2].spread()
    total = tile[8]
    loss_out[...] = total[4:5, 0:1]
    all_width = total.shape[1]
    shift = (all_width - (place.ctx * 8 + place.wsh) * norms_out.shape[1]) % all_width
    norms_out[...] = pltpu.roll(total, shift, 1)[0:4, 0 : norms_out.shape[1]]
    for r in rest:
        r.drain()
    for r in by_group:
        r.finish()
    tiles = [by_group[g].out[:, i * 128 : i * 128 + 128].astype(F32) for i in range(3) for g in range(3)]
    width = 72
    cut(jnp.concatenate(tiles, axis=1), (place.zlo % 2) * 8 * width + seat * width, out_q)
    for r in by_group:
        r.drain()
    doubling.drain()


def backward(grad_mixed, grad_first, small, x_turned, fq, kept, halves, nears):
    got, before, after, logsum, hot, cold, slot_row, slot_col = kept
    count = grad_mixed.shape[0]
    dma = pltpu.SemaphoreType.DMA
    vm = pltpu.VMEM
    rows_in = (halves[2].shape[2],)
    shapes = [(96, 384, 256), (96, 1536, 768), (rows_in[0], 384, 256)] + [(96, 384, 384)] * 3
    reduce_refs = []
    for shape in shapes:
        reduce_refs += reduce_scratch(*shape)
    loaded = (x_turned, fq, got, before, after, hot, cold)
    results = pl.pallas_call(
        backward_kernel,
        out_shape=[
            shaped(*grad_first.shape, dtype=F32),
            shaped(72, 96, dtype=F32),
            shaped(24, 96, dtype=F32),
            shaped(96, 96, dtype=F32),
            shaped(24, 384, dtype=F32),
            shaped(4, small.shape[1] // 256, dtype=F32),
            shaped(1, 1, dtype=F32),
        ],
        in_specs=[VMEM] * 6 + [ANY] * 12,
        out_specs=[VMEM] * 7,
        scratch_shapes=[vm(array.shape, array.dtype) for array in loaded]
        + [
            vm((6, count, 128), BF16),
            vm((6, 8, 64, 128), BF16),
            vm((6, 8, 64, 384), BF16),
            vm((6, 4, 64, 256), BF16),
            vm((6, 4, 64, 256), BF16),
            vm((6, 4, 64, 256), BF16),
            vm((6, 4, 64, 256), BF16),
            vm((6, 8, 64, 384), BF16),
        ]
        + [vm((2, 4, 96, 768), BF16)] * 3
        + reduce_refs
        + [
            vm((9, *small.shape), F32),
            vm((8, *small.shape), F32),
            dma((6, 7)), dma((6, 7)), dma((6,)), dma((6, 2)), dma((6, 2)),
            dma((6, 7)), dma((6, 7)), dma((6,)),
            dma((8,)), dma((8,)), dma((6, 17)), dma((6, 18)), dma((3, 2)), dma((7,)),
        ],
        compiler_params=pltpu.CompilerParams(
            collective_id=1, has_side_effects=True, vmem_limit_bytes=62 * 2**20
        ),
        name="backward_attention",
    )(grad_mixed, grad_first, logsum, slot_row, slot_col, small, *loaded, *halves, *nears)
    return results


CHUNK = 512


def norm_rows(values):
    centered = values - jnp.mean(values, axis=-1, keepdims=True)
    scale = lax.rsqrt(jnp.mean(centered * centered, axis=-1, keepdims=True) + 1e-05)
    return centered * scale, scale


def norm_rows_back(grad, normed, scale, gain):
    weighted = grad * gain
    return scale * (
        weighted
        - jnp.mean(weighted, axis=-1, keepdims=True)
        - normed * jnp.mean(weighted * normed, axis=-1, keepdims=True)
    )


def middle_kernel(
    everyone, ctx_size,
    mixed, x, teacher, slot_col, total, wo_hbm, wu_hbm, wd_hbm,
    result, grad_first, grad_mixed, small, go_hbm, gu_hbm, gd_hbm, near_u, near_d,
    wo, wu, wd, active, slope, normed, unit, scale, low, low_turned, acc, branch, grad_upper, go, gu, gd,
    held_o, held_u, held_d, in_sem, out_sem, send_sem, recv_sem, x_send, x_recv,
):
    place = Place()
    core, sibling = place.core, place.sibling()
    loads = [
        pltpu.make_async_copy(source, target, in_sem.at[i])
        for i, (source, target) in enumerate(((wo_hbm, wo), (wu_hbm, wu), (wd_hbm, wd)))
    ]
    for copy in loads:
        copy.start()
    greet([sibling, place.x_peer(1), place.x_peer(3)])
    count, width = x.shape
    tile = 128
    chunks = wd.shape[0] // CHUNK
    gains = total[0:4] / ctx_size
    small[...] = jnp.zeros_like(small)

    def rows_of(i):
        return pl.ds(pl.multiple_of(i * tile, tile), tile)

    def lanes_of(c):
        return pl.ds(pl.multiple_of(c * CHUNK, CHUNK), CHUNK)

    loads[0].wait()
    for i in range(2):
        rows = slice(i * 256, i * 256 + 256)
        acc[rows, :] = matmul(mixed[rows, :], wo[...])

    def first_norm(i, carry):
        rows = rows_of(i)
        unit_rows, scale_rows = norm_rows(x[rows, :].astype(F32) + acc[rows, :])
        unit[rows, :] = unit_rows
        scale[rows, :] = scale_rows
        value = unit_rows * gains[0:1] + gains[1:2]
        normed[rows, :] = value
        low[rows, :] = value.astype(BF16)
        acc[rows, :] = value
        return carry

    lax.fori_loop(0, count // tile, first_norm, 0)
    loads[1].wait()
    loads[2].wait()

    def expand(c, carry):
        lanes = lanes_of(c)
        up = wu[:, :, lanes].reshape(width, CHUNK)
        down = wd[lanes, :]
        for i in range(2):
            rows = slice(i * 256, i * 256 + 256)
            upper = matmul(low[rows, :], up)
            share = 0.5 + 0.5 * lax.erf(upper * 0.7071067811865476)
            density = jnp.exp(upper * upper * -0.5) * 0.3989422804014327
            value = (upper * share).astype(BF16)
            active[rows, lanes] = value
            slope[rows, lanes] = share + upper * density
            acc[rows, :] += matmul(value, down)
        return carry

    lax.fori_loop(0, chunks, expand, 0)
    low_turned[...] = normed[...].T.astype(BF16)

    def second_norm(i, carry):
        rows = rows_of(i)
        unit_rows, scale_rows = norm_rows(acc[rows, :])
        value = unit_rows * gains[2:3] + gains[3:4]
        result[rows, :] = value.astype(BF16)
        error = value - teacher[rows, :].astype(F32)
        mask = slot_col[rows, 12:13]
        losses = mask * jnp.mean(error * error, axis=-1, keepdims=True)
        grad = (everyone / total[4:5, 0:1]) * mask * error
        small[2:3, :] += jnp.sum(grad * unit_rows, axis=0, keepdims=True)
        small[3:4, :] += jnp.sum(grad, axis=0, keepdims=True)
        small[4:5, 0:1] += jnp.sum(losses, axis=0, keepdims=True) / total[4:5, 0:1]
        back = norm_rows_back(grad, unit_rows, scale_rows, gains[2:3])
        acc[rows, :] = back
        branch[rows, :] = back.astype(BF16)
        return carry

    lax.fori_loop(0, count // tile, second_norm, 0)

    half = chunks // 2
    theirs, ours = half_of(width, 1 - core), half_of(width, core)

    def down_copy(c):
        lanes = lanes_of(c)
        return remote(gd.at[lanes, theirs], held_d.at[lanes], send_sem.at[c], recv_sem.at[c], sibling)

    def up_copy(i):
        return remote(gu.at[i], held_u.at[i], send_sem.at[chunks + i], recv_sem.at[chunks + i], sibling)

    def up_out(i):
        return pltpu.make_async_copy(held_u.at[i], gu_hbm.at[:, :, lanes_of(i)], out_sem.at[chunks + i])

    deep = wd.shape[0] // 16
    shallow = width // 16

    def opposite(zh):
        return zh * 4 + (place.x + 2) % 4

    def down_across(k, zh):
        part = pl.ds(pl.multiple_of(opposite(zh) * 2 * deep + k * deep, 16), deep)
        return remote(
            held_d.at[part], near_d.at[k, zh], x_send.at[2 * k + zh], x_recv.at[2 * k + zh], place.x_peer(1 + 2 * k)
        )

    def up_across(i, k, zh):
        n = 4 + i * 4 + 2 * k + zh
        return remote(
            held_u.at[i, opposite(zh), k * shallow : (k + 1) * shallow], near_u.at[k, zh, :, lanes_of(i)],
            x_send.at[n], x_recv.at[n], place.x_peer(1 + 2 * k),
        )

    def make_down(c, carry):
        lanes = lanes_of(c)
        gd[lanes, :] = matmul(active[:, lanes], branch[...], TN).astype(BF16)
        down_copy(c).start()
        return carry

    lax.fori_loop(0, chunks, make_down, 0)

    def contract(c):
        lanes = lanes_of(c)
        up = wu[:, :, lanes].reshape(width, CHUNK)
        down = wd[lanes, :]
        for i in range(2):
            rows = slice(i * 256, i * 256 + 256)
            value = (matmul(branch[rows, :], down, NT) * slope[rows, lanes]).astype(BF16)
            grad_upper[rows, :] = value
            acc[rows, :] += matmul(value, up, NT)
        return matmul(low_turned[...], grad_upper[...]).reshape(8, width // 8, CHUNK)

    def for_sibling(i, carry):
        gu[i] = contract((1 - core) * half + i).astype(BF16)
        up_copy(i).start()
        return carry

    def for_own(i, carry):
        value = contract(core * half + i)
        up_copy(i).wait_recv()
        held_u[i] = (value + held_u[i].astype(F32)).astype(BF16)
        up_out(i).start()
        for k in range(2):
            for zh in range(2):
                up_across(i, k, zh).start()
        return carry

    def down_out(c):
        lanes = lanes_of(c)
        return pltpu.make_async_copy(held_d.at[lanes], gd_hbm.at[lanes], out_sem.at[c])

    def add_down(c, carry):
        lanes = lanes_of(c)
        down_copy(c).wait_recv()
        held_d[lanes, :] = (gd[lanes, ours].astype(F32) + held_d[lanes, :].astype(F32)).astype(BF16)
        down_out(c).start()
        return carry

    lax.fori_loop(0, chunks, add_down, 0)
    for k in range(2):
        for zh in range(2):
            down_across(k, zh).start()
    lax.fori_loop(0, half, for_sibling, 0)
    lax.fori_loop(0, half, for_own, 0)

    def first_back(i, carry):
        rows = rows_of(i)
        grad = acc[rows, :]
        small[0:1, :] += jnp.sum(grad * unit[rows, :], axis=0, keepdims=True)
        small[1:2, :] += jnp.sum(grad, axis=0, keepdims=True)
        back = norm_rows_back(grad, unit[rows, :], scale[rows, :], gains[0:1])
        grad_first[rows, :] = back
        branch[rows, :] = back.astype(BF16)
        return carry

    lax.fori_loop(0, count // tile, first_back, 0)
    go[...] = matmul(mixed[...], branch[...], TN).astype(BF16)
    last = remote(go.at[:, theirs], held_o, send_sem.at[chunks + half], recv_sem.at[chunks + half], sibling)
    last.start()
    for i in range(2):
        rows = slice(i * 256, i * 256 + 256)
        grad_mixed[rows, :] = matmul(branch[rows, :], wo[...], NT).astype(BF16)

    last.wait_recv()
    held_o[...] = (go[:, ours].astype(F32) + held_o[...].astype(F32)).astype(BF16)
    out = pltpu.make_async_copy(held_o, go_hbm, in_sem.at[0])
    out.start()

    def settle_down(c, carry):
        down_copy(c).wait_send()
        down_out(c).wait()
        return carry

    def settle_up(i, carry):
        up_copy(i).wait_send()
        up_out(i).wait()
        return carry

    lax.fori_loop(0, chunks, settle_down, 0)
    lax.fori_loop(0, half, settle_up, 0)
    last.wait_send()
    for k in range(2):
        for zh in range(2):
            down_across(k, zh).wait()
            for i in range(half):
                up_across(i, k, zh).wait()
    out.wait()


def middle(everyone, ctx_size, mixed, x, teacher, slot_col, total, wo, wu, wd):
    count, width = x.shape
    hidden = wd.shape[0]
    chunks = hidden // CHUNK
    dma = pltpu.SemaphoreType.DMA
    vm = pltpu.VMEM
    return pl.pallas_call(
        functools.partial(middle_kernel, everyone, ctx_size),
        out_shape=[
            shaped(count, width),
            shaped(count, width, dtype=F32),
            shaped(count, width),
            shaped(8, width, dtype=F32),
            shaped(width, width // 2),
            shaped(8, width // 8, hidden // 2),
            shaped(hidden, width // 2),
            shaped(2, 2, width // 16, hidden // 2),
            shaped(2, 2, hidden // 16, width // 2),
        ],
        in_specs=[VMEM] * 5 + [ANY] * 3,
        out_specs=[VMEM] * 4 + [ANY] * 5,
        scratch_shapes=[
            vm(wo.shape, BF16), vm(wu.shape, BF16), vm(wd.shape, BF16),
            vm((count, hidden), BF16), vm((count, hidden), F32),
            vm((count, width), F32), vm((count, width), F32), vm((count, 1), F32),
            vm((count, width), BF16), vm((width, count), BF16), vm((count, width), F32),
            vm((count, width), BF16), vm((count, CHUNK), BF16),
            vm(wo.shape, BF16), vm((chunks // 2, 8, width // 8, CHUNK), BF16), vm(wd.shape, BF16),
            vm((width, width // 2), BF16), vm((chunks // 2, 8, width // 8, CHUNK), BF16), vm((hidden, width // 2), BF16),
            dma((3,)), dma((chunks + chunks // 2,)), dma((chunks + chunks // 2 + 1,)), dma((chunks + chunks // 2 + 1,)),
            dma((4 + 2 * chunks,)), dma((4 + 2 * chunks,)),
        ],
        compiler_params=pltpu.CompilerParams(
            collective_id=2, has_side_effects=True, vmem_limit_bytes=62 * 2**20
        ),
        name="dense_middle",
    )(mixed, x, teacher, slot_col, total, wo, wu, wd)


def local(tokens, teacher, clusters, segments, counted, w_qkv, w_out, w_up, w_down, norms):
    x_rows = tokens[0]
    tok_count, model_dim = x_rows.shape
    ctx_size, wsh_size = lax.axis_size("ctx"), lax.axis_size("wsh")
    mixed, x_turned, fq, fo, fu, fd, *kept, total = forward(
        x_rows, clusters[0], segments, counted, norms, (w_qkv, w_out, w_up, w_down)
    )
    everyone = float(tok_count * ctx_size * wsh_size)
    result, grad_first, grad_mixed, small, go, gu, gd, *nears = middle(
        everyone, float(ctx_size), mixed, x_rows, teacher[0], kept[-1], total,
        fo.reshape(-1, model_dim), fu, fd.reshape(-1, model_dim),
    )
    grad_tokens, final_qkv, final_out, final_up, final_down, final_norms, loss = backward(
        grad_mixed, grad_first, small, x_turned, fq, kept,
        [g.reshape(2, 4, -1, g.shape[-1]) for g in (go, gu, gd)], nears,
    )
    return (
        result[None],
        grad_tokens[None],
        loss.reshape(()),
        final_qkv.T,
        final_out.T,
        final_up,
        final_down.T,
        final_norms,
    )


def solution(mesh):
    placed = (
        P("wsh", "ctx", None),
        P("wsh", "ctx", None),
        P("wsh", None, "ctx"),
        P("wsh", "ctx"),
        P("wsh", "ctx"),
        P("wsh", None),
        P("wsh", None),
        P("wsh", None),
        P("wsh", None),
        P(None, "wsh"),
    )
    return jax.shard_map(
        local,
        mesh=mesh,
        in_specs=placed,
        out_specs=(
            P("wsh", "ctx", None),
            P("wsh", "ctx", None),
            P(),
            P("wsh", "ctx"),
            P("wsh", "ctx"),
            P("wsh", "ctx"),
            P("wsh", "ctx"),
            P(None, ("ctx", "wsh")),
        ),
        check_vma=False,
    )
```

```python
import functools
import jax
import jax.numpy as jnp
from jax import lax
from jax.experimental import pallas as pl
from jax.experimental.pallas import tpu as pltpu
from jax.sharding import PartitionSpec as P

MESH = pl.DeviceIdType.MESH
BF16 = jnp.bfloat16
F32 = jnp.float32


class Place:
    def __init__(self):
        self.ctx = lax.axis_index("ctx")
        self.wsh = lax.axis_index("wsh")
        self.zlo = self.ctx // 8
        self.y = (self.ctx // 2) % 4
        self.core = self.ctx % 2
        self.zhi = self.wsh // 4
        self.x = self.wsh % 4

    def at(self, zlo=None, y=None, core=None, zhi=None, x=None):
        zlo = self.zlo if zlo is None else zlo
        y = self.y if y is None else y
        core = self.core if core is None else core
        zhi = self.zhi if zhi is None else zhi
        x = self.x if x is None else x
        return (zlo * 8 + y * 2 + core, zhi * 4 + x)

    def sibling(self):
        return self.at(core=1 - self.core)

    def x_peer(self, step):
        return self.at(x=(self.x + step) % 4)

    def y_peer(self, step):
        return self.at(y=(self.y + step) % 4)

    def z_peer(self, step):
        z = (self.zhi * 4 + self.zlo + step + 8) % 8
        return self.at(zlo=z % 4, zhi=z // 4)

    def plane(self):
        return [
            self.at(y=(self.y + d) % 4, core=(self.core + c) % 2)
            for d, c in ((0, 1), (1, 0), (1, 1), (2, 0), (2, 1), (3, 0), (3, 1))
        ]

    def rank(self):
        return self.y * 2 + self.core

    def z_far(self):
        return self.at(zhi=1 - self.zhi)

    def doubling(self):
        return (
            self.z_far(),
            self.sibling(),
            self.at(y=self.y + 1 - 2 * (self.y % 2)),
            self.at(y=(self.y + 2) % 4),
            self.at(x=self.x + 1 - 2 * (self.x % 2)),
            self.at(x=(self.x + 2) % 4),
            self.at(zlo=self.zlo + 1 - 2 * (self.zlo % 2)),
            self.at(zlo=(self.zlo + 2) % 4),
        )


def greet(devices):
    barrier = pltpu.get_barrier_semaphore()
    for device in devices:
        pl.semaphore_signal(barrier, inc=1, device_id=device, device_id_type=MESH)
    pl.semaphore_wait(barrier, len(devices))


def remote(source, target, send_sem, recv_sem, device):
    return pltpu.make_async_remote_copy(
        src_ref=source,
        dst_ref=target,
        send_sem=send_sem,
        recv_sem=recv_sem,
        device_id=device,
        device_id_type=MESH,
    )


def half_of(width, which):
    half = width // 2
    return pl.ds(pl.multiple_of(which * half, 128), half)


class Doubling:
    def __init__(self, place, tile, slots, send_sems, recv_sems):
        self.partners = place.doubling()
        self.tile, self.slots = tile, slots
        self.send_sems, self.recv_sems = send_sems, recv_sems
        self.step = 0
        self.copies = []

    def start(self):
        k = self.step
        copy = remote(
            self.tile.at[k], self.slots.at[k], self.send_sems.at[k], self.recv_sems.at[k], self.partners[k]
        )
        copy.start()
        self.copies.append(copy)

    def advance(self):
        k = self.step
        self.copies[k].wait_recv()
        self.tile[k + 1] = self.tile[k] + self.slots[k]
        self.step = k + 1
        if self.step < 8:
            self.start()

    def drain(self):
        for copy in self.copies:
            copy.wait_send()


NEG = -1e30
NT = (((1,), (1,)), ((), ()))
TN = (((0,), (0,)), ((), ()))


def matmul(left, right, dims=(((1,), (0,)), ((), ()))):
    return lax.dot_general(left, right, dims, preferred_element_type=F32)


class Gather:
    def __init__(self, place, shard, full, send_sems, recv_sems, local_sem):
        self.place, self.shard, self.full = place, shard, full
        self.send_sems, self.recv_sems = send_sems, recv_sems
        self.rows = shard.shape[0]
        self.lanes = half_of(shard.shape[1], place.core)
        self.local = pltpu.make_async_copy(shard, full.at[place.wsh], local_sem)
        self.copies = {}

    def part(self, index, which=None):
        block = self.full.at[index]
        if which is None:
            return block.at[:, self.lanes]
        half = self.rows // 2
        return block.at[which * half : (which + 1) * half, self.lanes]

    def send(self, k, source, target, device):
        copy = remote(source, target, self.send_sems.at[k], self.recv_sems.at[k], device)
        copy.start()
        self.copies[k] = copy

    def own(self, far, step):
        return (far * 4) + (self.place.x + step + 4) % 4

    def start_z(self):
        place = self.place
        self.local.start()
        self.send(2, self.shard.at[:, self.lanes], self.part(place.wsh), place.z_far())

    def step_z(self, k, source, block, step):
        part = self.part(block)
        return remote(
            part if source is None else source, part, self.send_sems.at[2 + 17 * k], self.recv_sems.at[2],
            self.place.z_peer(step),
        )

    def start_run(self):
        self.local.start()
        own = self.shard.at[:, self.lanes]
        for end, step in ((3, 1), (0, -1)):
            @pl.when(self.place.zlo == end)
            def _(step=step):
                self.step_z(0, own, self.place.wsh, step).start()

    def pass_run(self):
        far = self.own(1 - self.place.zhi, 0)
        for end, step in ((0, 1), (3, -1)):
            @pl.when(self.place.zlo == end)
            def _(step=step):
                copy = self.step_z(1, None, far, step)
                copy.wait_recv()
                copy.start()

    def from_run(self):
        place = self.place
        index = self.own(1 - place.zhi, 0)

        @pl.when(jnp.logical_or(place.zlo == 1, place.zlo == 2))
        def _():
            self.step_z(0, None, index, 1).wait_recv()

        self.send(10, self.part(index), self.part(index), place.x_peer(1))
        self.send(11, self.part(index), self.part(index), place.x_peer(3))
        self.send(9, self.part(index), self.part(index), place.sibling())

    def drain_run(self):
        @pl.when(jnp.logical_or(self.place.zlo == 0, self.place.zlo == 3))
        def _():
            for k in range(2):
                self.step_z(k, None, self.place.wsh, 1).wait_send()

    def start_x(self):
        place = self.place
        self.send(0, self.shard.at[:, self.lanes], self.part(place.wsh), place.x_peer(1))
        self.send(1, self.shard.at[:, self.lanes], self.part(place.wsh), place.x_peer(3))

    def pass_on(self, zh, base):
        place = self.place
        left, right = self.own(zh, -1), self.own(zh, 1)
        self.copies[base].wait_recv()
        self.send(base + 3, self.part(left, 0), self.part(left, 0), place.x_peer(1))
        self.send(base + 5, self.part(left), self.part(left), place.sibling())
        self.copies[base + 1].wait_recv()
        self.send(base + 4, self.part(right, 1), self.part(right, 1), place.x_peer(3))
        self.send(base + 6, self.part(right), self.part(right), place.sibling())

    def opposite(self, zh, base):
        place = self.place
        index = self.own(zh, 2)
        for which in range(2):
            self.copies[base + 3 + which].wait_recv()
            self.send(base + 7 + which, self.part(index, which), self.part(index, which), place.sibling())

    def near(self):
        self.pass_on(self.place.zhi, 0)

    def near_opposite(self):
        self.opposite(self.place.zhi, 0)

    def from_z(self):
        place = self.place
        index = self.own(1 - place.zhi, 0)
        self.copies[2].wait_recv()
        self.send(10, self.part(index), self.part(index), place.x_peer(1))
        self.send(11, self.part(index), self.part(index), place.x_peer(3))
        self.send(9, self.part(index), self.part(index), place.sibling())

    def far(self):
        self.pass_on(1 - self.place.zhi, 10)

    def far_opposite(self):
        self.opposite(1 - self.place.zhi, 10)

    def finish(self):
        self.local.wait()
        for k in (5, 6, 7, 8, 9, 15, 16, 17, 18):
            self.copies[k].wait_recv()

    def drain(self):
        for k in self.copies:
            self.copies[k].wait_send()


def head_mask(which):
    lane = lax.broadcasted_iota(jnp.int32, (1, 128), 1)
    return jnp.where((lane // 64) == which, 1.0, 0.0).astype(BF16)


def to_slots(slot_row, head, count):
    row = slot_row[pl.ds(head, 1), :]
    iota = lax.broadcasted_iota(jnp.int32, (count, count), 0).astype(F32)
    return jnp.where(iota == row, 1.0, 0.0).astype(BF16)


def to_tokens(slot_col, head, count):
    lane = lax.broadcasted_iota(jnp.int32, slot_col.shape, 1)
    column = jnp.sum(jnp.where(lane == head, slot_col[...], 0.0), axis=1, keepdims=True)
    iota = lax.broadcasted_iota(jnp.int32, (count, count), 1).astype(F32)
    return jnp.where(iota == column, 1.0, 0.0).astype(BF16)


def pair_select(first, second):
    lane = lax.broadcasted_iota(jnp.int32, first.shape, 1)
    return jnp.where((lane // 64) % 2 == 0, first, second)


def heads_home(turned):
    return jnp.concatenate([turned[0:64, 0:128], turned[64:128, 128:256]], axis=0).T


def make_slots(clusters, segments, counted, slot_row, slot_col, labels):
    heads, count = clusters.shape
    groups = lax.shift_right_logical(clusters[...], 2)
    iota = lax.broadcasted_iota(jnp.int32, (32, count), 0)
    before = lax.broadcasted_iota(jnp.int32, (count, count), 0)
    after = lax.broadcasted_iota(jnp.int32, (count, count), 1)
    upper = jnp.where(before <= after, 1.0, 0.0).astype(BF16)
    hot = [jnp.where(groups[h : h + 1, :] == iota, 1.0, 0.0) for h in range(heads)]
    counts = matmul(jnp.concatenate(hot, axis=0).astype(BF16), upper)
    group_f = groups.astype(F32)
    rows = []
    for h in range(heads):
        rank = jnp.sum(counts[32 * h : 32 * h + 32] * hot[h], axis=0, keepdims=True)
        rows.append(group_f[h : h + 1] * 16.0 + rank - 1.0)
    slots = jnp.concatenate(rows + [counted[...].astype(F32), jnp.zeros((127 - heads, count), F32)], axis=0)
    slot_row[...] = slots[:16]
    slot_col[...] = slots.T
    label = (segments[0:1, :] * 4 + (clusters[...] & 3)).astype(F32)
    labels[...] = jnp.concatenate([label, jnp.zeros((128 - heads, count), F32)], axis=0).T.astype(BF16)


def rows16(j):
    return slice(16 * j, 16 * j + 16)


def forward_kernel(
    x, clusters, segments, counted, norms, wq, wo, wu, wd,
    mixed, x_turned, fq_out, fo, fu, fd, got_out, before_out, after_out, logsum, hot_out, cold_out, slot_row, slot_col, total,
    pieces, fq, got, before, after, hot, cold,
    labels, sent_labels, got_labels, before_labels, after_labels, wide_labels, sent, out, back,
    tile, slots,
    w_send, w_recv, w_local, t_send, t_recv, a_send, a_recv, a_local, z_send, z_recv, b_send, b_recv, b_local, k_sem,
):
    place = Place()
    plane, rank = place.plane(), place.rank()
    up, down = place.z_peer(1), place.z_peer(-1)
    kept = []

    def keep(source, target):
        copy = pltpu.make_async_copy(source, target, k_sem.at[len(kept)])
        copy.start()
        kept.append(copy)

    partners = place.doubling()
    for g in range(3):
        for b in range(2):
            for t in range(3):
                lane = t * 768 + (2 * g + b) * 128
                pieces[g, :, b * 384 + t * 128 : b * 384 + t * 128 + 128] = wq[:, lane : lane + 128]
    greet(
        plane + [place.x_peer(1), place.x_peer(2), place.x_peer(3), place.z_far(), up, down, partners[6], partners[7]]
    )
    weights = [
        Gather(place, shard, full, w_send.at[i], w_recv.at[i], w_local.at[i])
        for i, (shard, full) in enumerate(
            [(pieces.at[g], fq.at[g]) for g in range(3)] + [(wo, fo), (wu, fu), (wd, fd)]
        )
    ]
    first, second, third, w_out, w_up, w_down = weights
    rest = (w_out, w_up, w_down)
    tile[0] = jnp.zeros_like(tile[0])
    tile[0, 0:4, 0 : norms.shape[1]] = norms[...].astype(F32)
    tile[0] = pltpu.roll(tile[0], place.wsh * norms.shape[1], 1)
    lane_zero = lax.broadcasted_iota(jnp.int32, (1, tile.shape[2]), 1) == 0
    tile[0, 4:5, :] = jnp.where(lane_zero, jnp.sum(counted[...].astype(F32), axis=1, keepdims=True), 0.0)
    doubling = Doubling(place, tile, slots, t_send, t_recv)
    doubling.start()
    first.start_z()
    first.start_x()
    count = x.shape[0]
    make_slots(clusters, segments, counted, slot_row, slot_col, labels)

    second.start_z()
    second.start_x()
    sent_labels[...] = jnp.zeros_like(sent_labels)

    def move_labels(head, carry):
        lane = lax.broadcasted_iota(jnp.int32, (count, 128), 1)
        moved = matmul(to_slots(slot_row, head, count), labels[...])
        sent_labels[...] = jnp.where(lane == head, moved, sent_labels[...])
        return carry

    lax.fori_loop(0, 6, move_labels, 0)
    first.near()
    third.start_z()
    third.start_x()
    lax.fori_loop(6, 12, move_labels, 0)
    labels[...] = sent_labels[...].astype(BF16)

    def block(which):
        return pl.ds(pl.multiple_of(which * 64, 64), 64)

    def ranks():
        return [dev[0] % 8 for dev in plane]

    label_copies = [
        remote(labels.at[block(to)], got_labels.at[rank], a_send.at[6, k], a_recv.at[6, k], plane[k])
        for k, to in enumerate(ranks())
    ]
    for copy in label_copies:
        copy.start()
    own_labels = pltpu.make_async_copy(labels.at[block(rank)], got_labels.at[rank], a_local.at[6])
    own_labels.start()
    first.from_z()
    second.near()
    first.near_opposite()
    doubling.advance()
    x_turned[...] = x[...].astype(F32).T.astype(BF16)
    doubling.advance()
    second.from_z()
    first.far()
    third.near()
    second.near_opposite()
    doubling.advance()
    third.from_z()
    own_labels.wait()
    for copy in label_copies:
        copy.wait_recv()
    label_up = remote(got_labels.at[4:8], before_labels, z_send.at[6, 0], z_recv.at[6, 0], up)
    label_down = remote(got_labels.at[0:4], after_labels, z_send.at[6, 1], z_recv.at[6, 1], down)
    label_up.start()
    label_down.start()
    for w in rest:
        w.start_run()
    first.far_opposite()
    first.finish()

    def make_hot(head, carry):
        lane = lax.broadcasted_iota(jnp.int32, (256, 128), 1)
        for j in range(4):
            column = jnp.sum(jnp.where(lane == head, wide_labels[j], 0.0), axis=1, keepdims=True)
            same = lane.astype(F32) == column
            cold[head * 4 + j] = jnp.where(same, 0.0, NEG).astype(BF16)
            hot[head * 4 + j] = jnp.where(same, 1.0, 0.0)[64:192].astype(BF16)
        return carry

    def send_copies(p, fn):
        for k, to in enumerate(ranks()):
            fn(remote(sent.at[p, block(to)], got.at[p, rank], a_send.at[p, k], a_recv.at[p, k], plane[k]))

    def own_copy(p):
        return pltpu.make_async_copy(sent.at[p, block(rank)], got.at[p, rank], a_local.at[p])

    def project(g):
        value = matmul(x[...], fq[g].reshape(768, 768))
        lane = lax.broadcasted_iota(jnp.int32, (1, 384), 1)
        scale = jnp.where(lane < 128, 0.125, 1.0)
        for b in range(2):
            p = 2 * g + b
            rows = (value[:, b * 384 : b * 384 + 384] * scale).astype(BF16)
            moved = [matmul(to_slots(slot_row, 2 * p + a, count), rows) for a in range(2)]
            sent[p] = pair_select(moved[0], moved[1]).astype(BF16)
            send_copies(p, lambda copy: copy.start())
            own_copy(p).start()

    project(0)
    second.far()
    third.near_opposite()
    third.far()
    second.far_opposite()
    second.finish()
    doubling.advance()
    for w in rest:
        w.start_x()
    project(1)
    w_out.pass_run()
    w_up.pass_run()
    third.far_opposite()
    third.finish()
    project(2)
    w_down.pass_run()
    keep(fq, fq_out)
    label_up.wait_recv()
    label_down.wait_recv()
    for j in range(4):
        wide_labels[j, 0:64] = jnp.where(
            place.zlo == 0, -1.0, before_labels[:, rows16(j), :].reshape(64, 128).astype(F32)
        )
        wide_labels[j, 64:192] = got_labels[:, rows16(j), :].reshape(128, 128).astype(F32)
        wide_labels[j, 192:256] = jnp.where(
            place.zlo == 3, -1.0, after_labels[:, rows16(j), :].reshape(64, 128).astype(F32)
        )
    lax.fori_loop(0, 12, make_hot, 0)
    keep(hot, hot_out)
    keep(cold, cold_out)
    w_out.near()
    w_out.from_run()
    w_up.near()
    doubling.advance()

    def halo(p):
        return (
            remote(got.at[p, 4:8, :, 128:384], before.at[p], z_send.at[p, 0], z_recv.at[p, 0], up),
            remote(got.at[p, 0:4, :, 128:384], after.at[p], z_send.at[p, 1], z_recv.at[p, 1], down),
        )

    def back_copies(p, fn):
        for k, to in enumerate(ranks()):
            fn(remote(out.at[p, to], back.at[p, rank], b_send.at[p, k], b_recv.at[p, k], plane[k]))

    def own_back(p):
        return pltpu.make_async_copy(out.at[p, rank], back.at[p, rank], b_local.at[p])

    def arrive(p):
        own_copy(p).wait()
        send_copies(p, lambda copy: copy.wait_recv())
        for copy in halo(p):
            copy.start()

    masks = [head_mask(a) for a in range(2)]

    def attend(p):
        for copy in halo(p):
            copy.wait_recv()
        for j in range(4):
            r = rows16(j)
            query = got[p, :, r, 0:128].reshape(128, 128)
            keys = jnp.concatenate(
                [before[p, :, r, 0:128].reshape(64, 128), got[p, :, r, 128:256].reshape(128, 128),
                 after[p, :, r, 0:128].reshape(64, 128)], axis=0)
            values = jnp.concatenate(
                [before[p, :, r, 128:256].reshape(64, 128), got[p, :, r, 256:384].reshape(128, 128),
                 after[p, :, r, 128:256].reshape(64, 128)], axis=0)
            probs = []
            for a in range(2):
                head = 2 * p + a
                scores = matmul(
                    jnp.concatenate([keys, cold[head * 4 + j]], axis=1),
                    jnp.concatenate([query * masks[a], hot[head * 4 + j]], axis=1), NT)
                top = jnp.max(scores, axis=0, keepdims=True)
                raised = jnp.exp(scores - top)
                sums = jnp.sum(raised, axis=0, keepdims=True)
                probs.append((raised * (1.0 / sums)).astype(BF16))
                logsum[j, pl.ds(head, 1), :] = top + jnp.log(sums)
            out[p, :, r, :] = heads_home(matmul(values, jnp.concatenate(probs, axis=1), TN)).astype(BF16).reshape(8, 16, 128)
        back_copies(p, lambda copy: copy.start())
        own_back(p).start()

    def home(p):
        own_back(p).wait()
        back_copies(p, lambda copy: copy.wait_recv())
        rows = back[p].reshape(count, 128)
        moved = [matmul(to_tokens(slot_col, 2 * p + a, count), rows) for a in range(2)]
        mixed[:, p * 128 : p * 128 + 128] = pair_select(moved[0], moved[1]).astype(BF16)

    arrive(0)
    w_up.from_run()
    arrive(1)
    attend(0)
    w_down.near()
    w_out.near_opposite()
    arrive(2)
    attend(1)
    w_down.from_run()
    w_up.near_opposite()
    doubling.advance()
    arrive(3)
    attend(2)
    home(0)
    w_out.far()
    arrive(4)
    attend(3)
    home(1)
    w_up.far()
    w_down.near_opposite()
    arrive(5)
    attend(4)
    home(2)
    home(3)
    doubling.advance()

    def settle_out(p, carry):
        send_copies(p, lambda copy: copy.wait_send())
        return carry

    def settle_back(p, carry):
        back_copies(p, lambda copy: copy.wait_send())
        for copy in halo(p):
            copy.wait_send()
        return carry

    lax.fori_loop(0, 6, settle_out, 0)
    for copy in label_copies + [label_up, label_down]:
        copy.wait_send()
    for w in (first, second, third):
        w.drain()
    w_down.far()
    attend(5)
    keep(got, got_out)
    keep(before, before_out)
    keep(after, after_out)
    w_out.far_opposite()
    w_up.far_opposite()
    home(4)
    lax.fori_loop(0, 5, settle_back, 0)
    w_down.far_opposite()
    home(5)
    doubling.advance()
    for w in rest:
        w.finish()
    total[...] = tile[8]
    settle_back(5, 0)
    for w in rest:
        w.drain()
        w.drain_run()
    for copy in kept:
        copy.wait()
    doubling.drain()


ANY = pl.BlockSpec(memory_space=pl.ANY)
VMEM = pl.BlockSpec(memory_space=pltpu.VMEM)


def shaped(*shape, dtype=BF16):
    return jax.ShapeDtypeStruct(shape, dtype)


def forward(x, clusters, segments, counted, norms, shards):
    count, width = x.shape
    dma = pltpu.SemaphoreType.DMA
    return pl.pallas_call(
        forward_kernel,
        out_shape=[
            shaped(*x.shape),
            shaped(width, count),
            shaped(3, 8, shards[0].shape[0], 768),
            *[shaped(8, *w.shape) for w in shards[1:]],
            shaped(6, 8, 64, 384),
            shaped(6, 4, 64, 256),
            shaped(6, 4, 64, 256),
            shaped(4, 16, 128, dtype=F32),
            shaped(48, 128, 128),
            shaped(48, 256, 128),
            shaped(16, count, dtype=F32),
            shaped(count, 128, dtype=F32),
            shaped(8, width, dtype=F32),
        ],
        in_specs=[VMEM] * 9,
        out_specs=[VMEM] * 2 + [ANY] * 7 + [VMEM] + [ANY] * 2 + [VMEM] * 3,
        scratch_shapes=[
            pltpu.VMEM((3, shards[0].shape[0], 768), BF16),
            pltpu.VMEM((3, 8, shards[0].shape[0], 768), BF16),
            pltpu.VMEM((6, 8, 64, 384), BF16),
            pltpu.VMEM((6, 4, 64, 256), BF16),
            pltpu.VMEM((6, 4, 64, 256), BF16),
            pltpu.VMEM((48, 128, 128), BF16),
            pltpu.VMEM((48, 256, 128), BF16),
            pltpu.VMEM((count, 128), BF16),
            pltpu.VMEM((count, 128), F32),
            pltpu.VMEM((8, 64, 128), BF16),
            pltpu.VMEM((4, 64, 128), BF16),
            pltpu.VMEM((4, 64, 128), BF16),
            pltpu.VMEM((4, 256, 128), F32),
            pltpu.VMEM((6, count, 384), BF16),
            pltpu.VMEM((6, 8, 64, 128), BF16),
            pltpu.VMEM((6, 8, 64, 128), BF16),
            pltpu.VMEM((9, 8, width), F32),
            pltpu.VMEM((8, 8, width), F32),
            dma((6, 20)), dma((6, 19)), dma((6,)), dma((8,)), dma((8,)),
            dma((7, 7)), dma((7, 7)), dma((7,)), dma((7, 2)), dma((7, 2)),
            dma((6, 7)), dma((6, 7)), dma((6,)), dma((6,)),
        ],
        compiler_params=pltpu.CompilerParams(
            collective_id=0, has_side_effects=True, vmem_limit_bytes=60 * 2**20
        ),
        name="forward_attention",
    )(x, clusters, segments, counted, norms, *shards)


class Reduce:
    def __init__(self, place, held, near, far, sum_x, from_y, sum_y, from_z, out, send_sems, recv_sems, grad=None, source=None, near_source=None, load_sems=None):
        self.place, self.held, self.grad = place, held, grad
        self.near, self.far, self.sum_x, self.from_y = near, far, sum_x, from_y
        self.sum_y, self.from_z, self.out = sum_y, from_z, out
        self.send_sems, self.recv_sems = send_sems, recv_sems
        self.rows, self.half = held.shape[2], held.shape[3]
        self.window = out.shape[1]
        self.owner = place.y // 2
        self.z = place.zhi * 4 + place.zlo
        self.final = jnp.logical_and(place.zhi == self.owner, place.core == place.zlo // 2)
        self.copies = {}
        if source is not None:
            self.loads = [pltpu.make_async_copy(source, held, load_sems.at[0])]
        self.begun = near_source is not None
        if self.begun:
            self.loads.append(pltpu.make_async_copy(near_source, near, load_sems.at[1]))

    def send(self, k, source, target, device):
        copy = remote(source, target, self.send_sems.at[k], self.recv_sems.at[k], device)
        copy.start()
        self.copies[k] = copy

    def each(self, count, body):
        def step(i, carry):
            body(pl.ds(pl.multiple_of(i * 48, 16), 48))
            return carry

        lax.fori_loop(0, count // 48, step, 0)

    def after(self, rows, offset):
        return pl.ds(pl.multiple_of(rows.start + offset, 16), rows.size)

    def blocks(self, body):
        def step(zh, carry):
            body(zh)
            return carry

        lax.fori_loop(0, 2, step, 0)

    def start(self):
        place = self.place
        self.send(0, self.grad.at[:, :, :, half_of(2 * self.half, 1 - place.core)], self.held, place.sibling())

    def add_pair(self, xx):
        mine = half_of(2 * self.half, self.place.core)

        def block(zh):
            def body(rows):
                self.held[zh, xx, rows, :] = (
                    self.grad[zh, xx, rows, mine].astype(F32) + self.held[zh, xx, rows, :].astype(F32)
                ).astype(BF16)

            self.each(self.rows, body)

        self.blocks(block)

    def to_opposite(self):
        place = self.place
        half = self.rows // 2
        opposite = (place.x + 2) % 4
        if self.grad is None:
            self.loads[0].wait()
        else:
            self.copies[0].wait_recv()
            self.add_pair(opposite)
        self.send(1, self.held.at[:, opposite, 0:half], self.near.at[0], place.x_peer(1))
        self.send(2, self.held.at[:, opposite, half : self.rows], self.near.at[1], place.x_peer(3))
        if self.grad is not None:
            for step in (1, 3, 0):
                self.add_pair((place.x + step) % 4)

    def to_near(self):
        place = self.place
        half = self.rows // 2
        if self.begun:
            for copy in self.loads:
                copy.wait()
        for k, step in enumerate((1, 3)):
            to = (place.x + step) % 4
            if not self.begun:
                self.copies[1 + k].wait_recv()

            def block(zh, k=k, to=to):
                def body(rows):
                    there = self.after(rows, k * half)
                    self.held[zh, to, there, :] = (
                        self.held[zh, to, there, :].astype(F32) + self.near[k, zh, rows, :].astype(F32)
                    ).astype(BF16)

                self.each(half, body)

            self.blocks(block)
            self.send(3 + k, self.held.at[:, to], self.far.at[k], place.x_peer(step))

    def to_y(self):
        place = self.place
        half = self.rows // 2
        for k in range(2):
            self.copies[3 + k].wait_recv()

        def block(zh):
            def body(rows):
                value = self.held[zh, place.x, rows, :].astype(F32)
                value = value + self.far[0, zh, rows, :].astype(F32) + self.far[1, zh, rows, :].astype(F32)
                self.sum_x[zh, rows, :] = value.astype(BF16)

            self.each(self.rows, body)

        self.blocks(block)
        for k, d in enumerate((1, 2, 3)):
            to = (place.y + d) % 4
            part = pl.ds(pl.multiple_of((to % 2) * half, 16), half)
            self.send(5 + k, self.sum_x.at[to // 2, part], self.from_y.at[k], place.y_peer(d))

    def lanes(self, zlo):
        offset = (zlo % 2) * (self.half - self.window)
        return pl.ds(pl.multiple_of(offset, 128), self.window)

    def z_copy(self, k):
        place = self.place
        zlo = 2 * place.core + k
        return remote(
            self.sum_y.at[:, self.lanes(zlo)], self.from_z.at[self.z],
            self.send_sems.at[8 + k], self.recv_sems.at[8 + self.z], place.at(zlo=zlo, zhi=self.owner),
        )

    def is_target(self, k):
        place = self.place
        return jnp.logical_and(place.zhi == self.owner, place.zlo == 2 * place.core + k)

    def to_z(self):
        place = self.place
        half = self.rows // 2
        for k in range(3):
            self.copies[5 + k].wait_recv()

        def body(rows):
            value = self.sum_x[self.owner, self.after(rows, (place.y % 2) * half), :].astype(F32)
            for k in range(3):
                value = value + self.from_y[k, rows, :].astype(F32)
            self.sum_y[rows, :] = value.astype(BF16)

        self.each(half, body)
        for k in range(2):
            @pl.when(jnp.logical_not(self.is_target(k)))
            def _(k=k):
                self.z_copy(k).start()

    def spread_copy(self, k, device):
        half = self.rows // 2
        part = self.out.at[pl.ds(pl.multiple_of((self.place.y % 2) * half, 16), half)]
        return remote(part, part, self.send_sems.at[10 + k], self.recv_sems.at[16 + self.place.y % 2], device)

    def spread(self):
        half = self.rows // 2

        @pl.when(self.final)
        def _():
            self.from_z[self.z] = self.sum_y[:, self.lanes(self.place.zlo)]
            for z in range(8):
                @pl.when(self.z != z)
                def _(z=z):
                    part = self.from_z.at[z]
                    remote(part, part, self.send_sems.at[8], self.recv_sems.at[8 + z], self.place.sibling()).wait_recv()

            def body(rows):
                there = self.after(rows, (self.place.y % 2) * half)
                value = self.from_z[0, rows, :].astype(F32)
                for z in range(1, 8):
                    value = value + self.from_z[z, rows, :].astype(F32)
                self.out[there, :] = value.astype(BF16)

            self.each(half, body)
            for k, device in enumerate(self.place.plane()):
                self.spread_copy(k, device).start()

    def finish(self):
        half = self.rows // 2
        for k in range(2):
            part = self.out.at[k * half : (k + 1) * half]

            @pl.when(jnp.logical_not(jnp.logical_and(self.final, self.place.y % 2 == k)))
            def _(k=k, part=part):
                remote(part, part, self.send_sems.at[10], self.recv_sems.at[16 + k], self.place.sibling()).wait_recv()

    def drain(self):
        for k in self.copies:
            self.copies[k].wait_send()
        for k in range(2):
            @pl.when(jnp.logical_not(self.is_target(k)))
            def _(k=k):
                self.z_copy(k).wait_send()

        @pl.when(self.final)
        def _():
            for k, device in enumerate(self.place.plane()):
                self.spread_copy(k, device).wait_send()


def reduce_scratch(rows, half, window):
    return [
        pltpu.VMEM((2, 4, rows, half), BF16),
        pltpu.VMEM((2, 2, rows // 2, half), BF16),
        pltpu.VMEM((2, 2, rows, half), BF16),
        pltpu.VMEM((2, rows, half), BF16),
        pltpu.VMEM((3, rows // 2, half), BF16),
        pltpu.VMEM((rows // 2, half), BF16),
        pltpu.VMEM((8, rows // 2, window), BF16),
        pltpu.VMEM((rows, window), BF16),
    ]


def cut(value, offset, target):
    rows, width = value.shape
    first = pltpu.roll(value, (width - offset) % width, 1)[:, 0:128]
    if target.shape[0] == rows:
        target[...] = first[:, : target.shape[1]]
        return
    if rows % 128:
        first = jnp.concatenate([first, jnp.zeros((128 - rows % 128, 128), F32)], axis=0)
    target[...] = first.T[: target.shape[0], :rows]


ORDER = (0, 3, 1, 4, 2, 5)


def backward_kernel(*refs):
    (grad_mixed, grad_first, logsum, slot_row, slot_col, small, x_hbm, fq_hbm, got_hbm, before_hbm, after_hbm,
     hot_hbm, cold_hbm, go, gu, gd, near_u, near_d) = refs[:18]
    refs = refs[2:]
    grad_x, out_q, out_o, out_u, out_d, norms_out, loss_out = refs[16:23]
    x_turned, fq, got, before, after, hot, cold = refs[23:30]
    sent, got_grad, grads, to_before, to_after, from_before, from_after, back = refs[30:38]
    grads_q = refs[38:41]
    reduce_refs = [refs[41 + 8 * i : 49 + 8 * i] for i in range(6)]
    (tile, slots, a_send, a_recv, a_local, z_send, z_recv, b_send, b_recv, b_local,
     t_send, t_recv, r_send, r_recv, r_load, l_sem) = refs[89:]
    place = Place()
    plane, rank = place.plane(), place.rank()
    up, down = place.z_peer(1), place.z_peer(-1)
    loads = [
        pltpu.make_async_copy(source, target, l_sem.at[i])
        for i, (source, target) in enumerate(
            ((got_hbm, got), (before_hbm, before), (after_hbm, after), (hot_hbm, hot), (cold_hbm, cold),
             (fq_hbm, fq), (x_hbm, x_turned))
        )
    ]
    rest = [
        Reduce(
            place, *reduce_refs[i], r_send.at[i], r_recv.at[i], source=source, near_source=near, load_sems=r_load.at[i]
        )
        for i, (source, near) in enumerate(((go, None), (gu, near_u), (gd, near_d)))
    ]
    by_group = [
        Reduce(place, *reduce_refs[3 + i], r_send.at[3 + i], r_recv.at[3 + i], grad=grads_q[i]) for i in range(3)
    ]
    for r in (rest[2], rest[1], rest[0]):
        for copy in r.loads:
            copy.start()
    for copy in loads:
        copy.start()
    greet(plane + [place.x_peer(d) for d in (1, 2, 3)] + [place.z_peer(d) for d in range(1, 8)])
    sum_o, sum_u, sum_d = rest
    sum_o.to_opposite()
    tile[0] = small[...]
    doubling = Doubling(place, tile, slots, t_send, t_recv)
    doubling.start()
    count = grad_mixed.shape[0]
    ranks = [dev[0] % 8 for dev in plane]

    def block(which):
        return pl.ds(pl.multiple_of(which * 64, 64), 64)

    def send_copies(p, fn):
        for k, to in enumerate(ranks):
            fn(remote(sent.at[p, block(to)], got_grad.at[p, rank], a_send.at[p, k], a_recv.at[p, k], plane[k]))

    def own_copy(p):
        return pltpu.make_async_copy(sent.at[p, block(rank)], got_grad.at[p, rank], a_local.at[p])

    def leave(i, carry):
        p = i // 2 + 3 * (i % 2)
        rows = grad_mixed[:, pl.ds(pl.multiple_of(p * 128, 128), 128)]
        moved = [matmul(to_slots(slot_row, 2 * p + a, count), rows) for a in range(2)]
        sent[p] = pair_select(moved[0], moved[1]).astype(BF16)
        send_copies(p, lambda copy: copy.start())
        own_copy(p).start()
        return carry

    lax.fori_loop(0, 6, leave, 0)
    doubling.advance()
    sum_d.to_near()
    sum_u.to_near()
    for copy in loads[:5]:
        copy.wait()

    def halo(p):
        return (
            remote(to_after.at[p], from_before.at[p], z_send.at[p, 0], z_recv.at[p, 0], up),
            remote(to_before.at[p], from_after.at[p], z_send.at[p, 1], z_recv.at[p, 1], down),
        )

    def back_copies(p, fn):
        for k, to in enumerate(ranks):
            fn(remote(grads.at[p, to], back.at[p, rank], b_send.at[p, k], b_recv.at[p, k], plane[k]))

    def own_back(p):
        return pltpu.make_async_copy(grads.at[p, rank], back.at[p, rank], b_local.at[p])

    masks = [head_mask(a) for a in range(2)]

    def attend(p):
        own_copy(p).wait()
        send_copies(p, lambda copy: copy.wait_recv())
        for j in range(4):
            r = rows16(j)
            query = got[p, :, r, 0:128].reshape(128, 128)
            keys = jnp.concatenate(
                [before[p, :, r, 0:128].reshape(64, 128), got[p, :, r, 128:256].reshape(128, 128),
                 after[p, :, r, 0:128].reshape(64, 128)], axis=0)
            values = jnp.concatenate(
                [before[p, :, r, 128:256].reshape(64, 128), got[p, :, r, 256:384].reshape(128, 128),
                 after[p, :, r, 128:256].reshape(64, 128)], axis=0)
            grad = got_grad[p, :, r, :].reshape(128, 128)
            queries = [query * masks[a] for a in range(2)]
            grad_both = jnp.concatenate([grad * masks[a] for a in range(2)], axis=0)
            grad_probs = matmul(values, grad_both, NT)
            probs, grad_scores = [], []
            for a in range(2):
                head = 2 * p + a
                scores = matmul(
                    jnp.concatenate([keys, cold[head * 4 + j]], axis=1),
                    jnp.concatenate([queries[a], hot[head * 4 + j]], axis=1), NT)
                prob = jnp.exp(scores - logsum[j, pl.ds(head, 1), :])
                own = grad_probs[:, a * 128 : a * 128 + 128]
                delta = jnp.sum(prob * own, axis=0, keepdims=True)
                probs.append(prob.astype(BF16))
                grad_scores.append((prob * (own - delta)).astype(BF16))
            grad_scores = jnp.concatenate(grad_scores, axis=1)
            dk = matmul(grad_scores, jnp.concatenate(queries, axis=0))
            dv = matmul(jnp.concatenate(probs, axis=1), grad_both)
            dq = heads_home(matmul(keys, grad_scores, TN)) * 0.125
            both = jnp.concatenate([dk, dv], axis=1).astype(BF16)
            to_before[p, :, r, :] = both[0:64].reshape(4, 16, 256)
            to_after[p, :, r, :] = both[192:256].reshape(4, 16, 256)
            grads[p, :, r, 0:128] = dq.astype(BF16).reshape(8, 16, 128)
            grads[p, :, r, 128:384] = both[64:192].reshape(8, 16, 256)
        for copy in halo(p):
            copy.start()

    def give(p):
        for copy in halo(p):
            copy.wait_recv()
        for part, extra in ((slice(0, 4), from_before), (slice(4, 8), from_after)):
            grads[p, part, :, 128:384] = (
                grads[p, part, :, 128:384].astype(F32) + extra[p].astype(F32)
            ).astype(BF16)
        back_copies(p, lambda copy: copy.start())
        own_back(p).start()

    def home(p):
        own_back(p).wait()
        back_copies(p, lambda copy: copy.wait_recv())
        rows = back[p].reshape(count, 384)
        moved = [matmul(to_tokens(slot_col, 2 * p + a, count), rows) for a in range(2)]
        grad_qkv = pair_select(moved[0], moved[1]).astype(BF16)
        back[p] = grad_qkv.reshape(8, 64, 384)
        weight = matmul(x_turned[...], grad_qkv).astype(BF16)
        group, late = p % 3, p // 3
        for t, lane in enumerate((late, 2 + late, 4 + late)):
            grads_q[group][:, :, :, lane * 128 : lane * 128 + 128] = weight[:, t * 128 : t * 128 + 128].reshape(2, 4, 96, 128)

    def turn_back(i):
        rows = slice(i * 128, i * 128 + 128)
        value = grad_first[rows, :]
        for g in range(3):
            pair = [back[2 * g + b, 2 * i : 2 * i + 2].reshape(128, 384) for b in range(2)]
            value = value + matmul(jnp.concatenate(pair, axis=1), fq[g].reshape(768, 768), NT)
        grad_x[rows, :] = value

    attend(0)
    doubling.advance()
    attend(3)
    sum_o.to_near()
    attend(1)
    give(0)
    give(3)
    attend(4)
    give(1)
    doubling.advance()
    attend(2)
    give(4)
    sum_d.to_y()
    attend(5)
    give(2)
    give(5)
    for copy in loads[5:]:
        copy.wait()
    home(0)
    home(3)
    by_group[0].start()
    sum_u.to_y()
    home(1)
    doubling.advance()
    by_group[0].to_opposite()
    sum_o.to_y()
    home(4)
    by_group[1].start()
    sum_d.to_z()
    by_group[0].to_near()
    home(2)
    doubling.advance()
    by_group[1].to_opposite()
    home(5)
    by_group[2].start()
    doubling.advance()
    sum_u.to_z()
    by_group[0].to_y()
    by_group[1].to_near()
    by_group[2].to_opposite()
    sum_o.to_z()
    turn_back(0)
    doubling.advance()
    by_group[1].to_y()
    by_group[0].to_z()
    by_group[2].to_near()
    sum_d.spread()
    turn_back(1)
    by_group[1].to_z()
    by_group[2].to_y()
    sum_u.spread()
    sum_o.spread()
    by_group[0].spread()
    turn_back(2)
    by_group[2].to_z()
    doubling.advance()
    by_group[1].spread()

    def settle(p, carry):
        send_copies(p, lambda copy: copy.wait_send())
        back_copies(p, lambda copy: copy.wait_send())
        for copy in halo(p):
            copy.wait_send()
        return carry

    lax.fori_loop(0, 6, settle, 0)
    seat = place.y * 2 + place.core
    for r, target in zip((sum_d, sum_u, sum_o), (out_d, out_u, out_o)):
        r.finish()
        width = r.half // 16
        offset = (place.zlo % 2) * (8 * width - (r.half - r.window)) + seat * width
        cut(r.out[...].astype(F32), offset, target)
    turn_back(3)
    by_group[2].spread()
    total = tile[8]
    loss_out[...] = total[4:5, 0:1]
    all_width = total.shape[1]
    shift = (all_width - (place.ctx * 8 + place.wsh) * norms_out.shape[1]) % all_width
    norms_out[...] = pltpu.roll(total, shift, 1)[0:4, 0 : norms_out.shape[1]]
    for r in rest:
        r.drain()
    for r in by_group:
        r.finish()
    tiles = [by_group[g].out[:, i * 128 : i * 128 + 128].astype(F32) for i in range(3) for g in range(3)]
    width = 72
    cut(jnp.concatenate(tiles, axis=1), (place.zlo % 2) * 8 * width + seat * width, out_q)
    for r in by_group:
        r.drain()
    doubling.drain()


def backward(grad_mixed, grad_first, small, x_turned, fq, kept, halves, nears):
    got, before, after, logsum, hot, cold, slot_row, slot_col = kept
    count = grad_mixed.shape[0]
    dma = pltpu.SemaphoreType.DMA
    vm = pltpu.VMEM
    rows_in = (halves[2].shape[2],)
    shapes = [(96, 384, 256), (96, 1536, 768), (rows_in[0], 384, 256)] + [(96, 384, 384)] * 3
    reduce_refs = []
    for shape in shapes:
        reduce_refs += reduce_scratch(*shape)
    loaded = (x_turned, fq, got, before, after, hot, cold)
    results = pl.pallas_call(
        backward_kernel,
        out_shape=[
            shaped(*grad_first.shape, dtype=F32),
            shaped(72, 96, dtype=F32),
            shaped(24, 96, dtype=F32),
            shaped(96, 96, dtype=F32),
            shaped(24, 384, dtype=F32),
            shaped(4, small.shape[1] // 256, dtype=F32),
            shaped(1, 1, dtype=F32),
        ],
        in_specs=[VMEM] * 6 + [ANY] * 12,
        out_specs=[VMEM] * 7,
        scratch_shapes=[vm(array.shape, array.dtype) for array in loaded]
        + [
            vm((6, count, 128), BF16),
            vm((6, 8, 64, 128), BF16),
            vm((6, 8, 64, 384), BF16),
            vm((6, 4, 64, 256), BF16),
            vm((6, 4, 64, 256), BF16),
            vm((6, 4, 64, 256), BF16),
            vm((6, 4, 64, 256), BF16),
            vm((6, 8, 64, 384), BF16),
        ]
        + [vm((2, 4, 96, 768), BF16)] * 3
        + reduce_refs
        + [
            vm((9, *small.shape), F32),
            vm((8, *small.shape), F32),
            dma((6, 7)), dma((6, 7)), dma((6,)), dma((6, 2)), dma((6, 2)),
            dma((6, 7)), dma((6, 7)), dma((6,)),
            dma((8,)), dma((8,)), dma((6, 17)), dma((6, 18)), dma((3, 2)), dma((7,)),
        ],
        compiler_params=pltpu.CompilerParams(
            collective_id=1, has_side_effects=True, vmem_limit_bytes=62 * 2**20
        ),
        name="backward_attention",
    )(grad_mixed, grad_first, logsum, slot_row, slot_col, small, *loaded, *halves, *nears)
    return results


CHUNK = 512


def norm_rows(values):
    centered = values - jnp.mean(values, axis=-1, keepdims=True)
    scale = lax.rsqrt(jnp.mean(centered * centered, axis=-1, keepdims=True) + 1e-05)
    return centered * scale, scale


def norm_rows_back(grad, normed, scale, gain):
    weighted = grad * gain
    return scale * (
        weighted
        - jnp.mean(weighted, axis=-1, keepdims=True)
        - normed * jnp.mean(weighted * normed, axis=-1, keepdims=True)
    )


def middle_kernel(
    everyone, ctx_size,
    mixed, x, teacher, slot_col, total, wo_hbm, wu_hbm, wd_hbm,
    result, grad_first, grad_mixed, small, go_hbm, gu_hbm, gd_hbm, near_u, near_d,
    wo, wu, wd, active, slope, normed, unit, scale, low, low_turned, acc, branch, grad_upper, go, gu, gd,
    held_o, held_u, held_d, in_sem, out_sem, send_sem, recv_sem, x_send, x_recv,
):
    place = Place()
    core, sibling = place.core, place.sibling()
    loads = [
        pltpu.make_async_copy(source, target, in_sem.at[i])
        for i, (source, target) in enumerate(((wo_hbm, wo), (wu_hbm, wu), (wd_hbm, wd)))
    ]
    for copy in loads:
        copy.start()
    greet([sibling, place.x_peer(1), place.x_peer(3)])
    count, width = x.shape
    tile = 128
    chunks = wd.shape[0] // CHUNK
    gains = total[0:4] / ctx_size
    small[...] = jnp.zeros_like(small)

    def rows_of(i):
        return pl.ds(pl.multiple_of(i * tile, tile), tile)

    def lanes_of(c):
        return pl.ds(pl.multiple_of(c * CHUNK, CHUNK), CHUNK)

    loads[0].wait()
    for i in range(2):
        rows = slice(i * 256, i * 256 + 256)
        acc[rows, :] = matmul(mixed[rows, :], wo[...])

    def first_norm(i, carry):
        rows = rows_of(i)
        unit_rows, scale_rows = norm_rows(x[rows, :].astype(F32) + acc[rows, :])
        unit[rows, :] = unit_rows
        scale[rows, :] = scale_rows
        value = unit_rows * gains[0:1] + gains[1:2]
        normed[rows, :] = value
        low[rows, :] = value.astype(BF16)
        acc[rows, :] = value
        return carry

    lax.fori_loop(0, count // tile, first_norm, 0)
    loads[1].wait()
    loads[2].wait()

    def expand(c, carry):
        lanes = lanes_of(c)
        up = wu[:, :, lanes].reshape(width, CHUNK)
        down = wd[lanes, :]
        for i in range(2):
            rows = slice(i * 256, i * 256 + 256)
            upper = matmul(low[rows, :], up)
            share = 0.5 + 0.5 * lax.erf(upper * 0.7071067811865476)
            density = jnp.exp(upper * upper * -0.5) * 0.3989422804014327
            value = (upper * share).astype(BF16)
            active[rows, lanes] = value
            slope[rows, lanes] = share + upper * density
            acc[rows, :] += matmul(value, down)
        return carry

    lax.fori_loop(0, chunks, expand, 0)
    low_turned[...] = normed[...].T.astype(BF16)

    def second_norm(i, carry):
        rows = rows_of(i)
        unit_rows, scale_rows = norm_rows(acc[rows, :])
        value = unit_rows * gains[2:3] + gains[3:4]
        result[rows, :] = value.astype(BF16)
        error = value - teacher[rows, :].astype(F32)
        mask = slot_col[rows, 12:13]
        losses = mask * jnp.mean(error * error, axis=-1, keepdims=True)
        grad = (everyone / total[4:5, 0:1]) * mask * error
        small[2:3, :] += jnp.sum(grad * unit_rows, axis=0, keepdims=True)
        small[3:4, :] += jnp.sum(grad, axis=0, keepdims=True)
        small[4:5, 0:1] += jnp.sum(losses, axis=0, keepdims=True) / total[4:5, 0:1]
        back = norm_rows_back(grad, unit_rows, scale_rows, gains[2:3])
        acc[rows, :] = back
        branch[rows, :] = back.astype(BF16)
        return carry

    lax.fori_loop(0, count // tile, second_norm, 0)

    half = chunks // 2
    theirs, ours = half_of(width, 1 - core), half_of(width, core)

    def down_copy(c):
        lanes = lanes_of(c)
        return remote(gd.at[lanes, theirs], held_d.at[lanes], send_sem.at[c], recv_sem.at[c], sibling)

    def up_copy(i):
        return remote(gu.at[i], held_u.at[i], send_sem.at[chunks + i], recv_sem.at[chunks + i], sibling)

    def up_out(i):
        return pltpu.make_async_copy(held_u.at[i], gu_hbm.at[:, :, lanes_of(i)], out_sem.at[chunks + i])

    deep = wd.shape[0] // 16
    shallow = width // 16

    def opposite(zh):
        return zh * 4 + (place.x + 2) % 4

    def down_across(k, zh):
        part = pl.ds(pl.multiple_of(opposite(zh) * 2 * deep + k * deep, 16), deep)
        return remote(
            held_d.at[part], near_d.at[k, zh], x_send.at[2 * k + zh], x_recv.at[2 * k + zh], place.x_peer(1 + 2 * k)
        )

    def up_across(i, k, zh):
        n = 4 + i * 4 + 2 * k + zh
        return remote(
            held_u.at[i, opposite(zh), k * shallow : (k + 1) * shallow], near_u.at[k, zh, :, lanes_of(i)],
            x_send.at[n], x_recv.at[n], place.x_peer(1 + 2 * k),
        )

    def make_down(c, carry):
        lanes = lanes_of(c)
        gd[lanes, :] = matmul(active[:, lanes], branch[...], TN).astype(BF16)
        down_copy(c).start()
        return carry

    lax.fori_loop(0, chunks, make_down, 0)

    def contract(c):
        lanes = lanes_of(c)
        up = wu[:, :, lanes].reshape(width, CHUNK)
        down = wd[lanes, :]
        for i in range(2):
            rows = slice(i * 256, i * 256 + 256)
            value = (matmul(branch[rows, :], down, NT) * slope[rows, lanes]).astype(BF16)
            grad_upper[rows, :] = value
            acc[rows, :] += matmul(value, up, NT)
        return matmul(low_turned[...], grad_upper[...]).reshape(8, width // 8, CHUNK)

    def for_sibling(i, carry):
        gu[i] = contract((1 - core) * half + i).astype(BF16)
        up_copy(i).start()
        return carry

    def for_own(i, carry):
        value = contract(core * half + i)
        up_copy(i).wait_recv()
        held_u[i] = (value + held_u[i].astype(F32)).astype(BF16)
        up_out(i).start()
        for k in range(2):
            for zh in range(2):
                up_across(i, k, zh).start()
        return carry

    def down_out(c):
        lanes = lanes_of(c)
        return pltpu.make_async_copy(held_d.at[lanes], gd_hbm.at[lanes], out_sem.at[c])

    def add_down(c, carry):
        lanes = lanes_of(c)
        down_copy(c).wait_recv()
        held_d[lanes, :] = (gd[lanes, ours].astype(F32) + held_d[lanes, :].astype(F32)).astype(BF16)
        down_out(c).start()
        return carry

    lax.fori_loop(0, chunks, add_down, 0)
    for k in range(2):
        for zh in range(2):
            down_across(k, zh).start()
    lax.fori_loop(0, half, for_sibling, 0)
    lax.fori_loop(0, half, for_own, 0)

    def first_back(i, carry):
        rows = rows_of(i)
        grad = acc[rows, :]
        small[0:1, :] += jnp.sum(grad * unit[rows, :], axis=0, keepdims=True)
        small[1:2, :] += jnp.sum(grad, axis=0, keepdims=True)
        back = norm_rows_back(grad, unit[rows, :], scale[rows, :], gains[0:1])
        grad_first[rows, :] = back
        branch[rows, :] = back.astype(BF16)
        return carry

    lax.fori_loop(0, count // tile, first_back, 0)
    go[...] = matmul(mixed[...], branch[...], TN).astype(BF16)
    last = remote(go.at[:, theirs], held_o, send_sem.at[chunks + half], recv_sem.at[chunks + half], sibling)
    last.start()
    for i in range(2):
        rows = slice(i * 256, i * 256 + 256)
        grad_mixed[rows, :] = matmul(branch[rows, :], wo[...], NT).astype(BF16)

    last.wait_recv()
    held_o[...] = (go[:, ours].astype(F32) + held_o[...].astype(F32)).astype(BF16)
    out = pltpu.make_async_copy(held_o, go_hbm, in_sem.at[0])
    out.start()

    def settle_down(c, carry):
        down_copy(c).wait_send()
        down_out(c).wait()
        return carry

    def settle_up(i, carry):
        up_copy(i).wait_send()
        up_out(i).wait()
        return carry

    lax.fori_loop(0, chunks, settle_down, 0)
    lax.fori_loop(0, half, settle_up, 0)
    last.wait_send()
    for k in range(2):
        for zh in range(2):
            down_across(k, zh).wait()
            for i in range(half):
                up_across(i, k, zh).wait()
    out.wait()


def middle(everyone, ctx_size, mixed, x, teacher, slot_col, total, wo, wu, wd):
    count, width = x.shape
    hidden = wd.shape[0]
    chunks = hidden // CHUNK
    dma = pltpu.SemaphoreType.DMA
    vm = pltpu.VMEM
    return pl.pallas_call(
        functools.partial(middle_kernel, everyone, ctx_size),
        out_shape=[
            shaped(count, width),
            shaped(count, width, dtype=F32),
            shaped(count, width),
            shaped(8, width, dtype=F32),
            shaped(width, width // 2),
            shaped(8, width // 8, hidden // 2),
            shaped(hidden, width // 2),
            shaped(2, 2, width // 16, hidden // 2),
            shaped(2, 2, hidden // 16, width // 2),
        ],
        in_specs=[VMEM] * 5 + [ANY] * 3,
        out_specs=[VMEM] * 4 + [ANY] * 5,
        scratch_shapes=[
            vm(wo.shape, BF16), vm(wu.shape, BF16), vm(wd.shape, BF16),
            vm((count, hidden), BF16), vm((count, hidden), F32),
            vm((count, width), F32), vm((count, width), F32), vm((count, 1), F32),
            vm((count, width), BF16), vm((width, count), BF16), vm((count, width), F32),
            vm((count, width), BF16), vm((count, CHUNK), BF16),
            vm(wo.shape, BF16), vm((chunks // 2, 8, width // 8, CHUNK), BF16), vm(wd.shape, BF16),
            vm((width, width // 2), BF16), vm((chunks // 2, 8, width // 8, CHUNK), BF16), vm((hidden, width // 2), BF16),
            dma((3,)), dma((chunks + chunks // 2,)), dma((chunks + chunks // 2 + 1,)), dma((chunks + chunks // 2 + 1,)),
            dma((4 + 2 * chunks,)), dma((4 + 2 * chunks,)),
        ],
        compiler_params=pltpu.CompilerParams(
            collective_id=2, has_side_effects=True, vmem_limit_bytes=62 * 2**20
        ),
        name="dense_middle",
    )(mixed, x, teacher, slot_col, total, wo, wu, wd)


def local(tokens, teacher, clusters, segments, counted, w_qkv, w_out, w_up, w_down, norms):
    x_rows = tokens[0]
    tok_count, model_dim = x_rows.shape
    ctx_size, wsh_size = lax.axis_size("ctx"), lax.axis_size("wsh")
    mixed, x_turned, fq, fo, fu, fd, *kept, total = forward(
        x_rows, clusters[0], segments, counted, norms, (w_qkv, w_out, w_up, w_down)
    )
    everyone = float(tok_count * ctx_size * wsh_size)
    result, grad_first, grad_mixed, small, go, gu, gd, *nears = middle(
        everyone, float(ctx_size), mixed, x_rows, teacher[0], kept[-1], total,
        fo.reshape(-1, model_dim), fu, fd.reshape(-1, model_dim),
    )
    grad_tokens, final_qkv, final_out, final_up, final_down, final_norms, loss = backward(
        grad_mixed, grad_first, small, x_turned, fq, kept,
        [g.reshape(2, 4, -1, g.shape[-1]) for g in (go, gu, gd)], nears,
    )
    return (
        result[None],
        grad_tokens[None],
        loss.reshape(()),
        final_qkv.T,
        final_out.T,
        final_up,
        final_down.T,
        final_norms,
    )


def solution(mesh):
    placed = (
        P("wsh", "ctx", None),
        P("wsh", "ctx", None),
        P("wsh", None, "ctx"),
        P("wsh", "ctx"),
        P("wsh", "ctx"),
        P("wsh", None),
        P("wsh", None),
        P("wsh", None),
        P("wsh", None),
        P(None, "wsh"),
    )
    return jax.shard_map(
        local,
        mesh=mesh,
        in_specs=placed,
        out_specs=(
            P("wsh", "ctx", None),
            P("wsh", "ctx", None),
            P(),
            P("wsh", "ctx"),
            P("wsh", "ctx"),
            P("wsh", "ctx"),
            P("wsh", "ctx"),
            P(None, ("ctx", "wsh")),
        ),
        check_vma=False,
    )
```

```python
import functools
import jax
import jax.numpy as jnp
from jax import lax
from jax.experimental import pallas as pl
from jax.experimental.pallas import tpu as pltpu
from jax.sharding import PartitionSpec as P

MESH = pl.DeviceIdType.MESH
BF16 = jnp.bfloat16
F32 = jnp.float32


class Place:
    def __init__(self):
        self.ctx = lax.axis_index("ctx")
        self.wsh = lax.axis_index("wsh")
        self.zlo = self.ctx // 8
        self.y = (self.ctx // 2) % 4
        self.core = self.ctx % 2
        self.zhi = self.wsh // 4
        self.x = self.wsh % 4

    def at(self, zlo=None, y=None, core=None, zhi=None, x=None):
        zlo = self.zlo if zlo is None else zlo
        y = self.y if y is None else y
        core = self.core if core is None else core
        zhi = self.zhi if zhi is None else zhi
        x = self.x if x is None else x
        return (zlo * 8 + y * 2 + core, zhi * 4 + x)

    def sibling(self):
        return self.at(core=1 - self.core)

    def x_peer(self, step):
        return self.at(x=(self.x + step) % 4)

    def y_peer(self, step):
        return self.at(y=(self.y + step) % 4)

    def z_peer(self, step):
        z = (self.zhi * 4 + self.zlo + step + 8) % 8
        return self.at(zlo=z % 4, zhi=z // 4)

    def plane(self):
        return [
            self.at(y=(self.y + d) % 4, core=(self.core + c) % 2)
            for d, c in ((0, 1), (1, 0), (1, 1), (2, 0), (2, 1), (3, 0), (3, 1))
        ]

    def rank(self):
        return self.y * 2 + self.core

    def z_far(self):
        return self.at(zhi=1 - self.zhi)

    def doubling(self):
        return (
            self.z_far(),
            self.sibling(),
            self.at(y=self.y + 1 - 2 * (self.y % 2)),
            self.at(y=(self.y + 2) % 4),
            self.at(x=self.x + 1 - 2 * (self.x % 2)),
            self.at(x=(self.x + 2) % 4),
            self.at(zlo=self.zlo + 1 - 2 * (self.zlo % 2)),
            self.at(zlo=(self.zlo + 2) % 4),
        )


def greet(devices):
    barrier = pltpu.get_barrier_semaphore()
    for device in devices:
        pl.semaphore_signal(barrier, inc=1, device_id=device, device_id_type=MESH)
    pl.semaphore_wait(barrier, len(devices))


def remote(source, target, send_sem, recv_sem, device):
    return pltpu.make_async_remote_copy(
        src_ref=source,
        dst_ref=target,
        send_sem=send_sem,
        recv_sem=recv_sem,
        device_id=device,
        device_id_type=MESH,
    )


def half_of(width, which):
    half = width // 2
    return pl.ds(pl.multiple_of(which * half, 128), half)


class Doubling:
    def __init__(self, place, tile, slots, send_sems, recv_sems):
        self.partners = place.doubling()
        self.tile, self.slots = tile, slots
        self.send_sems, self.recv_sems = send_sems, recv_sems
        self.step = 0
        self.copies = []

    def start(self):
        k = self.step
        copy = remote(
            self.tile.at[k], self.slots.at[k], self.send_sems.at[k], self.recv_sems.at[k], self.partners[k]
        )
        copy.start()
        self.copies.append(copy)

    def advance(self):
        k = self.step
        self.copies[k].wait_recv()
        self.tile[k + 1] = self.tile[k] + self.slots[k]
        self.step = k + 1
        if self.step < 8:
            self.start()

    def drain(self):
        for copy in self.copies:
            copy.wait_send()


NEG = -1e30
NT = (((1,), (1,)), ((), ()))
TN = (((0,), (0,)), ((), ()))


def matmul(left, right, dims=(((1,), (0,)), ((), ()))):
    return lax.dot_general(left, right, dims, preferred_element_type=F32)


class Gather:
    def __init__(self, place, shard, full, send_sems, recv_sems, local_sem):
        self.place, self.shard, self.full = place, shard, full
        self.send_sems, self.recv_sems = send_sems, recv_sems
        self.rows = shard.shape[0]
        self.lanes = half_of(shard.shape[1], place.core)
        self.local = pltpu.make_async_copy(shard, full.at[place.wsh], local_sem)
        self.copies = {}

    def part(self, index, which=None):
        block = self.full.at[index]
        if which is None:
            return block.at[:, self.lanes]
        half = self.rows // 2
        return block.at[which * half : (which + 1) * half, self.lanes]

    def send(self, k, source, target, device):
        copy = remote(source, target, self.send_sems.at[k], self.recv_sems.at[k], device)
        copy.start()
        self.copies[k] = copy

    def own(self, far, step):
        return (far * 4) + (self.place.x + step + 4) % 4

    def start_z(self):
        place = self.place
        self.local.start()
        self.send(2, self.shard.at[:, self.lanes], self.part(place.wsh), place.z_far())

    def step_z(self, k, source, block, step):
        part = self.part(block)
        return remote(
            part if source is None else source, part, self.send_sems.at[2 + 17 * k], self.recv_sems.at[2],
            self.place.z_peer(step),
        )

    def start_run(self):
        self.local.start()
        own = self.shard.at[:, self.lanes]
        for end, step in ((3, 1), (0, -1)):
            @pl.when(self.place.zlo == end)
            def _(step=step):
                self.step_z(0, own, self.place.wsh, step).start()

    def pass_run(self):
        far = self.own(1 - self.place.zhi, 0)
        for end, step in ((0, 1), (3, -1)):
            @pl.when(self.place.zlo == end)
            def _(step=step):
                copy = self.step_z(1, None, far, step)
                copy.wait_recv()
                copy.start()

    def from_run(self):
        place = self.place
        index = self.own(1 - place.zhi, 0)

        @pl.when(jnp.logical_or(place.zlo == 1, place.zlo == 2))
        def _():
            self.step_z(0, None, index, 1).wait_recv()

        self.send(10, self.part(index), self.part(index), place.x_peer(1))
        self.send(11, self.part(index), self.part(index), place.x_peer(3))
        self.send(9, self.part(index), self.part(index), place.sibling())

    def drain_run(self):
        @pl.when(jnp.logical_or(self.place.zlo == 0, self.place.zlo == 3))
        def _():
            for k in range(2):
                self.step_z(k, None, self.place.wsh, 1).wait_send()

    def start_x(self):
        place = self.place
        self.send(0, self.shard.at[:, self.lanes], self.part(place.wsh), place.x_peer(1))
        self.send(1, self.shard.at[:, self.lanes], self.part(place.wsh), place.x_peer(3))

    def pass_on(self, zh, base):
        place = self.place
        left, right = self.own(zh, -1), self.own(zh, 1)
        self.copies[base].wait_recv()
        self.send(base + 3, self.part(left, 0), self.part(left, 0), place.x_peer(1))
        self.send(base + 5, self.part(left), self.part(left), place.sibling())
        self.copies[base + 1].wait_recv()
        self.send(base + 4, self.part(right, 1), self.part(right, 1), place.x_peer(3))
        self.send(base + 6, self.part(right), self.part(right), place.sibling())

    def opposite(self, zh, base):
        place = self.place
        index = self.own(zh, 2)
        for which in range(2):
            self.copies[base + 3 + which].wait_recv()
            self.send(base + 7 + which, self.part(index, which), self.part(index, which), place.sibling())

    def near(self):
        self.pass_on(self.place.zhi, 0)

    def near_opposite(self):
        self.opposite(self.place.zhi, 0)

    def from_z(self):
        place = self.place
        index = self.own(1 - place.zhi, 0)
        self.copies[2].wait_recv()
        self.send(10, self.part(index), self.part(index), place.x_peer(1))
        self.send(11, self.part(index), self.part(index), place.x_peer(3))
        self.send(9, self.part(index), self.part(index), place.sibling())

    def far(self):
        self.pass_on(1 - self.place.zhi, 10)

    def far_opposite(self):
        self.opposite(1 - self.place.zhi, 10)

    def finish(self):
        self.local.wait()
        for k in (5, 6, 7, 8, 9, 15, 16, 17, 18):
            self.copies[k].wait_recv()

    def drain(self):
        for k in self.copies:
            self.copies[k].wait_send()


def head_mask(which):
    lane = lax.broadcasted_iota(jnp.int32, (1, 128), 1)
    return jnp.where((lane // 64) == which, 1.0, 0.0).astype(BF16)


def to_slots(slot_row, head, count):
    row = slot_row[pl.ds(head, 1), :]
    iota = lax.broadcasted_iota(jnp.int32, (count, count), 0).astype(F32)
    return jnp.where(iota == row, 1.0, 0.0).astype(BF16)


def to_tokens(slot_col, head, count):
    lane = lax.broadcasted_iota(jnp.int32, slot_col.shape, 1)
    column = jnp.sum(jnp.where(lane == head, slot_col[...], 0.0), axis=1, keepdims=True)
    iota = lax.broadcasted_iota(jnp.int32, (count, count), 1).astype(F32)
    return jnp.where(iota == column, 1.0, 0.0).astype(BF16)


def pair_select(first, second):
    lane = lax.broadcasted_iota(jnp.int32, first.shape, 1)
    return jnp.where((lane // 64) % 2 == 0, first, second)


def heads_home(turned):
    return jnp.concatenate([turned[0:64, 0:128], turned[64:128, 128:256]], axis=0).T


def make_slots(clusters, segments, counted, slot_row, slot_col, labels):
    heads, count = clusters.shape
    groups = lax.shift_right_logical(clusters[...], 2)
    iota = lax.broadcasted_iota(jnp.int32, (32, count), 0)
    before = lax.broadcasted_iota(jnp.int32, (count, count), 0)
    after = lax.broadcasted_iota(jnp.int32, (count, count), 1)
    upper = jnp.where(before <= after, 1.0, 0.0).astype(BF16)
    hot = [jnp.where(groups[h : h + 1, :] == iota, 1.0, 0.0) for h in range(heads)]
    counts = matmul(jnp.concatenate(hot, axis=0).astype(BF16), upper)
    group_f = groups.astype(F32)
    rows = []
    for h in range(heads):
        rank = jnp.sum(counts[32 * h : 32 * h + 32] * hot[h], axis=0, keepdims=True)
        rows.append(group_f[h : h + 1] * 16.0 + rank - 1.0)
    slots = jnp.concatenate(rows + [counted[...].astype(F32), jnp.zeros((127 - heads, count), F32)], axis=0)
    slot_row[...] = slots[:16]
    slot_col[...] = slots.T
    label = (segments[0:1, :] * 4 + (clusters[...] & 3)).astype(F32)
    labels[...] = jnp.concatenate([label, jnp.zeros((128 - heads, count), F32)], axis=0).T.astype(BF16)


def rows16(j):
    return slice(16 * j, 16 * j + 16)


def forward_kernel(
    x, clusters, segments, counted, norms, wq, wo, wu, wd,
    mixed, x_turned, fq_out, fo, fu, fd, got_out, before_out, after_out, logsum, hot_out, cold_out, slot_row, slot_col, total,
    pieces, fq, got, before, after, hot, cold,
    labels, sent_labels, got_labels, before_labels, after_labels, wide_labels, sent, out, back,
    tile, slots,
    w_send, w_recv, w_local, t_send, t_recv, a_send, a_recv, a_local, z_send, z_recv, b_send, b_recv, b_local, k_sem,
):
    place = Place()
    plane, rank = place.plane(), place.rank()
    up, down = place.z_peer(1), place.z_peer(-1)
    kept = []

    def keep(source, target):
        copy = pltpu.make_async_copy(source, target, k_sem.at[len(kept)])
        copy.start()
        kept.append(copy)

    partners = place.doubling()
    for g in range(3):
        for b in range(2):
            for t in range(3):
                lane = t * 768 + (2 * g + b) * 128
                pieces[g, :, b * 384 + t * 128 : b * 384 + t * 128 + 128] = wq[:, lane : lane + 128]
    greet(
        plane + [place.x_peer(1), place.x_peer(2), place.x_peer(3), place.z_far(), up, down, partners[6], partners[7]]
    )
    weights = [
        Gather(place, shard, full, w_send.at[i], w_recv.at[i], w_local.at[i])
        for i, (shard, full) in enumerate(
            [(pieces.at[g], fq.at[g]) for g in range(3)] + [(wo, fo), (wu, fu), (wd, fd)]
        )
    ]
    first, second, third, w_out, w_up, w_down = weights
    rest = (w_out, w_up, w_down)
    tile[0] = jnp.zeros_like(tile[0])
    tile[0, 0:4, 0 : norms.shape[1]] = norms[...].astype(F32)
    tile[0] = pltpu.roll(tile[0], place.wsh * norms.shape[1], 1)
    lane_zero = lax.broadcasted_iota(jnp.int32, (1, tile.shape[2]), 1) == 0
    tile[0, 4:5, :] = jnp.where(lane_zero, jnp.sum(counted[...].astype(F32), axis=1, keepdims=True), 0.0)
    doubling = Doubling(place, tile, slots, t_send, t_recv)
    doubling.start()
    first.start_z()
    first.start_x()
    count = x.shape[0]
    make_slots(clusters, segments, counted, slot_row, slot_col, labels)

    second.start_z()
    second.start_x()
    sent_labels[...] = jnp.zeros_like(sent_labels)

    def move_labels(head, carry):
        lane = lax.broadcasted_iota(jnp.int32, (count, 128), 1)
        moved = matmul(to_slots(slot_row, head, count), labels[...])
        sent_labels[...] = jnp.where(lane == head, moved, sent_labels[...])
        return carry

    lax.fori_loop(0, 6, move_labels, 0)
    first.near()
    third.start_z()
    third.start_x()
    lax.fori_loop(6, 12, move_labels, 0)
    labels[...] = sent_labels[...].astype(BF16)

    def block(which):
        return pl.ds(pl.multiple_of(which * 64, 64), 64)

    def ranks():
        return [dev[0] % 8 for dev in plane]

    label_copies = [
        remote(labels.at[block(to)], got_labels.at[rank], a_send.at[6, k], a_recv.at[6, k], plane[k])
        for k, to in enumerate(ranks())
    ]
    for copy in label_copies:
        copy.start()
    own_labels = pltpu.make_async_copy(labels.at[block(rank)], got_labels.at[rank], a_local.at[6])
    own_labels.start()
    first.from_z()
    second.near()
    first.near_opposite()
    doubling.advance()
    x_turned[...] = x[...].astype(F32).T.astype(BF16)
    doubling.advance()
    second.from_z()
    first.far()
    third.near()
    second.near_opposite()
    doubling.advance()
    third.from_z()
    own_labels.wait()
    for copy in label_copies:
        copy.wait_recv()
    label_up = remote(got_labels.at[4:8], before_labels, z_send.at[6, 0], z_recv.at[6, 0], up)
    label_down = remote(got_labels.at[0:4], after_labels, z_send.at[6, 1], z_recv.at[6, 1], down)
    label_up.start()
    label_down.start()
    for w in rest:
        w.start_run()
    first.far_opposite()
    first.finish()

    def make_hot(head, carry):
        lane = lax.broadcasted_iota(jnp.int32, (256, 128), 1)
        for j in range(4):
            column = jnp.sum(jnp.where(lane == head, wide_labels[j], 0.0), axis=1, keepdims=True)
            same = lane.astype(F32) == column
            cold[head * 4 + j] = jnp.where(same, 0.0, NEG).astype(BF16)
            hot[head * 4 + j] = jnp.where(same, 1.0, 0.0)[64:192].astype(BF16)
        return carry

    def send_copies(p, fn):
        for k, to in enumerate(ranks()):
            fn(remote(sent.at[p, block(to)], got.at[p, rank], a_send.at[p, k], a_recv.at[p, k], plane[k]))

    def own_copy(p):
        return pltpu.make_async_copy(sent.at[p, block(rank)], got.at[p, rank], a_local.at[p])

    def project(g):
        value = matmul(x[...], fq[g].reshape(768, 768))
        lane = lax.broadcasted_iota(jnp.int32, (1, 384), 1)
        scale = jnp.where(lane < 128, 0.125, 1.0)
        for b in range(2):
            p = 2 * g + b
            rows = (value[:, b * 384 : b * 384 + 384] * scale).astype(BF16)
            moved = [matmul(to_slots(slot_row, 2 * p + a, count), rows) for a in range(2)]
            sent[p] = pair_select(moved[0], moved[1]).astype(BF16)
            send_copies(p, lambda copy: copy.start())
            own_copy(p).start()

    project(0)
    second.far()
    third.near_opposite()
    third.far()
    second.far_opposite()
    second.finish()
    doubling.advance()
    for w in rest:
        w.start_x()
    project(1)
    w_out.pass_run()
    w_up.pass_run()
    third.far_opposite()
    third.finish()
    project(2)
    w_down.pass_run()
    keep(fq, fq_out)
    label_up.wait_recv()
    label_down.wait_recv()
    for j in range(4):
        wide_labels[j, 0:64] = jnp.where(
            place.zlo == 0, -1.0, before_labels[:, rows16(j), :].reshape(64, 128).astype(F32)
        )
        wide_labels[j, 64:192] = got_labels[:, rows16(j), :].reshape(128, 128).astype(F32)
        wide_labels[j, 192:256] = jnp.where(
            place.zlo == 3, -1.0, after_labels[:, rows16(j), :].reshape(64, 128).astype(F32)
        )
    lax.fori_loop(0, 12, make_hot, 0)
    keep(hot, hot_out)
    keep(cold, cold_out)
    w_out.near()
    w_out.from_run()
    w_up.near()
    doubling.advance()

    def halo(p):
        return (
            remote(got.at[p, 4:8, :, 128:384], before.at[p], z_send.at[p, 0], z_recv.at[p, 0], up),
            remote(got.at[p, 0:4, :, 128:384], after.at[p], z_send.at[p, 1], z_recv.at[p, 1], down),
        )

    def back_copies(p, fn):
        for k, to in enumerate(ranks()):
            fn(remote(out.at[p, to], back.at[p, rank], b_send.at[p, k], b_recv.at[p, k], plane[k]))

    def own_back(p):
        return pltpu.make_async_copy(out.at[p, rank], back.at[p, rank], b_local.at[p])

    def arrive(p):
        own_copy(p).wait()
        send_copies(p, lambda copy: copy.wait_recv())
        for copy in halo(p):
            copy.start()

    masks = [head_mask(a) for a in range(2)]

    def attend(p):
        for copy in halo(p):
            copy.wait_recv()
        for j in range(4):
            r = rows16(j)
            query = got[p, :, r, 0:128].reshape(128, 128)
            keys = jnp.concatenate(
                [before[p, :, r, 0:128].reshape(64, 128), got[p, :, r, 128:256].reshape(128, 128),
                 after[p, :, r, 0:128].reshape(64, 128)], axis=0)
            values = jnp.concatenate(
                [before[p, :, r, 128:256].reshape(64, 128), got[p, :, r, 256:384].reshape(128, 128),
                 after[p, :, r, 128:256].reshape(64, 128)], axis=0)
            probs = []
            for a in range(2):
                head = 2 * p + a
                scores = matmul(
                    jnp.concatenate([keys, cold[head * 4 + j]], axis=1),
                    jnp.concatenate([query * masks[a], hot[head * 4 + j]], axis=1), NT)
                top = jnp.max(scores, axis=0, keepdims=True)
                raised = jnp.exp(scores - top)
                sums = jnp.sum(raised, axis=0, keepdims=True)
                probs.append((raised * (1.0 / sums)).astype(BF16))
                logsum[j, pl.ds(head, 1), :] = top + jnp.log(sums)
            out[p, :, r, :] = heads_home(matmul(values, jnp.concatenate(probs, axis=1), TN)).astype(BF16).reshape(8, 16, 128)
        back_copies(p, lambda copy: copy.start())
        own_back(p).start()

    def home(p):
        own_back(p).wait()
        back_copies(p, lambda copy: copy.wait_recv())
        rows = back[p].reshape(count, 128)
        moved = [matmul(to_tokens(slot_col, 2 * p + a, count), rows) for a in range(2)]
        mixed[:, p * 128 : p * 128 + 128] = pair_select(moved[0], moved[1]).astype(BF16)

    arrive(0)
    w_up.from_run()
    arrive(1)
    attend(0)
    w_down.near()
    w_out.near_opposite()
    arrive(2)
    attend(1)
    w_down.from_run()
    w_up.near_opposite()
    doubling.advance()
    arrive(3)
    attend(2)
    home(0)
    w_out.far()
    arrive(4)
    attend(3)
    home(1)
    w_up.far()
    w_down.near_opposite()
    arrive(5)
    attend(4)
    home(2)
    home(3)
    doubling.advance()

    def settle_out(p, carry):
        send_copies(p, lambda copy: copy.wait_send())
        return carry

    def settle_back(p, carry):
        back_copies(p, lambda copy: copy.wait_send())
        for copy in halo(p):
            copy.wait_send()
        return carry

    lax.fori_loop(0, 6, settle_out, 0)
    for copy in label_copies + [label_up, label_down]:
        copy.wait_send()
    for w in (first, second, third):
        w.drain()
    w_down.far()
    attend(5)
    keep(got, got_out)
    keep(before, before_out)
    keep(after, after_out)
    w_out.far_opposite()
    w_up.far_opposite()
    home(4)
    lax.fori_loop(0, 5, settle_back, 0)
    w_down.far_opposite()
    home(5)
    doubling.advance()
    for w in rest:
        w.finish()
    total[...] = tile[8]
    settle_back(5, 0)
    for w in rest:
        w.drain()
        w.drain_run()
    for copy in kept:
        copy.wait()
    doubling.drain()


ANY = pl.BlockSpec(memory_space=pl.ANY)
VMEM = pl.BlockSpec(memory_space=pltpu.VMEM)


def shaped(*shape, dtype=BF16):
    return jax.ShapeDtypeStruct(shape, dtype)


def forward(x, clusters, segments, counted, norms, shards):
    count, width = x.shape
    dma = pltpu.SemaphoreType.DMA
    return pl.pallas_call(
        forward_kernel,
        out_shape=[
            shaped(*x.shape),
            shaped(width, count),
            shaped(3, 8, shards[0].shape[0], 768),
            *[shaped(8, *w.shape) for w in shards[1:]],
            shaped(6, 8, 64, 384),
            shaped(6, 4, 64, 256),
            shaped(6, 4, 64, 256),
            shaped(4, 16, 128, dtype=F32),
            shaped(48, 128, 128),
            shaped(48, 256, 128),
            shaped(16, count, dtype=F32),
            shaped(count, 128, dtype=F32),
            shaped(8, width, dtype=F32),
        ],
        in_specs=[VMEM] * 9,
        out_specs=[VMEM] * 2 + [ANY] * 7 + [VMEM] + [ANY] * 2 + [VMEM] * 3,
        scratch_shapes=[
            pltpu.VMEM((3, shards[0].shape[0], 768), BF16),
            pltpu.VMEM((3, 8, shards[0].shape[0], 768), BF16),
            pltpu.VMEM((6, 8, 64, 384), BF16),
            pltpu.VMEM((6, 4, 64, 256), BF16),
            pltpu.VMEM((6, 4, 64, 256), BF16),
            pltpu.VMEM((48, 128, 128), BF16),
            pltpu.VMEM((48, 256, 128), BF16),
            pltpu.VMEM((count, 128), BF16),
            pltpu.VMEM((count, 128), F32),
            pltpu.VMEM((8, 64, 128), BF16),
            pltpu.VMEM((4, 64, 128), BF16),
            pltpu.VMEM((4, 64, 128), BF16),
            pltpu.VMEM((4, 256, 128), F32),
            pltpu.VMEM((6, count, 384), BF16),
            pltpu.VMEM((6, 8, 64, 128), BF16),
            pltpu.VMEM((6, 8, 64, 128), BF16),
            pltpu.VMEM((9, 8, width), F32),
            pltpu.VMEM((8, 8, width), F32),
            dma((6, 20)), dma((6, 19)), dma((6,)), dma((8,)), dma((8,)),
            dma((7, 7)), dma((7, 7)), dma((7,)), dma((7, 2)), dma((7, 2)),
            dma((6, 7)), dma((6, 7)), dma((6,)), dma((6,)),
        ],
        compiler_params=pltpu.CompilerParams(
            collective_id=0, has_side_effects=True, vmem_limit_bytes=60 * 2**20
        ),
        name="forward_attention",
    )(x, clusters, segments, counted, norms, *shards)


class Reduce:
    def __init__(self, place, held, near, far, sum_x, from_y, sum_y, from_z, out, send_sems, recv_sems, grad=None, source=None, near_source=None, load_sems=None):
        self.place, self.held, self.grad = place, held, grad
        self.near, self.far, self.sum_x, self.from_y = near, far, sum_x, from_y
        self.sum_y, self.from_z, self.out = sum_y, from_z, out
        self.send_sems, self.recv_sems = send_sems, recv_sems
        self.rows, self.half = held.shape[2], held.shape[3]
        self.window = out.shape[1]
        self.owner = place.y // 2
        self.z = place.zhi * 4 + place.zlo
        self.final = jnp.logical_and(place.zhi == self.owner, place.core == place.zlo // 2)
        self.copies = {}
        if source is not None:
            self.loads = [pltpu.make_async_copy(source, held, load_sems.at[0])]
        self.begun = near_source is not None
        if self.begun:
            self.loads.append(pltpu.make_async_copy(near_source, near, load_sems.at[1]))

    def send(self, k, source, target, device):
        copy = remote(source, target, self.send_sems.at[k], self.recv_sems.at[k], device)
        copy.start()
        self.copies[k] = copy

    def each(self, count, body):
        def step(i, carry):
            body(pl.ds(pl.multiple_of(i * 48, 16), 48))
            return carry

        lax.fori_loop(0, count // 48, step, 0)

    def after(self, rows, offset):
        return pl.ds(pl.multiple_of(rows.start + offset, 16), rows.size)

    def blocks(self, body):
        def step(zh, carry):
            body(zh)
            return carry

        lax.fori_loop(0, 2, step, 0)

    def start(self):
        place = self.place
        self.send(0, self.grad.at[:, :, :, half_of(2 * self.half, 1 - place.core)], self.held, place.sibling())

    def add_pair(self, xx):
        mine = half_of(2 * self.half, self.place.core)

        def block(zh):
            def body(rows):
                self.held[zh, xx, rows, :] = (
                    self.grad[zh, xx, rows, mine].astype(F32) + self.held[zh, xx, rows, :].astype(F32)
                ).astype(BF16)

            self.each(self.rows, body)

        self.blocks(block)

    def to_opposite(self):
        place = self.place
        half = self.rows // 2
        opposite = (place.x + 2) % 4
        if self.grad is None:
            self.loads[0].wait()
        else:
            self.copies[0].wait_recv()
            self.add_pair(opposite)
        self.send(1, self.held.at[:, opposite, 0:half], self.near.at[0], place.x_peer(1))
        self.send(2, self.held.at[:, opposite, half : self.rows], self.near.at[1], place.x_peer(3))
        if self.grad is not None:
            for step in (1, 3, 0):
                self.add_pair((place.x + step) % 4)

    def to_near(self):
        place = self.place
        half = self.rows // 2
        if self.begun:
            for copy in self.loads:
                copy.wait()
        for k, step in enumerate((1, 3)):
            to = (place.x + step) % 4
            if not self.begun:
                self.copies[1 + k].wait_recv()

            def block(zh, k=k, to=to):
                def body(rows):
                    there = self.after(rows, k * half)
                    self.held[zh, to, there, :] = (
                        self.held[zh, to, there, :].astype(F32) + self.near[k, zh, rows, :].astype(F32)
                    ).astype(BF16)

                self.each(half, body)

            self.blocks(block)
            self.send(3 + k, self.held.at[:, to], self.far.at[k], place.x_peer(step))

    def to_y(self):
        place = self.place
        half = self.rows // 2
        for k in range(2):
            self.copies[3 + k].wait_recv()

        def block(zh):
            def body(rows):
                value = self.held[zh, place.x, rows, :].astype(F32)
                value = value + self.far[0, zh, rows, :].astype(F32) + self.far[1, zh, rows, :].astype(F32)
                self.sum_x[zh, rows, :] = value.astype(BF16)

            self.each(self.rows, body)

        self.blocks(block)
        for k, d in enumerate((1, 2, 3)):
            to = (place.y + d) % 4
            part = pl.ds(pl.multiple_of((to % 2) * half, 16), half)
            self.send(5 + k, self.sum_x.at[to // 2, part], self.from_y.at[k], place.y_peer(d))

    def lanes(self, zlo):
        offset = (zlo % 2) * (self.half - self.window)
        return pl.ds(pl.multiple_of(offset, 128), self.window)

    def z_copy(self, k):
        place = self.place
        zlo = 2 * place.core + k
        return remote(
            self.sum_y.at[:, self.lanes(zlo)], self.from_z.at[self.z],
            self.send_sems.at[8 + k], self.recv_sems.at[8 + self.z], place.at(zlo=zlo, zhi=self.owner),
        )

    def is_target(self, k):
        place = self.place
        return jnp.logical_and(place.zhi == self.owner, place.zlo == 2 * place.core + k)

    def to_z(self):
        place = self.place
        half = self.rows // 2
        for k in range(3):
            self.copies[5 + k].wait_recv()

        def body(rows):
            value = self.sum_x[self.owner, self.after(rows, (place.y % 2) * half), :].astype(F32)
            for k in range(3):
                value = value + self.from_y[k, rows, :].astype(F32)
            self.sum_y[rows, :] = value.astype(BF16)

        self.each(half, body)
        for k in range(2):
            @pl.when(jnp.logical_not(self.is_target(k)))
            def _(k=k):
                self.z_copy(k).start()

    def spread_copy(self, k, device):
        half = self.rows // 2
        part = self.out.at[pl.ds(pl.multiple_of((self.place.y % 2) * half, 16), half)]
        return remote(part, part, self.send_sems.at[10 + k], self.recv_sems.at[16 + self.place.y % 2], device)

    def spread(self):
        half = self.rows // 2

        @pl.when(self.final)
        def _():
            self.from_z[self.z] = self.sum_y[:, self.lanes(self.place.zlo)]
            for z in range(8):
                @pl.when(self.z != z)
                def _(z=z):
                    part = self.from_z.at[z]
                    remote(part, part, self.send_sems.at[8], self.recv_sems.at[8 + z], self.place.sibling()).wait_recv()

            def body(rows):
                there = self.after(rows, (self.place.y % 2) * half)
                value = self.from_z[0, rows, :].astype(F32)
                for z in range(1, 8):
                    value = value + self.from_z[z, rows, :].astype(F32)
                self.out[there, :] = value.astype(BF16)

            self.each(half, body)
            for k, device in enumerate(self.place.plane()):
                self.spread_copy(k, device).start()

    def finish(self):
        half = self.rows // 2
        for k in range(2):
            part = self.out.at[k * half : (k + 1) * half]

            @pl.when(jnp.logical_not(jnp.logical_and(self.final, self.place.y % 2 == k)))
            def _(k=k, part=part):
                remote(part, part, self.send_sems.at[10], self.recv_sems.at[16 + k], self.place.sibling()).wait_recv()

    def drain(self):
        for k in self.copies:
            self.copies[k].wait_send()
        for k in range(2):
            @pl.when(jnp.logical_not(self.is_target(k)))
            def _(k=k):
                self.z_copy(k).wait_send()

        @pl.when(self.final)
        def _():
            for k, device in enumerate(self.place.plane()):
                self.spread_copy(k, device).wait_send()


def reduce_scratch(rows, half, window):
    return [
        pltpu.VMEM((2, 4, rows, half), BF16),
        pltpu.VMEM((2, 2, rows // 2, half), BF16),
        pltpu.VMEM((2, 2, rows, half), BF16),
        pltpu.VMEM((2, rows, half), BF16),
        pltpu.VMEM((3, rows // 2, half), BF16),
        pltpu.VMEM((rows // 2, half), BF16),
        pltpu.VMEM((8, rows // 2, window), BF16),
        pltpu.VMEM((rows, window), BF16),
    ]


def cut(value, offset, target):
    rows, width = value.shape
    first = pltpu.roll(value, (width - offset) % width, 1)[:, 0:128]
    if target.shape[0] == rows:
        target[...] = first[:, : target.shape[1]]
        return
    if rows % 128:
        first = jnp.concatenate([first, jnp.zeros((128 - rows % 128, 128), F32)], axis=0)
    target[...] = first.T[: target.shape[0], :rows]


ORDER = (0, 3, 1, 4, 2, 5)


def backward_kernel(*refs):
    (grad_mixed, grad_first, logsum, slot_row, slot_col, small, x_hbm, fq_hbm, got_hbm, before_hbm, after_hbm,
     hot_hbm, cold_hbm, go, gu, gd, near_u, near_d) = refs[:18]
    refs = refs[2:]
    grad_x, out_q, out_o, out_u, out_d, norms_out, loss_out = refs[16:23]
    x_turned, fq, got, before, after, hot, cold = refs[23:30]
    sent, got_grad, grads, to_before, to_after, from_before, from_after, back = refs[30:38]
    grads_q = refs[38:41]
    reduce_refs = [refs[41 + 8 * i : 49 + 8 * i] for i in range(6)]
    (tile, slots, a_send, a_recv, a_local, z_send, z_recv, b_send, b_recv, b_local,
     t_send, t_recv, r_send, r_recv, r_load, l_sem) = refs[89:]
    place = Place()
    plane, rank = place.plane(), place.rank()
    up, down = place.z_peer(1), place.z_peer(-1)
    loads = [
        pltpu.make_async_copy(source, target, l_sem.at[i])
        for i, (source, target) in enumerate(
            ((got_hbm, got), (before_hbm, before), (after_hbm, after), (hot_hbm, hot), (cold_hbm, cold),
             (fq_hbm, fq), (x_hbm, x_turned))
        )
    ]
    rest = [
        Reduce(
            place, *reduce_refs[i], r_send.at[i], r_recv.at[i], source=source, near_source=near, load_sems=r_load.at[i]
        )
        for i, (source, near) in enumerate(((go, None), (gu, near_u), (gd, near_d)))
    ]
    by_group = [
        Reduce(place, *reduce_refs[3 + i], r_send.at[3 + i], r_recv.at[3 + i], grad=grads_q[i]) for i in range(3)
    ]
    for r in (rest[2], rest[1], rest[0]):
        for copy in r.loads:
            copy.start()
    for copy in loads:
        copy.start()
    greet(plane + [place.x_peer(d) for d in (1, 2, 3)] + [place.z_peer(d) for d in range(1, 8)])
    sum_o, sum_u, sum_d = rest
    sum_o.to_opposite()
    tile[0] = small[...]
    doubling = Doubling(place, tile, slots, t_send, t_recv)
    doubling.start()
    count = grad_mixed.shape[0]
    ranks = [dev[0] % 8 for dev in plane]

    def block(which):
        return pl.ds(pl.multiple_of(which * 64, 64), 64)

    def send_copies(p, fn):
        for k, to in enumerate(ranks):
            fn(remote(sent.at[p, block(to)], got_grad.at[p, rank], a_send.at[p, k], a_recv.at[p, k], plane[k]))

    def own_copy(p):
        return pltpu.make_async_copy(sent.at[p, block(rank)], got_grad.at[p, rank], a_local.at[p])

    def leave(i, carry):
        p = i // 2 + 3 * (i % 2)
        rows = grad_mixed[:, pl.ds(pl.multiple_of(p * 128, 128), 128)]
        moved = [matmul(to_slots(slot_row, 2 * p + a, count), rows) for a in range(2)]
        sent[p] = pair_select(moved[0], moved[1]).astype(BF16)
        send_copies(p, lambda copy: copy.start())
        own_copy(p).start()
        return carry

    lax.fori_loop(0, 6, leave, 0)
    doubling.advance()
    sum_d.to_near()
    sum_u.to_near()
    for copy in loads[:5]:
        copy.wait()

    def halo(p):
        return (
            remote(to_after.at[p], from_before.at[p], z_send.at[p, 0], z_recv.at[p, 0], up),
            remote(to_before.at[p], from_after.at[p], z_send.at[p, 1], z_recv.at[p, 1], down),
        )

    def back_copies(p, fn):
        for k, to in enumerate(ranks):
            fn(remote(grads.at[p, to], back.at[p, rank], b_send.at[p, k], b_recv.at[p, k], plane[k]))

    def own_back(p):
        return pltpu.make_async_copy(grads.at[p, rank], back.at[p, rank], b_local.at[p])

    masks = [head_mask(a) for a in range(2)]

    def attend(p):
        own_copy(p).wait()
        send_copies(p, lambda copy: copy.wait_recv())
        for j in range(4):
            r = rows16(j)
            query = got[p, :, r, 0:128].reshape(128, 128)
            keys = jnp.concatenate(
                [before[p, :, r, 0:128].reshape(64, 128), got[p, :, r, 128:256].reshape(128, 128),
                 after[p, :, r, 0:128].reshape(64, 128)], axis=0)
            values = jnp.concatenate(
                [before[p, :, r, 128:256].reshape(64, 128), got[p, :, r, 256:384].reshape(128, 128),
                 after[p, :, r, 128:256].reshape(64, 128)], axis=0)
            grad = got_grad[p, :, r, :].reshape(128, 128)
            queries = [query * masks[a] for a in range(2)]
            grad_both = jnp.concatenate([grad * masks[a] for a in range(2)], axis=0)
            grad_probs = matmul(values, grad_both, NT)
            probs, grad_scores = [], []
            for a in range(2):
                head = 2 * p + a
                scores = matmul(
                    jnp.concatenate([keys, cold[head * 4 + j]], axis=1),
                    jnp.concatenate([queries[a], hot[head * 4 + j]], axis=1), NT)
                prob = jnp.exp(scores - logsum[j, pl.ds(head, 1), :])
                own = grad_probs[:, a * 128 : a * 128 + 128]
                delta = jnp.sum(prob * own, axis=0, keepdims=True)
                probs.append(prob.astype(BF16))
                grad_scores.append((prob * (own - delta)).astype(BF16))
            grad_scores = jnp.concatenate(grad_scores, axis=1)
            dk = matmul(grad_scores, jnp.concatenate(queries, axis=0))
            dv = matmul(jnp.concatenate(probs, axis=1), grad_both)
            dq = heads_home(matmul(keys, grad_scores, TN)) * 0.125
            both = jnp.concatenate([dk, dv], axis=1).astype(BF16)
            to_before[p, :, r, :] = both[0:64].reshape(4, 16, 256)
            to_after[p, :, r, :] = both[192:256].reshape(4, 16, 256)
            grads[p, :, r, 0:128] = dq.astype(BF16).reshape(8, 16, 128)
            grads[p, :, r, 128:384] = both[64:192].reshape(8, 16, 256)
        for copy in halo(p):
            copy.start()

    def give(p):
        for copy in halo(p):
            copy.wait_recv()
        for part, extra in ((slice(0, 4), from_before), (slice(4, 8), from_after)):
            grads[p, part, :, 128:384] = (
                grads[p, part, :, 128:384].astype(F32) + extra[p].astype(F32)
            ).astype(BF16)
        back_copies(p, lambda copy: copy.start())
        own_back(p).start()

    def home(p):
        own_back(p).wait()
        back_copies(p, lambda copy: copy.wait_recv())
        rows = back[p].reshape(count, 384)
        moved = [matmul(to_tokens(slot_col, 2 * p + a, count), rows) for a in range(2)]
        grad_qkv = pair_select(moved[0], moved[1]).astype(BF16)
        back[p] = grad_qkv.reshape(8, 64, 384)
        weight = matmul(x_turned[...], grad_qkv).astype(BF16)
        group, late = p % 3, p // 3
        for t, lane in enumerate((late, 2 + late, 4 + late)):
            grads_q[group][:, :, :, lane * 128 : lane * 128 + 128] = weight[:, t * 128 : t * 128 + 128].reshape(2, 4, 96, 128)

    def turn_back(i):
        rows = slice(i * 128, i * 128 + 128)
        value = grad_first[rows, :]
        for g in range(3):
            pair = [back[2 * g + b, 2 * i : 2 * i + 2].reshape(128, 384) for b in range(2)]
            value = value + matmul(jnp.concatenate(pair, axis=1), fq[g].reshape(768, 768), NT)
        grad_x[rows, :] = value

    attend(0)
    doubling.advance()
    attend(3)
    sum_o.to_near()
    attend(1)
    give(0)
    give(3)
    attend(4)
    give(1)
    doubling.advance()
    attend(2)
    give(4)
    sum_d.to_y()
    attend(5)
    give(2)
    give(5)
    for copy in loads[5:]:
        copy.wait()
    home(0)
    home(3)
    by_group[0].start()
    sum_u.to_y()
    home(1)
    doubling.advance()
    by_group[0].to_opposite()
    sum_o.to_y()
    home(4)
    by_group[1].start()
    sum_d.to_z()
    by_group[0].to_near()
    home(2)
    doubling.advance()
    by_group[1].to_opposite()
    home(5)
    by_group[2].start()
    doubling.advance()
    sum_u.to_z()
    by_group[0].to_y()
    by_group[1].to_near()
    by_group[2].to_opposite()
    sum_o.to_z()
    turn_back(0)
    doubling.advance()
    by_group[1].to_y()
    by_group[0].to_z()
    by_group[2].to_near()
    sum_d.spread()
    turn_back(1)
    by_group[1].to_z()
    by_group[2].to_y()
    sum_u.spread()
    sum_o.spread()
    by_group[0].spread()
    turn_back(2)
    by_group[2].to_z()
    doubling.advance()
    by_group[1].spread()

    def settle(p, carry):
        send_copies(p, lambda copy: copy.wait_send())
        back_copies(p, lambda copy: copy.wait_send())
        for copy in halo(p):
            copy.wait_send()
        return carry

    lax.fori_loop(0, 6, settle, 0)
    seat = place.y * 2 + place.core
    for r, target in zip((sum_d, sum_u, sum_o), (out_d, out_u, out_o)):
        r.finish()
        width = r.half // 16
        offset = (place.zlo % 2) * (8 * width - (r.half - r.window)) + seat * width
        cut(r.out[...].astype(F32), offset, target)
    turn_back(3)
    for r in by_group[:2]:
        r.finish()
    by_group[2].spread()
    total = tile[8]
    loss_out[...] = total[4:5, 0:1]
    all_width = total.shape[1]
    shift = (all_width - (place.ctx * 8 + place.wsh) * norms_out.shape[1]) % all_width
    norms_out[...] = pltpu.roll(total, shift, 1)[0:4, 0 : norms_out.shape[1]]
    for r in rest + by_group[:2]:
        r.drain()
    by_group[2].finish()
    tiles = [by_group[g].out[:, i * 128 : i * 128 + 128].astype(F32) for i in range(3) for g in range(3)]
    width = 72
    cut(jnp.concatenate(tiles, axis=1), (place.zlo % 2) * 8 * width + seat * width, out_q)
    by_group[2].drain()
    doubling.drain()


def backward(grad_mixed, grad_first, small, x_turned, fq, kept, halves, nears):
    got, before, after, logsum, hot, cold, slot_row, slot_col = kept
    count = grad_mixed.shape[0]
    dma = pltpu.SemaphoreType.DMA
    vm = pltpu.VMEM
    rows_in = (halves[2].shape[2],)
    shapes = [(96, 384, 256), (96, 1536, 768), (rows_in[0], 384, 256)] + [(96, 384, 384)] * 3
    reduce_refs = []
    for shape in shapes:
        reduce_refs += reduce_scratch(*shape)
    loaded = (x_turned, fq, got, before, after, hot, cold)
    results = pl.pallas_call(
        backward_kernel,
        out_shape=[
            shaped(*grad_first.shape, dtype=F32),
            shaped(72, 96, dtype=F32),
            shaped(24, 96, dtype=F32),
            shaped(96, 96, dtype=F32),
            shaped(24, 384, dtype=F32),
            shaped(4, small.shape[1] // 256, dtype=F32),
            shaped(1, 1, dtype=F32),
        ],
        in_specs=[VMEM] * 6 + [ANY] * 12,
        out_specs=[VMEM] * 7,
        scratch_shapes=[vm(array.shape, array.dtype) for array in loaded]
        + [
            vm((6, count, 128), BF16),
            vm((6, 8, 64, 128), BF16),
            vm((6, 8, 64, 384), BF16),
            vm((6, 4, 64, 256), BF16),
            vm((6, 4, 64, 256), BF16),
            vm((6, 4, 64, 256), BF16),
            vm((6, 4, 64, 256), BF16),
            vm((6, 8, 64, 384), BF16),
        ]
        + [vm((2, 4, 96, 768), BF16)] * 3
        + reduce_refs
        + [
            vm((9, *small.shape), F32),
            vm((8, *small.shape), F32),
            dma((6, 7)), dma((6, 7)), dma((6,)), dma((6, 2)), dma((6, 2)),
            dma((6, 7)), dma((6, 7)), dma((6,)),
            dma((8,)), dma((8,)), dma((6, 17)), dma((6, 18)), dma((3, 2)), dma((7,)),
        ],
        compiler_params=pltpu.CompilerParams(
            collective_id=1, has_side_effects=True, vmem_limit_bytes=62 * 2**20
        ),
        name="backward_attention",
    )(grad_mixed, grad_first, logsum, slot_row, slot_col, small, *loaded, *halves, *nears)
    return results


CHUNK = 512


def norm_rows(values):
    centered = values - jnp.mean(values, axis=-1, keepdims=True)
    scale = lax.rsqrt(jnp.mean(centered * centered, axis=-1, keepdims=True) + 1e-05)
    return centered * scale, scale


def norm_rows_back(grad, normed, scale, gain):
    weighted = grad * gain
    return scale * (
        weighted
        - jnp.mean(weighted, axis=-1, keepdims=True)
        - normed * jnp.mean(weighted * normed, axis=-1, keepdims=True)
    )


def middle_kernel(
    everyone, ctx_size,
    mixed, x, teacher, slot_col, total, wo_hbm, wu_hbm, wd_hbm,
    result, grad_first, grad_mixed, small, go_hbm, gu_hbm, gd_hbm, near_u, near_d,
    wo, wu, wd, active, slope, normed, unit, scale, low, low_turned, acc, branch, grad_upper, go, gu, gd,
    held_o, held_u, held_d, in_sem, out_sem, send_sem, recv_sem, x_send, x_recv,
):
    place = Place()
    core, sibling = place.core, place.sibling()
    loads = [
        pltpu.make_async_copy(source, target, in_sem.at[i])
        for i, (source, target) in enumerate(((wo_hbm, wo), (wu_hbm, wu), (wd_hbm, wd)))
    ]
    for copy in loads:
        copy.start()
    greet([sibling, place.x_peer(1), place.x_peer(3)])
    count, width = x.shape
    tile = 128
    chunks = wd.shape[0] // CHUNK
    gains = total[0:4] / ctx_size
    small[...] = jnp.zeros_like(small)

    def rows_of(i):
        return pl.ds(pl.multiple_of(i * tile, tile), tile)

    def lanes_of(c):
        return pl.ds(pl.multiple_of(c * CHUNK, CHUNK), CHUNK)

    loads[0].wait()
    for i in range(2):
        rows = slice(i * 256, i * 256 + 256)
        acc[rows, :] = matmul(mixed[rows, :], wo[...])

    def first_norm(i, carry):
        rows = rows_of(i)
        unit_rows, scale_rows = norm_rows(x[rows, :].astype(F32) + acc[rows, :])
        unit[rows, :] = unit_rows
        scale[rows, :] = scale_rows
        value = unit_rows * gains[0:1] + gains[1:2]
        normed[rows, :] = value
        low[rows, :] = value.astype(BF16)
        acc[rows, :] = value
        return carry

    lax.fori_loop(0, count // tile, first_norm, 0)
    loads[1].wait()
    loads[2].wait()

    def expand(c, carry):
        lanes = lanes_of(c)
        up = wu[:, :, lanes].reshape(width, CHUNK)
        down = wd[lanes, :]
        for i in range(2):
            rows = slice(i * 256, i * 256 + 256)
            upper = matmul(low[rows, :], up)
            share = 0.5 + 0.5 * lax.erf(upper * 0.7071067811865476)
            density = jnp.exp(upper * upper * -0.5) * 0.3989422804014327
            value = (upper * share).astype(BF16)
            active[rows, lanes] = value
            slope[rows, lanes] = share + upper * density
            acc[rows, :] += matmul(value, down)
        return carry

    lax.fori_loop(0, chunks, expand, 0)
    low_turned[...] = normed[...].T.astype(BF16)

    def second_norm(i, carry):
        rows = rows_of(i)
        unit_rows, scale_rows = norm_rows(acc[rows, :])
        value = unit_rows * gains[2:3] + gains[3:4]
        result[rows, :] = value.astype(BF16)
        error = value - teacher[rows, :].astype(F32)
        mask = slot_col[rows, 12:13]
        losses = mask * jnp.mean(error * error, axis=-1, keepdims=True)
        grad = (everyone / total[4:5, 0:1]) * mask * error
        small[2:3, :] += jnp.sum(grad * unit_rows, axis=0, keepdims=True)
        small[3:4, :] += jnp.sum(grad, axis=0, keepdims=True)
        small[4:5, 0:1] += jnp.sum(losses, axis=0, keepdims=True) / total[4:5, 0:1]
        back = norm_rows_back(grad, unit_rows, scale_rows, gains[2:3])
        acc[rows, :] = back
        branch[rows, :] = back.astype(BF16)
        return carry

    lax.fori_loop(0, count // tile, second_norm, 0)

    half = chunks // 2
    theirs, ours = half_of(width, 1 - core), half_of(width, core)

    def down_copy(c):
        lanes = lanes_of(c)
        return remote(gd.at[lanes, theirs], held_d.at[lanes], send_sem.at[c], recv_sem.at[c], sibling)

    def up_copy(i):
        return remote(gu.at[i], held_u.at[i], send_sem.at[chunks + i], recv_sem.at[chunks + i], sibling)

    def up_out(i):
        return pltpu.make_async_copy(held_u.at[i], gu_hbm.at[:, :, lanes_of(i)], out_sem.at[chunks + i])

    deep = wd.shape[0] // 16
    shallow = width // 16

    def opposite(zh):
        return zh * 4 + (place.x + 2) % 4

    def down_across(k, zh):
        part = pl.ds(pl.multiple_of(opposite(zh) * 2 * deep + k * deep, 16), deep)
        return remote(
            held_d.at[part], near_d.at[k, zh], x_send.at[2 * k + zh], x_recv.at[2 * k + zh], place.x_peer(1 + 2 * k)
        )

    def up_across(i, k, zh):
        n = 4 + i * 4 + 2 * k + zh
        return remote(
            held_u.at[i, opposite(zh), k * shallow : (k + 1) * shallow], near_u.at[k, zh, :, lanes_of(i)],
            x_send.at[n], x_recv.at[n], place.x_peer(1 + 2 * k),
        )

    def make_down(c, carry):
        lanes = lanes_of(c)
        gd[lanes, :] = matmul(active[:, lanes], branch[...], TN).astype(BF16)
        down_copy(c).start()
        return carry

    lax.fori_loop(0, chunks, make_down, 0)

    def contract(c):
        lanes = lanes_of(c)
        up = wu[:, :, lanes].reshape(width, CHUNK)
        down = wd[lanes, :]
        for i in range(2):
            rows = slice(i * 256, i * 256 + 256)
            value = (matmul(branch[rows, :], down, NT) * slope[rows, lanes]).astype(BF16)
            grad_upper[rows, :] = value
            acc[rows, :] += matmul(value, up, NT)
        return matmul(low_turned[...], grad_upper[...]).reshape(8, width // 8, CHUNK)

    def for_sibling(i, carry):
        gu[i] = contract((1 - core) * half + i).astype(BF16)
        up_copy(i).start()
        return carry

    def for_own(i, carry):
        value = contract(core * half + i)
        up_copy(i).wait_recv()
        held_u[i] = (value + held_u[i].astype(F32)).astype(BF16)
        up_out(i).start()
        for k in range(2):
            for zh in range(2):
                up_across(i, k, zh).start()
        return carry

    def down_out(c):
        lanes = lanes_of(c)
        return pltpu.make_async_copy(held_d.at[lanes], gd_hbm.at[lanes], out_sem.at[c])

    def add_down(c, carry):
        lanes = lanes_of(c)
        down_copy(c).wait_recv()
        held_d[lanes, :] = (gd[lanes, ours].astype(F32) + held_d[lanes, :].astype(F32)).astype(BF16)
        down_out(c).start()
        return carry

    lax.fori_loop(0, chunks, add_down, 0)
    for k in range(2):
        for zh in range(2):
            down_across(k, zh).start()
    lax.fori_loop(0, half, for_sibling, 0)
    lax.fori_loop(0, half, for_own, 0)

    def first_back(i, carry):
        rows = rows_of(i)
        grad = acc[rows, :]
        small[0:1, :] += jnp.sum(grad * unit[rows, :], axis=0, keepdims=True)
        small[1:2, :] += jnp.sum(grad, axis=0, keepdims=True)
        back = norm_rows_back(grad, unit[rows, :], scale[rows, :], gains[0:1])
        grad_first[rows, :] = back
        branch[rows, :] = back.astype(BF16)
        return carry

    lax.fori_loop(0, count // tile, first_back, 0)
    go[...] = matmul(mixed[...], branch[...], TN).astype(BF16)
    last = remote(go.at[:, theirs], held_o, send_sem.at[chunks + half], recv_sem.at[chunks + half], sibling)
    last.start()
    for i in range(2):
        rows = slice(i * 256, i * 256 + 256)
        grad_mixed[rows, :] = matmul(branch[rows, :], wo[...], NT).astype(BF16)

    last.wait_recv()
    held_o[...] = (go[:, ours].astype(F32) + held_o[...].astype(F32)).astype(BF16)
    out = pltpu.make_async_copy(held_o, go_hbm, in_sem.at[0])
    out.start()

    def settle_down(c, carry):
        down_copy(c).wait_send()
        down_out(c).wait()
        return carry

    def settle_up(i, carry):
        up_copy(i).wait_send()
        up_out(i).wait()
        return carry

    lax.fori_loop(0, chunks, settle_down, 0)
    lax.fori_loop(0, half, settle_up, 0)
    last.wait_send()
    for k in range(2):
        for zh in range(2):
            down_across(k, zh).wait()
            for i in range(half):
                up_across(i, k, zh).wait()
    out.wait()


def middle(everyone, ctx_size, mixed, x, teacher, slot_col, total, wo, wu, wd):
    count, width = x.shape
    hidden = wd.shape[0]
    chunks = hidden // CHUNK
    dma = pltpu.SemaphoreType.DMA
    vm = pltpu.VMEM
    return pl.pallas_call(
        functools.partial(middle_kernel, everyone, ctx_size),
        out_shape=[
            shaped(count, width),
            shaped(count, width, dtype=F32),
            shaped(count, width),
            shaped(8, width, dtype=F32),
            shaped(width, width // 2),
            shaped(8, width // 8, hidden // 2),
            shaped(hidden, width // 2),
            shaped(2, 2, width // 16, hidden // 2),
            shaped(2, 2, hidden // 16, width // 2),
        ],
        in_specs=[VMEM] * 5 + [ANY] * 3,
        out_specs=[VMEM] * 4 + [ANY] * 5,
        scratch_shapes=[
            vm(wo.shape, BF16), vm(wu.shape, BF16), vm(wd.shape, BF16),
            vm((count, hidden), BF16), vm((count, hidden), F32),
            vm((count, width), F32), vm((count, width), F32), vm((count, 1), F32),
            vm((count, width), BF16), vm((width, count), BF16), vm((count, width), F32),
            vm((count, width), BF16), vm((count, CHUNK), BF16),
            vm(wo.shape, BF16), vm((chunks // 2, 8, width // 8, CHUNK), BF16), vm(wd.shape, BF16),
            vm((width, width // 2), BF16), vm((chunks // 2, 8, width // 8, CHUNK), BF16), vm((hidden, width // 2), BF16),
            dma((3,)), dma((chunks + chunks // 2,)), dma((chunks + chunks // 2 + 1,)), dma((chunks + chunks // 2 + 1,)),
            dma((4 + 2 * chunks,)), dma((4 + 2 * chunks,)),
        ],
        compiler_params=pltpu.CompilerParams(
            collective_id=2, has_side_effects=True, vmem_limit_bytes=62 * 2**20
        ),
        name="dense_middle",
    )(mixed, x, teacher, slot_col, total, wo, wu, wd)


def local(tokens, teacher, clusters, segments, counted, w_qkv, w_out, w_up, w_down, norms):
    x_rows = tokens[0]
    tok_count, model_dim = x_rows.shape
    ctx_size, wsh_size = lax.axis_size("ctx"), lax.axis_size("wsh")
    mixed, x_turned, fq, fo, fu, fd, *kept, total = forward(
        x_rows, clusters[0], segments, counted, norms, (w_qkv, w_out, w_up, w_down)
    )
    everyone = float(tok_count * ctx_size * wsh_size)
    result, grad_first, grad_mixed, small, go, gu, gd, *nears = middle(
        everyone, float(ctx_size), mixed, x_rows, teacher[0], kept[-1], total,
        fo.reshape(-1, model_dim), fu, fd.reshape(-1, model_dim),
    )
    grad_tokens, final_qkv, final_out, final_up, final_down, final_norms, loss = backward(
        grad_mixed, grad_first, small, x_turned, fq, kept,
        [g.reshape(2, 4, -1, g.shape[-1]) for g in (go, gu, gd)], nears,
    )
    return (
        result[None],
        grad_tokens[None],
        loss.reshape(()),
        final_qkv.T,
        final_out.T,
        final_up,
        final_down.T,
        final_norms,
    )


def solution(mesh):
    placed = (
        P("wsh", "ctx", None),
        P("wsh", "ctx", None),
        P("wsh", None, "ctx"),
        P("wsh", "ctx"),
        P("wsh", "ctx"),
        P("wsh", None),
        P("wsh", None),
        P("wsh", None),
        P("wsh", None),
        P(None, "wsh"),
    )
    return jax.shard_map(
        local,
        mesh=mesh,
        in_specs=placed,
        out_specs=(
            P("wsh", "ctx", None),
            P("wsh", "ctx", None),
            P(),
            P("wsh", "ctx"),
            P("wsh", "ctx"),
            P("wsh", "ctx"),
            P("wsh", "ctx"),
            P(None, ("ctx", "wsh")),
        ),
        check_vma=False,
    )
```
